32 devices in a mesh: dp: 8 (over z, y), expert: 4 (over x, core).
Axes of the slice: x: 2, y: 2, z: 4, core: 2. Of those that a mesh axis runs over, the one named last changes fastest.
Arguments:
- tokens: bfloat16 [16, 1024, 384], P('dp', 'expert'), may hold values from -6 to 6
- task_ids: int32 [16], P('dp'), may hold values from 0 to 12
- attention_picks: int32 [16, 1024, 4], P('dp', 'expert'), may hold values from 0 to 14, all different within a row
- feedforward_picks: int32 [8, 4, 512, 4], P('dp', 'expert'), may hold values from 0 to 14, all different within a row; in each aligned block of 512 rows (0 to 511, 512 to 1023, ..., all dimensions but the last counted through in order) at most 256 rows name the same one
- norm_gain: float32 [2, 384], replicated, may hold values from 0.5 to 1.5
- norm_bias: float32 [2, 384], replicated, may hold values from -1.2 to 1.2
- query_weight: bfloat16 [384, 960], replicated, may hold values from -0.3125 to 0.3125
- key_weight: bfloat16 [384, 64], replicated, may hold values from -0.3125 to 0.3125
- value_weight: bfloat16 [384, 64], replicated, may hold values from -0.3125 to 0.3125
- output_weight: bfloat16 [960, 384], replicated, may hold values from -24 to 24
- attention_router: bfloat16 [13, 384, 15], replicated, may hold values from -0.15625 to 0.15625
- feedforward_router: bfloat16 [13, 384, 15], replicated, may hold values from -0.15625 to 0.15625
- expand_weight: bfloat16 [16, 384, 1536], P('expert'), may hold values from -0.3125 to 0.3125
- reduce_weight: bfloat16 [16, 1536, 384], P('expert'), may hold values from -0.3125 to 0.3125
- cotangent: bfloat16 [16, 1024, 384], P('dp', 'expert'), may hold values from -6 to 6
Outputs:
- output: bfloat16 [16, 1024, 384], P('dp', 'expert')
- grad_tokens: float32 [16, 1024, 384], P('dp', 'expert')
- grad_norm_gain: float32 [2, 384], replicated
- grad_first_bias: float32 [384], replicated
- grad_second_bias: float32 [384], replicated
- grad_query_weight: float32 [384, 960], replicated
- grad_key_weight: float32 [384, 64], replicated
- grad_value_weight: float32 [384, 64], replicated
- grad_output_weight: float32 [960, 384], replicated
- grad_attention_router: float32 [13, 384, 15], replicated
- grad_feedforward_router: float32 [13, 384, 15], replicated
- grad_expand_weight: float32 [16, 384, 1536], P('expert')
- grad_reduce_weight: float32 [16, 1536, 384], P('expert')
- usage: float32 [2, 13, 15], replicated
The draws below stay inside these ranges and needn't reach their ends.
Inputs may be any that keep to these rules, and one draw needn't show every extreme that they name: `attention_picks`: each row names 4 different attention experts. `feedforward_picks`: each row names 4 different feed-forward experts; among the 512 rows of one device no expert is named by more than 256 rows.
All inputs are finite; a program needn't handle non-finite values.
Results may differ from the reference program's by a relative error of at most 0.014.
Values may be sent and summed in bfloat16 or wider, within the bound.
A program may use at most 192 MiB of HBM per device.

```python
import math
import jax
import jax.numpy as jnp
import numpy as np
from jax import lax

D = 384
HEAD = 64
EXPERTS = 15
FF = 1536
TOPK = 4
TASKS = 13
PATCHES = 1024
TOK_DEV = 512
CAP = 256
IMG_DP = 2
PATCH_DEV = 256
IMAGES = 16
N_DP = 8
N_EXPERT = 4


def set_ends(drawn, rng, least, largest):
    shape = drawn.shape
    spot = [jax.random.randint(jax.random.fold_in(rng, axis), (), 0, shape[axis]) for axis in range(len(shape))]
    drawn = drawn.at[tuple(spot)].set(least)
    longest = shape.index(max(shape))
    spot[longest] = (spot[longest] + 1) % shape[longest]
    return drawn.at[tuple(spot)].set(largest)


def shard_levels(key, dims, cuts, smallest, high):
    def one(dim, shards_of):
        draws = jax.random.uniform(jax.random.fold_in(jax.random.fold_in(key, 6), dim), (shards_of,), jnp.float32, smallest / len(cuts), high / len(cuts))
        return jnp.repeat(jnp.exp(draws), dims[dim] // shards_of).reshape((-1,) + (1,) * (len(dims) - dim - 1))

    loudness = one(*cuts[0])
    for cut in cuts[1:]:
        loudness = loudness * one(*cut)
    return loudness


def choose_distinct(rng, rows, amount, top, lift):
    sequence = jax.random.permutation(jax.random.fold_in(rng, 1), amount)
    boost = sequence
    for power in range(3):
        boost = boost * boost // amount
    boost = boost * lift // amount
    tickets = jax.random.randint(jax.random.fold_in(rng, 2), (rows, amount), 0, 4096) + boost
    holders = jax.random.permutation(jax.random.fold_in(rng, 3), rows)[jnp.arange(amount) % rows]
    tickets = jnp.where(jnp.arange(rows)[:, None] == holders[None, :], 1 << 14, tickets)
    priority = tickets * amount + jnp.arange(amount)
    return lax.top_k(priority.astype(jnp.int32), top)[1].astype(jnp.int32)


def assign_block(rng, own, number, rows, count, top, bound, slope):
    sequence = jax.random.permutation(rng, count)
    crowded, ordinary = load_shares(count, rows * top, bound, slope, True), load_shares(count, rows * top, bound, slope, False)
    places = jnp.arange(count)

    def named(lengths, offset_by):
        used = int((lengths > 0).sum())
        fixed = max(1, used // 4)
        passed = fixed + (places - fixed + offset_by * (used - fixed)) % max(1, count - fixed)
        return jnp.zeros((count,), jnp.int32).at[sequence[jnp.where(places < fixed, places, passed)]].set(jnp.asarray(lengths, jnp.int32))

    lengths = jnp.where(number % 4 == 0, named(crowded, number // 4), named(ordinary, number - number // 4 - 1))
    mixed = jax.random.permutation(jax.random.fold_in(own, 3), count)
    giver, receiver = mixed[0:count // 2 * 2:2], mixed[1:count // 2 * 2:2]
    margin = jnp.minimum(lengths[giver] - 1, bound - lengths[receiver]) // 2
    margin = jnp.where((giver == sequence[0]) | (receiver == sequence[0]) | (lengths[receiver] == 0), 0, jnp.maximum(margin, 0))
    passed = jax.random.randint(jax.random.fold_in(own, 4), (count // 2,), 0, 1 << 20) % (margin + 1)
    lengths = lengths.at[giver].add(-passed).at[receiver].add(passed)
    members = jnp.searchsorted(jnp.cumsum(lengths), jnp.arange(rows * top), side="right").astype(jnp.int32)
    grid = members.reshape(top, rows).T
    grid = grid[jax.random.permutation(jax.random.fold_in(own, 1), rows)]
    offset_by = jax.random.randint(jax.random.fold_in(own, 2), (rows, 1), 0, top)
    return jnp.take_along_axis(grid, (jnp.arange(top)[None, :] + offset_by) % top, axis=1)


def load_shares(count, total, reach, skew, full):
    weights = [(1 << 20) // math.isqrt(standing ** skew) + 1 for standing in range(1, count + 1)]
    largest = reach if full else min(reach, max(-(-total // count), total * weights[0] // sum(weights)))
    least = 1 if total - largest >= count - 1 else 0
    given, spare = [largest] + [least] * (count - 1), total - largest - least * (count - 1)
    while spare > 0:
        candidates = [i for i in range(1, count) if given[i] < largest] or [i for i in range(1, count) if given[i] < reach]
        whole, budget = sum([weights[i] for i in candidates]), spare
        for i in candidates:
            extra = min(reach - given[i], max(1, budget * weights[i] // whole), spare)
            given[i] = given[i] + extra
            spare = spare - extra
    return np.array(given)


def normal_values(stream_key, shape, width, bound, cuts=(), held_as=jnp.bfloat16):
    level = shard_levels(stream_key, shape, cuts, -0.22, 0.18) if cuts else 1.0
    values = jax.random.normal(stream_key, shape, jnp.float32) * width * level
    return jnp.minimum(jnp.maximum(values, -bound), bound).astype(held_as)


def setup_inputs(seed: int = 0) -> dict:
    splits = jax.random.split(jax.random.key(seed), 16)
    tokens = normal_values(splits[0], (IMAGES, PATCHES, D), 1.0, 6.0, ((0, 8), (1, 4)))
    task_ids = set_ends(jax.random.randint(splits[1], (IMAGES,), 0, TASKS), jax.random.fold_in(splits[1], 1), 0, TASKS - 1).astype(jnp.int32)
    attention_picks = choose_distinct(splits[2], IMAGES * PATCHES, EXPERTS, TOPK, 4369).reshape((IMAGES, PATCHES, TOPK))
    feedforward_picks_keys = jax.random.split(jax.random.fold_in(splits[3], 1), N_DP * N_EXPERT * TOK_DEV // TOK_DEV)
    feedforward_picks_turns = jax.random.permutation(jax.random.fold_in(splits[3], 3), N_DP * N_EXPERT * TOK_DEV // TOK_DEV)
    feedforward_picks = jax.vmap(lambda own, number: assign_block(jax.random.fold_in(splits[3], 2), own, number, TOK_DEV, EXPERTS, TOPK, CAP, 2))(feedforward_picks_keys, feedforward_picks_turns).reshape((N_DP, N_EXPERT, TOK_DEV, TOPK))
    norm_gain = jnp.clip(1.0 + 0.1 * jax.random.normal(splits[4], (2, D), jnp.float32), 0.5, 1.5)
    norm_bias = normal_values(splits[5], (2, D), 0.2, 1.2, (), jnp.float32)
    query_weight = normal_values(splits[6], (D, EXPERTS * HEAD), D ** -0.5, 0.3125)
    key_weight = normal_values(splits[7], (D, HEAD), D ** -0.5, 0.3125)
    value_weight = normal_values(splits[8], (D, HEAD), D ** -0.5, 0.3125)
    output_weight = normal_values(splits[9], (EXPERTS * HEAD, D), 4.0, 24.0)
    attention_router = normal_values(splits[10], (TASKS, D, EXPERTS), (4 * D) ** -0.5, 0.15625)
    feedforward_router = normal_values(splits[11], (TASKS, D, EXPERTS), (4 * D) ** -0.5, 0.15625)
    expand_weight = normal_values(splits[12], (EXPERTS + 1, D, FF), D ** -0.5, 0.3125, ((0, 4),))
    reduce_weight = normal_values(splits[13], (EXPERTS + 1, FF, D), (FF // 4) ** -0.5, 0.3125, ((0, 4),))
    cotangent = normal_values(splits[14], (IMAGES, PATCHES, D), 1.0, 6.0, ((0, 8), (1, 4)))
    return dict(tokens=tokens, task_ids=task_ids, attention_picks=attention_picks, feedforward_picks=feedforward_picks, norm_gain=norm_gain, norm_bias=norm_bias, query_weight=query_weight, key_weight=key_weight, value_weight=value_weight, output_weight=output_weight, attention_router=attention_router, feedforward_router=feedforward_router, expand_weight=expand_weight, reduce_weight=reduce_weight, cotangent=cotangent)


EPS = 1e-06
HIGH = lax.Precision.HIGHEST

@jax.custom_vjp
def low(v):
    return lax.optimization_barrier(v.astype(jnp.bfloat16)).astype(jnp.float32)

@jax.custom_vjp
def low_back(v):
    return v

def low_keep(v):
    return (low(v), None)

def low_pass(kept, grad):
    return (grad,)

def back_keep(v):
    return (v, None)

def back_low(kept, grad):
    return (low(grad),)
low.defvjp(low_keep, low_pass)
low_back.defvjp(back_keep, back_low)

def normalize(value, gain, bias):
    mean = lax.optimization_barrier(jnp.mean(value, -1, keepdims=True))
    centred = value - mean
    spread = lax.optimization_barrier(jnp.mean(centred * centred, -1, keepdims=True))
    return centred * lax.rsqrt(spread + EPS) * gain + bias

def gate_weights(logits, picks_hot):
    chosen = lax.optimization_barrier(jnp.sum(picks_hot * logits[..., None, :], -1))
    return jax.nn.softmax(chosen, -1)

def activate(value):
    return jax.nn.gelu(value, approximate=True)

def to_blocks(array):
    tail = array.shape[2:]
    shaped = array.reshape((N_DP, IMG_DP, N_EXPERT, PATCH_DEV) + tail)
    shaped = jnp.moveaxis(shaped, 2, 1)
    return shaped.reshape((N_DP * N_EXPERT, TOK_DEV) + tail)

def from_blocks(array):
    tail = array.shape[2:]
    shaped = array.reshape((N_DP, N_EXPERT, IMG_DP, PATCH_DEV) + tail)
    shaped = jnp.moveaxis(shaped, 1, 2)
    return shaped.reshape((IMAGES, PATCHES) + tail)

def attend_image(parts):
    queries, keys, values = parts
    scores = low_back(jnp.einsum('pkh,sh->pks', queries, keys, precision=HIGH) * 0.125)
    probs = jax.nn.softmax(scores, -1)
    return low_back(jnp.einsum('pks,sh->pkh', low(probs), values, precision=HIGH))

def expert_apply(parts):
    received, expand, reduce_part = parts
    hidden = low_back(jnp.einsum('ncd,df->ncf', received, expand, precision=HIGH))
    activated = low(activate(hidden))
    return low(low_back(jnp.einsum('ncf,fd->ncd', activated, reduce_part, precision=HIGH)))

def slot_positions(choices):
    marks = (choices[..., None] == jnp.arange(EXPERTS, dtype=jnp.int32)).astype(jnp.int32)
    before = (jnp.cumsum(marks, axis=1) - marks).astype(jnp.int32)
    rank = lax.optimization_barrier(jnp.sum(before * marks, axis=-1)).astype(jnp.int32)
    return (choices * CAP + rank).astype(jnp.int32)

def reference(tokens, task_ids, attention_picks, feedforward_picks, norm_gain, norm_bias, query_weight, key_weight, value_weight, output_weight, attention_router, feedforward_router, expand_weight, reduce_weight, cotangent):
    blocks = N_DP * N_EXPERT
    feed_blocks = feedforward_picks.reshape(blocks, TOK_DEV, TOPK)
    feed_images = from_blocks(feed_blocks)
    expert_range = jnp.arange(EXPERTS, dtype=jnp.int32)
    attend_hot = (attention_picks[..., None] == expert_range).astype(jnp.float32)
    feed_hot = (feed_images[..., None] == expert_range).astype(jnp.float32)
    position = slot_positions(feed_blocks.reshape(blocks, TOK_DEV * TOPK))
    lanes = jnp.arange(blocks, dtype=jnp.int32)[:, None]

    def forward(inputs, gain, bias, query_w, key_w, value_w, output_w, router_one, router_two, expand_w, reduce_w):
        first = low(normalize(inputs, gain[0], bias[0]))
        logits_one = low_back(jnp.einsum('ipd,ide->ipe', first, router_one[task_ids], precision=HIGH))
        gates_one = gate_weights(logits_one, attend_hot)
        queries_all = low(low_back(jnp.einsum('ipd,dc->ipc', first, query_w, precision=HIGH)))
        queries_all = queries_all.reshape(IMAGES, PATCHES, EXPERTS, HEAD)
        queries = jnp.einsum('ipke,ipeh->ipkh', attend_hot, queries_all, precision=HIGH)
        keys = low(low_back(jnp.einsum('ipd,dh->iph', first, key_w, precision=HIGH)))
        values = low(low_back(jnp.einsum('ipd,dh->iph', first, value_w, precision=HIGH)))
        attended = lax.map(jax.checkpoint(attend_image), (queries, keys, values))
        weighted = gates_one[..., None] * attended
        heads = jnp.einsum('ipke,ipkh->ipeh', attend_hot, weighted, precision=HIGH).reshape(IMAGES, PATCHES, EXPERTS * HEAD)
        branch = low_back(jnp.einsum('ipc,cd->ipd', low(low_back(heads)), output_w, precision=HIGH))
        middle = inputs + branch
        second = low(normalize(middle, gain[1], bias[1]))
        logits_two = low_back(jnp.einsum('ipd,ide->ipe', second, router_two[task_ids], precision=HIGH))
        gates_two = gate_weights(logits_two, feed_hot)
        sent = jnp.repeat(to_blocks(second), TOPK, axis=1)
        buffer = jnp.zeros((blocks, EXPERTS * CAP, D), jnp.float32).at[lanes, position].set(sent)
        buffer = low_back(buffer)
        per_expert = jnp.transpose(buffer.reshape(blocks, EXPERTS, CAP, D), (1, 0, 2, 3))
        produced = lax.map(jax.checkpoint(expert_apply), (per_expert, expand_w[:EXPERTS], reduce_w[:EXPERTS]))
        produced = jnp.transpose(produced, (1, 0, 2, 3)).reshape(blocks, EXPERTS * CAP, D)
        picked = produced[lanes, position].reshape(blocks, TOK_DEV, TOPK, D)
        feed = jnp.einsum('ntk,ntkd->ntd', to_blocks(gates_two), picked, precision=HIGH)
        return middle + from_blocks(feed)
    params = (tokens.astype(jnp.float32), norm_gain, norm_bias, query_weight.astype(jnp.float32), key_weight.astype(jnp.float32), value_weight.astype(jnp.float32), output_weight.astype(jnp.float32), attention_router.astype(jnp.float32), feedforward_router.astype(jnp.float32), expand_weight.astype(jnp.float32), reduce_weight.astype(jnp.float32))
    final, pullback = jax.vjp(forward, *params)
    grads = pullback(cotangent.astype(jnp.float32))
    task_hot = jax.nn.one_hot(task_ids, TASKS, dtype=jnp.float32)
    usage = jnp.stack([jnp.einsum('it,ipke->te', task_hot, attend_hot, precision=HIGH), jnp.einsum('it,ipke->te', task_hot, feed_hot, precision=HIGH)])
    return (final.astype(jnp.bfloat16), grads[0], grads[1], grads[2][0], grads[2][1], grads[3], grads[4], grads[5], grads[6], grads[7], grads[8], grads[9], grads[10], usage)
```

```python
import jax
import jax.numpy as jnp
from jax import lax
from jax.experimental import pallas as pl
from jax.experimental.pallas import tpu as pltpu
from jax.sharding import PartitionSpec as P

CAP = 256


EPS = 1e-06
HIGH = lax.Precision.HIGHEST


def normalize(value, gain, bias):
    mean = jnp.mean(value, -1, keepdims=True)
    centred = value - mean
    spread = jnp.mean(centred * centred, -1, keepdims=True)
    return centred * lax.rsqrt(spread + EPS) * gain + bias


def gate_weights(logits, picks_hot):
    chosen = jnp.sum(picks_hot * logits[..., None, :], -1)
    return jax.nn.softmax(chosen, -1)


def activate(value):
    return jax.nn.gelu(value, approximate=True)


F32 = jnp.float32
LOW = jnp.bfloat16
MESH = pl.DeviceIdType.MESH
MIB = 2**20


def dot(a, b):
    return jnp.dot(a, b, preferred_element_type=F32)


def dot_nt(a, b):
    return lax.dot_general(a, b, (((1,), (1,)), ((), ())), preferred_element_type=F32)


def gelu_parts(value):
    square = value * value
    inner = value * (0.7978845608028654 + 0.035677408136300125 * square)
    half = 0.5 + 0.5 * jnp.tanh(inner)
    act = value * half
    slope = half + act * (1.0 - half) * (1.5957691216057308 + 0.2140644488178007 * square)
    return act, slope


def expert_kernel(
    x_ref, c_ref, m_ref, we_hbm, wr_hbm,
    fin_ref, grn_ref, dg_ref, gout,
    xa, ca, ma, we, wr, xr, gp, xrt, gpt, cr, act, gh, pr, gr, ra, rb, rt2, rc, rx, dgs,
    wsem, xs, xv, cs, cv, ms, mv, gs, gv, s1s, s1r, s2s, s2r, s3s, ys, yr, ls, k1s, k1r, k2s, k2r,
):
    dp = lax.axis_index("dp")
    ex = lax.axis_index("expert")
    y = lax.rem(dp, 2)
    z = lax.div(dp, 2)
    is_end = (z == 0) | (z == 3)
    is_mid = (z == 1) | (z == 2)
    toward = jnp.where(z < 2, dp + 2, dp - 2)
    outer = jnp.where(z == 1, dp - 2, jnp.where(z == 2, dp + 2, dp))
    chunks = ra.shape[0]
    per_slot = chunks // 2
    rows = CAP

    def peer(r):
        return (dp ^ (r // 4), ex ^ (r % 4))

    def group(r):
        return 2 * (ex ^ (r % 4)) + (y ^ (r // 4))

    def remote(src, dst, send, recv, device):
        return pltpu.make_async_remote_copy(
            src_ref=src, dst_ref=dst, send_sem=send, recv_sem=recv,
            device_id=device, device_id_type=MESH,
        )

    barrier = pltpu.get_barrier_semaphore()
    for r in range(1, 8):
        pl.semaphore_signal(barrier, 1, device_id=peer(r), device_id_type=MESH)
    pl.semaphore_signal(barrier, 1, device_id=(toward, ex), device_id_type=MESH)

    @pl.when(is_mid)
    def _():
        pl.semaphore_signal(barrier, 1, device_id=(outer, ex), device_id_type=MESH)

    loads = []
    for j in range(2):
        loads.append(pltpu.make_async_copy(we_hbm.at[y * 2 + j], we.at[j], wsem.at[2 * j]))
        loads.append(pltpu.make_async_copy(wr_hbm.at[y * 2 + j], wr.at[j], wsem.at[2 * j + 1]))
    for load in loads:
        load.start()
    xa[0] = x_ref[...]
    ca[0] = c_ref[...]
    ma[0] = m_ref[group(0)]

    pl.semaphore_wait(barrier, jnp.where(is_mid, 9, 8))

    def gather_copies(r):
        device = peer(r)
        return (
            remote(xa.at[0], xa.at[r], xs.at[r], xv.at[r], device),
            remote(ca.at[0], ca.at[r], cs.at[r], cv.at[r], device),
        )

    def meta_copy(r):
        return remote(m_ref.at[group(r)], ma.at[r], ms.at[r], mv.at[r], peer(r))

    def forward_copies(r):
        device = peer(1)
        return (
            remote(xa.at[r], xa.at[r + 1], xs.at[r + 1], xv.at[r + 1], device),
            remote(ca.at[r], ca.at[r + 1], cs.at[r + 1], cv.at[r + 1], device),
        )

    direct = (1, 2, 4, 6)
    sent = [copy for r in direct for copy in gather_copies(r)]
    sent += [meta_copy(r) for r in range(1, 8)]
    for copy in sent:
        copy.start()
    for load in loads:
        load.wait()

    def s1(c):
        return remote(ra.at[c], rb.at[c], s1s.at[c], s1r.at[c], (toward, ex))

    def s2(c):
        return remote(rb.at[c], rt2.at[c], s2s.at[c], s2r.at[c], (toward, ex))

    def s3(c):
        return remote(ra.at[c], rt2.at[c], s3s.at[c], s2r.at[c], (outer, ex))

    def out_index(c):
        return y * chunks + c

    def to_pair(src, c):
        return remote(src.at[c], gout.at[out_index(c)], ys.at[c], yr.at[c], (dp ^ 1, ex))

    def to_own(src, c):
        return pltpu.make_async_copy(src.at[c], gout.at[out_index(c)], ls.at[c])

    def tick(t):
        @pl.when(is_mid & (t < chunks))
        def _():
            s1(t).wait_recv()
            rb[t] = (ra[t].astype(F32) + rb[t].astype(F32)).astype(LOW)
            s2(t).start()

        u = jnp.maximum(t - 1, 0)

        @pl.when(is_mid & (t >= 1) & (t < chunks + 1))
        def _():
            s2(u).wait_recv()
            ra[u] = (rb[u].astype(F32) + rt2[u].astype(F32)).astype(LOW)
            s3(u).start()
            to_pair(ra, u).start()
            to_own(ra, u).start()

        w = jnp.maximum(t - 2, 0)

        @pl.when(is_end & (t >= 2) & (t < chunks + 2))
        def _():
            s2(w).wait_recv()
            to_pair(rt2, w).start()
            to_own(rt2, w).start()

    sub = lax.broadcasted_iota(jnp.int32, (rows, 2 * rows), 0).astype(F32)
    lane = lax.broadcasted_iota(jnp.int32, (2 * rows, rows), 1).astype(F32)

    def step(it, carry):
        j = lax.div(it, 4)
        s = lax.rem(it, 4)

        @pl.when(it == 0)
        def _():
            for copy in gather_copies(1):
                copy.wait_recv()
            meta_copy(1).wait_recv()

        @pl.when(it == 1)
        def _():
            for r in (2, 4, 6):
                for copy in gather_copies(r):
                    copy.wait_recv()
                for copy in forward_copies(r):
                    copy.start()
            for r in (3, 5, 7):
                for copy in gather_copies(r):
                    copy.wait_recv()
            for r in range(2, 8):
                meta_copy(r).wait_recv()

        for i in range(2):
            r = 2 * s + i
            hit = sub == ma[r, pl.ds(j, 1), :]
            pick = jnp.where(hit, 1.0, 0.0).astype(LOW)
            gate = jnp.sum(jnp.where(hit, ma[r, pl.ds(j + 2, 1), :], 0.0), 1, keepdims=True)
            at = pl.ds(pl.multiple_of(r * rows, rows), rows)
            x_rows = dot(pick, xa[r])
            xr[at, :] = x_rows.astype(LOW)
            xrt[:, at] = x_rows.T.astype(LOW)
            c_rows = dot(pick, ca[r])
            cr[i * rows:(i + 1) * rows, :] = c_rows.astype(LOW)
            g_rows = gate * c_rows
            gp[at, :] = g_rows.astype(LOW)
            gpt[:, at] = g_rows.T.astype(LOW)

        both = pl.ds(pl.multiple_of(s * 2 * rows, 2 * rows), 2 * rows)
        x_rows = xr[both, :]
        g_rows = gp[both, :]
        width = 512
        for f in range(act.shape[1] // width):
            cols = slice(f * width, (f + 1) * width)
            value, slope = gelu_parts(dot(x_rows, we[j, :, cols]))
            act[both, cols] = value.astype(LOW)
            gh[both, cols] = (dot_nt(g_rows, wr[j, cols, :]) * slope).astype(LOW)
        made = dot(act[both, :], wr[j]).astype(LOW)
        pr[j, both, :] = made
        gr[j, both, :] = dot_nt(gh[both, :], we[j]).astype(LOW)
        inner = jnp.sum(made.astype(F32) * cr[...].astype(F32), 1, keepdims=True)
        for i in range(2):
            r = 2 * s + i
            hit = sub == ma[r, pl.ds(j, 1), :]
            part = jnp.sum(jnp.where(hit, inner[i * rows:(i + 1) * rows], 0.0), 0, keepdims=True)
            dgs[r, j] = jnp.broadcast_to(part, (8, 2 * rows))

        @pl.when(s == 3)
        def _():
            def grads(f, carry):
                cols = pl.ds(pl.multiple_of(f * 256, 256), 256)
                first = j * per_slot + f
                ra[first] = dot(gpt[...], act[:, cols]).astype(LOW)
                second = first + per_slot // 2
                ra[second] = dot(xrt[...], gh[:, cols]).astype(LOW)

                @pl.when(is_end)
                def _():
                    s1(first).start()
                    s1(second).start()

                return carry

            lax.fori_loop(0, per_slot // 2, grads, 0)

        @pl.when(it >= 5)
        def _():
            tick(it - 5)

        return carry

    lax.fori_loop(0, 8, step, 0)

    def gate_copy(r):
        return remote(dgs.at[r], dg_ref.at[group(0)], gs.at[r], gv.at[r], peer(r))

    for r in range(1, 8):
        gate_copy(r).start()
    dg_ref[group(0)] = dgs[0]

    def block(r):
        return act.at[pl.ds(pl.multiple_of(r * rows, rows), rows), :]

    def k1(r):
        return remote(block(r), rc.at[lax.div(r, 2)], k1s.at[lax.div(r, 2)], k1r.at[lax.div(r, 2)], peer(1))

    def k2(r):
        q = lax.div(r, 2)
        return remote(block(r), rx.at[q], k2s.at[q], k2r.at[q], (dp ^ lax.div(r, 4), ex ^ lax.rem(r, 4)))

    def combine(q, carry):
        r = jnp.where(q < 4, 7 - 2 * q, 14 - 2 * q)
        meta = ma[r].T
        at = pl.ds(pl.multiple_of(r * rows, rows), rows)
        fin = jnp.zeros((2 * rows, x_ref.shape[1]), F32)
        grn = jnp.zeros((2 * rows, x_ref.shape[1]), F32)
        for j in range(2):
            hit = lane == meta[:, j:j + 1]
            fin = fin + dot(jnp.where(hit, meta[:, 2 + j:3 + j], 0.0).astype(LOW), pr[j, at, :])
            grn = grn + dot(jnp.where(hit, 1.0, 0.0).astype(LOW), gr[j, at, :])
        d = x_ref.shape[1]
        act[at, 0:d] = fin[:rows].astype(LOW)
        act[at, d:2 * d] = fin[rows:].astype(LOW)
        act[at, 2 * d:3 * d] = grn[:rows].astype(LOW)
        act[at, 3 * d:4 * d] = grn[rows:].astype(LOW)

        @pl.when(q < 4)
        def _():
            k1(r).start()

        @pl.when(q >= 4)
        def _():
            h = lax.div(r, 2)
            k1(r).wait_recv()
            act[at, :] = (act[at, :].astype(F32) + rc[h].astype(F32)).astype(LOW)

            @pl.when(r > 0)
            def _():
                k2(r).start()

        tick(q + 3)
        return carry

    lax.fori_loop(0, 8, combine, 0)
    for r in (2, 4, 6):
        k2(r).wait_recv()
    total = act[0:rows, :].astype(F32) + rx[1].astype(F32) + rx[2].astype(F32) + rx[3].astype(F32)
    d = x_ref.shape[1]
    fin_ref[0:rows, :] = total[:, 0:d]
    fin_ref[rows:2 * rows, :] = total[:, d:2 * d]
    grn_ref[0:rows, :] = total[:, 2 * d:3 * d]
    grn_ref[rows:2 * rows, :] = total[:, 3 * d:4 * d]

    def rest(t, carry):
        tick(t)
        return carry

    lax.fori_loop(11, chunks + 2, rest, 0)

    for copy in sent:
        copy.wait_send()
    for r in (2, 4, 6):
        for copy in forward_copies(r):
            copy.wait_send()
        k2(r).wait_send()
    for r in (1, 3, 5, 7):
        k1(r).wait_send()
    for r in range(1, 8):
        gate_copy(r).wait_send()
        gate_copy(r).wait_recv()

    def finish(c, carry):
        @pl.when(is_end)
        def _():
            s1(c).wait_send()
            to_pair(rt2, c).wait_send()
            to_own(rt2, c).wait()

        @pl.when(is_mid)
        def _():
            s2(c).wait_send()
            s3(c).wait_send()
            to_pair(ra, c).wait_send()
            to_own(ra, c).wait()

        remote(ra.at[c], gout.at[(1 - y) * chunks + c], ys.at[c], yr.at[c], (dp ^ 1, ex)).wait_recv()
        return carry

    lax.fori_loop(0, chunks, finish, 0)


def experts_call(x, c, meta, expand_weight, reduce_weight):
    count, d = x.shape
    ff = expand_weight.shape[2]
    chunks = 4 * ff // 256
    dma = pltpu.SemaphoreType.DMA
    vmem = pl.BlockSpec(memory_space=pltpu.VMEM)
    anywhere = pl.BlockSpec(memory_space=pl.ANY)
    return pl.pallas_call(
        expert_kernel,
        name="experts",
        out_shape=(
            jax.ShapeDtypeStruct((count, d), F32),
            jax.ShapeDtypeStruct((count, d), F32),
            jax.ShapeDtypeStruct((8, 2, 8, count), F32),
            jax.ShapeDtypeStruct((2 * chunks, d, 256), LOW),
        ),
        in_specs=[vmem, vmem, vmem, anywhere, anywhere],
        out_specs=(vmem, vmem, vmem, anywhere),
        scratch_shapes=[
            pltpu.VMEM((8, count, d), LOW),
            pltpu.VMEM((8, count, d), LOW),
            pltpu.VMEM((8, 16, count), F32),
            pltpu.VMEM((2, d, ff), LOW),
            pltpu.VMEM((2, ff, d), LOW),
            pltpu.VMEM((8 * CAP, d), LOW),
            pltpu.VMEM((8 * CAP, d), LOW),
            pltpu.VMEM((d, 8 * CAP), LOW),
            pltpu.VMEM((d, 8 * CAP), LOW),
            pltpu.VMEM((2 * CAP, d), LOW),
            pltpu.VMEM((8 * CAP, ff), LOW),
            pltpu.VMEM((8 * CAP, ff), LOW),
            pltpu.VMEM((2, 8 * CAP, d), LOW),
            pltpu.VMEM((2, 8 * CAP, d), LOW),
            pltpu.VMEM((chunks, d, 256), LOW),
            pltpu.VMEM((chunks, d, 256), LOW),
            pltpu.VMEM((chunks, d, 256), LOW),
            pltpu.VMEM((4, CAP, ff), LOW),
            pltpu.VMEM((4, CAP, ff), LOW),
            pltpu.VMEM((8, 2, 8, count), F32),
            dma((4,)),
            dma((8,)), dma((8,)), dma((8,)), dma((8,)), dma((8,)), dma((8,)), dma((8,)), dma((8,)),
            dma((chunks,)), dma((chunks,)), dma((chunks,)), dma((chunks,)), dma((chunks,)),
            dma((chunks,)), dma((chunks,)), dma((chunks,)),
            dma((4,)), dma((4,)), dma((4,)), dma((4,)),
        ],
        compiler_params=pltpu.CompilerParams(
            collective_id=0, has_side_effects=True, vmem_limit_bytes=62 * MIB
        ),
    )(x, c, meta, expand_weight, reduce_weight)


def widen_kernel(r_ref, e_ref, reduce_ref, expand_ref):
    reduce_ref[0] = r_ref[0].astype(F32).T
    expand_ref[0] = e_ref[0].astype(F32)


def widen_call(chunks, slots, d, ff):
    n = ff // 256
    return pl.pallas_call(
        widen_kernel,
        name="widen",
        grid=(slots, n),
        in_specs=[
            pl.BlockSpec((1, d, 256), lambda s, f: (s * 2 * n + f, 0, 0)),
            pl.BlockSpec((1, d, 256), lambda s, f: (s * 2 * n + n + f, 0, 0)),
        ],
        out_specs=(
            pl.BlockSpec((1, 256, d), lambda s, f: (s, f, 0)),
            pl.BlockSpec((1, d, 256), lambda s, f: (s, 0, f)),
        ),
        out_shape=(
            jax.ShapeDtypeStruct((slots, ff, d), F32),
            jax.ShapeDtypeStruct((slots, d, ff), F32),
        ),
    )(chunks, chunks)


def masked_softmax(logits, chosen):
    top = jnp.max(jnp.where(chosen > 0, logits, -jnp.inf), -1, keepdims=True)
    expo = jnp.where(chosen > 0, jnp.exp(logits - top), 0.0)
    return expo / jnp.sum(expo, -1, keepdims=True)


def body(
    tokens,
    task_ids,
    attention_picks,
    feedforward_picks,
    norm_gain,
    norm_bias,
    query_weight,
    key_weight,
    value_weight,
    output_weight,
    attention_router,
    feedforward_router,
    expand_weight,
    reduce_weight,
    cotangent,
):
    images, patches, width = tokens.shape
    count = images * patches
    tasks = attention_router.shape[0]
    experts = attention_router.shape[2]
    head = key_weight.shape[1]
    picks = attention_picks.shape[2]
    slots = expand_weight.shape[0]
    groups = lax.axis_size("expert")
    lanes = groups * slots
    f32 = jnp.float32
    low_type = jnp.bfloat16
    inputs = tokens.astype(f32).reshape(count, width)
    expert_range = jnp.arange(experts, dtype=jnp.int32)
    task_hot = (task_ids[:, None] == jnp.arange(tasks, dtype=jnp.int32)[None, :]).astype(f32)
    task_low = task_hot.astype(low_type)
    attend_hot = (attention_picks[..., None] == expert_range).astype(f32)
    attend_low = attend_hot.astype(low_type)
    choices = feedforward_picks.reshape(count, picks)
    feed_hot = (choices[..., None] == expert_range).astype(f32)
    flat = choices.reshape(count * picks)
    marks = (flat[:, None] == expert_range[None, :]).astype(jnp.int32)
    before = jnp.cumsum(marks, axis=0) - marks
    position = flat * CAP + jnp.sum(before * marks, axis=1)
    first, first_back = jax.vjp(normalize, inputs, norm_gain[0], norm_bias[0])
    normed_one = first.astype(low_type)
    shaped_one = normed_one.reshape(images, patches, width)
    router_one = jnp.einsum(
        "it,tde->ide", task_low, attention_router, preferred_element_type=f32
    ).astype(low_type)
    logits_one = jnp.einsum("ipd,ide->ipe", shaped_one, router_one, preferred_element_type=f32)
    gates_one, gates_one_back = jax.vjp(lambda value: gate_weights(value, attend_hot), logits_one)
    queries_all = jnp.dot(normed_one, query_weight, preferred_element_type=f32).astype(low_type)
    queries_all = queries_all.reshape(images, patches, experts, head)
    queries = jnp.einsum(
        "ipke,ipeh->ipkh", attend_low, queries_all, preferred_element_type=f32
    ).astype(low_type)
    queries = queries.reshape(images, patches * picks, head)
    key_value = jnp.concatenate([key_weight, value_weight], 1)
    pair = jnp.dot(normed_one, key_value, preferred_element_type=f32).astype(low_type)
    pair = pair.reshape(images, patches, 2 * head)
    pair_all = lax.all_gather(pair, "expert", axis=1, tiled=True)
    keys_all = pair_all[:, :, :head]
    values_all = pair_all[:, :, head:]
    scores = jnp.einsum("irh,ish->irs", queries, keys_all, preferred_element_type=f32) * 0.125
    top = jnp.max(scores, -1, keepdims=True)
    expo = jnp.exp(scores - top)
    total = jnp.sum(expo, -1, keepdims=True)
    log_total = top + jnp.log(total)
    probs_low = (expo / total).astype(low_type)
    attended = jnp.einsum("irs,ish->irh", probs_low, values_all, preferred_element_type=f32)
    attended = attended.reshape(images, patches, picks, head)
    weighted = gates_one[..., None] * attended
    heads = jnp.einsum("ipke,ipkh->ipeh", attend_hot, weighted, precision=HIGH)
    heads = heads.reshape(count, experts * head).astype(low_type)
    middle = inputs + jnp.dot(heads, output_weight, preferred_element_type=f32)
    second, second_back = jax.vjp(normalize, middle, norm_gain[1], norm_bias[1])
    normed_two = second.astype(low_type)
    shaped_two = normed_two.reshape(images, patches, width)
    router_two = jnp.einsum(
        "it,tde->ide", task_low, feedforward_router, preferred_element_type=f32
    ).astype(low_type)
    logits_two = jnp.einsum(
        "ipd,ide->ipe", shaped_two, router_two, preferred_element_type=f32
    ).reshape(count, experts)
    gates_two, gates_two_back = jax.vjp(lambda value: gate_weights(value, feed_hot), logits_two)
    outgoing = (
        jnp.zeros((lanes * CAP, width), low_type)
        .at[position]
        .set(jnp.repeat(normed_two, picks, axis=0))
    )
    outgoing = outgoing.reshape(groups, slots * CAP, width)
    received = lax.all_to_all(outgoing, "expert", split_axis=0, concat_axis=0, tiled=True).reshape(
        groups, slots, CAP, width
    )
    hidden = jnp.einsum("nscd,sdf->nscf", received, expand_weight, preferred_element_type=f32)
    activated, activate_back = jax.vjp(activate, hidden)
    active_low = activated.astype(low_type)
    produced = jnp.einsum(
        "nscf,sfd->nscd", active_low, reduce_weight, preferred_element_type=f32
    ).astype(low_type)
    produced = produced.reshape(groups, slots * CAP, width)
    returned = lax.all_to_all(produced, "expert", split_axis=0, concat_axis=0, tiled=True).reshape(
        lanes * CAP, width
    )
    picked = returned[position].astype(f32).reshape(count, picks, width)
    final = middle + jnp.sum(gates_two[..., None] * picked, 1)
    output = final.astype(low_type).reshape(images, patches, width)
    grad_final = cotangent.astype(f32).reshape(count, width)
    grad_gates_two = jnp.sum(picked * grad_final[:, None, :], -1)
    grad_picked = (
        (gates_two[..., None] * grad_final[:, None, :])
        .astype(low_type)
        .reshape(count * picks, width)
    )
    grad_send = jnp.zeros((lanes * CAP, width), low_type).at[position].set(grad_picked)
    grad_send = grad_send.reshape(groups, slots * CAP, width)
    grad_produced = lax.all_to_all(
        grad_send, "expert", split_axis=0, concat_axis=0, tiled=True
    ).reshape(groups, slots, CAP, width)
    grad_reduce = jnp.einsum(
        "nscf,nscd->sfd", active_low, grad_produced, preferred_element_type=f32
    )
    grad_active = jnp.einsum(
        "nscd,sfd->nscf", grad_produced, reduce_weight, preferred_element_type=f32
    )
    grad_hidden = activate_back(grad_active)[0].astype(low_type)
    grad_expand = jnp.einsum("nscd,nscf->sdf", received, grad_hidden, preferred_element_type=f32)
    grad_rows = jnp.einsum(
        "nscf,sdf->nscd", grad_hidden, expand_weight, preferred_element_type=f32
    ).astype(low_type)
    grad_rows = grad_rows.reshape(groups, slots * CAP, width)
    grad_back = lax.all_to_all(
        grad_rows, "expert", split_axis=0, concat_axis=0, tiled=True
    ).reshape(lanes * CAP, width)
    grad_normed_two = jnp.sum(grad_back[position].astype(f32).reshape(count, picks, width), 1)
    grad_logits_two = (
        gates_two_back(grad_gates_two)[0].astype(low_type).reshape(images, patches, experts)
    )
    per_image_two = jnp.einsum(
        "ipd,ipe->ide", shaped_two, grad_logits_two, preferred_element_type=f32
    )
    grad_feed_router = jnp.einsum("it,ide->tde", task_hot, per_image_two, precision=HIGH)
    grad_normed_two = grad_normed_two + jnp.einsum(
        "ipe,ide->ipd", grad_logits_two, router_two, preferred_element_type=f32
    ).reshape(count, width)
    grad_middle_norm, grad_gain_two, grad_bias_two = second_back(grad_normed_two)
    grad_middle = grad_final + grad_middle_norm
    grad_branch = grad_middle.astype(low_type)
    grad_output = jnp.einsum("tc,td->cd", heads, grad_branch, preferred_element_type=f32)
    grad_heads = jnp.einsum(
        "td,cd->tc", grad_branch, output_weight, preferred_element_type=f32
    ).astype(low_type)
    grad_heads = grad_heads.reshape(images, patches, experts, head)
    grad_selected = jnp.einsum(
        "ipke,ipeh->ipkh", attend_low, grad_heads, preferred_element_type=f32
    )
    grad_gates_one = jnp.sum(attended * grad_selected, -1)
    grad_attended = (
        (gates_one[..., None] * grad_selected)
        .astype(low_type)
        .reshape(images, patches * picks, head)
    )
    scores_back = jnp.einsum("irh,ish->irs", queries, keys_all, preferred_element_type=f32) * 0.125
    probs_back = jnp.exp(scores_back - log_total)
    grad_values = jnp.einsum(
        "irs,irh->ish", probs_back.astype(low_type), grad_attended, preferred_element_type=f32
    )
    grad_probs = jnp.einsum("irh,ish->irs", grad_attended, values_all, preferred_element_type=f32)
    inner_sum = jnp.sum(probs_back * grad_probs, -1, keepdims=True)
    grad_scores = (probs_back * (grad_probs - inner_sum)).astype(low_type)
    grad_query_sel = (
        jnp.einsum("irs,ish->irh", grad_scores, keys_all, preferred_element_type=f32) * 0.125
    )
    grad_keys = jnp.einsum("irs,irh->ish", grad_scores, queries, preferred_element_type=f32) * 0.125
    grad_pair = jnp.concatenate([grad_keys, grad_values], -1)
    pair_sum = lax.psum_scatter(
        grad_pair.astype(jnp.bfloat16), "expert", scatter_dimension=1, tiled=True
    ).astype(jnp.float32)
    pair_sum = pair_sum.astype(low_type).reshape(count, 2 * head)
    grad_query_sel = grad_query_sel.reshape(images, patches, picks, head)
    grad_queries_all = jnp.einsum("ipke,ipkh->ipeh", attend_hot, grad_query_sel, precision=HIGH)
    grad_queries_all = grad_queries_all.astype(low_type).reshape(count, experts * head)
    grad_logits_one = gates_one_back(grad_gates_one)[0].astype(low_type)
    per_image_one = jnp.einsum(
        "ipd,ipe->ide", shaped_one, grad_logits_one, preferred_element_type=f32
    )
    grad_attend_router = jnp.einsum("it,ide->tde", task_hot, per_image_one, precision=HIGH)
    grad_query = jnp.einsum("td,tc->dc", normed_one, grad_queries_all, preferred_element_type=f32)
    grad_key_value = jnp.einsum("td,tc->dc", normed_one, pair_sum, preferred_element_type=f32)
    grad_normed_one = jnp.einsum(
        "tc,dc->td", grad_queries_all, query_weight, preferred_element_type=f32
    )
    grad_normed_one = grad_normed_one + jnp.einsum(
        "tc,dc->td", pair_sum, key_value, preferred_element_type=f32
    )
    grad_normed_one = grad_normed_one + jnp.einsum(
        "ipe,ide->ipd", grad_logits_one, router_one, preferred_element_type=f32
    ).reshape(count, width)
    grad_inputs_norm, grad_gain_one, grad_bias_one = first_back(grad_normed_one)
    grad_tokens = (grad_middle + grad_inputs_norm).reshape(images, patches, width)
    grad_gain = jnp.stack([grad_gain_one, grad_gain_two])
    grad_bias = jnp.stack([grad_bias_one, grad_bias_two])
    feed_shaped = feed_hot.reshape(images, patches, picks, experts)
    usage = jnp.stack(
        [
            jnp.einsum("it,ipke->te", task_hot, attend_hot, precision=HIGH),
            jnp.einsum("it,ipke->te", task_hot, feed_shaped, precision=HIGH),
        ]
    )
    shared = lax.psum(
        (
            grad_query,
            grad_key_value,
            grad_output,
            grad_attend_router,
            grad_feed_router,
            grad_gain,
            grad_bias,
            usage,
        ),
        ("dp", "expert"),
    )
    grad_expand_sum, grad_reduce_sum = (
        lax.psum(grad_expand.astype(jnp.bfloat16), "dp").astype(jnp.float32),
        lax.psum(grad_reduce.astype(jnp.bfloat16), "dp").astype(jnp.float32),
    )
    grad_key_sum = shared[1][:, :head]
    grad_value_sum = shared[1][:, head:]
    return (
        output,
        grad_tokens,
        shared[5],
        shared[6][0],
        shared[6][1],
        shared[0],
        grad_key_sum,
        grad_value_sum,
        shared[2],
        shared[3],
        shared[4],
        grad_expand_sum,
        grad_reduce_sum,
        shared[7],
    )


def body_fast(
    tokens,
    task_ids,
    attention_picks,
    feedforward_picks,
    norm_gain,
    norm_bias,
    query_weight,
    key_weight,
    value_weight,
    output_weight,
    attention_router,
    feedforward_router,
    expand_weight,
    reduce_weight,
    cotangent,
):
    images, patches, width = tokens.shape
    count = images * patches
    tasks = attention_router.shape[0]
    experts = attention_router.shape[2]
    head = key_weight.shape[1]
    picks = attention_picks.shape[2]
    slots = expand_weight.shape[0]
    groups = lax.axis_size("expert")
    lanes = groups * slots
    f32 = jnp.float32
    low_type = jnp.bfloat16
    inputs = tokens.astype(f32).reshape(count, width)
    expert_range = jnp.arange(experts, dtype=jnp.int32)
    task_hot = (task_ids[:, None] == jnp.arange(tasks, dtype=jnp.int32)[None, :]).astype(f32)
    task_low = task_hot.astype(low_type)
    attend_hot = (attention_picks[..., None] == expert_range).astype(f32)
    attend_low = attend_hot.astype(low_type)
    choices = feedforward_picks.reshape(count, picks)
    wide = jnp.arange(experts + 1, dtype=jnp.int32)
    feed_hot = (choices[..., None] == expert_range).astype(f32)
    chosen = jnp.sum((choices[..., None] == wide).astype(f32), 1)
    earlier = jnp.arange(count)[:, None] > jnp.arange(count)[None, :]
    before = jnp.dot(earlier.astype(low_type), chosen.astype(low_type), preferred_element_type=f32)
    rank = jnp.where(chosen > 0, before, -1.0).T
    first, first_back = jax.vjp(normalize, inputs, norm_gain[0], norm_bias[0])
    normed_one = first.astype(low_type)
    shaped_one = normed_one.reshape(images, patches, width)
    router_one = jnp.einsum(
        "it,tde->ide", task_low, attention_router, preferred_element_type=f32
    ).astype(low_type)
    logits_one = jnp.einsum("ipd,ide->ipe", shaped_one, router_one, preferred_element_type=f32)
    gates_one, gates_one_back = jax.vjp(lambda value: gate_weights(value, attend_hot), logits_one)
    queries_all = jnp.dot(normed_one, query_weight, preferred_element_type=f32).astype(low_type)
    queries_all = queries_all.reshape(images, patches, experts, head)
    queries = jnp.einsum(
        "ipke,ipeh->ipkh", attend_low, queries_all, preferred_element_type=f32
    ).astype(low_type)
    queries = queries.reshape(images, patches * picks, head)
    key_value = jnp.concatenate([key_weight, value_weight], 1)
    pair = jnp.dot(normed_one, key_value, preferred_element_type=f32).astype(low_type)
    pair = pair.reshape(images, patches, 2 * head)
    pair_all = lax.all_gather(pair, "expert", axis=1, tiled=True)
    keys_all = pair_all[:, :, :head]
    values_all = pair_all[:, :, head:]
    scores = jnp.einsum("irh,ish->irs", queries, keys_all, preferred_element_type=f32) * 0.125
    top = jnp.max(scores, -1, keepdims=True)
    expo = jnp.exp(scores - top)
    total = jnp.sum(expo, -1, keepdims=True)
    log_total = top + jnp.log(total)
    probs_low = (expo / total).astype(low_type)
    attended = jnp.einsum("irs,ish->irh", probs_low, values_all, preferred_element_type=f32)
    attended = attended.reshape(images, patches, picks, head)
    weighted = gates_one[..., None] * attended
    heads = jnp.einsum("ipke,ipkh->ipeh", attend_hot, weighted, precision=HIGH)
    heads = heads.reshape(count, experts * head).astype(low_type)
    middle = inputs + jnp.dot(heads, output_weight, preferred_element_type=f32)
    second, second_back = jax.vjp(normalize, middle, norm_gain[1], norm_bias[1])
    normed_two = second.astype(low_type)
    shaped_two = normed_two.reshape(images, patches, width)
    router_two = jnp.einsum(
        "it,tde->ide", task_low, feedforward_router, preferred_element_type=f32
    ).astype(low_type)
    logits_two = jnp.einsum(
        "ipd,ide->ipe", shaped_two, router_two, preferred_element_type=f32
    ).reshape(count, experts)
    gates_two = masked_softmax(logits_two, chosen[:, :experts])
    gate_rows = jnp.pad(gates_two, ((0, 0), (0, 1))).T
    pairs = lanes // 2
    meta = jnp.concatenate(
        [
            rank.reshape(pairs, 2, count),
            gate_rows.reshape(pairs, 2, count),
            jnp.zeros((pairs, 12, count), f32),
        ],
        1,
    )
    final_part, grad_normed_two, grad_gate_rows, grad_chunks = experts_call(
        normed_two, cotangent.reshape(count, width), meta, expand_weight, reduce_weight
    )
    output = (middle + final_part).astype(low_type).reshape(images, patches, width)
    grad_final = cotangent.astype(f32).reshape(count, width)
    grad_gates = grad_gate_rows[:, :, 0].reshape(2 * pairs, count)[:experts].T
    grad_logits_two = gates_two * (
        grad_gates - jnp.sum(gates_two * grad_gates, -1, keepdims=True)
    )
    grad_logits_two = grad_logits_two.astype(low_type).reshape(images, patches, experts)
    per_image_two = jnp.einsum(
        "ipd,ipe->ide", shaped_two, grad_logits_two, preferred_element_type=f32
    )
    grad_feed_router = jnp.einsum("it,ide->tde", task_hot, per_image_two, precision=HIGH)
    grad_normed_two = grad_normed_two + jnp.einsum(
        "ipe,ide->ipd", grad_logits_two, router_two, preferred_element_type=f32
    ).reshape(count, width)
    grad_middle_norm, grad_gain_two, grad_bias_two = second_back(grad_normed_two)
    grad_middle = grad_final + grad_middle_norm
    grad_branch = grad_middle.astype(low_type)
    grad_output = jnp.einsum("tc,td->cd", heads, grad_branch, preferred_element_type=f32)
    grad_heads = jnp.einsum(
        "td,cd->tc", grad_branch, output_weight, preferred_element_type=f32
    ).astype(low_type)
    grad_heads = grad_heads.reshape(images, patches, experts, head)
    grad_selected = jnp.einsum(
        "ipke,ipeh->ipkh", attend_low, grad_heads, preferred_element_type=f32
    )
    grad_gates_one = jnp.sum(attended * grad_selected, -1)
    grad_attended = (
        (gates_one[..., None] * grad_selected)
        .astype(low_type)
        .reshape(images, patches * picks, head)
    )
    scores_back = jnp.einsum("irh,ish->irs", queries, keys_all, preferred_element_type=f32) * 0.125
    probs_back = jnp.exp(scores_back - log_total)
    grad_values = jnp.einsum(
        "irs,irh->ish", probs_back.astype(low_type), grad_attended, preferred_element_type=f32
    )
    grad_probs = jnp.einsum("irh,ish->irs", grad_attended, values_all, preferred_element_type=f32)
    inner_sum = jnp.sum(probs_back * grad_probs, -1, keepdims=True)
    grad_scores = (probs_back * (grad_probs - inner_sum)).astype(low_type)
    grad_query_sel = (
        jnp.einsum("irs,ish->irh", grad_scores, keys_all, preferred_element_type=f32) * 0.125
    )
    grad_keys = jnp.einsum("irs,irh->ish", grad_scores, queries, preferred_element_type=f32) * 0.125
    grad_pair = jnp.concatenate([grad_keys, grad_values], -1)
    pair_sum = lax.psum_scatter(
        grad_pair.astype(jnp.bfloat16), "expert", scatter_dimension=1, tiled=True
    ).astype(jnp.float32)
    pair_sum = pair_sum.astype(low_type).reshape(count, 2 * head)
    grad_query_sel = grad_query_sel.reshape(images, patches, picks, head)
    grad_queries_all = jnp.einsum("ipke,ipkh->ipeh", attend_hot, grad_query_sel, precision=HIGH)
    grad_queries_all = grad_queries_all.astype(low_type).reshape(count, experts * head)
    grad_logits_one = gates_one_back(grad_gates_one)[0].astype(low_type)
    per_image_one = jnp.einsum(
        "ipd,ipe->ide", shaped_one, grad_logits_one, preferred_element_type=f32
    )
    grad_attend_router = jnp.einsum("it,ide->tde", task_hot, per_image_one, precision=HIGH)
    grad_query = jnp.einsum("td,tc->dc", normed_one, grad_queries_all, preferred_element_type=f32)
    grad_key_value = jnp.einsum("td,tc->dc", normed_one, pair_sum, preferred_element_type=f32)
    grad_normed_one = jnp.einsum(
        "tc,dc->td", grad_queries_all, query_weight, preferred_element_type=f32
    )
    grad_normed_one = grad_normed_one + jnp.einsum(
        "tc,dc->td", pair_sum, key_value, preferred_element_type=f32
    )
    grad_normed_one = grad_normed_one + jnp.einsum(
        "ipe,ide->ipd", grad_logits_one, router_one, preferred_element_type=f32
    ).reshape(count, width)
    grad_inputs_norm, grad_gain_one, grad_bias_one = first_back(grad_normed_one)
    grad_tokens = (grad_middle + grad_inputs_norm).reshape(images, patches, width)
    grad_gain = jnp.stack([grad_gain_one, grad_gain_two])
    grad_bias = jnp.stack([grad_bias_one, grad_bias_two])
    feed_shaped = feed_hot.reshape(images, patches, picks, experts)
    usage = jnp.stack(
        [
            jnp.einsum("it,ipke->te", task_hot, attend_hot, precision=HIGH),
            jnp.einsum("it,ipke->te", task_hot, feed_shaped, precision=HIGH),
        ]
    )
    shared = lax.psum(
        (
            grad_query,
            grad_key_value,
            grad_output,
            grad_attend_router,
            grad_feed_router,
            grad_gain,
            grad_bias,
            usage,
        ),
        ("dp", "expert"),
    )
    grad_reduce_sum, grad_expand_sum = widen_call(
        grad_chunks, slots, width, expand_weight.shape[2]
    )
    grad_key_sum = shared[1][:, :head]
    grad_value_sum = shared[1][:, head:]
    return (
        output,
        grad_tokens,
        shared[5],
        shared[6][0],
        shared[6][1],
        shared[0],
        grad_key_sum,
        grad_value_sum,
        shared[2],
        shared[3],
        shared[4],
        grad_expand_sum,
        grad_reduce_sum,
        shared[7],
    )


def solution(mesh):
    placed = (
        P("dp", "expert", None),
        P("dp"),
        P("dp", "expert", None),
        P("dp", "expert", None, None),
        P(),
        P(),
        P(),
        P(),
        P(),
        P(),
        P(),
        P(),
        P("expert", None, None),
        P("expert", None, None),
        P("dp", "expert", None),
    )
    fast = mesh.shape["dp"] == 8 and mesh.shape["expert"] == 4
    return jax.shard_map(
        body_fast if fast else body,
        mesh=mesh,
        in_specs=placed,
        out_specs=(
            P("dp", "expert", None),
            P("dp", "expert", None),
            P(),
            P(),
            P(),
            P(),
            P(),
            P(),
            P(),
            P(),
            P(),
            P("expert", None, None),
            P("expert", None, None),
            P(),
        ),
        check_vma=False,
    )
```

```python
import types

import jax
import jax.numpy as jnp
from jax import lax
from jax.experimental import pallas as pl
from jax.experimental.pallas import tpu as pltpu
from jax.sharding import PartitionSpec as P

CAP = 256


EPS = 1e-06
HIGH = lax.Precision.HIGHEST
F32 = jnp.float32
LOW = jnp.bfloat16
MESH = pl.DeviceIdType.MESH
MIB = 2**20


def dot(a, b):
    return jnp.dot(a, b, preferred_element_type=F32)


def dot_nt(a, b):
    return lax.dot_general(a, b, (((1,), (1,)), ((), ())), preferred_element_type=F32)


def dot_tn(a, b):
    return lax.dot_general(a, b, (((0,), (0,)), ((), ())), preferred_element_type=F32)


def remote(src, dst, send, recv, device):
    return pltpu.make_async_remote_copy(
        src_ref=src, dst_ref=dst, send_sem=send, recv_sem=recv,
        device_id=device, device_id_type=MESH,
    )


def run_kernel(kernel, name, ins, outs, scratch, collective):
    names = [*ins, *outs, *scratch]

    def body(*refs):
        kernel(types.SimpleNamespace(**dict(zip(names, refs, strict=True))))

    made = pl.pallas_call(
        body,
        name=name,
        out_shape=[jax.ShapeDtypeStruct(shape, dtype) for shape, dtype, _ in outs.values()],
        in_specs=[pl.BlockSpec(memory_space=space) for _, space in ins.values()],
        out_specs=[pl.BlockSpec(memory_space=space) for _, _, space in outs.values()],
        scratch_shapes=list(scratch.values()),
        compiler_params=pltpu.CompilerParams(
            collective_id=collective, has_side_effects=True, vmem_limit_bytes=62 * MIB
        ),
    )(*[array for array, _ in ins.values()])
    return types.SimpleNamespace(**dict(zip(outs, made, strict=True)))


def center(value):
    mean = jnp.mean(value, -1, keepdims=True)
    centred = value - mean
    scale = lax.rsqrt(jnp.mean(centred * centred, -1, keepdims=True) + EPS)
    return centred * scale, scale


def center_back(grad, normal, scale, gain):
    inner = grad * gain
    mean = jnp.mean(inner, -1, keepdims=True)
    along = jnp.mean(inner * normal, -1, keepdims=True)
    return scale * (inner - mean - normal * along)


def head_maps(heads, head):
    row = lax.broadcasted_iota(jnp.int32, (heads * head, 2 * head), 0)
    row = lax.rem(row, head)
    col = lax.broadcasted_iota(jnp.int32, (heads * head, 2 * head), 1)
    low = jnp.where(row == col, 1.0, 0.0).astype(LOW)
    high = jnp.where(row + head == col, 1.0, 0.0).astype(LOW)
    return low, high


def masked_softmax(logits, chosen, axis):
    top = jnp.max(jnp.where(chosen, logits, -1e30), axis, keepdims=True)
    expo = jnp.where(chosen, jnp.exp(jnp.minimum(logits - top, 0.0)), 0.0)
    return expo / jnp.sum(expo, axis, keepdims=True)


def front_kernel(v):
    dp = lax.axis_index("dp")
    ex = lax.axis_index("expert")
    count, d = v.tok.shape
    half = count // 2
    heads = v.qa.shape[1]
    head = v.kv.shape[2] // 2
    picks = v.pick.shape[1]

    def peer(r):
        return (dp ^ (r // 4), ex ^ (r % 4))

    barrier = pltpu.get_barrier_semaphore()
    for r in range(1, 8):
        pl.semaphore_signal(barrier, 1, device_id=peer(r), device_id_type=MESH)

    def cot_copy(r):
        return remote(v.cot, v.ca.at[r], v.cs.at[r], v.cv.at[r], peer(r))

    def cot_forward(r):
        return remote(v.ca.at[r], v.ca.at[r + 1], v.cs.at[r + 1], v.cv.at[r + 1], peer(1))

    def kv_copy(r):
        return remote(
            v.kv.at[:, pl.ds(0, half), :], v.kv.at[:, pl.ds(r * half, half), :],
            v.ks.at[r], v.kr.at[r], peer(r),
        )

    gain = v.gain[...]
    bias = v.bias[...]
    for i in range(2):
        rows = slice(i * half, (i + 1) * half)
        normal, _ = center(v.tok[rows, :].astype(F32))
        normed = (normal * gain[0:1] + bias[0:1]).astype(LOW)
        v.n1[rows, :] = normed
        v.kv[i, 0:half, :] = dot(normed, v.wkv[...]).astype(LOW)
    pl.semaphore_wait(barrier, 7)
    for r in (1, 2, 3):
        kv_copy(r).start()
    for r in (1, 2, 4, 6):
        cot_copy(r).start()
    v.qa[...] = dot(v.n1[...], v.wq[...]).astype(LOW)

    experts = v.router1.shape[1]
    number = lax.broadcasted_iota(jnp.int32, (experts, count), 0)
    chosen = number == v.pickt[0:1, :]
    for k in range(1, picks):
        chosen = chosen | (number == v.pickt[k:k + 1, :])
    earlier = lax.broadcasted_iota(jnp.int32, (count, count), 0) < lax.broadcasted_iota(
        jnp.int32, (count, count), 1
    )
    before = dot(jnp.where(chosen, 1.0, 0.0).astype(LOW), jnp.where(earlier, 1.0, 0.0).astype(LOW))
    rank = jnp.where(chosen, before, -1.0)

    to_query, to_value = head_maps(heads // head, head)
    owner = lax.broadcasted_iota(jnp.int32, (half, heads), 1)
    owner = lax.div(owner, head)
    lane = lax.broadcasted_iota(jnp.int32, (half, experts), 1)
    wide = lax.broadcasted_iota(jnp.int32, (half, 2 * head), 1)
    for r in (1, 2, 3):
        kv_copy(r).wait_recv()

    for i in range(2):
        rows = slice(i * half, (i + 1) * half)
        logits = dot_nt(v.n1[rows, :], v.router1[v.task[i]])
        named = [lane == v.pick[rows, k:k + 1] for k in range(picks)]
        allowed = named[0]
        for k in range(1, picks):
            allowed = allowed | named[k]
        gates = masked_softmax(logits, allowed, 1)
        v.g1[rows, :] = gates
        kv = v.kv[i]
        for k in range(picks):
            mine = owner == v.pick[rows, k:k + 1]
            gate = jnp.sum(jnp.where(named[k], gates, 0.0), 1, keepdims=True)
            all_queries = v.qa[rows, :]
            query = dot(jnp.where(mine, all_queries, jnp.zeros_like(all_queries)), to_query)
            query = (query * head ** -0.5).astype(LOW)
            v.q8[picks * i + k] = query
            scores = dot_nt(query, kv)
            expo = jnp.exp(scores - jnp.max(scores, 1, keepdims=True))
            total = jnp.sum(expo, 1, keepdims=True)
            low = expo.astype(LOW)
            v.eb[picks * i + k] = low
            attended = dot(low, kv) / total
            v.att[picks * i + k] = jnp.where(wide == 0, total, attended)
            spread = dot_nt((gate * attended).astype(LOW), to_value).astype(LOW)
            if k == 0:
                v.heads[rows, :] = jnp.where(mine, spread, jnp.zeros_like(spread))
            else:
                v.heads[rows, :] = jnp.where(mine, spread, v.heads[rows, :])
        middle = v.tok[rows, :].astype(F32) + dot(v.heads[rows, :], v.wo[...])
        v.mid[rows, :] = middle
        normal, _ = center(middle)
        normed = (normal * gain[1:2] + bias[1:2]).astype(LOW)
        v.n2[rows, :] = normed
        logits = dot_nt(v.router2[v.task[i]], normed)
        gates = masked_softmax(logits, rank[:, rows] >= 0.0, 0)
        v.g2[:, rows] = gates
        for g in range(8):
            v.meta[g, 0:2, rows] = rank[2 * g:2 * g + 2, rows]
            v.meta[g, 2:4, rows] = gates[2 * g:2 * g + 2, :]
            v.meta[g, 4:16, rows] = jnp.zeros((12, half), F32)
        if i == 0:
            for r in (2, 4, 6):
                cot_copy(r).wait_recv()
                cot_forward(r).start()

    v.ca[0] = v.cot[...]
    for r in (1, 3, 5, 7):
        cot_copy(r).wait_recv()
    for r in (1, 2, 3):
        kv_copy(r).wait_send()
    for r in (1, 2, 4, 6):
        cot_copy(r).wait_send()
    for r in (2, 4, 6):
        cot_forward(r).wait_send()


def front_call(tok, cot, pick, pickt, task, gain, bias, wq, wkv, wo, router1, router2):
    count, d = tok.shape
    heads = wq.shape[1]
    width = wkv.shape[1]
    picks = pick.shape[1]
    half = count // 2
    vm = pltpu.VMEM
    dma = pltpu.SemaphoreType.DMA
    return run_kernel(
        front_kernel, "front",
        dict(
            tok=(tok, vm), cot=(cot, vm), pick=(pick, vm), pickt=(pickt, vm), task=(task, pltpu.SMEM),
            gain=(gain, vm), bias=(bias, vm), wq=(wq, vm), wkv=(wkv, vm), wo=(wo, vm),
            router1=(router1, vm), router2=(router2, vm),
        ),
        dict(
            n1=((count, d), LOW, vm), n2=((count, d), LOW, vm), mid=((count, d), F32, vm),
            ca=((8, count, d), LOW, vm), heads=((count, heads), LOW, vm),
            kv=((2, 4 * half, width), LOW, vm), q8=((2 * picks, half, width), LOW, vm),
            eb=((2 * picks, half, 4 * half), LOW, vm), att=((2 * picks, half, width), F32, vm),
            g1=((count, 16), F32, vm), g2=((16, count), F32, vm), meta=((8, 16, count), F32, vm),
        ),
        dict(
            qa=pltpu.VMEM((count, heads), LOW),
            cs=dma((8,)), cv=dma((8,)), ks=dma((4,)), kr=dma((4,)),
        ),
        1,
    )


def gelu_parts(value):
    square = value * value
    inner = value * (0.7978845608028654 + 0.035677408136300125 * square)
    half = 0.5 + 0.5 * jnp.tanh(inner)
    act = value * half
    slope = half + act * (1.0 - half) * (1.5957691216057308 + 0.2140644488178007 * square)
    return act, slope


def expert_kernel(
    x_ref, ca, m_ref, we_hbm, wr_hbm,
    fin_ref, grn_ref, dg_ref, gout,
    xa, ma, we, wr, xr, gp, xrt, gpt, cr, act, gh, pr, gr, ra, rb, rt2, rc, rx, dgs,
    wsem, xs, xv, ms, mv, gs, gv, s1s, s1r, s2s, s2r, s3s, ys, yr, ls, k1s, k1r, k2s, k2r,
):
    dp = lax.axis_index("dp")
    ex = lax.axis_index("expert")
    y = lax.rem(dp, 2)
    z = lax.div(dp, 2)
    is_end = (z == 0) | (z == 3)
    is_mid = (z == 1) | (z == 2)
    toward = jnp.where(z < 2, dp + 2, dp - 2)
    outer = jnp.where(z == 1, dp - 2, jnp.where(z == 2, dp + 2, dp))
    chunks = ra.shape[0]
    per_slot = chunks // 2
    rows = CAP

    def peer(r):
        return (dp ^ (r // 4), ex ^ (r % 4))

    def group(r):
        return 2 * (ex ^ (r % 4)) + (y ^ (r // 4))

    barrier = pltpu.get_barrier_semaphore()
    for r in range(1, 8):
        pl.semaphore_signal(barrier, 1, device_id=peer(r), device_id_type=MESH)
    pl.semaphore_signal(barrier, 1, device_id=(toward, ex), device_id_type=MESH)

    @pl.when(is_mid)
    def _():
        pl.semaphore_signal(barrier, 1, device_id=(outer, ex), device_id_type=MESH)

    loads = []
    for j in range(2):
        loads.append(pltpu.make_async_copy(we_hbm.at[y * 2 + j], we.at[j], wsem.at[2 * j]))
        loads.append(pltpu.make_async_copy(wr_hbm.at[y * 2 + j], wr.at[j], wsem.at[2 * j + 1]))
    for load in loads:
        load.start()
    xa[0] = x_ref[...]
    ma[0] = m_ref[group(0)]

    pl.semaphore_wait(barrier, jnp.where(is_mid, 9, 8))

    def gather_copies(r):
        device = peer(r)
        return (remote(xa.at[0], xa.at[r], xs.at[r], xv.at[r], device),)

    def meta_copy(r):
        return remote(m_ref.at[group(r)], ma.at[r], ms.at[r], mv.at[r], peer(r))

    def forward_copies(r):
        device = peer(1)
        return (remote(xa.at[r], xa.at[r + 1], xs.at[r + 1], xv.at[r + 1], device),)

    direct = (1, 2, 4, 6)
    sent = [copy for r in direct for copy in gather_copies(r)]
    sent += [meta_copy(r) for r in range(1, 8)]
    for copy in sent:
        copy.start()
    for load in loads:
        load.wait()

    def s1(c):
        return remote(ra.at[c], rb.at[c], s1s.at[c], s1r.at[c], (toward, ex))

    def s2(c):
        return remote(rb.at[c], rt2.at[c], s2s.at[c], s2r.at[c], (toward, ex))

    def s3(c):
        return remote(ra.at[c], rt2.at[c], s3s.at[c], s2r.at[c], (outer, ex))

    def out_index(c):
        return y * chunks + c

    def to_pair(src, c):
        return remote(src.at[c], gout.at[out_index(c)], ys.at[c], yr.at[c], (dp ^ 1, ex))

    def to_own(src, c):
        return pltpu.make_async_copy(src.at[c], gout.at[out_index(c)], ls.at[c])

    def tick(t):
        @pl.when(is_mid & (t < chunks))
        def _():
            s1(t).wait_recv()
            rb[t] = (ra[t].astype(F32) + rb[t].astype(F32)).astype(LOW)
            s2(t).start()

        u = jnp.maximum(t - 1, 0)

        @pl.when(is_mid & (t >= 1) & (t < chunks + 1))
        def _():
            s2(u).wait_recv()
            ra[u] = (rb[u].astype(F32) + rt2[u].astype(F32)).astype(LOW)
            s3(u).start()
            to_pair(ra, u).start()
            to_own(ra, u).start()

        w = jnp.maximum(t - 2, 0)

        @pl.when(is_end & (t >= 2) & (t < chunks + 2))
        def _():
            s2(w).wait_recv()
            to_pair(rt2, w).start()
            to_own(rt2, w).start()

    sub = lax.broadcasted_iota(jnp.int32, (rows, 2 * rows), 0).astype(F32)
    lane = lax.broadcasted_iota(jnp.int32, (2 * rows, rows), 1).astype(F32)

    def step(it, carry):
        j = lax.div(it, 4)
        s = lax.rem(it, 4)

        @pl.when(it == 0)
        def _():
            for copy in gather_copies(1):
                copy.wait_recv()
            meta_copy(1).wait_recv()

        @pl.when(it == 1)
        def _():
            for r in (2, 4, 6):
                for copy in gather_copies(r):
                    copy.wait_recv()
                for copy in forward_copies(r):
                    copy.start()
            for r in (3, 5, 7):
                for copy in gather_copies(r):
                    copy.wait_recv()
            for r in range(2, 8):
                meta_copy(r).wait_recv()

        for i in range(2):
            r = 2 * s + i
            hit = sub == ma[r, pl.ds(j, 1), :]
            pick = jnp.where(hit, 1.0, 0.0).astype(LOW)
            gate = jnp.sum(jnp.where(hit, ma[r, pl.ds(j + 2, 1), :], 0.0), 1, keepdims=True)
            at = pl.ds(pl.multiple_of(r * rows, rows), rows)
            x_rows = dot(pick, xa[r])
            xr[at, :] = x_rows.astype(LOW)
            xrt[:, at] = x_rows.T.astype(LOW)
            c_rows = dot(pick, ca[r])
            cr[i * rows:(i + 1) * rows, :] = c_rows.astype(LOW)
            g_rows = gate * c_rows
            gp[at, :] = g_rows.astype(LOW)
            gpt[:, at] = g_rows.T.astype(LOW)

        both = pl.ds(pl.multiple_of(s * 2 * rows, 2 * rows), 2 * rows)
        x_rows = xr[both, :]
        g_rows = gp[both, :]
        width = 512
        for f in range(act.shape[1] // width):
            cols = slice(f * width, (f + 1) * width)
            value, slope = gelu_parts(dot(x_rows, we[j, :, cols]))
            act[both, cols] = value.astype(LOW)
            gh[both, cols] = (dot_nt(g_rows, wr[j, cols, :]) * slope).astype(LOW)
        made = dot(act[both, :], wr[j]).astype(LOW)
        pr[j, both, :] = made
        gr[j, both, :] = dot_nt(gh[both, :], we[j]).astype(LOW)
        inner = jnp.sum(made.astype(F32) * cr[...].astype(F32), 1, keepdims=True)
        for i in range(2):
            r = 2 * s + i
            hit = sub == ma[r, pl.ds(j, 1), :]
            part = jnp.sum(jnp.where(hit, inner[i * rows:(i + 1) * rows], 0.0), 0, keepdims=True)
            dgs[r, j] = jnp.broadcast_to(part, (8, 2 * rows))

        @pl.when(s == 3)
        def _():
            def grads(f, carry):
                cols = pl.ds(pl.multiple_of(f * 256, 256), 256)
                first = j * per_slot + f
                ra[first] = dot(gpt[...], act[:, cols]).astype(LOW)
                second = first + per_slot // 2
                ra[second] = dot(xrt[...], gh[:, cols]).astype(LOW)

                @pl.when(is_end)
                def _():
                    s1(first).start()
                    s1(second).start()

                return carry

            lax.fori_loop(0, per_slot // 2, grads, 0)

        @pl.when(it >= 5)
        def _():
            tick(it - 5)

        return carry

    lax.fori_loop(0, 8, step, 0)

    def gate_copy(r):
        return remote(dgs.at[r], dg_ref.at[group(0)], gs.at[r], gv.at[r], peer(r))

    for r in range(1, 8):
        gate_copy(r).start()
    dg_ref[group(0)] = dgs[0]

    def block(r):
        return act.at[pl.ds(pl.multiple_of(r * rows, rows), rows), :]

    def k1(r):
        return remote(block(r), rc.at[lax.div(r, 2)], k1s.at[lax.div(r, 2)], k1r.at[lax.div(r, 2)], peer(1))

    def k2(r):
        q = lax.div(r, 2)
        return remote(block(r), rx.at[q], k2s.at[q], k2r.at[q], (dp ^ lax.div(r, 4), ex ^ lax.rem(r, 4)))

    def combine(q, carry):
        r = jnp.where(q < 4, 7 - 2 * q, 14 - 2 * q)
        meta = ma[r].T
        at = pl.ds(pl.multiple_of(r * rows, rows), rows)
        fin = jnp.zeros((2 * rows, x_ref.shape[1]), F32)
        grn = jnp.zeros((2 * rows, x_ref.shape[1]), F32)
        for j in range(2):
            hit = lane == meta[:, j:j + 1]
            fin = fin + dot(jnp.where(hit, meta[:, 2 + j:3 + j], 0.0).astype(LOW), pr[j, at, :])
            grn = grn + dot(jnp.where(hit, 1.0, 0.0).astype(LOW), gr[j, at, :])
        d = x_ref.shape[1]
        act[at, 0:d] = fin[:rows].astype(LOW)
        act[at, d:2 * d] = fin[rows:].astype(LOW)
        act[at, 2 * d:3 * d] = grn[:rows].astype(LOW)
        act[at, 3 * d:4 * d] = grn[rows:].astype(LOW)

        @pl.when(q < 4)
        def _():
            k1(r).start()

        @pl.when(q >= 4)
        def _():
            h = lax.div(r, 2)
            k1(r).wait_recv()
            act[at, :] = (act[at, :].astype(F32) + rc[h].astype(F32)).astype(LOW)

            @pl.when(r > 0)
            def _():
                k2(r).start()

        tick(q + 3)
        return carry

    lax.fori_loop(0, 8, combine, 0)
    for r in (2, 4, 6):
        k2(r).wait_recv()
    total = act[0:rows, :].astype(F32) + rx[1].astype(F32) + rx[2].astype(F32) + rx[3].astype(F32)
    d = x_ref.shape[1]
    fin_ref[0:rows, :] = total[:, 0:d]
    fin_ref[rows:2 * rows, :] = total[:, d:2 * d]
    grn_ref[0:rows, :] = total[:, 2 * d:3 * d]
    grn_ref[rows:2 * rows, :] = total[:, 3 * d:4 * d]

    def rest(t, carry):
        tick(t)
        return carry

    lax.fori_loop(11, chunks + 2, rest, 0)

    for copy in sent:
        copy.wait_send()
    for r in (2, 4, 6):
        for copy in forward_copies(r):
            copy.wait_send()
        k2(r).wait_send()
    for r in (1, 3, 5, 7):
        k1(r).wait_send()
    for r in range(1, 8):
        gate_copy(r).wait_send()
        gate_copy(r).wait_recv()

    def finish(c, carry):
        @pl.when(is_end)
        def _():
            s1(c).wait_send()
            to_pair(rt2, c).wait_send()
            to_own(rt2, c).wait()

        @pl.when(is_mid)
        def _():
            s2(c).wait_send()
            s3(c).wait_send()
            to_pair(ra, c).wait_send()
            to_own(ra, c).wait()

        remote(ra.at[c], gout.at[(1 - y) * chunks + c], ys.at[c], yr.at[c], (dp ^ 1, ex)).wait_recv()
        return carry

    lax.fori_loop(0, chunks, finish, 0)


def experts_call(x, c, meta, expand_weight, reduce_weight):
    count, d = x.shape
    ff = expand_weight.shape[2]
    chunks = 4 * ff // 256
    dma = pltpu.SemaphoreType.DMA
    vmem = pl.BlockSpec(memory_space=pltpu.VMEM)
    anywhere = pl.BlockSpec(memory_space=pl.ANY)
    return pl.pallas_call(
        expert_kernel,
        name="experts",
        out_shape=(
            jax.ShapeDtypeStruct((count, d), F32),
            jax.ShapeDtypeStruct((count, d), F32),
            jax.ShapeDtypeStruct((8, 2, 8, count), F32),
            jax.ShapeDtypeStruct((2 * chunks, d, 256), LOW),
        ),
        in_specs=[vmem, vmem, vmem, anywhere, anywhere],
        out_specs=(vmem, vmem, vmem, anywhere),
        scratch_shapes=[
            pltpu.VMEM((8, count, d), LOW),
            pltpu.VMEM((8, 16, count), F32),
            pltpu.VMEM((2, d, ff), LOW),
            pltpu.VMEM((2, ff, d), LOW),
            pltpu.VMEM((8 * CAP, d), LOW),
            pltpu.VMEM((8 * CAP, d), LOW),
            pltpu.VMEM((d, 8 * CAP), LOW),
            pltpu.VMEM((d, 8 * CAP), LOW),
            pltpu.VMEM((2 * CAP, d), LOW),
            pltpu.VMEM((8 * CAP, ff), LOW),
            pltpu.VMEM((8 * CAP, ff), LOW),
            pltpu.VMEM((2, 8 * CAP, d), LOW),
            pltpu.VMEM((2, 8 * CAP, d), LOW),
            pltpu.VMEM((chunks, d, 256), LOW),
            pltpu.VMEM((chunks, d, 256), LOW),
            pltpu.VMEM((chunks, d, 256), LOW),
            pltpu.VMEM((4, CAP, ff), LOW),
            pltpu.VMEM((4, CAP, ff), LOW),
            pltpu.VMEM((8, 2, 8, count), F32),
            dma((4,)),
            dma((8,)), dma((8,)), dma((8,)), dma((8,)), dma((8,)), dma((8,)),
            dma((chunks,)), dma((chunks,)), dma((chunks,)), dma((chunks,)), dma((chunks,)),
            dma((chunks,)), dma((chunks,)), dma((chunks,)),
            dma((4,)), dma((4,)), dma((4,)), dma((4,)),
        ],
        compiler_params=pltpu.CompilerParams(
            collective_id=0, has_side_effects=True, vmem_limit_bytes=62 * MIB
        ),
    )(x, c, meta, expand_weight, reduce_weight)


def widen_kernel(r_ref, e_ref, reduce_ref, expand_ref):
    reduce_ref[0] = r_ref[0].astype(F32).T
    expand_ref[0] = e_ref[0].astype(F32)


def widen_call(chunks, slots, d, ff):
    n = ff // 256
    return pl.pallas_call(
        widen_kernel,
        name="widen",
        grid=(slots, n),
        in_specs=[
            pl.BlockSpec((1, d, 256), lambda s, f: (s * 2 * n + f, 0, 0)),
            pl.BlockSpec((1, d, 256), lambda s, f: (s * 2 * n + n + f, 0, 0)),
        ],
        out_specs=(
            pl.BlockSpec((1, 256, d), lambda s, f: (s, f, 0)),
            pl.BlockSpec((1, d, 256), lambda s, f: (s, 0, f)),
        ),
        out_shape=(
            jax.ShapeDtypeStruct((slots, ff, d), F32),
            jax.ShapeDtypeStruct((slots, d, ff), F32),
        ),
    )(chunks, chunks)


ROWS_OUT, ROWS_TWO, ROWS_QUERY, ROWS_PAIR, ROWS_ONE = 0, 960, 1168, 2128, 2256
PIECE = 320


def back_first(v):
    count, d = v.cot.shape
    half = count // 2
    experts = v.router2.shape[1]
    grad_gates = jnp.concatenate([v.dg[g, j, 0:1, :] for g in range(8) for j in range(2)], 0)
    gates = v.g2[...]
    grad_logits = gates * (grad_gates - jnp.sum(gates * grad_gates, 0, keepdims=True))
    grad_logits = grad_logits.astype(LOW)
    gain = v.gain[1:2]
    v.pay[...] = jnp.zeros_like(v.pay)
    v.small[0] = jnp.zeros_like(v.small[0])
    per_image = []
    grad_gain = jnp.zeros((1, d), F32)
    grad_bias = jnp.zeros((1, d), F32)
    for i in range(2):
        rows = slice(i * half, (i + 1) * half)
        grad = v.grn[rows, :] + dot_tn(grad_logits[:, rows], v.router2[v.task[i]])
        per_image.append(dot(grad_logits[:, rows], v.n2[rows, :]))
        normal, scale = center(v.mid[rows, :])
        grad_gain = grad_gain + jnp.sum(grad * normal, 0, keepdims=True)
        grad_bias = grad_bias + jnp.sum(grad, 0, keepdims=True)
        total = v.cot[rows, :].astype(F32) + center_back(grad, normal, scale, gain)
        v.gmid[rows, :] = total
        low = total.astype(LOW)
        v.gbranch[rows, :] = low
        v.gheads[rows, :] = dot_nt(low, v.wo[...]).astype(LOW)
    v.small[0, 1:2, :] = grad_gain
    v.small[0, 3:4, :] = grad_bias
    v.pay[ROWS_OUT:ROWS_OUT + v.heads.shape[1], :] = dot_tn(v.heads[...], v.gbranch[...]).astype(LOW)
    place_tasks(v, ROWS_TWO, per_image, experts)


def place_tasks(v, start, per_image, experts):
    for j in range(v.router1.shape[0]):
        mine = [jnp.where(v.task[i] == j, per_image[i], 0.0) for i in range(2)]
        at = start + j * experts
        v.pay[at:at + experts, :] = (mine[0] + mine[1]).astype(LOW)


def back_attention(v, i, dp, ex):
    count, d = v.cot.shape
    half = count // 2
    heads = v.heads.shape[1]
    head = v.kv.shape[2] // 2
    picks = v.pick.shape[1]
    experts = v.router1.shape[1]
    to_query, to_value = head_maps(heads // head, head)
    owner = lax.div(lax.broadcasted_iota(jnp.int32, (half, heads), 1), head)
    lane = lax.broadcasted_iota(jnp.int32, (half, experts), 1)
    rows = slice(i * half, (i + 1) * half)
    kv = v.kv[i]
    gates = v.g1[rows, :]
    grad_gates = jnp.zeros((half, experts), F32)
    grad_pair = jnp.zeros((2 * head, 4 * half), F32)
    for k in range(picks):
        at = picks * i + k
        mine = owner == v.pick[rows, k:k + 1]
        named = lane == v.pick[rows, k:k + 1]
        gate = jnp.sum(jnp.where(named, gates, 0.0), 1, keepdims=True)
        grad_heads = v.gheads[rows, :]
        grad = dot(jnp.where(mine, grad_heads, jnp.zeros_like(grad_heads)), to_value)
        attended = v.att[at]
        total = attended[:, 0:1]
        grad_gates = grad_gates + jnp.where(named, jnp.sum(grad * attended, 1, keepdims=True), 0.0)
        grad = ((gate * grad).astype(LOW).astype(F32) / total).astype(LOW)
        inner = jnp.sum(grad.astype(F32) * attended, 1, keepdims=True)
        expo = v.eb[at]
        grad_scores = (expo.astype(F32) * (dot_nt(grad, kv) - inner)).astype(LOW)
        grad_query = (dot(grad_scores, kv) * head ** -0.5).astype(LOW)
        spread = dot_nt(grad_query, to_query).astype(LOW)
        if k == 0:
            v.gqa[rows, :] = jnp.where(mine, spread, jnp.zeros_like(spread))
        else:
            v.gqa[rows, :] = jnp.where(mine, spread, v.gqa[rows, :])
        grad_pair = grad_pair + dot(v.q8[at].astype(F32).T.astype(LOW), grad_scores)
        grad_pair = grad_pair + dot(grad.astype(F32).T.astype(LOW), expo)
    grad_logits = gates * (grad_gates - jnp.sum(gates * grad_gates, 1, keepdims=True))
    v.gl1[rows, :] = grad_logits.astype(LOW)
    for r in range(4):
        v.dkv[r, i] = grad_pair[:, r * half:(r + 1) * half].astype(LOW)


def pair_copy(v, r, dp, ex):
    return remote(v.dkv.at[r], v.din.at[r], v.ps.at[r], v.pr.at[r], (dp, ex ^ r))


def back_last(v):
    count, d = v.cot.shape
    half = count // 2
    experts = v.router1.shape[1]
    heads = v.heads.shape[1]
    width = v.kv.shape[2]
    gain = v.gain[0:1]
    grad_gain = jnp.zeros((1, d), F32)
    grad_bias = jnp.zeros((1, d), F32)
    grad_pair = jnp.zeros((width, d), F32)
    per_image = []
    for i in range(2):
        rows = slice(i * half, (i + 1) * half)
        pair = v.dkv[0, i].astype(F32)
        for r in (1, 2, 3):
            pair = pair + v.din[r, i].astype(F32)
        grad_pair = grad_pair + dot(pair.astype(LOW), v.n1[rows, :])
        grad = dot_nt(v.gqa[rows, :], v.wq[...]) + dot_nt(pair.T.astype(LOW), v.wkv[...])
        grad = grad + dot(v.gl1[rows, :], v.router1[v.task[i]])
        per_image.append(dot_tn(v.gl1[rows, :], v.n1[rows, :]))
        normal, scale = center(v.tok[rows, :].astype(F32))
        grad_gain = grad_gain + jnp.sum(grad * normal, 0, keepdims=True)
        grad_bias = grad_bias + jnp.sum(grad, 0, keepdims=True)
        v.gtok[rows, :] = v.gmid[rows, :] + center_back(grad, normal, scale, gain)
    v.small[0, 0:1, :] = grad_gain
    v.small[0, 2:3, :] = grad_bias
    v.pay[ROWS_QUERY:ROWS_QUERY + heads, :] = dot_tn(v.gqa[...], v.n1[...]).astype(LOW)
    v.pay[ROWS_PAIR:ROWS_PAIR + width, :] = grad_pair.astype(LOW)
    place_tasks(v, ROWS_ONE, per_image, experts)


def count_usage(v):
    count, d = v.cot.shape
    half = count // 2
    experts = v.router1.shape[1]
    picks = v.pick.shape[1]
    lane = lax.broadcasted_iota(jnp.int32, (half, d), 1)
    task = lax.broadcasted_iota(jnp.int32, (experts, d), 0)
    for which, ref in enumerate((v.pick, v.pick2)):
        table = jnp.zeros((experts, d), F32)
        for i in range(2):
            rows = slice(i * half, (i + 1) * half)
            named = jnp.zeros((half, d), F32)
            for k in range(picks):
                named = named + jnp.where(lane == ref[rows, k:k + 1], 1.0, 0.0)
            table = table + jnp.where(task == v.task[i], jnp.sum(named, 0, keepdims=True), 0.0)
        v.small[0, 8 + which * experts:8 + (which + 1) * experts, :] = table


def shared_reduce(v, dp, ex, pause):
    y = lax.rem(dp, 2)
    z = lax.div(dp, 2)
    is_end = (z == 0) | (z == 3)
    is_mid = (z == 1) | (z == 2)
    toward = jnp.where(z < 2, dp + 2, dp - 2)
    outer = jnp.where(z == 1, dp - 2, jnp.where(z == 2, dp + 2, dp))
    core = lax.rem(ex, 2)
    mine = y * 2 + lax.div(ex, 2)
    side = 4 * PIECE

    def part(ref, c, q):
        return ref.at[pl.ds(pl.multiple_of(c * side + q * PIECE, PIECE), PIECE), :]

    def whole(ref, c):
        return ref.at[pl.ds(pl.multiple_of(c * side, side), side), :]

    def exchange(stage, device):
        return remote(v.small.at[stage], v.small_in.at[stage], v.ss.at[stage], v.sr.at[stage], device)

    def plane(r):
        return (dp ^ (r // 2), ex ^ (2 * (r % 2)))

    partner = (dp, ex ^ 1)
    first = remote(whole(v.pay, 1 - core), v.half_in, v.as_.at[0], v.ar.at[0], partner)
    first.start()
    small = exchange(0, partner)
    small.start()
    small.wait_recv()
    v.small[1] = v.small[0] + v.small_in[0]
    small1 = exchange(1, plane(1))
    small1.start()
    first.wait_recv()
    own = whole(v.pay, core)
    own[...] = (own[...].astype(F32) + v.half_in[...].astype(F32)).astype(LOW)
    scatter = [
        remote(part(v.pay, core, mine ^ r), v.piece_in.at[r], v.as_.at[r], v.ar.at[r], plane(r))
        for r in (1, 2, 3)
    ]
    for copy in scatter:
        copy.start()
    small1.wait_recv()
    v.small[2] = v.small[1] + v.small_in[1]
    small2 = exchange(2, plane(2))
    small2.start()
    pause(0)
    small2.wait_recv()
    v.small[3] = v.small[2] + v.small_in[2]
    for copy in scatter:
        copy.wait_recv()
    own = part(v.pay, core, mine)
    total = own[...].astype(F32)
    for r in (1, 2, 3):
        total = total + v.piece_in[r].astype(F32)
    own[...] = total.astype(LOW)

    in_end = remote(own, v.zb, v.zs.at[0], v.zr.at[0], (toward, ex))
    in_small = remote(v.small.at[3], v.small_in.at[3], v.zs.at[1], v.zr.at[1], (toward, ex))
    mid = remote(v.zb, v.zc, v.zs.at[0], v.zr.at[2], (toward, ex))
    mid_small = remote(v.small.at[4], v.small_in.at[4], v.zs.at[1], v.zr.at[3], (toward, ex))
    spread = part(v.shared, core, mine)
    out_mid = remote(spread, spread, v.zs.at[2], v.zr.at[4], (outer, ex))
    out_small = remote(v.stats, v.stats, v.zs.at[3], v.zr.at[5], (outer, ex))

    @pl.when(is_end)
    def _():
        in_end.start()
        in_small.start()

    pause(1)

    @pl.when(is_mid)
    def _():
        in_end.wait_recv()
        v.zb[...] = (own[...].astype(F32) + v.zb[...].astype(F32)).astype(LOW)
        mid.start()
        in_small.wait_recv()
        v.small[4] = v.small[3] + v.small_in[3]
        mid_small.start()

    pause(2)

    @pl.when(is_mid)
    def _():
        mid.wait_recv()
        spread[...] = (v.zb[...].astype(F32) + v.zc[...].astype(F32)).astype(LOW)
        out_mid.start()
        mid_small.wait_recv()
        v.stats[...] = v.small[4] + v.small_in[4]
        out_small.start()

    pause(3)

    @pl.when(is_end)
    def _():
        out_mid.wait_recv()
        out_small.wait_recv()

    gather = [remote(spread, spread, v.bs.at[r], v.br.at[r], plane(r)) for r in (1, 2, 3)]
    for copy in gather:
        copy.start()
    pause(4)
    for r in (1, 2, 3):
        there = part(v.shared, core, mine ^ r)
        remote(there, there, v.bs.at[r], v.br.at[r], plane(r)).wait_recv()
    last = remote(whole(v.shared, core), whole(v.shared, core), v.bs.at[0], v.br.at[0], partner)
    last.start()
    other = whole(v.shared, 1 - core)
    remote(other, other, v.bs.at[0], v.br.at[0], partner).wait_recv()

    first.wait_send()
    for copy in [small, small1, small2, *scatter, *gather, last]:
        copy.wait_send()

    @pl.when(is_end)
    def _():
        in_end.wait_send()
        in_small.wait_send()

    @pl.when(is_mid)
    def _():
        mid.wait_send()
        mid_small.wait_send()
        out_mid.wait_send()
        out_small.wait_send()


def back_kernel(v):
    dp = lax.axis_index("dp")
    ex = lax.axis_index("expert")
    z = lax.div(dp, 2)
    is_mid = (z == 1) | (z == 2)
    toward = jnp.where(z < 2, dp + 2, dp - 2)
    outer = jnp.where(z == 1, dp - 2, jnp.where(z == 2, dp + 2, dp))
    barrier = pltpu.get_barrier_semaphore()
    for r in range(1, 8):
        pl.semaphore_signal(
            barrier, 1, device_id=(dp ^ (r // 4), ex ^ (r % 4)), device_id_type=MESH
        )
    pl.semaphore_signal(barrier, 1, device_id=(toward, ex), device_id_type=MESH)

    @pl.when(is_mid)
    def _():
        pl.semaphore_signal(barrier, 1, device_id=(outer, ex), device_id_type=MESH)

    v.out[...] = (v.mid[...] + v.fin[...]).astype(LOW)
    back_first(v)
    count_usage(v)
    pl.semaphore_wait(barrier, jnp.where(is_mid, 9, 8))
    for i in range(2):
        back_attention(v, i, dp, ex)
    for r in (1, 2, 3):
        pair_copy(v, r, dp, ex).start()
    for r in (1, 2, 3):
        pair_copy(v, r, dp, ex).wait_recv()
    back_last(v)
    shared_reduce(v, dp, ex, lambda stage: None)
    for r in (1, 2, 3):
        pair_copy(v, r, dp, ex).wait_send()


def back_scratch(count, d, heads, width):
    half = count // 2
    dma = pltpu.SemaphoreType.DMA
    return dict(
        pay=pltpu.VMEM((8 * PIECE, d), LOW),
        small=pltpu.VMEM((5, 40, d), F32), small_in=pltpu.VMEM((5, 40, d), F32),
        gmid=pltpu.VMEM((count, d), F32), gbranch=pltpu.VMEM((count, d), LOW),
        gheads=pltpu.VMEM((count, heads), LOW), gqa=pltpu.VMEM((count, heads), LOW),
        gl1=pltpu.VMEM((count, 16), LOW),
        dkv=pltpu.VMEM((4, 2, width, half), LOW), din=pltpu.VMEM((4, 2, width, half), LOW),
        half_in=pltpu.VMEM((4 * PIECE, d), LOW), piece_in=pltpu.VMEM((4, PIECE, d), LOW),
        zb=pltpu.VMEM((PIECE, d), LOW), zc=pltpu.VMEM((PIECE, d), LOW),
        ps=dma((4,)), pr=dma((4,)), ss=dma((4,)), sr=dma((4,)), as_=dma((4,)), ar=dma((4,)),
        zs=dma((4,)), zr=dma((6,)), bs=dma((4,)), br=dma((4,)),
    )


def back_call(f, tok, cot, pick, pick2, task, gain, wq, wkv, wo, router1, router2, fin, grn, dg):
    count, d = tok.shape
    vm = pltpu.VMEM
    return run_kernel(
        back_kernel, "back",
        dict(
            tok=(tok, vm), cot=(cot, vm), pick=(pick, vm), pick2=(pick2, vm), task=(task, pltpu.SMEM),
            gain=(gain, vm), wq=(wq, vm), wkv=(wkv, vm), wo=(wo, vm),
            router1=(router1, vm), router2=(router2, vm),
            n1=(f.n1, vm), n2=(f.n2, vm), mid=(f.mid, vm), heads=(f.heads, vm), kv=(f.kv, vm),
            q8=(f.q8, vm), eb=(f.eb, vm), att=(f.att, vm), g1=(f.g1, vm), g2=(f.g2, vm),
            fin=(fin, vm), grn=(grn, vm), dg=(dg, vm),
        ),
        dict(
            out=((count, d), LOW, vm), gtok=((count, d), F32, vm),
            shared=((8 * PIECE, d), LOW, vm), stats=((40, d), F32, vm),
        ),
        back_scratch(count, d, wq.shape[1], wkv.shape[1]),
        2,
    )


def body_fast(
    tokens,
    task_ids,
    attention_picks,
    feedforward_picks,
    norm_gain,
    norm_bias,
    query_weight,
    key_weight,
    value_weight,
    output_weight,
    attention_router,
    feedforward_router,
    expand_weight,
    reduce_weight,
    cotangent,
):
    images, patches, width = tokens.shape
    count = images * patches
    tasks, _, experts = attention_router.shape
    head = key_weight.shape[1]
    picks = attention_picks.shape[2]
    slots = expand_weight.shape[0]
    ff = expand_weight.shape[2]
    wide = query_weight.shape[1]
    tok = tokens.reshape(count, width)
    cot = cotangent.reshape(count, width)
    pick = attention_picks.reshape(count, picks)
    pick2 = feedforward_picks.reshape(count, picks)
    wkv = jnp.concatenate([key_weight, value_weight], 1)

    def experts_first(router):
        return jnp.pad(jnp.swapaxes(router, 1, 2), ((0, 0), (0, 16 - experts), (0, 0)))

    router1 = experts_first(attention_router)
    router2 = experts_first(feedforward_router)
    f = front_call(
        tok, cot, pick, pick2.T, task_ids, norm_gain, norm_bias, query_weight, wkv, output_weight,
        router1, router2,
    )
    fin, grn, dg, chunks = experts_call(f.n2, f.ca, f.meta, expand_weight, reduce_weight)
    b = back_call(
        f, tok, cot, pick, pick2, task_ids, norm_gain, query_weight, wkv, output_weight,
        router1, router2, fin, grn, dg,
    )
    grad_reduce, grad_expand = widen_call(chunks, slots, width, ff)

    def section(start, rows):
        return b.shared[start:start + rows].astype(F32)

    def experts_last(start):
        table = section(start, tasks * 16).reshape(tasks, 16, width)[:, :experts]
        return jnp.swapaxes(table, 1, 2)

    pair = section(ROWS_PAIR, 2 * head)
    usage = b.stats[8:40, :experts].reshape(2, 16, experts)[:, :tasks]
    return (
        b.out.reshape(images, patches, width),
        b.gtok.reshape(images, patches, width),
        b.stats[0:2],
        b.stats[2],
        b.stats[3],
        section(ROWS_QUERY, wide).T,
        pair[:head].T,
        pair[head:].T,
        section(ROWS_OUT, wide),
        experts_last(ROWS_ONE),
        experts_last(ROWS_TWO),
        grad_expand,
        grad_reduce,
        usage,
    )


def normalize(value, gain, bias):
    mean = jnp.mean(value, -1, keepdims=True)
    centred = value - mean
    spread = jnp.mean(centred * centred, -1, keepdims=True)
    return centred * lax.rsqrt(spread + EPS) * gain + bias


def gate_weights(logits, picks_hot):
    chosen = jnp.sum(picks_hot * logits[..., None, :], -1)
    return jax.nn.softmax(chosen, -1)


def activate(value):
    return jax.nn.gelu(value, approximate=True)


def body(
    tokens,
    task_ids,
    attention_picks,
    feedforward_picks,
    norm_gain,
    norm_bias,
    query_weight,
    key_weight,
    value_weight,
    output_weight,
    attention_router,
    feedforward_router,
    expand_weight,
    reduce_weight,
    cotangent,
):
    images, patches, width = tokens.shape
    count = images * patches
    tasks = attention_router.shape[0]
    experts = attention_router.shape[2]
    head = key_weight.shape[1]
    picks = attention_picks.shape[2]
    slots = expand_weight.shape[0]
    groups = lax.axis_size("expert")
    lanes = groups * slots
    f32 = jnp.float32
    low_type = jnp.bfloat16
    inputs = tokens.astype(f32).reshape(count, width)
    expert_range = jnp.arange(experts, dtype=jnp.int32)
    task_hot = (task_ids[:, None] == jnp.arange(tasks, dtype=jnp.int32)[None, :]).astype(f32)
    task_low = task_hot.astype(low_type)
    attend_hot = (attention_picks[..., None] == expert_range).astype(f32)
    attend_low = attend_hot.astype(low_type)
    choices = feedforward_picks.reshape(count, picks)
    feed_hot = (choices[..., None] == expert_range).astype(f32)
    flat = choices.reshape(count * picks)
    marks = (flat[:, None] == expert_range[None, :]).astype(jnp.int32)
    before = jnp.cumsum(marks, axis=0) - marks
    position = flat * CAP + jnp.sum(before * marks, axis=1)
    first, first_back = jax.vjp(normalize, inputs, norm_gain[0], norm_bias[0])
    normed_one = first.astype(low_type)
    shaped_one = normed_one.reshape(images, patches, width)
    router_one = jnp.einsum(
        "it,tde->ide", task_low, attention_router, preferred_element_type=f32
    ).astype(low_type)
    logits_one = jnp.einsum("ipd,ide->ipe", shaped_one, router_one, preferred_element_type=f32)
    gates_one, gates_one_back = jax.vjp(lambda value: gate_weights(value, attend_hot), logits_one)
    queries_all = jnp.dot(normed_one, query_weight, preferred_element_type=f32).astype(low_type)
    queries_all = queries_all.reshape(images, patches, experts, head)
    queries = jnp.einsum(
        "ipke,ipeh->ipkh", attend_low, queries_all, preferred_element_type=f32
    ).astype(low_type)
    queries = queries.reshape(images, patches * picks, head)
    key_value = jnp.concatenate([key_weight, value_weight], 1)
    pair = jnp.dot(normed_one, key_value, preferred_element_type=f32).astype(low_type)
    pair = pair.reshape(images, patches, 2 * head)
    pair_all = lax.all_gather(pair, "expert", axis=1, tiled=True)
    keys_all = pair_all[:, :, :head]
    values_all = pair_all[:, :, head:]
    scores = jnp.einsum("irh,ish->irs", queries, keys_all, preferred_element_type=f32) * 0.125
    top = jnp.max(scores, -1, keepdims=True)
    expo = jnp.exp(scores - top)
    total = jnp.sum(expo, -1, keepdims=True)
    log_total = top + jnp.log(total)
    probs_low = (expo / total).astype(low_type)
    attended = jnp.einsum("irs,ish->irh", probs_low, values_all, preferred_element_type=f32)
    attended = attended.reshape(images, patches, picks, head)
    weighted = gates_one[..., None] * attended
    heads = jnp.einsum("ipke,ipkh->ipeh", attend_hot, weighted, precision=HIGH)
    heads = heads.reshape(count, experts * head).astype(low_type)
    middle = inputs + jnp.dot(heads, output_weight, preferred_element_type=f32)
    second, second_back = jax.vjp(normalize, middle, norm_gain[1], norm_bias[1])
    normed_two = second.astype(low_type)
    shaped_two = normed_two.reshape(images, patches, width)
    router_two = jnp.einsum(
        "it,tde->ide", task_low, feedforward_router, preferred_element_type=f32
    ).astype(low_type)
    logits_two = jnp.einsum(
        "ipd,ide->ipe", shaped_two, router_two, preferred_element_type=f32
    ).reshape(count, experts)
    gates_two, gates_two_back = jax.vjp(lambda value: gate_weights(value, feed_hot), logits_two)
    outgoing = (
        jnp.zeros((lanes * CAP, width), low_type)
        .at[position]
        .set(jnp.repeat(normed_two, picks, axis=0))
    )
    outgoing = outgoing.reshape(groups, slots * CAP, width)
    received = lax.all_to_all(outgoing, "expert", split_axis=0, concat_axis=0, tiled=True).reshape(
        groups, slots, CAP, width
    )
    hidden = jnp.einsum("nscd,sdf->nscf", received, expand_weight, preferred_element_type=f32)
    activated, activate_back = jax.vjp(activate, hidden)
    active_low = activated.astype(low_type)
    produced = jnp.einsum(
        "nscf,sfd->nscd", active_low, reduce_weight, preferred_element_type=f32
    ).astype(low_type)
    produced = produced.reshape(groups, slots * CAP, width)
    returned = lax.all_to_all(produced, "expert", split_axis=0, concat_axis=0, tiled=True).reshape(
        lanes * CAP, width
    )
    picked = returned[position].astype(f32).reshape(count, picks, width)
    final = middle + jnp.sum(gates_two[..., None] * picked, 1)
    output = final.astype(low_type).reshape(images, patches, width)
    grad_final = cotangent.astype(f32).reshape(count, width)
    grad_gates_two = jnp.sum(picked * grad_final[:, None, :], -1)
    grad_picked = (
        (gates_two[..., None] * grad_final[:, None, :])
        .astype(low_type)
        .reshape(count * picks, width)
    )
    grad_send = jnp.zeros((lanes * CAP, width), low_type).at[position].set(grad_picked)
    grad_send = grad_send.reshape(groups, slots * CAP, width)
    grad_produced = lax.all_to_all(
        grad_send, "expert", split_axis=0, concat_axis=0, tiled=True
    ).reshape(groups, slots, CAP, width)
    grad_reduce = jnp.einsum(
        "nscf,nscd->sfd", active_low, grad_produced, preferred_element_type=f32
    )
    grad_active = jnp.einsum(
        "nscd,sfd->nscf", grad_produced, reduce_weight, preferred_element_type=f32
    )
    grad_hidden = activate_back(grad_active)[0].astype(low_type)
    grad_expand = jnp.einsum("nscd,nscf->sdf", received, grad_hidden, preferred_element_type=f32)
    grad_rows = jnp.einsum(
        "nscf,sdf->nscd", grad_hidden, expand_weight, preferred_element_type=f32
    ).astype(low_type)
    grad_rows = grad_rows.reshape(groups, slots * CAP, width)
    grad_back = lax.all_to_all(
        grad_rows, "expert", split_axis=0, concat_axis=0, tiled=True
    ).reshape(lanes * CAP, width)
    grad_normed_two = jnp.sum(grad_back[position].astype(f32).reshape(count, picks, width), 1)
    grad_logits_two = (
        gates_two_back(grad_gates_two)[0].astype(low_type).reshape(images, patches, experts)
    )
    per_image_two = jnp.einsum(
        "ipd,ipe->ide", shaped_two, grad_logits_two, preferred_element_type=f32
    )
    grad_feed_router = jnp.einsum("it,ide->tde", task_hot, per_image_two, precision=HIGH)
    grad_normed_two = grad_normed_two + jnp.einsum(
        "ipe,ide->ipd", grad_logits_two, router_two, preferred_element_type=f32
    ).reshape(count, width)
    grad_middle_norm, grad_gain_two, grad_bias_two = second_back(grad_normed_two)
    grad_middle = grad_final + grad_middle_norm
    grad_branch = grad_middle.astype(low_type)
    grad_output = jnp.einsum("tc,td->cd", heads, grad_branch, preferred_element_type=f32)
    grad_heads = jnp.einsum(
        "td,cd->tc", grad_branch, output_weight, preferred_element_type=f32
    ).astype(low_type)
    grad_heads = grad_heads.reshape(images, patches, experts, head)
    grad_selected = jnp.einsum(
        "ipke,ipeh->ipkh", attend_low, grad_heads, preferred_element_type=f32
    )
    grad_gates_one = jnp.sum(attended * grad_selected, -1)
    grad_attended = (
        (gates_one[..., None] * grad_selected)
        .astype(low_type)
        .reshape(images, patches * picks, head)
    )
    scores_back = jnp.einsum("irh,ish->irs", queries, keys_all, preferred_element_type=f32) * 0.125
    probs_back = jnp.exp(scores_back - log_total)
    grad_values = jnp.einsum(
        "irs,irh->ish", probs_back.astype(low_type), grad_attended, preferred_element_type=f32
    )
    grad_probs = jnp.einsum("irh,ish->irs", grad_attended, values_all, preferred_element_type=f32)
    inner_sum = jnp.sum(probs_back * grad_probs, -1, keepdims=True)
    grad_scores = (probs_back * (grad_probs - inner_sum)).astype(low_type)
    grad_query_sel = (
        jnp.einsum("irs,ish->irh", grad_scores, keys_all, preferred_element_type=f32) * 0.125
    )
    grad_keys = jnp.einsum("irs,irh->ish", grad_scores, queries, preferred_element_type=f32) * 0.125
    grad_pair = jnp.concatenate([grad_keys, grad_values], -1)
    pair_sum = lax.psum_scatter(
        grad_pair.astype(jnp.bfloat16), "expert", scatter_dimension=1, tiled=True
    ).astype(jnp.float32)
    pair_sum = pair_sum.astype(low_type).reshape(count, 2 * head)
    grad_query_sel = grad_query_sel.reshape(images, patches, picks, head)
    grad_queries_all = jnp.einsum("ipke,ipkh->ipeh", attend_hot, grad_query_sel, precision=HIGH)
    grad_queries_all = grad_queries_all.astype(low_type).reshape(count, experts * head)
    grad_logits_one = gates_one_back(grad_gates_one)[0].astype(low_type)
    per_image_one = jnp.einsum(
        "ipd,ipe->ide", shaped_one, grad_logits_one, preferred_element_type=f32
    )
    grad_attend_router = jnp.einsum("it,ide->tde", task_hot, per_image_one, precision=HIGH)
    grad_query = jnp.einsum("td,tc->dc", normed_one, grad_queries_all, preferred_element_type=f32)
    grad_key_value = jnp.einsum("td,tc->dc", normed_one, pair_sum, preferred_element_type=f32)
    grad_normed_one = jnp.einsum(
        "tc,dc->td", grad_queries_all, query_weight, preferred_element_type=f32
    )
    grad_normed_one = grad_normed_one + jnp.einsum(
        "tc,dc->td", pair_sum, key_value, preferred_element_type=f32
    )
    grad_normed_one = grad_normed_one + jnp.einsum(
        "ipe,ide->ipd", grad_logits_one, router_one, preferred_element_type=f32
    ).reshape(count, width)
    grad_inputs_norm, grad_gain_one, grad_bias_one = first_back(grad_normed_one)
    grad_tokens = (grad_middle + grad_inputs_norm).reshape(images, patches, width)
    grad_gain = jnp.stack([grad_gain_one, grad_gain_two])
    grad_bias = jnp.stack([grad_bias_one, grad_bias_two])
    feed_shaped = feed_hot.reshape(images, patches, picks, experts)
    usage = jnp.stack(
        [
            jnp.einsum("it,ipke->te", task_hot, attend_hot, precision=HIGH),
            jnp.einsum("it,ipke->te", task_hot, feed_shaped, precision=HIGH),
        ]
    )
    shared = lax.psum(
        (
            grad_query,
            grad_key_value,
            grad_output,
            grad_attend_router,
            grad_feed_router,
            grad_gain,
            grad_bias,
            usage,
        ),
        ("dp", "expert"),
    )
    grad_expand_sum, grad_reduce_sum = (
        lax.psum(grad_expand.astype(jnp.bfloat16), "dp").astype(jnp.float32),
        lax.psum(grad_reduce.astype(jnp.bfloat16), "dp").astype(jnp.float32),
    )
    grad_key_sum = shared[1][:, :head]
    grad_value_sum = shared[1][:, head:]
    return (
        output,
        grad_tokens,
        shared[5],
        shared[6][0],
        shared[6][1],
        shared[0],
        grad_key_sum,
        grad_value_sum,
        shared[2],
        shared[3],
        shared[4],
        grad_expand_sum,
        grad_reduce_sum,
        shared[7],
    )


def solution(mesh):
    placed = (
        P("dp", "expert", None),
        P("dp"),
        P("dp", "expert", None),
        P("dp", "expert", None, None),
        P(),
        P(),
        P(),
        P(),
        P(),
        P(),
        P(),
        P(),
        P("expert", None, None),
        P("expert", None, None),
        P("dp", "expert", None),
    )
    fast = mesh.shape["dp"] == 8 and mesh.shape["expert"] == 4
    return jax.shard_map(
        body_fast if fast else body,
        mesh=mesh,
        in_specs=placed,
        out_specs=(
            P("dp", "expert", None),
            P("dp", "expert", None),
            P(),
            P(),
            P(),
            P(),
            P(),
            P(),
            P(),
            P(),
            P(),
            P("expert", None, None),
            P("expert", None, None),
            P(),
        ),
        check_vma=False,
    )
```

```python
import types

import jax
import jax.numpy as jnp
from jax import lax
from jax.experimental import pallas as pl
from jax.experimental.pallas import tpu as pltpu
from jax.sharding import PartitionSpec as P

CAP = 256


EPS = 1e-06
HIGH = lax.Precision.HIGHEST
F32 = jnp.float32
LOW = jnp.bfloat16
MESH = pl.DeviceIdType.MESH
MIB = 2**20


def dot(a, b):
    return jnp.dot(a, b, preferred_element_type=F32)


def dot_nt(a, b):
    return lax.dot_general(a, b, (((1,), (1,)), ((), ())), preferred_element_type=F32)


def dot_tn(a, b):
    return lax.dot_general(a, b, (((0,), (0,)), ((), ())), preferred_element_type=F32)


def remote(src, dst, send, recv, device):
    return pltpu.make_async_remote_copy(
        src_ref=src, dst_ref=dst, send_sem=send, recv_sem=recv,
        device_id=device, device_id_type=MESH,
    )


def run_kernel(kernel, name, ins, outs, scratch, collective):
    names = [*ins, *outs, *scratch]

    def body(*refs):
        kernel(types.SimpleNamespace(**dict(zip(names, refs, strict=True))))

    made = pl.pallas_call(
        body,
        name=name,
        out_shape=[jax.ShapeDtypeStruct(shape, dtype) for shape, dtype, _ in outs.values()],
        in_specs=[pl.BlockSpec(memory_space=space) for _, space in ins.values()],
        out_specs=[pl.BlockSpec(memory_space=space) for _, _, space in outs.values()],
        scratch_shapes=list(scratch.values()),
        compiler_params=pltpu.CompilerParams(
            collective_id=collective, has_side_effects=True, vmem_limit_bytes=62 * MIB
        ),
    )(*[array for array, _ in ins.values()])
    return types.SimpleNamespace(**dict(zip(outs, made, strict=True)))


def center(value):
    mean = jnp.mean(value, -1, keepdims=True)
    centred = value - mean
    scale = lax.rsqrt(jnp.mean(centred * centred, -1, keepdims=True) + EPS)
    return centred * scale, scale


def center_back(grad, normal, scale, gain):
    inner = grad * gain
    mean = jnp.mean(inner, -1, keepdims=True)
    along = jnp.mean(inner * normal, -1, keepdims=True)
    return scale * (inner - mean - normal * along)


def head_maps(heads, head):
    row = lax.broadcasted_iota(jnp.int32, (heads * head, 2 * head), 0)
    row = lax.rem(row, head)
    col = lax.broadcasted_iota(jnp.int32, (heads * head, 2 * head), 1)
    low = jnp.where(row == col, 1.0, 0.0).astype(LOW)
    high = jnp.where(row + head == col, 1.0, 0.0).astype(LOW)
    return low, high


def masked_softmax(logits, chosen, axis):
    top = jnp.max(jnp.where(chosen, logits, -1e30), axis, keepdims=True)
    expo = jnp.where(chosen, jnp.exp(jnp.minimum(logits - top, 0.0)), 0.0)
    return expo / jnp.sum(expo, axis, keepdims=True)


PIECE = 336
USED = 320
TASK_ROWS = 208
PAY = 1024


def gelu_parts(value):
    square = value * value
    inner = value * (0.7978845608028654 + 0.035677408136300125 * square)
    half = 0.5 + 0.5 * jnp.tanh(inner)
    act = value * half
    slope = half + act * (1.0 - half) * (1.5957691216057308 + 0.2140644488178007 * square)
    return act, slope


class Place:
    def __init__(self):
        self.dp = dp = lax.axis_index("dp")
        self.ex = lax.axis_index("expert")
        self.y = lax.rem(dp, 2)
        z = lax.div(dp, 2)
        self.is_end = (z == 0) | (z == 3)
        self.is_mid = (z == 1) | (z == 2)
        self.toward = (jnp.where(z < 2, dp + 2, dp - 2), self.ex)
        self.outer = (jnp.where(z == 1, dp - 2, jnp.where(z == 2, dp + 2, dp)), self.ex)
        self.core = lax.rem(self.ex, 2)
        self.spot = self.y * 2 + lax.div(self.ex, 2)

    def peer(self, r):
        return (self.dp ^ lax.div(r, 4), self.ex ^ lax.rem(r, 4))

    def plane(self, q):
        return (self.dp ^ lax.div(q, 2), self.ex ^ (2 * lax.rem(q, 2)))

    def group(self, r):
        return 2 * (self.ex ^ lax.rem(r, 4)) + (self.y ^ lax.div(r, 4))


def cot_copy(v, p, r):
    return remote(v.cot, v.ca.at[r], v.cs.at[r], v.cv.at[r], p.peer(r))


def cot_forward(v, p, r):
    return remote(v.ca.at[r], v.ca.at[r + 1], v.cs.at[r + 1], v.cv.at[r + 1], p.peer(1))


def row_copy(v, p, r, i):
    return remote(v.n2.at[i], v.xa.at[r, i], v.xs.at[r, i], v.xv.at[r, i], p.peer(r))


def row_forward(v, p, r, i):
    return remote(v.xa.at[r, i], v.xa.at[r + 1, i], v.xs.at[r + 1, i], v.xv.at[r + 1, i], p.peer(1))


def meta_copy(v, p, r):
    return remote(v.meta.at[p.group(r)], v.ma.at[r], v.ms.at[r], v.mv.at[r], p.peer(r))


def kv_copy(v, p, r):
    half = v.kv.shape[1] // 4
    return remote(
        v.kv.at[:, pl.ds(0, half), :], v.kv.at[:, pl.ds(r * half, half), :],
        v.ks.at[r], v.kr.at[r], p.peer(r),
    )


def front(v, p):
    count, d = v.tok.shape
    half = count // 2
    heads = v.heads.shape[1]
    head = v.kv.shape[2] // 2
    picks = v.pick.shape[1]
    gain = v.gain[...]
    bias = v.bias[...]
    for i in range(2):
        rows = slice(i * half, (i + 1) * half)
        normal, _ = center(v.tok[rows, :].astype(F32))
        normed = (normal * gain[0:1] + bias[0:1]).astype(LOW)
        v.n1[rows, :] = normed
        v.kv[i, 0:half, :] = dot(normed, v.wkv[...]).astype(LOW)
    pl.semaphore_wait(v.barrier, jnp.where(p.is_mid, 9, 8))
    for r in (1, 2, 3):
        kv_copy(v, p, r).start()
    for r in (2, 4, 6, 1):
        cot_copy(v, p, r).start()
    v.ca[0] = v.cot[...]
    v.gh[0:count, 0:heads] = dot(v.n1[...], v.wq[...]).astype(LOW)

    experts = v.router1.shape[1]
    number = lax.broadcasted_iota(jnp.int32, (experts, count), 0)
    chosen = number == v.pickt[0:1, :]
    for k in range(1, picks):
        chosen = chosen | (number == v.pickt[k:k + 1, :])
    earlier = lax.broadcasted_iota(jnp.int32, (count, count), 0) < lax.broadcasted_iota(
        jnp.int32, (count, count), 1
    )
    before = dot(jnp.where(chosen, 1.0, 0.0).astype(LOW), jnp.where(earlier, 1.0, 0.0).astype(LOW))
    rank = jnp.where(chosen, before, -1.0)

    to_query, to_value = head_maps(heads // head, head)
    owner = lax.div(lax.broadcasted_iota(jnp.int32, (half, heads), 1), head)
    lane = lax.broadcasted_iota(jnp.int32, (half, experts), 1)
    wide = lax.broadcasted_iota(jnp.int32, (half, 2 * head), 1)
    for r in (1, 2, 3):
        kv_copy(v, p, r).wait_recv()

    for i in range(2):
        rows = slice(i * half, (i + 1) * half)
        logits = dot_nt(v.n1[rows, :], v.router1[v.task[i]])
        named = [lane == v.pick[rows, k:k + 1] for k in range(picks)]
        allowed = named[0]
        for k in range(1, picks):
            allowed = allowed | named[k]
        gates = masked_softmax(logits, allowed, 1)
        v.g1[rows, :] = gates
        kv = v.kv[i]
        for k in range(picks):
            at = picks * i + k
            mine = owner == v.pick[rows, k:k + 1]
            gate = jnp.sum(jnp.where(named[k], gates, 0.0), 1, keepdims=True)
            all_queries = v.gh[rows, 0:heads]
            query = dot(jnp.where(mine, all_queries, jnp.zeros_like(all_queries)), to_query)
            query = (query * head ** -0.5).astype(LOW)
            v.q8[at] = query
            scores = dot_nt(query, kv)
            expo = jnp.exp(scores - jnp.max(scores, 1, keepdims=True))
            total = jnp.sum(expo, 1, keepdims=True)
            low = expo.astype(LOW)
            v.act[at * half:(at + 1) * half, 0:4 * half] = low
            attended = dot(low, kv) / total
            v.att[at] = jnp.where(wide == 0, total, attended)
            spread = dot_nt((gate * attended).astype(LOW), to_value).astype(LOW)
            if k == 0:
                v.heads[rows, :] = jnp.where(mine, spread, jnp.zeros_like(spread))
            else:
                v.heads[rows, :] = jnp.where(mine, spread, v.heads[rows, :])
        middle = v.tok[rows, :].astype(F32) + dot(v.heads[rows, :], v.wo[...])
        v.mid[rows, :] = middle
        normal, _ = center(middle)
        normed = (normal * gain[1:2] + bias[1:2]).astype(LOW)
        v.n2[i] = normed
        for r in (2, 4, 6, 1):
            row_copy(v, p, r, i).start()
        v.xa[0, i] = normed
        logits = dot_nt(v.router2[v.task[i]], normed)
        gates = masked_softmax(logits, rank[:, rows] >= 0.0, 0)
        v.g2[:, rows] = gates
        for g in range(8):
            v.meta[g, 0:2, rows] = rank[2 * g:2 * g + 2, rows]
            v.meta[g, 2:4, rows] = gates[2 * g:2 * g + 2, :]
            v.meta[g, 4:16, rows] = jnp.zeros((12, half), F32)
        if i == 0:
            for r in (2, 4, 6):
                cot_copy(v, p, r).wait_recv()
                cot_forward(v, p, r).start()
    v.ma[0] = v.meta[p.group(0)]
    for r in range(1, 8):
        meta_copy(v, p, r).start()


def chunk_first(v, p, c):
    return remote(v.ra.at[c], v.rb.at[c], v.s1s.at[c], v.s1r.at[c], p.toward)


def chunk_middle(v, p, c):
    return remote(v.rb.at[c], v.rc.at[c], v.s2s.at[c], v.s2r.at[c], p.toward)


def chunk_back(v, p, c):
    return remote(v.ra.at[c], v.rc.at[c], v.s3s.at[c], v.s2r.at[c], p.outer)


def chunk_pair(v, p, src, c):
    to = p.y * v.ra.shape[0] + c
    return remote(src.at[c], v.chunks.at[to], v.ys.at[c], v.yr.at[c], (p.dp ^ 1, p.ex))


def chunk_own(v, p, src, c):
    to = p.y * v.ra.shape[0] + c
    return pltpu.make_async_copy(src.at[c], v.chunks.at[to], v.ls.at[c])


def tick(v, p, t):
    chunks = v.ra.shape[0]

    @pl.when(p.is_mid & (t < chunks))
    def _():
        c = jnp.minimum(t, chunks - 1)
        chunk_first(v, p, c).wait_recv()
        v.rb[c] = (v.ra[c].astype(F32) + v.rb[c].astype(F32)).astype(LOW)
        chunk_middle(v, p, c).start()

    @pl.when(p.is_mid & (t >= 1) & (t < chunks + 1))
    def _():
        c = jnp.maximum(t - 1, 0)
        chunk_middle(v, p, c).wait_recv()
        v.ra[c] = (v.rb[c].astype(F32) + v.rc[c].astype(F32)).astype(LOW)
        chunk_back(v, p, c).start()
        chunk_pair(v, p, v.ra, c).start()
        chunk_own(v, p, v.ra, c).start()

    @pl.when(p.is_end & (t >= 2) & (t < chunks + 2))
    def _():
        c = jnp.maximum(t - 2, 0)
        chunk_middle(v, p, c).wait_recv()
        chunk_pair(v, p, v.rc, c).start()
        chunk_own(v, p, v.rc, c).start()


def ticks(v, p, first, after):
    def one(t, carry):
        tick(v, p, t)
        return carry

    lax.fori_loop(first, after, one, 0)


def chunks_done(v, p):
    chunks = v.ra.shape[0]

    def one(c, carry):
        @pl.when(p.is_end)
        def _():
            chunk_first(v, p, c).wait_send()
            chunk_pair(v, p, v.rc, c).wait_send()
            chunk_own(v, p, v.rc, c).wait()

        @pl.when(p.is_mid)
        def _():
            chunk_middle(v, p, c).wait_send()
            chunk_back(v, p, c).wait_send()
            chunk_pair(v, p, v.ra, c).wait_send()
            chunk_own(v, p, v.ra, c).wait()

        other = v.chunks.at[(1 - p.y) * chunks + c]
        remote(v.ra.at[c], other, v.ys.at[c], v.yr.at[c], (p.dp ^ 1, p.ex)).wait_recv()
        return carry

    lax.fori_loop(0, chunks, one, 0)


def weight_loads(v, p, j):
    return (
        pltpu.make_async_copy(v.we_all.at[p.y * 2 + j], v.we, v.wsem.at[0]),
        pltpu.make_async_copy(v.wr_all.at[p.y * 2 + j], v.wr, v.wsem.at[1]),
    )


def source_rows(r):
    return pl.ds(pl.multiple_of(r * CAP, CAP), CAP)


def slot_hits(v, r, j):
    sub = lax.broadcasted_iota(jnp.int32, (CAP, 2 * CAP), 0).astype(F32)
    return sub == v.ma[r, j:j + 1, :]


def dispatch(v, r, j):
    d = v.xa.shape[3]
    hit = slot_hits(v, r, j)
    pick = jnp.where(hit, 1.0, 0.0).astype(LOW)
    gate = jnp.sum(jnp.where(hit, v.ma[r, j + 2:j + 3, :], 0.0), 1, keepdims=True)
    at = source_rows(r)
    rows = dot(pick, v.xa[r].reshape(2 * CAP, d))
    v.pr[j, at, :] = rows.astype(LOW)
    v.xrt[:, at] = rows.T.astype(LOW)
    rows = gate * dot(pick, v.ca[r].reshape(2 * CAP, d))
    v.gr[j, at, :] = rows.astype(LOW)
    v.gpt[:, at] = rows.T.astype(LOW)


def columns(v, p, j, f):
    cols = pl.ds(pl.multiple_of(f * 256, 256), 256)
    step = 512
    for b in range(v.act.shape[0] // step):
        rows = slice(b * step, (b + 1) * step)
        value, slope = gelu_parts(dot(v.pr[j, rows, :], v.we[:, cols]))
        v.act[rows, cols] = value.astype(LOW)
        v.gh[rows, cols] = (dot_nt(v.gr[j, rows, :], v.wr[cols, :]) * slope).astype(LOW)
    first = j * (v.ra.shape[0] // 2) + 2 * f
    v.ra[first] = dot(v.gpt[...], v.act[:, cols]).astype(LOW)
    v.ra[first + 1] = dot(v.xrt[...], v.gh[:, cols]).astype(LOW)

    @pl.when(p.is_end)
    def _():
        chunk_first(v, p, first).start()
        chunk_first(v, p, first + 1).start()


def produce(v, r, j):
    at = source_rows(r)
    made = dot(v.act[at, :], v.wr[...]).astype(LOW)
    v.pr[j, at, :] = made
    v.gr[j, at, :] = dot_nt(v.gh[at, :], v.we[...]).astype(LOW)
    hit = slot_hits(v, r, j)
    seen = dot(jnp.where(hit, 1.0, 0.0).astype(LOW), v.ca[r].reshape(2 * CAP, made.shape[1]))
    inner = jnp.sum(made.astype(F32) * seen, 1, keepdims=True)
    part = jnp.sum(jnp.where(hit, inner, 0.0), 0, keepdims=True)
    v.dgs[r, j] = jnp.broadcast_to(part, (8, 2 * CAP))


def gate_copy(v, p, r):
    return remote(v.dgs.at[r], v.dg.at[p.group(0)], v.gs.at[r], v.gv.at[r], p.peer(r))


def part_core(v, p, r, which):
    ref = (v.gr, v.pr)[which]
    at = 4 * which + lax.div(r, 2)
    return remote(ref.at[:, source_rows(r), :], v.xa.at[at], v.k1s.at[at], v.k1r.at[at], p.peer(1))


def part_plane(v, p, r, which):
    ref = (v.gr, v.pr)[which]
    q = lax.div(r, 2)
    at = 4 * which + q
    return remote(ref.at[:, source_rows(r), :], v.ca.at[at], v.k2s.at[at], v.k2r.at[at], p.plane(q))


def combine(v, r, which):
    lane = lax.broadcasted_iota(jnp.int32, (2 * CAP, CAP), 1).astype(F32)
    meta = v.ma[r].T
    at = source_rows(r)
    ref = (v.gr, v.pr)[which]
    total = jnp.zeros((2 * CAP, ref.shape[2]), F32)
    for j in range(2):
        hit = lane == meta[:, j:j + 1]
        weight = 1.0 if which == 0 else meta[:, 2 + j:3 + j]
        total = total + dot(jnp.where(hit, weight, 0.0).astype(LOW), ref[j, at, :])
    ref[0, at, :] = total[:CAP].astype(LOW)
    ref[1, at, :] = total[CAP:].astype(LOW)


def send_parts(v, p, which, first_tick):
    def odd(n, carry):
        r = 7 - 2 * n
        combine(v, r, which)
        part_core(v, p, r, which).start()
        return carry

    lax.fori_loop(0, 4, odd, 0)
    if which == 0:
        pl.semaphore_wait(v.free_plane, 3)
    ticks(v, p, first_tick, first_tick + 1)

    def even(n, carry):
        r = 6 - 2 * n
        combine(v, r, which)

        @pl.when(r > 0)
        def _():
            part_core(v, p, r, which).wait_recv()
            ref = (v.gr, v.pr)[which]
            at = source_rows(r)
            ref[:, at, :] = (
                ref[:, at, :].astype(F32) + v.xa[4 * which + lax.div(r, 2)].astype(F32)
            ).astype(LOW)
            part_plane(v, p, r, which).start()

        return carry

    lax.fori_loop(0, 4, even, 0)
    ticks(v, p, first_tick + 1, first_tick + 2)


def own_sum(v, i, which):
    ref = (v.gr, v.pr)[which]
    total = ref[i, 0:CAP, :].astype(F32) + v.xa[4 * which, i].astype(F32)
    for q in (1, 2, 3):
        total = total + v.ca[4 * which + q, i].astype(F32)
    return total


def wait_parts(v, p, which):
    part_core(v, p, 0, which).wait_recv()
    for r in (2, 4, 6):
        part_plane(v, p, r, which).wait_recv()


def piece(v, c, q):
    return v.act.at[
        pl.ds(pl.multiple_of(PAY + c * PIECE, 16), PIECE), pl.ds(pl.multiple_of(q * 384, 128), 384)
    ]


def place_tasks(v, c, per_image):
    experts, d = per_image[0].shape
    for j in range(v.router1.shape[0]):
        mine = [jnp.where(v.task[i] == j, per_image[i], 0.0) for i in range(2)]
        at = PAY + c * PIECE + j * experts
        v.act[at:at + experts, 3 * d:4 * d] = (mine[0] + mine[1]).astype(LOW)


def place_rows(v, c, value):
    d = value.shape[1]
    for q in range(3):
        at = PAY + c * PIECE
        v.act[at:at + USED, q * d:(q + 1) * d] = value[q * USED:(q + 1) * USED].astype(LOW)


def back_first(v, p):
    count, d = v.tok.shape
    half = count // 2
    heads = v.heads.shape[1]
    grad_gates = jnp.concatenate([v.dg[g, j, 0:1, :] for g in range(8) for j in range(2)], 0)
    gates = v.g2[...]
    grad_logits = gates * (grad_gates - jnp.sum(gates * grad_gates, 0, keepdims=True))
    grad_logits = grad_logits.astype(LOW)
    gain = v.gain[1:2]
    v.act[PAY:PAY + 2 * PIECE, :] = jnp.zeros((2 * PIECE, v.act.shape[1]), LOW)
    v.small[0] = jnp.zeros_like(v.small[0])
    per_image = []
    grad_gain = jnp.zeros((1, d), F32)
    grad_bias = jnp.zeros((1, d), F32)
    for i in range(2):
        rows = slice(i * half, (i + 1) * half)
        grad = own_sum(v, i, 0) + dot_tn(grad_logits[:, rows], v.router2[v.task[i]])
        per_image.append(dot(grad_logits[:, rows], v.n2[i]))
        normal, scale = center(v.mid[rows, :])
        grad_gain = grad_gain + jnp.sum(grad * normal, 0, keepdims=True)
        grad_bias = grad_bias + jnp.sum(grad, 0, keepdims=True)
        total = v.cot[i].astype(F32) + center_back(grad, normal, scale, gain)
        v.gmid[rows, :] = total
        low = total.astype(LOW)
        v.act[rows, PAY:PAY + d] = low
        v.act[rows, 0:heads] = dot_nt(low, v.wo[...]).astype(LOW)
    v.small[0, 1:2, :] = grad_gain
    v.small[0, 3:4, :] = grad_bias
    place_rows(v, 0, dot_tn(v.heads[...], v.act[0:count, PAY:PAY + d]))
    place_tasks(v, 0, per_image)


def back_attention(v, i):
    count, d = v.tok.shape
    half = count // 2
    heads = v.heads.shape[1]
    head = v.kv.shape[2] // 2
    picks = v.pick.shape[1]
    experts = v.router1.shape[1]
    to_query, to_value = head_maps(heads // head, head)
    owner = lax.div(lax.broadcasted_iota(jnp.int32, (half, heads), 1), head)
    lane = lax.broadcasted_iota(jnp.int32, (half, experts), 1)
    rows = slice(i * half, (i + 1) * half)
    lower = slice(count + i * half, count + (i + 1) * half)
    kv = v.kv[i]
    gates = v.g1[rows, :]
    grad_gates = jnp.zeros((half, experts), F32)
    grad_pair = jnp.zeros((2 * head, 4 * half), F32)
    for k in range(picks):
        at = picks * i + k
        mine = owner == v.pick[rows, k:k + 1]
        named = lane == v.pick[rows, k:k + 1]
        gate = jnp.sum(jnp.where(named, gates, 0.0), 1, keepdims=True)
        grad_heads = v.act[rows, 0:heads]
        grad = dot(jnp.where(mine, grad_heads, jnp.zeros_like(grad_heads)), to_value)
        attended = v.att[at]
        total = attended[:, 0:1]
        grad_gates = grad_gates + jnp.where(named, jnp.sum(grad * attended, 1, keepdims=True), 0.0)
        grad = ((gate * grad).astype(LOW).astype(F32) / total).astype(LOW)
        inner = jnp.sum(grad.astype(F32) * attended, 1, keepdims=True)
        expo = v.gh[at * half:(at + 1) * half, 0:4 * half]
        grad_scores = (expo.astype(F32) * (dot_nt(grad, kv) - inner)).astype(LOW)
        grad_query = (dot(grad_scores, kv) * head ** -0.5).astype(LOW)
        spread = dot_nt(grad_query, to_query).astype(LOW)
        if k == 0:
            v.act[lower, 0:heads] = jnp.where(mine, spread, jnp.zeros_like(spread))
        else:
            v.act[lower, 0:heads] = jnp.where(mine, spread, v.act[lower, 0:heads])
        grad_pair = grad_pair + dot(v.q8[at].astype(F32).T.astype(LOW), grad_scores)
        grad_pair = grad_pair + dot(grad.astype(F32).T.astype(LOW), expo)
    grad_logits = gates * (grad_gates - jnp.sum(gates * grad_gates, 1, keepdims=True))
    v.gl1[rows, :] = grad_logits.astype(LOW)
    for r in range(4):
        v.dkv[r, i] = grad_pair[:, r * half:(r + 1) * half].astype(LOW)


def pair_copy(v, p, r):
    return remote(v.dkv.at[r], v.din.at[r], v.ps.at[r], v.pr_sem.at[r], p.peer(r))


def back_last(v, p):
    count, d = v.tok.shape
    half = count // 2
    heads = v.heads.shape[1]
    width = v.kv.shape[2]
    gain = v.gain[0:1]
    grad_gain = jnp.zeros((1, d), F32)
    grad_bias = jnp.zeros((1, d), F32)
    grad_pair = jnp.zeros((width, d), F32)
    per_image = []
    for i in range(2):
        rows = slice(i * half, (i + 1) * half)
        lower = slice(count + i * half, count + (i + 1) * half)
        pair = v.dkv[0, i].astype(F32)
        for r in (1, 2, 3):
            pair = pair + v.din[r, i].astype(F32)
        grad_pair = grad_pair + dot(pair.astype(LOW), v.n1[rows, :])
        grad = dot_nt(v.act[lower, 0:heads], v.wq[...]) + dot_nt(pair.T.astype(LOW), v.wkv[...])
        grad = grad + dot(v.gl1[rows, :], v.router1[v.task[i]])
        per_image.append(dot_tn(v.gl1[rows, :], v.n1[rows, :]))
        normal, scale = center(v.tok[rows, :].astype(F32))
        grad_gain = grad_gain + jnp.sum(grad * normal, 0, keepdims=True)
        grad_bias = grad_bias + jnp.sum(grad, 0, keepdims=True)
        v.gtok[rows, :] = v.gmid[rows, :] + center_back(grad, normal, scale, gain)
    v.small[0, 0:1, :] = grad_gain
    v.small[0, 2:3, :] = grad_bias
    place_rows(v, 1, dot_tn(v.act[count:2 * count, 0:heads], v.n1[...]))
    at = PAY + TASK_ROWS
    v.act[at:at + width, 3 * d:4 * d] = grad_pair.astype(LOW)
    place_tasks(v, 1, per_image)


def count_usage(v):
    count, d = v.tok.shape
    half = count // 2
    experts = v.router1.shape[1]
    picks = v.pick.shape[1]
    lane = lax.broadcasted_iota(jnp.int32, (half, 128), 1)
    task = lax.broadcasted_iota(jnp.int32, (experts, 128), 0)
    for which, ref in enumerate((v.pick, v.pick2)):
        table = jnp.zeros((experts, 128), F32)
        for i in range(2):
            rows = slice(i * half, (i + 1) * half)
            named = jnp.zeros((half, 128), F32)
            for k in range(picks):
                named = named + jnp.where(lane == ref[rows, k:k + 1], 1.0, 0.0)
            table = table + jnp.where(task == v.task[i], jnp.sum(named, 0, keepdims=True), 0.0)
        v.small[0, 8 + which * experts:8 + (which + 1) * experts, 0:128] = table


def shared_reduce(v, p, pause):
    core, mine = p.core, p.spot

    def half(c):
        return v.act.at[pl.ds(pl.multiple_of(PAY + c * PIECE, 16), PIECE), :]

    def exchange(stage, device):
        return remote(v.small.at[stage], v.small_in.at[stage], v.ss.at[stage], v.sr.at[stage], device)

    partner = p.peer(1)
    first = remote(half(1 - core), v.half_in, v.hs.at[0], v.hr.at[0], partner)
    first.start()
    small = exchange(0, partner)
    small.start()
    small.wait_recv()
    v.small[1] = v.small[0] + v.small_in[0]
    small1 = exchange(1, p.plane(1))
    small1.start()
    first.wait_recv()
    own = half(core)
    own[...] = (own[...].astype(F32) + v.half_in[...].astype(F32)).astype(LOW)
    scatter = [
        remote(piece(v, core, mine ^ q), v.piece_in.at[q - 1], v.hs.at[q], v.hr.at[q], p.plane(q))
        for q in (1, 2, 3)
    ]
    for copy in scatter:
        copy.start()
    small1.wait_recv()
    v.small[2] = v.small[1] + v.small_in[1]
    small2 = exchange(2, p.plane(2))
    small2.start()
    pause(0)
    small2.wait_recv()
    v.small[3] = v.small[2] + v.small_in[2]
    for copy in scatter:
        copy.wait_recv()
    own = piece(v, core, mine)
    total = own[...].astype(F32)
    for q in (1, 2, 3):
        total = total + v.piece_in[q - 1].astype(F32)
    v.zown[...] = total.astype(LOW)

    in_end = remote(v.zown, v.zb, v.zs.at[0], v.zr.at[0], p.toward)
    in_small = remote(v.small.at[3], v.small_in.at[3], v.zs.at[1], v.zr.at[1], p.toward)
    mid = remote(v.zb, v.zc, v.zs.at[0], v.zr.at[2], p.toward)
    mid_small = remote(v.small.at[4], v.small_in.at[4], v.zs.at[1], v.zr.at[3], p.toward)
    out_mid = remote(v.zall, v.zall, v.zs.at[2], v.zr.at[4], p.outer)
    out_small = remote(v.stats, v.stats, v.zs.at[3], v.zr.at[5], p.outer)

    @pl.when(p.is_end)
    def _():
        in_end.start()
        in_small.start()

    pause(1)

    @pl.when(p.is_mid)
    def _():
        in_end.wait_recv()
        v.zb[...] = (v.zown[...].astype(F32) + v.zb[...].astype(F32)).astype(LOW)
        mid.start()
        in_small.wait_recv()
        v.small[4] = v.small[3] + v.small_in[3]
        mid_small.start()

    pause(2)

    @pl.when(p.is_mid)
    def _():
        mid.wait_recv()
        v.zall[...] = (v.zb[...].astype(F32) + v.zc[...].astype(F32)).astype(LOW)
        out_mid.start()
        mid_small.wait_recv()
        v.stats[...] = v.small[4] + v.small_in[4]
        out_small.start()

    pause(3)

    @pl.when(p.is_end)
    def _():
        out_mid.wait_recv()
        out_small.wait_recv()

    place = core * 4 + mine
    own_copy = pltpu.make_async_copy(v.zall, v.shared.at[place], v.osem.at[0])
    own_copy.start()
    gather = [
        remote(v.zall, v.shared.at[place], v.bs.at[q], v.br.at[q], p.plane(q)) for q in (1, 2, 3)
    ]
    for copy in gather:
        copy.start()
    pause(4)
    own_copy.wait()
    for q in (1, 2, 3):
        there = v.shared.at[core * 4 + (mine ^ q)]
        remote(v.zall, there, v.bs.at[q], v.br.at[q], p.plane(q)).wait_recv()
    ours = v.shared.at[pl.ds(core * 4, 4)]
    theirs = v.shared.at[pl.ds((1 - core) * 4, 4)]
    last = remote(ours, ours, v.bs.at[0], v.br.at[0], partner)
    last.start()
    pause(5)
    remote(theirs, theirs, v.bs.at[0], v.br.at[0], partner).wait_recv()

    for copy in [first, small, small1, small2, *scatter, *gather, last]:
        copy.wait_send()

    @pl.when(p.is_end)
    def _():
        in_end.wait_send()
        in_small.wait_send()

    @pl.when(p.is_mid)
    def _():
        mid.wait_send()
        mid_small.wait_send()
        out_mid.wait_send()
        out_small.wait_send()


def layer_kernel(v):
    p = Place()
    v.barrier = pltpu.get_barrier_semaphore()
    for r in range(1, 8):
        pl.semaphore_signal(v.barrier, 1, device_id=p.peer(r), device_id_type=MESH)
    pl.semaphore_signal(v.barrier, 1, device_id=p.toward, device_id_type=MESH)

    @pl.when(p.is_mid)
    def _():
        pl.semaphore_signal(v.barrier, 1, device_id=p.outer, device_id_type=MESH)

    for load in weight_loads(v, p, 0):
        load.start()
    front(v, p)

    spill = pltpu.make_async_copy(v.act.at[:, pl.ds(0, v.expo.shape[1])], v.expo, v.osem.at[1])
    spill.start()
    row_copy(v, p, 1, 0).wait_recv()
    row_copy(v, p, 1, 1).wait_recv()
    cot_copy(v, p, 1).wait_recv()
    meta_copy(v, p, 1).wait_recv()
    dispatch(v, 0, 0)
    dispatch(v, 1, 0)
    for load in weight_loads(v, p, 0):
        load.wait()
    for r in (2, 4, 6):
        for i in range(2):
            row_copy(v, p, r, i).wait_recv()
            row_forward(v, p, r, i).start()
        meta_copy(v, p, r).wait_recv()
        dispatch(v, r, 0)
    for r in (3, 5, 7):
        for i in range(2):
            row_copy(v, p, r, i).wait_recv()
        cot_copy(v, p, r).wait_recv()
        meta_copy(v, p, r).wait_recv()
        dispatch(v, r, 0)
    spill.wait()

    def first_columns(f, carry):
        columns(v, p, 0, f)

        @pl.when(lax.rem(f, 2) == 1)
        def _():
            tick(v, p, lax.div(f, 2))

        return carry

    lax.fori_loop(0, 6, first_columns, 0)

    def first_produce(r, carry):
        produce(v, r, 0)
        return carry

    lax.fori_loop(0, 8, first_produce, 0)
    for load in weight_loads(v, p, 1):
        load.start()
    ticks(v, p, 3, 5)

    def second_dispatch(r, carry):
        dispatch(v, r, 1)
        return carry

    lax.fori_loop(0, 8, second_dispatch, 0)
    for i in range(2):
        for r in (1, 2, 4, 6):
            row_copy(v, p, r, i).wait_send()
        for r in (2, 4, 6):
            row_forward(v, p, r, i).wait_send()
    pl.semaphore_signal(v.free_core, 1, device_id=p.peer(1), device_id_type=MESH)
    for load in weight_loads(v, p, 1):
        load.wait()

    def second_columns(f, carry):
        columns(v, p, 1, f)

        @pl.when(lax.rem(f, 2) == 1)
        def _():
            tick(v, p, 5 + lax.div(f, 2))

        return carry

    lax.fori_loop(0, 6, second_columns, 0)

    def second_produce(r, carry):
        produce(v, r, 1)
        return carry

    lax.fori_loop(0, 8, second_produce, 0)
    for r in range(1, 8):
        gate_copy(v, p, r).start()
    v.dg[p.group(0)] = v.dgs[0]
    refill = pltpu.make_async_copy(v.expo, v.gh.at[:, pl.ds(0, v.expo.shape[1])], v.osem.at[1])
    refill.start()
    ticks(v, p, 8, 10)
    for r in (2, 4, 6):
        cot_forward(v, p, r).wait_send()
    for q in (1, 2, 3):
        pl.semaphore_signal(v.free_plane, 1, device_id=p.plane(q), device_id_type=MESH)
    pl.semaphore_wait(v.free_core, 1)
    send_parts(v, p, 0, 10)
    send_parts(v, p, 1, 12)
    refill.wait()
    for r in range(1, 8):
        gate_copy(v, p, r).wait_recv()
    ticks(v, p, 14, 16)
    wait_parts(v, p, 0)
    back_first(v, p)
    count_usage(v)
    ticks(v, p, 16, 18)
    back_attention(v, 0)
    ticks(v, p, 18, 19)
    back_attention(v, 1)
    for r in (1, 2, 3):
        pair_copy(v, p, r).start()
    ticks(v, p, 19, 20)
    wait_parts(v, p, 1)
    for i in range(2):
        rows = slice(i * CAP, (i + 1) * CAP)
        v.out[rows, :] = (v.mid[rows, :] + own_sum(v, i, 1)).astype(LOW)
    for r in (1, 2, 3):
        pair_copy(v, p, r).wait_recv()
    back_last(v, p)
    schedule = {0: (20, 22), 1: (22, 23), 2: (23, 24), 3: (24, 25), 4: (25, 26)}

    def pause(stage):
        if stage in schedule:
            ticks(v, p, *schedule[stage])

    shared_reduce(v, p, pause)

    for r in (1, 2, 3):
        kv_copy(v, p, r).wait_send()
        pair_copy(v, p, r).wait_send()
    for r in (1, 2, 4, 6):
        cot_copy(v, p, r).wait_send()
    for r in range(1, 8):
        meta_copy(v, p, r).wait_send()
        gate_copy(v, p, r).wait_send()
    for which in range(2):
        for r in (1, 3, 5, 7):
            part_core(v, p, r, which).wait_send()
        for r in (2, 4, 6):
            part_plane(v, p, r, which).wait_send()
    chunks_done(v, p)


def layer_call(
    tok, cot, pick, pick2, pickt, task, gain, bias, wq, wkv, wo, router1, router2, we, wr
):
    count, d = tok.shape
    half = count // 2
    heads = wq.shape[1]
    width = wkv.shape[1]
    picks = pick.shape[1]
    ff = we.shape[2]
    chunks = 4 * ff // 256
    vm = pltpu.VMEM
    anywhere = pl.ANY
    dma = pltpu.SemaphoreType.DMA
    return run_kernel(
        layer_kernel, "layer",
        dict(
            tok=(tok, vm), cot=(cot, vm), pick=(pick, vm), pick2=(pick2, vm), pickt=(pickt, vm),
            task=(task, pltpu.SMEM), gain=(gain, vm), bias=(bias, vm), wq=(wq, vm), wkv=(wkv, vm),
            wo=(wo, vm), router1=(router1, vm), router2=(router2, vm),
            we_all=(we, anywhere), wr_all=(wr, anywhere),
        ),
        dict(
            out=((count, d), LOW, vm), gtok=((count, d), F32, vm),
            chunks=((2 * chunks, d, 256), LOW, anywhere), shared=((8, PIECE, d), LOW, anywhere),
            stats=((40, d), F32, vm), expo=((8 * CAP, 4 * half), LOW, anywhere),
        ),
        dict(
            n1=vm((count, d), LOW), n2=vm((2, half, d), LOW), mid=vm((count, d), F32),
            heads=vm((count, heads), LOW), kv=vm((2, 4 * half, width), LOW),
            q8=vm((2 * picks, half, width), LOW), att=vm((2 * picks, half, width), F32),
            g1=vm((count, 16), F32), g2=vm((16, count), F32), meta=vm((8, 16, count), F32),
            xa=vm((8, 2, half, d), LOW), ca=vm((8, 2, half, d), LOW),
            ma=vm((8, 16, count), F32), we=vm((d, ff), LOW), wr=vm((ff, d), LOW),
            xrt=vm((d, 8 * CAP), LOW), gpt=vm((d, 8 * CAP), LOW),
            act=vm((8 * CAP, ff), LOW), gh=vm((8 * CAP, ff), LOW),
            pr=vm((2, 8 * CAP, d), LOW), gr=vm((2, 8 * CAP, d), LOW),
            ra=vm((chunks, d, 256), LOW), rb=vm((chunks, d, 256), LOW), rc=vm((chunks, d, 256), LOW),
            dgs=vm((8, 2, 8, count), F32), dg=vm((8, 2, 8, count), F32),
            small=vm((5, 40, d), F32), small_in=vm((5, 40, d), F32),
            gmid=vm((count, d), F32), gl1=vm((count, 16), LOW),
            dkv=vm((4, 2, width, half), LOW), din=vm((4, 2, width, half), LOW),
            half_in=vm((PIECE, 4 * d), LOW), piece_in=vm((3, PIECE, d), LOW),
            zown=vm((PIECE, d), LOW), zb=vm((PIECE, d), LOW), zc=vm((PIECE, d), LOW),
            zall=vm((PIECE, d), LOW),
            cs=dma((8,)), cv=dma((8,)), ks=dma((4,)), kr=dma((4,)), xs=dma((8, 2)), xv=dma((8, 2)),
            ms=dma((8,)), mv=dma((8,)), gs=dma((8,)), gv=dma((8,)), wsem=dma((2,)), osem=dma((2,)),
            s1s=dma((chunks,)), s1r=dma((chunks,)), s2s=dma((chunks,)), s2r=dma((chunks,)),
            s3s=dma((chunks,)), ys=dma((chunks,)), yr=dma((chunks,)), ls=dma((chunks,)),
            k1s=dma((8,)), k1r=dma((8,)), k2s=dma((8,)), k2r=dma((8,)),
            ps=dma((4,)), pr_sem=dma((4,)), ss=dma((4,)), sr=dma((4,)), hs=dma((4,)), hr=dma((4,)),
            zs=dma((4,)), zr=dma((6,)), bs=dma((4,)), br=dma((4,)),
            free_core=pltpu.SemaphoreType.REGULAR, free_plane=pltpu.SemaphoreType.REGULAR,
        ),
        0,
    )


def widen_kernel(r_ref, e_ref, reduce_ref, expand_ref):
    reduce_ref[0] = r_ref[0].astype(F32).T
    expand_ref[0] = e_ref[0].astype(F32)


def widen_call(chunks, slots, d, ff):
    n = ff // 256
    return pl.pallas_call(
        widen_kernel,
        name="widen",
        grid=(slots, n),
        in_specs=[
            pl.BlockSpec((1, d, 256), lambda s, f: (s * 2 * n + 2 * f, 0, 0)),
            pl.BlockSpec((1, d, 256), lambda s, f: (s * 2 * n + 2 * f + 1, 0, 0)),
        ],
        out_specs=(
            pl.BlockSpec((1, 256, d), lambda s, f: (s, f, 0)),
            pl.BlockSpec((1, d, 256), lambda s, f: (s, 0, f)),
        ),
        out_shape=(
            jax.ShapeDtypeStruct((slots, ff, d), F32),
            jax.ShapeDtypeStruct((slots, d, ff), F32),
        ),
    )(chunks, chunks)


def body_fast(
    tokens,
    task_ids,
    attention_picks,
    feedforward_picks,
    norm_gain,
    norm_bias,
    query_weight,
    key_weight,
    value_weight,
    output_weight,
    attention_router,
    feedforward_router,
    expand_weight,
    reduce_weight,
    cotangent,
):
    images, patches, width = tokens.shape
    count = images * patches
    tasks, _, experts = attention_router.shape
    head = key_weight.shape[1]
    picks = attention_picks.shape[2]
    slots = expand_weight.shape[0]
    ff = expand_weight.shape[2]
    wide = query_weight.shape[1]
    tok = tokens.reshape(count, width)
    pick = attention_picks.reshape(count, picks)
    pick2 = feedforward_picks.reshape(count, picks)
    wkv = jnp.concatenate([key_weight, value_weight], 1)

    def experts_first(router):
        return jnp.pad(jnp.swapaxes(router, 1, 2), ((0, 0), (0, 16 - experts), (0, 0)))

    router1 = experts_first(attention_router)
    router2 = experts_first(feedforward_router)
    b = layer_call(
        tok, cotangent, pick, pick2, pick2.T, task_ids, norm_gain, norm_bias, query_weight, wkv,
        output_weight, router1, router2, expand_weight, reduce_weight,
    )
    grad_reduce, grad_expand = widen_call(b.chunks, slots, width, ff)

    def columns_of(c):
        return b.shared[4 * c:4 * c + 3, :USED].reshape(wide, width).astype(F32)

    def experts_last(c):
        table = b.shared[4 * c + 3, :TASK_ROWS].astype(F32).reshape(tasks, 16, width)[:, :experts]
        return jnp.swapaxes(table, 1, 2)

    pair = b.shared[3, TASK_ROWS:TASK_ROWS + 2 * head].astype(F32)
    usage = b.stats[8:40, :experts].reshape(2, 16, experts)[:, :tasks]
    return (
        b.out.reshape(images, patches, width),
        b.gtok.reshape(images, patches, width),
        b.stats[0:2],
        b.stats[2],
        b.stats[3],
        columns_of(1).T,
        pair[:head].T,
        pair[head:].T,
        columns_of(0),
        experts_last(1),
        experts_last(0),
        grad_expand,
        grad_reduce,
        usage,
    )


def normalize(value, gain, bias):
    mean = jnp.mean(value, -1, keepdims=True)
    centred = value - mean
    spread = jnp.mean(centred * centred, -1, keepdims=True)
    return centred * lax.rsqrt(spread + EPS) * gain + bias


def gate_weights(logits, picks_hot):
    chosen = jnp.sum(picks_hot * logits[..., None, :], -1)
    return jax.nn.softmax(chosen, -1)


def activate(value):
    return jax.nn.gelu(value, approximate=True)


def body(
    tokens,
    task_ids,
    attention_picks,
    feedforward_picks,
    norm_gain,
    norm_bias,
    query_weight,
    key_weight,
    value_weight,
    output_weight,
    attention_router,
    feedforward_router,
    expand_weight,
    reduce_weight,
    cotangent,
):
    images, patches, width = tokens.shape
    count = images * patches
    tasks = attention_router.shape[0]
    experts = attention_router.shape[2]
    head = key_weight.shape[1]
    picks = attention_picks.shape[2]
    slots = expand_weight.shape[0]
    groups = lax.axis_size("expert")
    lanes = groups * slots
    f32 = jnp.float32
    low_type = jnp.bfloat16
    inputs = tokens.astype(f32).reshape(count, width)
    expert_range = jnp.arange(experts, dtype=jnp.int32)
    task_hot = (task_ids[:, None] == jnp.arange(tasks, dtype=jnp.int32)[None, :]).astype(f32)
    task_low = task_hot.astype(low_type)
    attend_hot = (attention_picks[..., None] == expert_range).astype(f32)
    attend_low = attend_hot.astype(low_type)
    choices = feedforward_picks.reshape(count, picks)
    feed_hot = (choices[..., None] == expert_range).astype(f32)
    flat = choices.reshape(count * picks)
    marks = (flat[:, None] == expert_range[None, :]).astype(jnp.int32)
    before = jnp.cumsum(marks, axis=0) - marks
    position = flat * CAP + jnp.sum(before * marks, axis=1)
    first, first_back = jax.vjp(normalize, inputs, norm_gain[0], norm_bias[0])
    normed_one = first.astype(low_type)
    shaped_one = normed_one.reshape(images, patches, width)
    router_one = jnp.einsum(
        "it,tde->ide", task_low, attention_router, preferred_element_type=f32
    ).astype(low_type)
    logits_one = jnp.einsum("ipd,ide->ipe", shaped_one, router_one, preferred_element_type=f32)
    gates_one, gates_one_back = jax.vjp(lambda value: gate_weights(value, attend_hot), logits_one)
    queries_all = jnp.dot(normed_one, query_weight, preferred_element_type=f32).astype(low_type)
    queries_all = queries_all.reshape(images, patches, experts, head)
    queries = jnp.einsum(
        "ipke,ipeh->ipkh", attend_low, queries_all, preferred_element_type=f32
    ).astype(low_type)
    queries = queries.reshape(images, patches * picks, head)
    key_value = jnp.concatenate([key_weight, value_weight], 1)
    pair = jnp.dot(normed_one, key_value, preferred_element_type=f32).astype(low_type)
    pair = pair.reshape(images, patches, 2 * head)
    pair_all = lax.all_gather(pair, "expert", axis=1, tiled=True)
    keys_all = pair_all[:, :, :head]
    values_all = pair_all[:, :, head:]
    scores = jnp.einsum("irh,ish->irs", queries, keys_all, preferred_element_type=f32) * 0.125
    top = jnp.max(scores, -1, keepdims=True)
    expo = jnp.exp(scores - top)
    total = jnp.sum(expo, -1, keepdims=True)
    log_total = top + jnp.log(total)
    probs_low = (expo / total).astype(low_type)
    attended = jnp.einsum("irs,ish->irh", probs_low, values_all, preferred_element_type=f32)
    attended = attended.reshape(images, patches, picks, head)
    weighted = gates_one[..., None] * attended
    heads = jnp.einsum("ipke,ipkh->ipeh", attend_hot, weighted, precision=HIGH)
    heads = heads.reshape(count, experts * head).astype(low_type)
    middle = inputs + jnp.dot(heads, output_weight, preferred_element_type=f32)
    second, second_back = jax.vjp(normalize, middle, norm_gain[1], norm_bias[1])
    normed_two = second.astype(low_type)
    shaped_two = normed_two.reshape(images, patches, width)
    router_two = jnp.einsum(
        "it,tde->ide", task_low, feedforward_router, preferred_element_type=f32
    ).astype(low_type)
    logits_two = jnp.einsum(
        "ipd,ide->ipe", shaped_two, router_two, preferred_element_type=f32
    ).reshape(count, experts)
    gates_two, gates_two_back = jax.vjp(lambda value: gate_weights(value, feed_hot), logits_two)
    outgoing = (
        jnp.zeros((lanes * CAP, width), low_type)
        .at[position]
        .set(jnp.repeat(normed_two, picks, axis=0))
    )
    outgoing = outgoing.reshape(groups, slots * CAP, width)
    received = lax.all_to_all(outgoing, "expert", split_axis=0, concat_axis=0, tiled=True).reshape(
        groups, slots, CAP, width
    )
    hidden = jnp.einsum("nscd,sdf->nscf", received, expand_weight, preferred_element_type=f32)
    activated, activate_back = jax.vjp(activate, hidden)
    active_low = activated.astype(low_type)
    produced = jnp.einsum(
        "nscf,sfd->nscd", active_low, reduce_weight, preferred_element_type=f32
    ).astype(low_type)
    produced = produced.reshape(groups, slots * CAP, width)
    returned = lax.all_to_all(produced, "expert", split_axis=0, concat_axis=0, tiled=True).reshape(
        lanes * CAP, width
    )
    picked = returned[position].astype(f32).reshape(count, picks, width)
    final = middle + jnp.sum(gates_two[..., None] * picked, 1)
    output = final.astype(low_type).reshape(images, patches, width)
    grad_final = cotangent.astype(f32).reshape(count, width)
    grad_gates_two = jnp.sum(picked * grad_final[:, None, :], -1)
    grad_picked = (
        (gates_two[..., None] * grad_final[:, None, :])
        .astype(low_type)
        .reshape(count * picks, width)
    )
    grad_send = jnp.zeros((lanes * CAP, width), low_type).at[position].set(grad_picked)
    grad_send = grad_send.reshape(groups, slots * CAP, width)
    grad_produced = lax.all_to_all(
        grad_send, "expert", split_axis=0, concat_axis=0, tiled=True
    ).reshape(groups, slots, CAP, width)
    grad_reduce = jnp.einsum(
        "nscf,nscd->sfd", active_low, grad_produced, preferred_element_type=f32
    )
    grad_active = jnp.einsum(
        "nscd,sfd->nscf", grad_produced, reduce_weight, preferred_element_type=f32
    )
    grad_hidden = activate_back(grad_active)[0].astype(low_type)
    grad_expand = jnp.einsum("nscd,nscf->sdf", received, grad_hidden, preferred_element_type=f32)
    grad_rows = jnp.einsum(
        "nscf,sdf->nscd", grad_hidden, expand_weight, preferred_element_type=f32
    ).astype(low_type)
    grad_rows = grad_rows.reshape(groups, slots * CAP, width)
    grad_back = lax.all_to_all(
        grad_rows, "expert", split_axis=0, concat_axis=0, tiled=True
    ).reshape(lanes * CAP, width)
    grad_normed_two = jnp.sum(grad_back[position].astype(f32).reshape(count, picks, width), 1)
    grad_logits_two = (
        gates_two_back(grad_gates_two)[0].astype(low_type).reshape(images, patches, experts)
    )
    per_image_two = jnp.einsum(
        "ipd,ipe->ide", shaped_two, grad_logits_two, preferred_element_type=f32
    )
    grad_feed_router = jnp.einsum("it,ide->tde", task_hot, per_image_two, precision=HIGH)
    grad_normed_two = grad_normed_two + jnp.einsum(
        "ipe,ide->ipd", grad_logits_two, router_two, preferred_element_type=f32
    ).reshape(count, width)
    grad_middle_norm, grad_gain_two, grad_bias_two = second_back(grad_normed_two)
    grad_middle = grad_final + grad_middle_norm
    grad_branch = grad_middle.astype(low_type)
    grad_output = jnp.einsum("tc,td->cd", heads, grad_branch, preferred_element_type=f32)
    grad_heads = jnp.einsum(
        "td,cd->tc", grad_branch, output_weight, preferred_element_type=f32
    ).astype(low_type)
    grad_heads = grad_heads.reshape(images, patches, experts, head)
    grad_selected = jnp.einsum(
        "ipke,ipeh->ipkh", attend_low, grad_heads, preferred_element_type=f32
    )
    grad_gates_one = jnp.sum(attended * grad_selected, -1)
    grad_attended = (
        (gates_one[..., None] * grad_selected)
        .astype(low_type)
        .reshape(images, patches * picks, head)
    )
    scores_back = jnp.einsum("irh,ish->irs", queries, keys_all, preferred_element_type=f32) * 0.125
    probs_back = jnp.exp(scores_back - log_total)
    grad_values = jnp.einsum(
        "irs,irh->ish", probs_back.astype(low_type), grad_attended, preferred_element_type=f32
    )
    grad_probs = jnp.einsum("irh,ish->irs", grad_attended, values_all, preferred_element_type=f32)
    inner_sum = jnp.sum(probs_back * grad_probs, -1, keepdims=True)
    grad_scores = (probs_back * (grad_probs - inner_sum)).astype(low_type)
    grad_query_sel = (
        jnp.einsum("irs,ish->irh", grad_scores, keys_all, preferred_element_type=f32) * 0.125
    )
    grad_keys = jnp.einsum("irs,irh->ish", grad_scores, queries, preferred_element_type=f32) * 0.125
    grad_pair = jnp.concatenate([grad_keys, grad_values], -1)
    pair_sum = lax.psum_scatter(
        grad_pair.astype(jnp.bfloat16), "expert", scatter_dimension=1, tiled=True
    ).astype(jnp.float32)
    pair_sum = pair_sum.astype(low_type).reshape(count, 2 * head)
    grad_query_sel = grad_query_sel.reshape(images, patches, picks, head)
    grad_queries_all = jnp.einsum("ipke,ipkh->ipeh", attend_hot, grad_query_sel, precision=HIGH)
    grad_queries_all = grad_queries_all.astype(low_type).reshape(count, experts * head)
    grad_logits_one = gates_one_back(grad_gates_one)[0].astype(low_type)
    per_image_one = jnp.einsum(
        "ipd,ipe->ide", shaped_one, grad_logits_one, preferred_element_type=f32
    )
    grad_attend_router = jnp.einsum("it,ide->tde", task_hot, per_image_one, precision=HIGH)
    grad_query = jnp.einsum("td,tc->dc", normed_one, grad_queries_all, preferred_element_type=f32)
    grad_key_value = jnp.einsum("td,tc->dc", normed_one, pair_sum, preferred_element_type=f32)
    grad_normed_one = jnp.einsum(
        "tc,dc->td", grad_queries_all, query_weight, preferred_element_type=f32
    )
    grad_normed_one = grad_normed_one + jnp.einsum(
        "tc,dc->td", pair_sum, key_value, preferred_element_type=f32
    )
    grad_normed_one = grad_normed_one + jnp.einsum(
        "ipe,ide->ipd", grad_logits_one, router_one, preferred_element_type=f32
    ).reshape(count, width)
    grad_inputs_norm, grad_gain_one, grad_bias_one = first_back(grad_normed_one)
    grad_tokens = (grad_middle + grad_inputs_norm).reshape(images, patches, width)
    grad_gain = jnp.stack([grad_gain_one, grad_gain_two])
    grad_bias = jnp.stack([grad_bias_one, grad_bias_two])
    feed_shaped = feed_hot.reshape(images, patches, picks, experts)
    usage = jnp.stack(
        [
            jnp.einsum("it,ipke->te", task_hot, attend_hot, precision=HIGH),
            jnp.einsum("it,ipke->te", task_hot, feed_shaped, precision=HIGH),
        ]
    )
    shared = lax.psum(
        (
            grad_query,
            grad_key_value,
            grad_output,
            grad_attend_router,
            grad_feed_router,
            grad_gain,
            grad_bias,
            usage,
        ),
        ("dp", "expert"),
    )
    grad_expand_sum, grad_reduce_sum = (
        lax.psum(grad_expand.astype(jnp.bfloat16), "dp").astype(jnp.float32),
        lax.psum(grad_reduce.astype(jnp.bfloat16), "dp").astype(jnp.float32),
    )
    grad_key_sum = shared[1][:, :head]
    grad_value_sum = shared[1][:, head:]
    return (
        output,
        grad_tokens,
        shared[5],
        shared[6][0],
        shared[6][1],
        shared[0],
        grad_key_sum,
        grad_value_sum,
        shared[2],
        shared[3],
        shared[4],
        grad_expand_sum,
        grad_reduce_sum,
        shared[7],
    )


def solution(mesh):
    placed = (
        P("dp", "expert", None),
        P("dp"),
        P("dp", "expert", None),
        P("dp", "expert", None, None),
        P(),
        P(),
        P(),
        P(),
        P(),
        P(),
        P(),
        P(),
        P("expert", None, None),
        P("expert", None, None),
        P("dp", "expert", None),
    )
    fast = mesh.shape["dp"] == 8 and mesh.shape["expert"] == 4
    return jax.shard_map(
        body_fast if fast else body,
        mesh=mesh,
        in_specs=placed,
        out_specs=(
            P("dp", "expert", None),
            P("dp", "expert", None),
            P(),
            P(),
            P(),
            P(),
            P(),
            P(),
            P(),
            P(),
            P(),
            P("expert", None, None),
            P("expert", None, None),
            P(),
        ),
        check_vma=False,
    )
```

```python
import types

import jax
import jax.numpy as jnp
from jax import lax
from jax.experimental import pallas as pl
from jax.experimental.pallas import tpu as pltpu
from jax.sharding import PartitionSpec as P

CAP = 256


EPS = 1e-06
HIGH = lax.Precision.HIGHEST
F32 = jnp.float32
LOW = jnp.bfloat16
MESH = pl.DeviceIdType.MESH
MIB = 2**20


def dot(a, b):
    return jnp.dot(a, b, preferred_element_type=F32)


def dot_nt(a, b):
    return lax.dot_general(a, b, (((1,), (1,)), ((), ())), preferred_element_type=F32)


def dot_tn(a, b):
    return lax.dot_general(a, b, (((0,), (0,)), ((), ())), preferred_element_type=F32)


def remote(src, dst, send, recv, device):
    return pltpu.make_async_remote_copy(
        src_ref=src, dst_ref=dst, send_sem=send, recv_sem=recv,
        device_id=device, device_id_type=MESH,
    )


def run_kernel(kernel, name, ins, outs, scratch, collective):
    names = [*ins, *outs, *scratch]

    def body(*refs):
        kernel(types.SimpleNamespace(**dict(zip(names, refs, strict=True))))

    made = pl.pallas_call(
        body,
        name=name,
        out_shape=[jax.ShapeDtypeStruct(shape, dtype) for shape, dtype, _ in outs.values()],
        in_specs=[pl.BlockSpec(memory_space=space) for _, space in ins.values()],
        out_specs=[pl.BlockSpec(memory_space=space) for _, _, space in outs.values()],
        scratch_shapes=list(scratch.values()),
        compiler_params=pltpu.CompilerParams(
            collective_id=collective, has_side_effects=True, vmem_limit_bytes=62 * MIB
        ),
    )(*[array for array, _ in ins.values()])
    return types.SimpleNamespace(**dict(zip(outs, made, strict=True)))


def center(value):
    mean = jnp.mean(value, -1, keepdims=True)
    centred = value - mean
    scale = lax.rsqrt(jnp.mean(centred * centred, -1, keepdims=True) + EPS)
    return centred * scale, scale


def center_back(grad, normal, scale, gain):
    inner = grad * gain
    mean = jnp.mean(inner, -1, keepdims=True)
    along = jnp.mean(inner * normal, -1, keepdims=True)
    return scale * (inner - mean - normal * along)


def head_maps(heads, head):
    row = lax.broadcasted_iota(jnp.int32, (heads * head, 2 * head), 0)
    row = lax.rem(row, head)
    col = lax.broadcasted_iota(jnp.int32, (heads * head, 2 * head), 1)
    low = jnp.where(row == col, 1.0, 0.0).astype(LOW)
    high = jnp.where(row + head == col, 1.0, 0.0).astype(LOW)
    return low, high


def masked_softmax(logits, chosen, axis):
    top = jnp.max(jnp.where(chosen, logits, -1e30), axis, keepdims=True)
    expo = jnp.where(chosen, jnp.exp(jnp.minimum(logits - top, 0.0)), 0.0)
    return expo / jnp.sum(expo, axis, keepdims=True)


PIECE = 176
USED = 160
PAY = 1024


def gelu_parts(value):
    square = value * value
    inner = value * (0.7978845608028654 + 0.035677408136300125 * square)
    half = 0.5 + 0.5 * jnp.tanh(inner)
    act = value * half
    slope = half + act * (1.0 - half) * (1.5957691216057308 + 0.2140644488178007 * square)
    return act, slope


class Place:
    def __init__(self):
        self.dp = dp = lax.axis_index("dp")
        self.ex = lax.axis_index("expert")
        self.y = lax.rem(dp, 2)
        z = lax.div(dp, 2)
        self.is_end = (z == 0) | (z == 3)
        self.is_mid = (z == 1) | (z == 2)
        self.toward = (jnp.where(z < 2, dp + 2, dp - 2), self.ex)
        self.outer = (jnp.where(z == 1, dp - 2, jnp.where(z == 2, dp + 2, dp)), self.ex)
        self.core = lax.rem(self.ex, 2)
        self.spot = self.y * 2 + lax.div(self.ex, 2)

    def peer(self, r):
        return (self.dp ^ lax.div(r, 4), self.ex ^ lax.rem(r, 4))

    def plane(self, q):
        return (self.dp ^ lax.div(q, 2), self.ex ^ (2 * lax.rem(q, 2)))

    def group(self, r):
        return 2 * (self.ex ^ lax.rem(r, 4)) + (self.y ^ lax.div(r, 4))


def cot_copy(v, p, r):
    return remote(v.cot, v.ca.at[r], v.cs.at[r], v.cv.at[r], p.peer(r))


def cot_relay(v, p, to):
    at = pl.ds(0 if to == 2 else CAP // 2, CAP // 2)
    return remote(
        v.ca.at[6 - to, :, at, :], v.ca.at[6, :, at, :], v.cs.at[to + 1], v.cv.at[to + 8], p.peer(to)
    )


def cot_forward(v, p, r):
    return remote(v.ca.at[r], v.ca.at[r + 1], v.cs.at[r + 6], v.cv.at[r + 1], p.peer(1))


def row_copy(v, p, r, i):
    return remote(v.n2.at[i], v.xa.at[r, i], v.xs.at[r, i], v.xv.at[r, i], p.peer(r))


def row_relay(v, p, to, i):
    at = pl.ds(0 if to == 2 else CAP // 2, CAP // 2)
    return remote(
        v.xa.at[6 - to, i, at, :], v.xa.at[6, i, at, :],
        v.xs.at[to + 1, i], v.xv.at[to + 8, i], p.peer(to),
    )


def row_forward(v, p, r, i):
    return remote(
        v.xa.at[r, i], v.xa.at[r + 1, i], v.xs.at[r + 6, i], v.xv.at[r + 1, i], p.peer(1)
    )


def cot_near(v, p):
    for r in (4, 2):
        cot_copy(v, p, r).wait_recv()
        cot_relay(v, p, 6 - r).start()
        cot_forward(v, p, r).start()


def cot_far(v, p):
    cot_relay(v, p, 2).wait_recv()
    cot_relay(v, p, 4).wait_recv()
    cot_forward(v, p, 6).start()


def rows_near(v, p, i):
    for r in (4, 2):
        row_copy(v, p, r, i).wait_recv()
        row_relay(v, p, 6 - r, i).start()
        row_forward(v, p, r, i).start()


def rows_far(v, p, i):
    row_relay(v, p, 2, i).wait_recv()
    row_relay(v, p, 4, i).wait_recv()
    row_forward(v, p, 6, i).start()


def meta_copy(v, p, r):
    return remote(v.meta.at[p.group(r)], v.ma.at[r], v.ms.at[r], v.mv.at[r], p.peer(r))


def kv_copy(v, p, r):
    half = v.kv.shape[1] // 4
    return remote(
        v.kv.at[:, pl.ds(0, half), :], v.kv.at[:, pl.ds(r * half, half), :],
        v.ks.at[r], v.kr.at[r], p.peer(r),
    )


def kv_forward(v, p):
    half = v.kv.shape[1] // 4
    return remote(
        v.kv.at[:, pl.ds(2 * half, half), :], v.kv.at[:, pl.ds(3 * half, half), :],
        v.ks.at[3], v.kr.at[3], p.peer(1),
    )


def front(v, p):
    count, d = v.tok.shape
    half = count // 2
    heads = v.heads.shape[1]
    head = v.kv.shape[2] // 2
    picks = v.pick.shape[1]
    for i in range(2):
        named = jnp.concatenate([v.pick[i].astype(F32), jnp.zeros((8 - picks, half), F32)], 0)
        v.pickc[i] = named.T
    gain = v.gain[...]
    bias = v.bias[...]
    v.wkv[0:head, :] = v.wk[...]
    v.wkv[head:2 * head, :] = v.wv[...]
    for i in range(2):
        rows = slice(i * half, (i + 1) * half)
        normal, _ = center(v.tok[rows, :].astype(F32))
        normed = (normal * gain[0:1] + bias[0:1]).astype(LOW)
        v.n1[rows, :] = normed
        v.kv[i, 0:half, :] = dot_nt(normed, v.wkv[...]).astype(LOW)
    pl.semaphore_wait(v.barrier, jnp.where(p.is_mid, 9, 8))
    for r in (2, 1):
        kv_copy(v, p, r).start()
    for r in (4, 2, 1):
        cot_copy(v, p, r).start()
    v.ca[0] = v.cot[...]
    v.gh[0:count, 0:heads] = dot_nt(v.n1[...], v.wq[...]).astype(LOW)

    experts = v.router1.shape[1]
    number = lax.broadcasted_iota(jnp.int32, (16, count), 0)
    chosen = number == v.pickt[0:1, :]
    for k in range(1, picks):
        chosen = chosen | (number == v.pickt[k:k + 1, :])
    earlier = lax.broadcasted_iota(jnp.int32, (count, count), 0) < lax.broadcasted_iota(
        jnp.int32, (count, count), 1
    )
    before = dot(jnp.where(chosen, 1.0, 0.0).astype(LOW), jnp.where(earlier, 1.0, 0.0).astype(LOW))
    rank = jnp.where(chosen, before, -1.0)

    to_query, to_value = head_maps(heads // head, head)
    owner = lax.div(lax.broadcasted_iota(jnp.int32, (half, heads), 1), head).astype(F32)
    lane = lax.broadcasted_iota(jnp.int32, (half, experts), 1).astype(F32)
    wide = lax.broadcasted_iota(jnp.int32, (half, 2 * head), 1)
    kv_copy(v, p, 2).wait_recv()
    kv_forward(v, p).start()
    kv_copy(v, p, 1).wait_recv()
    kv_forward(v, p).wait_recv()

    for i in range(2):
        rows = slice(i * half, (i + 1) * half)
        logits = dot_nt(v.n1[rows, :], v.router1[v.task[i]])
        named = [lane == v.pickc[i, :, k:k + 1] for k in range(picks)]
        allowed = named[0]
        for k in range(1, picks):
            allowed = allowed | named[k]
        gates = masked_softmax(logits, allowed, 1)
        v.g1[rows, :] = gates
        kv = v.kv[i]
        for k in range(picks):
            at = picks * i + k
            if i == 1 and k == 2:
                cot_far(v, p)
                rows_near(v, p, 0)
            mine = owner == v.pickc[i, :, k:k + 1]
            gate = jnp.sum(jnp.where(named[k], gates, 0.0), 1, keepdims=True)
            all_queries = v.gh[rows, 0:heads]
            query = dot(jnp.where(mine, all_queries, jnp.zeros_like(all_queries)), to_query)
            query = (query * head ** -0.5).astype(LOW)
            v.q8[at] = query
            scores = dot_nt(query, kv)
            expo = jnp.exp(scores - jnp.max(scores, 1, keepdims=True))
            total = jnp.sum(expo, 1, keepdims=True)
            low = expo.astype(LOW)
            v.act[at * half:(at + 1) * half, 0:4 * half] = low
            attended = dot(low, kv) / total
            v.att[at] = jnp.where(wide == 0, total, attended)
            spread = dot_nt((gate * attended).astype(LOW), to_value).astype(LOW)
            if k == 0:
                v.heads[rows, :] = jnp.where(mine, spread, jnp.zeros_like(spread))
            else:
                v.heads[rows, :] = jnp.where(mine, spread, v.heads[rows, :])
        middle = v.tok[rows, :].astype(F32) + dot(v.heads[rows, :], v.wo[...])
        v.mid[rows, :] = middle
        normal, _ = center(middle)
        normed = (normal * gain[1:2] + bias[1:2]).astype(LOW)
        v.n2[i] = normed
        for r in (4, 2, 1):
            row_copy(v, p, r, i).start()
        v.xa[0, i] = normed
        logits = dot_nt(v.router2[v.task[i]], normed)
        logits = jnp.concatenate([logits, jnp.zeros((16 - experts, half), F32)], 0)
        gates = masked_softmax(logits, rank[:, rows] >= 0.0, 0)
        v.g2[:, rows] = gates
        for g in range(8):
            v.meta[g, 0:2, rows] = rank[2 * g:2 * g + 2, rows]
            v.meta[g, 2:4, rows] = gates[2 * g:2 * g + 2, :]
            v.meta[g, 4:16, rows] = jnp.zeros((12, half), F32)
        if i == 0:
            cot_near(v, p)
    v.ma[0] = v.meta[p.group(0)]
    for r in range(1, 8):
        meta_copy(v, p, r).start()


def chunk_first(v, p, c):
    return remote(v.ra.at[c], v.rb.at[c], v.s1s.at[c], v.s1r.at[c], p.toward)


def chunk_middle(v, p, c):
    return remote(v.rb.at[c], v.rc.at[c], v.s2s.at[c], v.s2r.at[c], p.toward)


def chunk_back(v, p, c):
    return remote(v.ra.at[c], v.rc.at[c], v.s3s.at[c], v.s2r.at[c], p.outer)


def chunk_pair(v, p, src, c):
    to = p.y * v.ra.shape[0] + c
    return remote(src.at[c], v.chunks.at[to], v.ys.at[c], v.yr.at[c], (p.dp ^ 1, p.ex))


def chunk_own(v, p, src, c):
    to = p.y * v.ra.shape[0] + c
    return pltpu.make_async_copy(src.at[c], v.chunks.at[to], v.ls.at[c])


def tick(v, p, t):
    chunks = v.ra.shape[0]

    @pl.when(p.is_mid & (t < chunks))
    def _():
        c = jnp.minimum(t, chunks - 1)
        chunk_first(v, p, c).wait_recv()
        v.rb[c] = (v.ra[c].astype(F32) + v.rb[c].astype(F32)).astype(LOW)
        chunk_middle(v, p, c).start()

    @pl.when(p.is_mid & (t >= 2) & (t < chunks + 2))
    def _():
        c = jnp.maximum(t - 2, 0)
        chunk_middle(v, p, c).wait_recv()
        v.ra[c] = (v.rb[c].astype(F32) + v.rc[c].astype(F32)).astype(LOW)
        chunk_back(v, p, c).start()
        chunk_pair(v, p, v.ra, c).start()
        chunk_own(v, p, v.ra, c).start()

    @pl.when(p.is_end & (t >= 4) & (t < chunks + 4))
    def _():
        c = jnp.maximum(t - 4, 0)
        chunk_middle(v, p, c).wait_recv()
        chunk_pair(v, p, v.rc, c).start()
        chunk_own(v, p, v.rc, c).start()


def ticks(v, p, first, after):
    def one(t, carry):
        tick(v, p, t)
        return carry

    lax.fori_loop(first, after, one, 0)


def chunks_done(v, p):
    chunks = v.ra.shape[0]

    def one(c, carry):
        @pl.when(p.is_end)
        def _():
            chunk_first(v, p, c).wait_send()
            chunk_pair(v, p, v.rc, c).wait_send()
            chunk_own(v, p, v.rc, c).wait()

        @pl.when(p.is_mid)
        def _():
            chunk_middle(v, p, c).wait_send()
            chunk_back(v, p, c).wait_send()
            chunk_pair(v, p, v.ra, c).wait_send()
            chunk_own(v, p, v.ra, c).wait()

        other = v.chunks.at[(1 - p.y) * chunks + c]
        remote(v.ra.at[c], other, v.ys.at[c], v.yr.at[c], (p.dp ^ 1, p.ex)).wait_recv()
        return carry

    lax.fori_loop(0, chunks, one, 0)


def weight_loads(v, p, j):
    return (
        pltpu.make_async_copy(v.we_all.at[p.y * 2 + j], v.we, v.wsem.at[0]),
        pltpu.make_async_copy(v.wr_all.at[p.y * 2 + j], v.wr, v.wsem.at[1]),
    )


def source_rows(r):
    return pl.ds(pl.multiple_of(r * CAP, CAP), CAP)


def slot_hits(v, r, j):
    sub = lax.broadcasted_iota(jnp.int32, (CAP, 2 * CAP), 0).astype(F32)
    return sub == v.ma[r, j:j + 1, :]


def dispatch(v, r, j):
    d = v.xa.shape[3]
    hit = slot_hits(v, r, j)
    pick = jnp.where(hit, 1.0, 0.0).astype(LOW)
    gate = jnp.sum(jnp.where(hit, v.ma[r, j + 2:j + 3, :], 0.0), 1, keepdims=True)
    at = source_rows(r)
    rows = dot(pick, v.xa[r].reshape(2 * CAP, d))
    v.pr[j, at, :] = rows.astype(LOW)
    v.xrt[:, at] = rows.T.astype(LOW)
    rows = gate * dot(pick, v.ca[r].reshape(2 * CAP, d))
    v.gr[j, at, :] = rows.astype(LOW)
    v.gpt[:, at] = rows.T.astype(LOW)


def columns(v, j, f):
    cols = pl.ds(pl.multiple_of(f * 256, 256), 256)
    step = 512
    for b in range(v.act.shape[0] // step):
        rows = slice(b * step, (b + 1) * step)
        value, slope = gelu_parts(dot(v.pr[j, rows, :], v.we[:, cols]))
        v.act[rows, cols] = value.astype(LOW)
        v.gh[rows, cols] = (dot_nt(v.gr[j, rows, :], v.wr[cols, :]) * slope).astype(LOW)


def weight_grads(v, p, j, f):
    cols = pl.ds(pl.multiple_of(f * 256, 256), 256)
    first = j * (v.ra.shape[0] // 2) + 2 * f
    v.ra[first] = dot(v.gpt[...], v.act[:, cols]).astype(LOW)
    v.ra[first + 1] = dot(v.xrt[...], v.gh[:, cols]).astype(LOW)

    @pl.when(p.is_end)
    def _():
        chunk_first(v, p, first).start()
        chunk_first(v, p, first + 1).start()


def produce(v, n, j):
    size = v.act.shape[0] // 2
    at = pl.ds(pl.multiple_of(n * size, size), size)
    v.pr[j, at, :] = dot(v.act[at, :], v.wr[...]).astype(LOW)
    v.gr[j, at, :] = dot_nt(v.gh[at, :], v.we[...]).astype(LOW)

    def gates(m, carry):
        r = n * (size // CAP) + m
        made = v.pr[j, source_rows(r), :].astype(F32)
        hit = slot_hits(v, r, j)
        pick = jnp.where(hit, 1.0, 0.0).astype(LOW)
        seen = dot(pick, v.ca[r].reshape(2 * CAP, made.shape[1]))
        inner = jnp.sum(made * seen, 1, keepdims=True)
        part = jnp.sum(jnp.where(hit, inner, 0.0), 0, keepdims=True)
        v.dgs[r, j] = jnp.broadcast_to(part, (8, 2 * CAP))
        return carry

    lax.fori_loop(0, size // CAP, gates, 0)


def gate_copy(v, p, r):
    return remote(v.dgs.at[r], v.dg.at[p.group(0)], v.gs.at[r], v.gv.at[r], p.peer(r))


def part_core(v, p, r, which):
    ref = (v.gr, v.pr)[which]
    at = 4 * which + lax.div(r, 2)
    return remote(ref.at[:, source_rows(r), :], v.xa.at[at], v.k1s.at[at], v.k1r.at[at], p.peer(1))


def part_x(v, p, r, which, i):
    ref = (v.gr, v.pr)[which]
    at = 4 * which + r // 2 - 1
    return remote(
        ref.at[i, source_rows(r), :], v.ca.at[at, i], v.k2s.at[at, i], v.k2r.at[at, i], p.peer(2)
    )


def part_y(v, p, which, i):
    ref = (v.gr, v.pr)[which]
    at = 4 * which + 1
    return remote(
        ref.at[i, source_rows(4), :], v.ca.at[at, i], v.k2s.at[at, i], v.k2r.at[at, i], p.peer(4)
    )


def combine(v, r, which):
    lane = lax.broadcasted_iota(jnp.int32, (2 * CAP, CAP), 1).astype(F32)
    meta = v.ma[r].T
    at = source_rows(r)
    ref = (v.gr, v.pr)[which]
    total = jnp.zeros((2 * CAP, ref.shape[2]), F32)
    for j in range(2):
        hit = lane == meta[:, j:j + 1]
        weight = 1.0 if which == 0 else meta[:, 2 + j:3 + j]
        total = total + dot(jnp.where(hit, weight, 0.0).astype(LOW), ref[j, at, :])
    ref[0, at, :] = total[:CAP].astype(LOW)
    ref[1, at, :] = total[CAP:].astype(LOW)


def send_parts(v, p, which):
    def odd(n, carry):
        r = 7 - 2 * n
        combine(v, r, which)
        part_core(v, p, r, which).start()
        return carry

    lax.fori_loop(0, 4, odd, 0)

    def even(n, carry):
        r = jnp.where(n < 2, 6 - 4 * n, 12 - 4 * n)
        combine(v, r, which)
        part_core(v, p, r, which).wait_recv()
        ref = (v.gr, v.pr)[which]
        at = source_rows(r)
        ref[:, at, :] = (
            ref[:, at, :].astype(F32) + v.xa[4 * which + lax.div(r, 2)].astype(F32)
        ).astype(LOW)
        return carry

    lax.fori_loop(0, 2, even, 0)
    if which == 0:
        for i in range(2):
            for r in (6, 2):
                part_x(v, p, r, which, i).start()
    lax.fori_loop(2, 4, even, 0)


def relay_parts(v, p, which, i):
    ref = (v.gr, v.pr)[which]
    part_x(v, p, 6, which, i).wait_recv()
    at = source_rows(4)
    ref[i, at, :] = (ref[i, at, :].astype(F32) + v.ca[4 * which + 2, i].astype(F32)).astype(LOW)
    part_y(v, p, which, i).start()
    part_x(v, p, 2, which, i).wait_recv()


def own_sum(v, i, which):
    ref = (v.gr, v.pr)[which]
    total = ref[i, 0:CAP, :].astype(F32) + v.ca[4 * which, i].astype(F32)
    return total + v.ca[4 * which + 1, i].astype(F32)


def piece(v, g, c, q):
    at = PAY + (2 * g + c) * PIECE
    return v.act.at[
        pl.ds(pl.multiple_of(at, 16), PIECE), pl.ds(pl.multiple_of(q * 384, 128), 384)
    ]


def place_tasks(v, g, per_image, start):
    experts, d = per_image[0].shape
    pad = jnp.zeros((16 - experts, d), F32)
    at = PAY + (2 * g + 1) * PIECE
    column, row = 2 * d, start
    for j in range(v.router1.shape[0]):
        if row + 16 > PIECE:
            column, row = 3 * d, 0
        mine = [jnp.where(v.task[i] == j, per_image[i], 0.0) for i in range(2)]
        total = mine[0] + mine[1]
        if experts < 16:
            total = jnp.concatenate([total, pad], 0)
        v.act[at + row:at + row + 16, column:column + d] = total.astype(LOW)
        row += 16


def place_rows(v, g, value):
    d = value.shape[1]
    for n in range(6):
        at = PAY + (2 * g + n // 4) * PIECE
        q = n % 4
        v.act[at:at + USED, q * d:(q + 1) * d] = value[n * USED:(n + 1) * USED].astype(LOW)


def back_first(v, i):
    count, d = v.tok.shape
    half = count // 2
    heads = v.heads.shape[1]
    experts = v.router2.shape[1]
    rows = slice(i * half, (i + 1) * half)
    grad_gates = jnp.concatenate([v.dg[g, j, 0:1, rows] for g in range(8) for j in range(2)], 0)
    gates = v.g2[:, rows]
    grad_logits = gates * (grad_gates - jnp.sum(gates * grad_gates, 0, keepdims=True))
    grad_logits = grad_logits[0:experts].astype(LOW)
    gain = v.gain[1:2]
    grad = own_sum(v, i, 0) + dot_tn(grad_logits, v.router2[v.task[i]])
    normal, scale = center(v.mid[rows, :])
    grad_gain = jnp.sum(grad * normal, 0, keepdims=True)
    grad_bias = jnp.sum(grad, 0, keepdims=True)
    if i == 0:
        v.small[0, 1:2, :] = grad_gain
        v.small[0, 3:4, :] = grad_bias
    else:
        v.small[0, 1:2, :] = v.small[0, 1:2, :] + grad_gain
        v.small[0, 3:4, :] = v.small[0, 3:4, :] + grad_bias
    total = v.cot[i].astype(F32) + center_back(grad, normal, scale, gain)
    v.gtok[rows, :] = total
    low = total.astype(LOW)
    v.act[rows, PAY:PAY + d] = low
    v.act[rows, 0:heads] = dot_nt(low, v.wo[...]).astype(LOW)
    return dot(grad_logits, v.n2[i])


def back_middle(v, per_image):
    count, d = v.tok.shape
    place_rows(v, 0, dot_tn(v.heads[...], v.act[0:count, PAY:PAY + d]))
    place_tasks(v, 0, per_image, 0)


def back_attention(v, i, pause):
    count, d = v.tok.shape
    half = count // 2
    heads = v.heads.shape[1]
    head = v.kv.shape[2] // 2
    picks = v.pick.shape[1]
    experts = v.router1.shape[1]
    to_query, to_value = head_maps(heads // head, head)
    owner = lax.div(lax.broadcasted_iota(jnp.int32, (half, heads), 1), head).astype(F32)
    lane = lax.broadcasted_iota(jnp.int32, (half, experts), 1).astype(F32)
    rows = slice(i * half, (i + 1) * half)
    lower = slice(count + i * half, count + (i + 1) * half)
    kv = v.kv[i]
    gates = v.g1[rows, :]
    grad_gates = jnp.zeros((half, experts), F32)
    grad_pair = jnp.zeros((2 * head, 4 * half), F32)
    for k in range(picks):
        at = picks * i + k
        mine = owner == v.pickc[i, :, k:k + 1]
        named = lane == v.pickc[i, :, k:k + 1]
        gate = jnp.sum(jnp.where(named, gates, 0.0), 1, keepdims=True)
        grad_heads = v.act[rows, 0:heads]
        grad = dot(jnp.where(mine, grad_heads, jnp.zeros_like(grad_heads)), to_value)
        attended = v.att[at]
        total = attended[:, 0:1]
        grad_gates = grad_gates + jnp.where(named, jnp.sum(grad * attended, 1, keepdims=True), 0.0)
        grad = ((gate * grad).astype(LOW).astype(F32) / total).astype(LOW)
        inner = jnp.sum(grad.astype(F32) * attended, 1, keepdims=True)
        expo = v.gh[at * half:(at + 1) * half, 0:4 * half]
        grad_scores = (expo.astype(F32) * (dot_nt(grad, kv) - inner)).astype(LOW)
        grad_query = (dot(grad_scores, kv) * head ** -0.5).astype(LOW)
        spread = dot_nt(grad_query, to_query).astype(LOW)
        if k == 0:
            v.act[lower, 0:heads] = jnp.where(mine, spread, jnp.zeros_like(spread))
        else:
            v.act[lower, 0:heads] = jnp.where(mine, spread, v.act[lower, 0:heads])
        grad_pair = grad_pair + dot(v.q8[at].astype(F32).T.astype(LOW), grad_scores)
        grad_pair = grad_pair + dot(grad.astype(F32).T.astype(LOW), expo)
        pause(i, k)
    grad_logits = gates * (grad_gates - jnp.sum(gates * grad_gates, 1, keepdims=True))
    v.gl1[rows, :] = grad_logits.astype(LOW)
    for r in range(4):
        v.dkv[r, i] = grad_pair[:, r * half:(r + 1) * half].astype(LOW)


def pair_copy(v, p, r):
    return remote(v.dkv.at[r], v.din.at[r], v.ps.at[r], v.pr_sem.at[r], p.peer(r))


def pair_sum(v, i):
    pair = v.dkv[0, i].astype(F32)
    for r in (1, 2, 3):
        pair = pair + v.din[r, i].astype(F32)
    return pair


def back_shared(v):
    count, d = v.tok.shape
    half = count // 2
    heads = v.heads.shape[1]
    width = v.kv.shape[2]
    grad_pair = jnp.zeros((width, d), F32)
    per_image = []
    for i in range(2):
        rows = slice(i * half, (i + 1) * half)
        grad_pair = grad_pair + dot(pair_sum(v, i).astype(LOW), v.n1[rows, :])
        per_image.append(dot_tn(v.gl1[rows, :], v.n1[rows, :]))
    place_rows(v, 1, dot_tn(v.act[count:2 * count, 0:heads], v.n1[...]))
    at = PAY + 3 * PIECE
    v.act[at:at + width, 2 * d:3 * d] = grad_pair.astype(LOW)
    place_tasks(v, 1, per_image, width)


def back_last(v):
    count, d = v.tok.shape
    half = count // 2
    heads = v.heads.shape[1]
    gain = v.gain[0:1]
    grad_gain = jnp.zeros((1, d), F32)
    grad_bias = jnp.zeros((1, d), F32)
    for i in range(2):
        rows = slice(i * half, (i + 1) * half)
        lower = slice(count + i * half, count + (i + 1) * half)
        grad = dot(v.act[lower, 0:heads], v.wq[...])
        grad = grad + dot(pair_sum(v, i).T.astype(LOW), v.wkv[...])
        grad = grad + dot(v.gl1[rows, :], v.router1[v.task[i]])
        normal, scale = center(v.tok[rows, :].astype(F32))
        grad_gain = grad_gain + jnp.sum(grad * normal, 0, keepdims=True)
        grad_bias = grad_bias + jnp.sum(grad, 0, keepdims=True)
        v.gtok[rows, :] = v.gtok[rows, :] + center_back(grad, normal, scale, gain)
    v.small[0, 0:1, :] = grad_gain
    v.small[0, 2:3, :] = grad_bias


def count_usage(v):
    count, d = v.tok.shape
    half = count // 2
    picks = v.pick.shape[1]
    number = lax.broadcasted_iota(jnp.int32, (16, half), 0)
    task = lax.broadcasted_iota(jnp.int32, (16, 128), 1)
    v.small[0] = jnp.zeros_like(v.small[0])
    for which in range(2):
        table = jnp.zeros((16, 128), F32)
        for i in range(2):
            named = jnp.zeros((16, half), F32)
            for k in range(picks):
                if which == 0:
                    row = v.pick[i, k:k + 1, :]
                else:
                    row = v.pickt[k:k + 1, i * half:(i + 1) * half]
                named = named + jnp.where(number == row, 1.0, 0.0)
            table = table + jnp.where(task == v.task[i], jnp.sum(named, 1, keepdims=True), 0.0)
        v.small[0, 8 + 16 * which:24 + 16 * which, 0:128] = table


class Shared:
    def __init__(self, v, p, g):
        self.v, self.p, self.g = v, p, g
        core, mine = p.core, p.spot
        side = PAY + 2 * g * PIECE

        def half(c):
            return v.act.at[pl.ds(pl.multiple_of(side + c * PIECE, 16), PIECE), :]

        partner = p.peer(1)
        s, r = v.hs.at[g], v.hr.at[g]
        self.own_half = half(core)
        self.first = remote(half(1 - core), v.half_in.at[g], s.at[0], r.at[0], partner)
        self.scatter = [
            remote(piece(v, g, core, mine ^ q), v.piece_in.at[g, q - 1], s.at[q], r.at[q], p.plane(q))
            for q in (1, 2, 3)
        ]
        self.own = piece(v, g, core, mine)
        zown, zb, zc, zall = (v.zbuf.at[g, n] for n in range(4))
        self.z = (zown, zb, zc, zall)
        self.in_end = remote(zown, zb, s.at[4], r.at[4], p.toward)
        self.mid = remote(zb, zc, s.at[4], r.at[5], p.toward)
        self.out_mid = remote(zall, zall, s.at[5], r.at[6], p.outer)
        place = core * 4 + mine
        self.own_copy = pltpu.make_async_copy(zall, v.shared.at[g, place], v.osem.at[2 + g])
        self.gather = [
            remote(zall, v.shared.at[g, place], s.at[5 + q], r.at[6 + q], p.plane(q))
            for q in (1, 2, 3)
        ]
        self.arrive = [
            remote(zall, v.shared.at[g, core * 4 + (mine ^ q)], s.at[5 + q], r.at[6 + q], p.plane(q))
            for q in (1, 2, 3)
        ]
        ours = v.shared.at[g, pl.ds(core * 4, 4)]
        theirs = v.shared.at[g, pl.ds((1 - core) * 4, 4)]
        self.last = remote(ours, ours, s.at[9], r.at[10], partner)
        self.last_in = remote(theirs, theirs, s.at[9], r.at[10], partner)

    def stage(self, n):
        v, p, g = self.v, self.p, self.g
        zown, zb, zc, zall = self.z
        if n == 0:
            self.first.start()
        if n == 1:
            self.first.wait_recv()
            own = self.own_half
            own[...] = (own[...].astype(F32) + v.half_in[g].astype(F32)).astype(LOW)
            for copy in self.scatter:
                copy.start()
        if n == 2:
            for copy in self.scatter:
                copy.wait_recv()
            total = self.own[...].astype(F32)
            for q in (1, 2, 3):
                total = total + v.piece_in[g, q - 1].astype(F32)
            zown[...] = total.astype(LOW)

            @pl.when(p.is_end)
            def _():
                self.in_end.start()

        if n == 3:
            @pl.when(p.is_mid)
            def _():
                self.in_end.wait_recv()
                zb[...] = (zown[...].astype(F32) + zb[...].astype(F32)).astype(LOW)
                self.mid.start()

        if n == 4:
            @pl.when(p.is_mid)
            def _():
                self.mid.wait_recv()
                zall[...] = (zb[...].astype(F32) + zc[...].astype(F32)).astype(LOW)
                self.out_mid.start()

        if n == 5:
            @pl.when(p.is_end)
            def _():
                self.out_mid.wait_recv()

            self.own_copy.start()
            for copy in self.gather:
                copy.start()
        if n == 6:
            self.own_copy.wait()
            for copy in self.arrive:
                copy.wait_recv()
            self.last.start()
        if n == 7:
            self.last_in.wait_recv()
            for copy in [self.first, self.last, *self.scatter, *self.gather]:
                copy.wait_send()

            @pl.when(p.is_end)
            def _():
                self.in_end.wait_send()

            @pl.when(p.is_mid)
            def _():
                self.mid.wait_send()
                self.out_mid.wait_send()


class Small:
    def __init__(self, v, p):
        self.v, self.p = v, p

        def exchange(n, device):
            return remote(v.small.at[n], v.small_in.at[n], v.ss.at[n], v.sr.at[n], device)

        self.around = [exchange(0, p.peer(1)), exchange(1, p.plane(1)), exchange(2, p.plane(2))]
        self.in_end = exchange(3, p.toward)
        self.mid = exchange(4, p.toward)
        self.out_mid = remote(v.stats, v.stats, v.ss.at[5], v.sr.at[5], p.outer)

    def stage(self, n):
        v, p = self.v, self.p
        if n == 0:
            self.around[0].start()
        if n in (1, 2, 3):
            self.around[n - 1].wait_recv()
            v.small[n] = v.small[n - 1] + v.small_in[n - 1]
            if n < 3:
                self.around[n].start()
            else:
                @pl.when(p.is_end)
                def _():
                    self.in_end.start()

        if n == 4:
            @pl.when(p.is_mid)
            def _():
                self.in_end.wait_recv()
                v.small[4] = v.small[3] + v.small_in[3]
                self.mid.start()

        if n == 5:
            @pl.when(p.is_mid)
            def _():
                self.mid.wait_recv()
                v.stats[...] = v.small[4] + v.small_in[4]
                self.out_mid.start()

        if n == 6:
            @pl.when(p.is_end)
            def _():
                self.out_mid.wait_recv()
                self.in_end.wait_send()

            @pl.when(p.is_mid)
            def _():
                self.mid.wait_send()
                self.out_mid.wait_send()

            for copy in self.around:
                copy.wait_send()


def layer_kernel(v):
    p = Place()
    v.barrier = pltpu.get_barrier_semaphore()
    for r in range(1, 8):
        pl.semaphore_signal(v.barrier, 1, device_id=p.peer(r), device_id_type=MESH)
    pl.semaphore_signal(v.barrier, 1, device_id=p.toward, device_id_type=MESH)

    @pl.when(p.is_mid)
    def _():
        pl.semaphore_signal(v.barrier, 1, device_id=p.outer, device_id_type=MESH)

    for load in weight_loads(v, p, 0):
        load.start()
    front(v, p)

    spill = pltpu.make_async_copy(v.act.at[:, pl.ds(0, v.expo.shape[1])], v.expo, v.osem.at[1])
    spill.start()
    rows_far(v, p, 0)
    row_copy(v, p, 1, 0).wait_recv()
    row_copy(v, p, 1, 1).wait_recv()
    cot_copy(v, p, 1).wait_recv()
    meta_copy(v, p, 1).wait_recv()
    dispatch(v, 0, 0)
    dispatch(v, 1, 0)
    rows_near(v, p, 1)
    for load in weight_loads(v, p, 0):
        load.wait()
    for r in (2, 4):
        meta_copy(v, p, r).wait_recv()
        dispatch(v, r, 0)
    for r in (3, 5):
        for i in range(2):
            row_forward(v, p, r - 1, i).wait_recv()
        cot_forward(v, p, r - 1).wait_recv()
        meta_copy(v, p, r).wait_recv()
        dispatch(v, r, 0)
    rows_far(v, p, 1)
    meta_copy(v, p, 6).wait_recv()
    dispatch(v, 6, 0)
    for i in range(2):
        row_forward(v, p, 6, i).wait_recv()
    cot_forward(v, p, 6).wait_recv()
    meta_copy(v, p, 7).wait_recv()
    dispatch(v, 7, 0)
    spill.wait()

    def first_columns(f, carry):
        columns(v, 0, f)
        weight_grads(v, p, 0, f)

        @pl.when(lax.rem(f, 2) == 1)
        def _():
            tick(v, p, lax.div(f, 2))

        return carry

    lax.fori_loop(0, 6, first_columns, 0)

    def first_produce(n, carry):
        produce(v, n, 0)
        tick(v, p, 3 + n)
        return carry

    lax.fori_loop(0, 2, first_produce, 0)
    for load in weight_loads(v, p, 1):
        load.start()

    def second_dispatch(r, carry):
        dispatch(v, r, 1)
        return carry

    lax.fori_loop(0, 8, second_dispatch, 0)
    for i in range(2):
        for r in (1, 2, 4):
            row_copy(v, p, r, i).wait_send()
        for r in (2, 4):
            row_relay(v, p, r, i).wait_send()
        for r in (2, 4, 6):
            row_forward(v, p, r, i).wait_send()
    pl.semaphore_signal(v.free_core, 1, device_id=p.peer(1), device_id_type=MESH)
    for load in weight_loads(v, p, 1):
        load.wait()

    def second_columns(f, carry):
        columns(v, 1, f)

        @pl.when(lax.rem(f, 2) == 1)
        def _():
            tick(v, p, 5 + lax.div(f, 2))

        return carry

    lax.fori_loop(0, 6, second_columns, 0)

    def second_produce(n, carry):
        produce(v, n, 1)
        tick(v, p, 8 + n)
        return carry

    lax.fori_loop(0, 2, second_produce, 0)
    for r in range(1, 8):
        gate_copy(v, p, r).start()
    v.dg[p.group(0)] = v.dgs[0]
    for r in (1, 2, 4):
        cot_copy(v, p, r).wait_send()
    for r in (2, 4):
        cot_relay(v, p, r).wait_send()
    for r in (2, 4, 6):
        cot_forward(v, p, r).wait_send()
    for q in (1, 2):
        pl.semaphore_signal(v.free_plane, 1, device_id=p.plane(q), device_id_type=MESH)
    pl.semaphore_wait(v.free_core, 1)
    pl.semaphore_wait(v.free_plane, 2)
    send_parts(v, p, 0)

    def second_grads(f, carry):
        weight_grads(v, p, 1, f)

        @pl.when(lax.rem(f, 3) == 2)
        def _():
            tick(v, p, 10 + lax.div(f, 3))

        return carry

    lax.fori_loop(0, 6, second_grads, 0)
    refill = pltpu.make_async_copy(v.expo, v.gh.at[:, pl.ds(0, v.expo.shape[1])], v.osem.at[1])
    refill.start()
    relay_parts(v, p, 0, 0)
    send_parts(v, p, 1)
    count_usage(v)
    v.act[PAY:PAY + 4 * PIECE, :] = jnp.zeros((4 * PIECE, v.act.shape[1]), LOW)
    for r in range(1, 8):
        gate_copy(v, p, r).wait_recv()
    ticks(v, p, 12, 14)
    part_y(v, p, 0, 0).wait_recv()
    per_image = [back_first(v, 0)]
    relay_parts(v, p, 0, 1)
    for i in range(2):
        for r in (6, 2):
            part_x(v, p, r, 1, i).start()
    ticks(v, p, 14, 15)
    refill.wait()
    early = Shared(v, p, 0)
    late = Shared(v, p, 1)
    small = Small(v, p)

    def pause(i, k):
        at = 4 * i + k
        if at in (1, 3):
            ticks(v, p, 15 + at // 2, 16 + at // 2)
        if at in (5, 7):
            ticks(v, p, 15 + at // 2, 16 + at // 2)
        if i == 1:
            early.stage(k + 1)
        if at == 3:
            relay_parts(v, p, 1, 0)
            relay_parts(v, p, 1, 1)

    back_attention(v, 0, pause)
    part_y(v, p, 0, 1).wait_recv()
    per_image.append(back_first(v, 1))
    back_middle(v, per_image)
    early.stage(0)
    back_attention(v, 1, pause)
    for r in (1, 2, 3):
        pair_copy(v, p, r).start()
    for i in range(2):
        part_y(v, p, 1, i).wait_recv()
        rows = slice(i * CAP, (i + 1) * CAP)
        v.out[rows, :] = (v.mid[rows, :] + own_sum(v, i, 1)).astype(LOW)
    early.stage(5)
    ticks(v, p, 19, 20)
    for r in (1, 2, 3):
        pair_copy(v, p, r).wait_recv()
    back_shared(v)
    late.stage(0)
    back_last(v)
    late.stage(1)
    small.stage(0)
    ticks(v, p, 20, 22)
    small.stage(1)
    late.stage(2)
    small.stage(2)
    early.stage(6)
    ticks(v, p, 22, 23)
    late.stage(3)
    small.stage(3)
    ticks(v, p, 23, 24)
    late.stage(4)
    small.stage(4)
    ticks(v, p, 24, 25)
    late.stage(5)
    small.stage(5)
    ticks(v, p, 25, 26)
    late.stage(6)
    small.stage(6)
    ticks(v, p, 26, 28)
    early.stage(7)
    late.stage(7)

    for r in (1, 2, 3):
        pair_copy(v, p, r).wait_send()
    for r in (1, 2):
        kv_copy(v, p, r).wait_send()
    kv_forward(v, p).wait_send()
    for r in range(1, 8):
        meta_copy(v, p, r).wait_send()
        gate_copy(v, p, r).wait_send()
    for which in range(2):
        for r in (1, 3, 5, 7):
            part_core(v, p, r, which).wait_send()
        for i in range(2):
            for r in (2, 6):
                part_x(v, p, r, which, i).wait_send()
            part_y(v, p, which, i).wait_send()
    chunks_done(v, p)


def layer_call(tok, cot, pick, pickt, task, gain, bias, wq, wk, wv, wo, router1, router2, we, wr):
    count, d = tok.shape
    half = count // 2
    heads = wq.shape[0]
    width = 2 * wk.shape[0]
    picks = pick.shape[1]
    experts = router1.shape[1]
    ff = we.shape[2]
    chunks = 4 * ff // 256
    vm = pltpu.VMEM
    anywhere = pl.ANY
    dma = pltpu.SemaphoreType.DMA
    return run_kernel(
        layer_kernel, "layer",
        dict(
            tok=(tok, vm), cot=(cot, vm), pick=(pick, vm), pickt=(pickt, vm),
            task=(task, pltpu.SMEM), gain=(gain, vm), bias=(bias, vm), wq=(wq, vm), wk=(wk, vm),
            wv=(wv, vm), wo=(wo, vm), router1=(router1, vm), router2=(router2, vm),
            we_all=(we, anywhere), wr_all=(wr, anywhere),
        ),
        dict(
            out=((count, d), LOW, vm), gtok=((count, d), F32, vm),
            chunks=((2 * chunks, d, 256), LOW, anywhere),
            shared=((2, 8, PIECE, d), LOW, anywhere),
            stats=((40, d), F32, vm), expo=((8 * CAP, 4 * half), LOW, anywhere),
        ),
        dict(
            n1=vm((count, d), LOW), n2=vm((2, half, d), LOW), mid=vm((count, d), F32),
            pickc=vm((2, half, 8), F32), wkv=vm((width, d), LOW),
            heads=vm((count, heads), LOW), kv=vm((2, 4 * half, width), LOW),
            q8=vm((2 * picks, half, width), LOW), att=vm((2 * picks, half, width), F32),
            g1=vm((count, experts), F32), g2=vm((16, count), F32), meta=vm((8, 16, count), F32),
            xa=vm((8, 2, half, d), LOW), ca=vm((8, 2, half, d), LOW),
            ma=vm((8, 16, count), F32), we=vm((d, ff), LOW), wr=vm((ff, d), LOW),
            xrt=vm((d, 8 * CAP), LOW), gpt=vm((d, 8 * CAP), LOW),
            act=vm((8 * CAP, ff), LOW), gh=vm((8 * CAP, ff), LOW),
            pr=vm((2, 8 * CAP, d), LOW), gr=vm((2, 8 * CAP, d), LOW),
            ra=vm((chunks, d, 256), LOW), rb=vm((chunks, d, 256), LOW), rc=vm((chunks, d, 256), LOW),
            dgs=vm((8, 2, 8, count), F32), dg=vm((8, 2, 8, count), F32),
            small=vm((5, 40, d), F32), small_in=vm((5, 40, d), F32),
            gl1=vm((count, experts), LOW),
            dkv=vm((4, 2, width, half), LOW), din=vm((4, 2, width, half), LOW),
            half_in=vm((2, PIECE, 4 * d), LOW), piece_in=vm((2, 3, PIECE, d), LOW),
            zbuf=vm((2, 4, PIECE, d), LOW),
            cs=dma((16,)), cv=dma((16,)), ks=dma((4,)), kr=dma((4,)), xs=dma((16, 2)), xv=dma((16, 2)),
            ms=dma((8,)), mv=dma((8,)), gs=dma((8,)), gv=dma((8,)), wsem=dma((2,)), osem=dma((4,)),
            s1s=dma((chunks,)), s1r=dma((chunks,)), s2s=dma((chunks,)), s2r=dma((chunks,)),
            s3s=dma((chunks,)), ys=dma((chunks,)), yr=dma((chunks,)), ls=dma((chunks,)),
            k1s=dma((8,)), k1r=dma((8,)), k2s=dma((8, 2)), k2r=dma((8, 2)),
            ps=dma((4,)), pr_sem=dma((4,)), ss=dma((6,)), sr=dma((6,)), hs=dma((2, 10)),
            hr=dma((2, 11)),
            free_core=pltpu.SemaphoreType.REGULAR, free_plane=pltpu.SemaphoreType.REGULAR,
        ),
        0,
    )


def widen_kernel(c_ref, s_ref, reduce_ref, expand_ref, query_ref, out_ref, pair_ref, one_ref, two_ref):
    for n in range(c_ref.shape[0] // 2):
        at = slice(n * 256, (n + 1) * 256)
        reduce_ref[0, at, :] = c_ref[2 * n].astype(F32).T
        expand_ref[0, :, at] = c_ref[2 * n + 1].astype(F32)

    @pl.when((pl.program_id(0) == 0) & (pl.program_id(1) == 0))
    def _():
        for n in range(6):
            at = slice(n * USED, (n + 1) * USED)
            out_ref[at, :] = s_ref[0, n, 0:USED, :].astype(F32)
            query_ref[at, :] = s_ref[1, n, 0:USED, :].astype(F32)
        width = pair_ref.shape[0]
        experts = one_ref.shape[1]
        pair_ref[...] = s_ref[1, 6, 0:width, :].astype(F32)
        for ref, g, start in ((one_ref, 1, width), (two_ref, 0, 0)):
            q, row = 6, start
            for j in range(ref.shape[0]):
                if row + 16 > PIECE:
                    q, row = 7, 0
                ref[j] = s_ref[g, q, row:row + 16, :].astype(F32)[0:experts]
                row += 16


def widen_call(chunks, shared, slots, d, ff, wide, width, tasks, experts):
    n = ff // 256
    per = 2
    whole = pl.BlockSpec(memory_space=pltpu.VMEM)
    return pl.pallas_call(
        widen_kernel,
        name="widen",
        grid=(slots, n // per),
        in_specs=[
            pl.BlockSpec((2 * per, d, 256), lambda s, f: (s * (n // per) + f, 0, 0)),
            whole,
        ],
        out_specs=(
            pl.BlockSpec((1, per * 256, d), lambda s, f: (s, f, 0)),
            pl.BlockSpec((1, d, per * 256), lambda s, f: (s, 0, f)),
            whole, whole, whole, whole, whole,
        ),
        out_shape=(
            jax.ShapeDtypeStruct((slots, ff, d), F32),
            jax.ShapeDtypeStruct((slots, d, ff), F32),
            jax.ShapeDtypeStruct((wide, d), F32),
            jax.ShapeDtypeStruct((wide, d), F32),
            jax.ShapeDtypeStruct((width, d), F32),
            jax.ShapeDtypeStruct((tasks, experts, d), F32),
            jax.ShapeDtypeStruct((tasks, experts, d), F32),
        ),
        compiler_params=pltpu.CompilerParams(vmem_limit_bytes=48 * MIB),
    )(chunks, shared)


def body_fast(
    tokens,
    task_ids,
    attention_picks,
    feedforward_picks,
    norm_gain,
    norm_bias,
    query_weight,
    key_weight,
    value_weight,
    output_weight,
    attention_router,
    feedforward_router,
    expand_weight,
    reduce_weight,
    cotangent,
):
    images, patches, width = tokens.shape
    count = images * patches
    tasks, _, experts = attention_router.shape
    head = key_weight.shape[1]
    picks = attention_picks.shape[2]
    slots = expand_weight.shape[0]
    ff = expand_weight.shape[2]
    wide = query_weight.shape[1]
    tok = tokens.reshape(count, width)
    pickt = feedforward_picks.reshape(count, picks).T
    b = layer_call(
        tok, cotangent, jnp.swapaxes(attention_picks, 1, 2), pickt, task_ids, norm_gain, norm_bias,
        query_weight.T, key_weight.T, value_weight.T, output_weight,
        jnp.swapaxes(attention_router, 1, 2), jnp.swapaxes(feedforward_router, 1, 2),
        expand_weight, reduce_weight,
    )
    grad_reduce, grad_expand, grad_query, grad_out, grad_pair, grad_one, grad_two = widen_call(
        b.chunks, b.shared, slots, width, ff, wide, 2 * head, tasks, experts
    )
    usage = jnp.swapaxes(b.stats[8:40, :tasks].reshape(2, 16, tasks), 1, 2)[:, :, :experts]
    return (
        b.out.reshape(images, patches, width),
        b.gtok.reshape(images, patches, width),
        b.stats[0:2],
        b.stats[2],
        b.stats[3],
        grad_query.T,
        grad_pair[:head].T,
        grad_pair[head:].T,
        grad_out,
        jnp.swapaxes(grad_one, 1, 2),
        jnp.swapaxes(grad_two, 1, 2),
        grad_expand,
        grad_reduce,
        usage,
    )


def normalize(value, gain, bias):
    mean = jnp.mean(value, -1, keepdims=True)
    centred = value - mean
    spread = jnp.mean(centred * centred, -1, keepdims=True)
    return centred * lax.rsqrt(spread + EPS) * gain + bias


def gate_weights(logits, picks_hot):
    chosen = jnp.sum(picks_hot * logits[..., None, :], -1)
    return jax.nn.softmax(chosen, -1)


def activate(value):
    return jax.nn.gelu(value, approximate=True)


def body(
    tokens,
    task_ids,
    attention_picks,
    feedforward_picks,
    norm_gain,
    norm_bias,
    query_weight,
    key_weight,
    value_weight,
    output_weight,
    attention_router,
    feedforward_router,
    expand_weight,
    reduce_weight,
    cotangent,
):
    images, patches, width = tokens.shape
    count = images * patches
    tasks = attention_router.shape[0]
    experts = attention_router.shape[2]
    head = key_weight.shape[1]
    picks = attention_picks.shape[2]
    slots = expand_weight.shape[0]
    groups = lax.axis_size("expert")
    lanes = groups * slots
    f32 = jnp.float32
    low_type = jnp.bfloat16
    inputs = tokens.astype(f32).reshape(count, width)
    expert_range = jnp.arange(experts, dtype=jnp.int32)
    task_hot = (task_ids[:, None] == jnp.arange(tasks, dtype=jnp.int32)[None, :]).astype(f32)
    task_low = task_hot.astype(low_type)
    attend_hot = (attention_picks[..., None] == expert_range).astype(f32)
    attend_low = attend_hot.astype(low_type)
    choices = feedforward_picks.reshape(count, picks)
    feed_hot = (choices[..., None] == expert_range).astype(f32)
    flat = choices.reshape(count * picks)
    marks = (flat[:, None] == expert_range[None, :]).astype(jnp.int32)
    before = jnp.cumsum(marks, axis=0) - marks
    position = flat * CAP + jnp.sum(before * marks, axis=1)
    first, first_back = jax.vjp(normalize, inputs, norm_gain[0], norm_bias[0])
    normed_one = first.astype(low_type)
    shaped_one = normed_one.reshape(images, patches, width)
    router_one = jnp.einsum(
        "it,tde->ide", task_low, attention_router, preferred_element_type=f32
    ).astype(low_type)
    logits_one = jnp.einsum("ipd,ide->ipe", shaped_one, router_one, preferred_element_type=f32)
    gates_one, gates_one_back = jax.vjp(lambda value: gate_weights(value, attend_hot), logits_one)
    queries_all = jnp.dot(normed_one, query_weight, preferred_element_type=f32).astype(low_type)
    queries_all = queries_all.reshape(images, patches, experts, head)
    queries = jnp.einsum(
        "ipke,ipeh->ipkh", attend_low, queries_all, preferred_element_type=f32
    ).astype(low_type)
    queries = queries.reshape(images, patches * picks, head)
    key_value = jnp.concatenate([key_weight, value_weight], 1)
    pair = jnp.dot(normed_one, key_value, preferred_element_type=f32).astype(low_type)
    pair = pair.reshape(images, patches, 2 * head)
    pair_all = lax.all_gather(pair, "expert", axis=1, tiled=True)
    keys_all = pair_all[:, :, :head]
    values_all = pair_all[:, :, head:]
    scores = jnp.einsum("irh,ish->irs", queries, keys_all, preferred_element_type=f32) * 0.125
    top = jnp.max(scores, -1, keepdims=True)
    expo = jnp.exp(scores - top)
    total = jnp.sum(expo, -1, keepdims=True)
    log_total = top + jnp.log(total)
    probs_low = (expo / total).astype(low_type)
    attended = jnp.einsum("irs,ish->irh", probs_low, values_all, preferred_element_type=f32)
    attended = attended.reshape(images, patches, picks, head)
    weighted = gates_one[..., None] * attended
    heads = jnp.einsum("ipke,ipkh->ipeh", attend_hot, weighted, precision=HIGH)
    heads = heads.reshape(count, experts * head).astype(low_type)
    middle = inputs + jnp.dot(heads, output_weight, preferred_element_type=f32)
    second, second_back = jax.vjp(normalize, middle, norm_gain[1], norm_bias[1])
    normed_two = second.astype(low_type)
    shaped_two = normed_two.reshape(images, patches, width)
    router_two = jnp.einsum(
        "it,tde->ide", task_low, feedforward_router, preferred_element_type=f32
    ).astype(low_type)
    logits_two = jnp.einsum(
        "ipd,ide->ipe", shaped_two, router_two, preferred_element_type=f32
    ).reshape(count, experts)
    gates_two, gates_two_back = jax.vjp(lambda value: gate_weights(value, feed_hot), logits_two)
    outgoing = (
        jnp.zeros((lanes * CAP, width), low_type)
        .at[position]
        .set(jnp.repeat(normed_two, picks, axis=0))
    )
    outgoing = outgoing.reshape(groups, slots * CAP, width)
    received = lax.all_to_all(outgoing, "expert", split_axis=0, concat_axis=0, tiled=True).reshape(
        groups, slots, CAP, width
    )
    hidden = jnp.einsum("nscd,sdf->nscf", received, expand_weight, preferred_element_type=f32)
    activated, activate_back = jax.vjp(activate, hidden)
    active_low = activated.astype(low_type)
    produced = jnp.einsum(
        "nscf,sfd->nscd", active_low, reduce_weight, preferred_element_type=f32
    ).astype(low_type)
    produced = produced.reshape(groups, slots * CAP, width)
    returned = lax.all_to_all(produced, "expert", split_axis=0, concat_axis=0, tiled=True).reshape(
        lanes * CAP, width
    )
    picked = returned[position].astype(f32).reshape(count, picks, width)
    final = middle + jnp.sum(gates_two[..., None] * picked, 1)
    output = final.astype(low_type).reshape(images, patches, width)
    grad_final = cotangent.astype(f32).reshape(count, width)
    grad_gates_two = jnp.sum(picked * grad_final[:, None, :], -1)
    grad_picked = (
        (gates_two[..., None] * grad_final[:, None, :])
        .astype(low_type)
        .reshape(count * picks, width)
    )
    grad_send = jnp.zeros((lanes * CAP, width), low_type).at[position].set(grad_picked)
    grad_send = grad_send.reshape(groups, slots * CAP, width)
    grad_produced = lax.all_to_all(
        grad_send, "expert", split_axis=0, concat_axis=0, tiled=True
    ).reshape(groups, slots, CAP, width)
    grad_reduce = jnp.einsum(
        "nscf,nscd->sfd", active_low, grad_produced, preferred_element_type=f32
    )
    grad_active = jnp.einsum(
        "nscd,sfd->nscf", grad_produced, reduce_weight, preferred_element_type=f32
    )
    grad_hidden = activate_back(grad_active)[0].astype(low_type)
    grad_expand = jnp.einsum("nscd,nscf->sdf", received, grad_hidden, preferred_element_type=f32)
    grad_rows = jnp.einsum(
        "nscf,sdf->nscd", grad_hidden, expand_weight, preferred_element_type=f32
    ).astype(low_type)
    grad_rows = grad_rows.reshape(groups, slots * CAP, width)
    grad_back = lax.all_to_all(
        grad_rows, "expert", split_axis=0, concat_axis=0, tiled=True
    ).reshape(lanes * CAP, width)
    grad_normed_two = jnp.sum(grad_back[position].astype(f32).reshape(count, picks, width), 1)
    grad_logits_two = (
        gates_two_back(grad_gates_two)[0].astype(low_type).reshape(images, patches, experts)
    )
    per_image_two = jnp.einsum(
        "ipd,ipe->ide", shaped_two, grad_logits_two, preferred_element_type=f32
    )
    grad_feed_router = jnp.einsum("it,ide->tde", task_hot, per_image_two, precision=HIGH)
    grad_normed_two = grad_normed_two + jnp.einsum(
        "ipe,ide->ipd", grad_logits_two, router_two, preferred_element_type=f32
    ).reshape(count, width)
    grad_middle_norm, grad_gain_two, grad_bias_two = second_back(grad_normed_two)
    grad_middle = grad_final + grad_middle_norm
    grad_branch = grad_middle.astype(low_type)
    grad_output = jnp.einsum("tc,td->cd", heads, grad_branch, preferred_element_type=f32)
    grad_heads = jnp.einsum(
        "td,cd->tc", grad_branch, output_weight, preferred_element_type=f32
    ).astype(low_type)
    grad_heads = grad_heads.reshape(images, patches, experts, head)
    grad_selected = jnp.einsum(
        "ipke,ipeh->ipkh", attend_low, grad_heads, preferred_element_type=f32
    )
    grad_gates_one = jnp.sum(attended * grad_selected, -1)
    grad_attended = (
        (gates_one[..., None] * grad_selected)
        .astype(low_type)
        .reshape(images, patches * picks, head)
    )
    scores_back = jnp.einsum("irh,ish->irs", queries, keys_all, preferred_element_type=f32) * 0.125
    probs_back = jnp.exp(scores_back - log_total)
    grad_values = jnp.einsum(
        "irs,irh->ish", probs_back.astype(low_type), grad_attended, preferred_element_type=f32
    )
    grad_probs = jnp.einsum("irh,ish->irs", grad_attended, values_all, preferred_element_type=f32)
    inner_sum = jnp.sum(probs_back * grad_probs, -1, keepdims=True)
    grad_scores = (probs_back * (grad_probs - inner_sum)).astype(low_type)
    grad_query_sel = (
        jnp.einsum("irs,ish->irh", grad_scores, keys_all, preferred_element_type=f32) * 0.125
    )
    grad_keys = jnp.einsum("irs,irh->ish", grad_scores, queries, preferred_element_type=f32) * 0.125
    grad_pair = jnp.concatenate([grad_keys, grad_values], -1)
    pair_sum = lax.psum_scatter(
        grad_pair.astype(jnp.bfloat16), "expert", scatter_dimension=1, tiled=True
    ).astype(jnp.float32)
    pair_sum = pair_sum.astype(low_type).reshape(count, 2 * head)
    grad_query_sel = grad_query_sel.reshape(images, patches, picks, head)
    grad_queries_all = jnp.einsum("ipke,ipkh->ipeh", attend_hot, grad_query_sel, precision=HIGH)
    grad_queries_all = grad_queries_all.astype(low_type).reshape(count, experts * head)
    grad_logits_one = gates_one_back(grad_gates_one)[0].astype(low_type)
    per_image_one = jnp.einsum(
        "ipd,ipe->ide", shaped_one, grad_logits_one, preferred_element_type=f32
    )
    grad_attend_router = jnp.einsum("it,ide->tde", task_hot, per_image_one, precision=HIGH)
    grad_query = jnp.einsum("td,tc->dc", normed_one, grad_queries_all, preferred_element_type=f32)
    grad_key_value = jnp.einsum("td,tc->dc", normed_one, pair_sum, preferred_element_type=f32)
    grad_normed_one = jnp.einsum(
        "tc,dc->td", grad_queries_all, query_weight, preferred_element_type=f32
    )
    grad_normed_one = grad_normed_one + jnp.einsum(
        "tc,dc->td", pair_sum, key_value, preferred_element_type=f32
    )
    grad_normed_one = grad_normed_one + jnp.einsum(
        "ipe,ide->ipd", grad_logits_one, router_one, preferred_element_type=f32
    ).reshape(count, width)
    grad_inputs_norm, grad_gain_one, grad_bias_one = first_back(grad_normed_one)
    grad_tokens = (grad_middle + grad_inputs_norm).reshape(images, patches, width)
    grad_gain = jnp.stack([grad_gain_one, grad_gain_two])
    grad_bias = jnp.stack([grad_bias_one, grad_bias_two])
    feed_shaped = feed_hot.reshape(images, patches, picks, experts)
    usage = jnp.stack(
        [
            jnp.einsum("it,ipke->te", task_hot, attend_hot, precision=HIGH),
            jnp.einsum("it,ipke->te", task_hot, feed_shaped, precision=HIGH),
        ]
    )
    shared = lax.psum(
        (
            grad_query,
            grad_key_value,
            grad_output,
            grad_attend_router,
            grad_feed_router,
            grad_gain,
            grad_bias,
            usage,
        ),
        ("dp", "expert"),
    )
    grad_expand_sum, grad_reduce_sum = (
        lax.psum(grad_expand.astype(jnp.bfloat16), "dp").astype(jnp.float32),
        lax.psum(grad_reduce.astype(jnp.bfloat16), "dp").astype(jnp.float32),
    )
    grad_key_sum = shared[1][:, :head]
    grad_value_sum = shared[1][:, head:]
    return (
        output,
        grad_tokens,
        shared[5],
        shared[6][0],
        shared[6][1],
        shared[0],
        grad_key_sum,
        grad_value_sum,
        shared[2],
        shared[3],
        shared[4],
        grad_expand_sum,
        grad_reduce_sum,
        shared[7],
    )


def solution(mesh):
    placed = (
        P("dp", "expert", None),
        P("dp"),
        P("dp", "expert", None),
        P("dp", "expert", None, None),
        P(),
        P(),
        P(),
        P(),
        P(),
        P(),
        P(),
        P(),
        P("expert", None, None),
        P("expert", None, None),
        P("dp", "expert", None),
    )
    fast = mesh.shape["dp"] == 8 and mesh.shape["expert"] == 4
    return jax.shard_map(
        body_fast if fast else body,
        mesh=mesh,
        in_specs=placed,
        out_specs=(
            P("dp", "expert", None),
            P("dp", "expert", None),
            P(),
            P(),
            P(),
            P(),
            P(),
            P(),
            P(),
            P(),
            P(),
            P("expert", None, None),
            P("expert", None, None),
            P(),
        ),
        check_vma=False,
    )
```

```python
import types

import jax
import jax.numpy as jnp
from jax import lax
from jax.experimental import pallas as pl
from jax.experimental.pallas import tpu as pltpu
from jax.sharding import PartitionSpec as P

CAP = 256


EPS = 1e-06
HIGH = lax.Precision.HIGHEST
F32 = jnp.float32
LOW = jnp.bfloat16
MESH = pl.DeviceIdType.MESH
MIB = 2**20


def dot(a, b):
    return jnp.dot(a, b, preferred_element_type=F32)


def dot_nt(a, b):
    return lax.dot_general(a, b, (((1,), (1,)), ((), ())), preferred_element_type=F32)


def dot_tn(a, b):
    return lax.dot_general(a, b, (((0,), (0,)), ((), ())), preferred_element_type=F32)


def remote(src, dst, send, recv, device):
    return pltpu.make_async_remote_copy(
        src_ref=src, dst_ref=dst, send_sem=send, recv_sem=recv,
        device_id=device, device_id_type=MESH,
    )


def run_kernel(kernel, name, ins, outs, scratch, collective):
    names = [*ins, *outs, *scratch]

    def body(*refs):
        kernel(types.SimpleNamespace(**dict(zip(names, refs, strict=True))))

    made = pl.pallas_call(
        body,
        name=name,
        out_shape=[jax.ShapeDtypeStruct(shape, dtype) for shape, dtype, _ in outs.values()],
        in_specs=[pl.BlockSpec(memory_space=space) for _, space in ins.values()],
        out_specs=[pl.BlockSpec(memory_space=space) for _, _, space in outs.values()],
        scratch_shapes=list(scratch.values()),
        compiler_params=pltpu.CompilerParams(
            collective_id=collective, has_side_effects=True, vmem_limit_bytes=62 * MIB
        ),
    )(*[array for array, _ in ins.values()])
    return types.SimpleNamespace(**dict(zip(outs, made, strict=True)))


def center(value):
    mean = jnp.mean(value, -1, keepdims=True)
    centred = value - mean
    scale = lax.rsqrt(jnp.mean(centred * centred, -1, keepdims=True) + EPS)
    return centred * scale, scale


def center_back(grad, normal, scale, gain):
    inner = grad * gain
    mean = jnp.mean(inner, -1, keepdims=True)
    along = jnp.mean(inner * normal, -1, keepdims=True)
    return scale * (inner - mean - normal * along)


def head_maps(heads, head):
    row = lax.broadcasted_iota(jnp.int32, (heads * head, 2 * head), 0)
    row = lax.rem(row, head)
    col = lax.broadcasted_iota(jnp.int32, (heads * head, 2 * head), 1)
    low = jnp.where(row == col, 1.0, 0.0).astype(LOW)
    high = jnp.where(row + head == col, 1.0, 0.0).astype(LOW)
    return low, high


def masked_softmax(logits, chosen, axis):
    top = jnp.max(jnp.where(chosen, logits, -1e30), axis, keepdims=True)
    expo = jnp.where(chosen, jnp.exp(jnp.minimum(logits - top, 0.0)), 0.0)
    return expo / jnp.sum(expo, axis, keepdims=True)


PIECE = (160, 80, 96)
FIRST = (1024, 1344, 1504)
SPLIT = 640
BRANCH = 1024
HAND = 6
PER = 6


def gelu_parts(value):
    square = value * value
    inner = value * (0.7978845608028654 + 0.035677408136300125 * square)
    half = 0.5 + 0.5 * jnp.tanh(inner)
    act = value * half
    slope = half + act * (1.0 - half) * (1.5957691216057308 + 0.2140644488178007 * square)
    return act, slope


class Place:
    def __init__(self):
        self.dp = dp = lax.axis_index("dp")
        self.ex = lax.axis_index("expert")
        self.y = lax.rem(dp, 2)
        z = lax.div(dp, 2)
        self.is_end = (z == 0) | (z == 3)
        self.is_mid = (z == 1) | (z == 2)
        self.toward = (jnp.where(z < 2, dp + 2, dp - 2), self.ex)
        self.outer = (jnp.where(z == 1, dp - 2, jnp.where(z == 2, dp + 2, dp)), self.ex)
        self.core = lax.rem(self.ex, 2)
        self.spot = self.y * 2 + lax.div(self.ex, 2)

    def peer(self, r):
        return (self.dp ^ lax.div(r, 4), self.ex ^ lax.rem(r, 4))

    def plane(self, q):
        return (self.dp ^ lax.div(q, 2), self.ex ^ (2 * lax.rem(q, 2)))

    def group(self, r):
        return 2 * (self.ex ^ lax.rem(r, 4)) + (self.y ^ lax.div(r, 4))


def cot_copy(v, p, r):
    return remote(v.cot, v.ca.at[r], v.cs.at[r], v.cv.at[r], p.peer(r))


def cot_relay(v, p, to):
    at = pl.ds(0 if to == 2 else CAP // 2, CAP // 2)
    return remote(
        v.ca.at[6 - to, :, at, :], v.ca.at[6, :, at, :], v.cs.at[to + 1], v.cv.at[to + 8], p.peer(to)
    )


def cot_forward(v, p, r):
    return remote(v.ca.at[r], v.ca.at[r + 1], v.cs.at[r + 6], v.cv.at[r + 1], p.peer(1))


def row_copy(v, p, r, i):
    return remote(v.n2.at[i], v.xa.at[r, i], v.xs.at[r, i], v.xv.at[r, i], p.peer(r))


def row_relay(v, p, to, i):
    at = pl.ds(0 if to == 2 else CAP // 2, CAP // 2)
    return remote(
        v.xa.at[6 - to, i, at, :], v.xa.at[6, i, at, :],
        v.xs.at[to + 1, i], v.xv.at[to + 8, i], p.peer(to),
    )


def row_forward(v, p, r, i):
    return remote(
        v.xa.at[r, i], v.xa.at[r + 1, i], v.xs.at[r + 6, i], v.xv.at[r + 1, i], p.peer(1)
    )


def cot_near(v, p):
    for r in (4, 2):
        cot_copy(v, p, r).wait_recv()
        cot_relay(v, p, 6 - r).start()
        cot_forward(v, p, r).start()


def cot_far(v, p):
    cot_relay(v, p, 2).wait_recv()
    cot_relay(v, p, 4).wait_recv()
    cot_forward(v, p, 6).start()


def rows_near(v, p, i):
    for r in (4, 2):
        row_copy(v, p, r, i).wait_recv()
        row_relay(v, p, 6 - r, i).start()
        row_forward(v, p, r, i).start()


def rows_far(v, p, i):
    row_relay(v, p, 2, i).wait_recv()
    row_relay(v, p, 4, i).wait_recv()
    row_forward(v, p, 6, i).start()


def meta_copy(v, p, r):
    return remote(v.meta.at[p.group(r)], v.ma.at[r], v.ms.at[r], v.mv.at[r], p.peer(r))


def kv_copy(v, p, r):
    half = v.kv.shape[1] // 4
    return remote(
        v.kv.at[:, pl.ds(0, half), :], v.kv.at[:, pl.ds(r * half, half), :],
        v.ks.at[r], v.kr.at[r], p.peer(r),
    )


def kv_forward(v, p):
    half = v.kv.shape[1] // 4
    return remote(
        v.kv.at[:, pl.ds(2 * half, half), :], v.kv.at[:, pl.ds(3 * half, half), :],
        v.ks.at[3], v.kr.at[3], p.peer(1),
    )


def front(v, p):
    count, d = v.tok.shape
    half = count // 2
    heads = v.heads.shape[1]
    head = v.kv.shape[2] // 2
    picks = v.pick.shape[1]
    for i in range(2):
        named = jnp.concatenate([v.pick[i].astype(F32), jnp.zeros((8 - picks, half), F32)], 0)
        v.pickc[i] = named.T
    gain = v.gain[...]
    bias = v.bias[...]
    v.wkv[0:head, :] = v.wk[...]
    v.wkv[head:2 * head, :] = v.wv[...]
    for i in range(2):
        rows = slice(i * half, (i + 1) * half)
        normal, _ = center(v.tok[rows, :].astype(F32))
        normed = (normal * gain[0:1] + bias[0:1]).astype(LOW)
        v.n1[rows, :] = normed
        v.kv[i, 0:half, :] = dot_nt(normed, v.wkv[...]).astype(LOW)
    pl.semaphore_wait(v.barrier, jnp.where(p.is_mid, 9, 8))
    for r in (2, 1):
        kv_copy(v, p, r).start()
    for r in (4, 2, 1):
        cot_copy(v, p, r).start()
    v.ca[0] = v.cot[...]
    v.gh[0:count, 0:heads] = dot_nt(v.n1[...], v.wq[...]).astype(LOW)

    experts = v.router1.shape[1]
    number = lax.broadcasted_iota(jnp.int32, (16, count), 0)
    chosen = number == v.pickt[0:1, :]
    for k in range(1, picks):
        chosen = chosen | (number == v.pickt[k:k + 1, :])
    earlier = lax.broadcasted_iota(jnp.int32, (count, count), 0) < lax.broadcasted_iota(
        jnp.int32, (count, count), 1
    )
    before = dot(jnp.where(chosen, 1.0, 0.0).astype(LOW), jnp.where(earlier, 1.0, 0.0).astype(LOW))
    rank = jnp.where(chosen, before, -1.0)

    to_query, to_value = head_maps(heads // head, head)
    owner = lax.div(lax.broadcasted_iota(jnp.int32, (half, heads), 1), head).astype(F32)
    lane = lax.broadcasted_iota(jnp.int32, (half, experts), 1).astype(F32)
    wide = lax.broadcasted_iota(jnp.int32, (half, 2 * head), 1)
    kv_copy(v, p, 2).wait_recv()
    kv_forward(v, p).start()
    kv_copy(v, p, 1).wait_recv()
    kv_forward(v, p).wait_recv()

    for i in range(2):
        rows = slice(i * half, (i + 1) * half)
        logits = dot_nt(v.n1[rows, :], v.router1[v.task[i]])
        named = [lane == v.pickc[i, :, k:k + 1] for k in range(picks)]
        allowed = named[0]
        for k in range(1, picks):
            allowed = allowed | named[k]
        gates = masked_softmax(logits, allowed, 1)
        v.g1[rows, :] = gates
        kv = v.kv[i]
        for k in range(picks):
            at = picks * i + k
            if i == 1 and k == 2:
                cot_far(v, p)
                rows_near(v, p, 0)
            mine = owner == v.pickc[i, :, k:k + 1]
            gate = jnp.sum(jnp.where(named[k], gates, 0.0), 1, keepdims=True)
            all_queries = v.gh[rows, 0:heads]
            query = dot(jnp.where(mine, all_queries, jnp.zeros_like(all_queries)), to_query)
            query = (query * head ** -0.5).astype(LOW)
            v.q8[at] = query
            scores = dot_nt(query, kv)
            expo = jnp.exp(scores - jnp.max(scores, 1, keepdims=True))
            total = jnp.sum(expo, 1, keepdims=True)
            low = expo.astype(LOW)
            v.act[at * half:(at + 1) * half, 0:4 * half] = low
            attended = dot(low, kv) / total
            v.att[at] = jnp.where(wide == 0, total, attended)
            spread = dot_nt((gate * attended).astype(LOW), to_value).astype(LOW)
            if k == 0:
                v.heads[rows, :] = jnp.where(mine, spread, jnp.zeros_like(spread))
            else:
                v.heads[rows, :] = jnp.where(mine, spread, v.heads[rows, :])
        middle = v.tok[rows, :].astype(F32) + dot(v.heads[rows, :], v.wo[...])
        v.mid[rows, :] = middle
        normal, _ = center(middle)
        normed = (normal * gain[1:2] + bias[1:2]).astype(LOW)
        v.n2[i] = normed
        for r in (4, 2, 1):
            row_copy(v, p, r, i).start()
        v.xa[0, i] = normed
        logits = dot_nt(v.router2[v.task[i]], normed)
        logits = jnp.concatenate([logits, jnp.zeros((16 - experts, half), F32)], 0)
        gates = masked_softmax(logits, rank[:, rows] >= 0.0, 0)
        v.g2[:, rows] = gates
        for g in range(8):
            v.meta[g, 0:2, rows] = rank[2 * g:2 * g + 2, rows]
            v.meta[g, 2:4, rows] = gates[2 * g:2 * g + 2, :]
            v.meta[g, 4:16, rows] = jnp.zeros((12, half), F32)
        if i == 0:
            cot_near(v, p)
    v.ma[0] = v.meta[p.group(0)]
    for r in range(1, 8):
        meta_copy(v, p, r).start()


def chunk_first(v, p, c):
    return remote(v.ra.at[c], v.rb.at[c], v.s1s.at[c], v.s1r.at[c], p.toward)


def chunk_middle(v, p, c):
    return remote(v.rb.at[c], v.rc.at[c], v.s2s.at[c], v.s2r.at[c], p.toward)


def chunk_back(v, p, c):
    return remote(v.ra.at[c], v.rc.at[c], v.s3s.at[c], v.s2r.at[c], p.outer)


def chunk_pair(v, p, src, c):
    to = p.y * v.ra.shape[0] + c
    return remote(src.at[c], v.chunks.at[to], v.ys.at[c], v.yr.at[c], (p.dp ^ 1, p.ex))


def chunk_cross(v, p, c, device):
    at = v.chunks.at[(1 - p.y) * v.ra.shape[0] + c]
    return remote(at, at, v.y2s.at[c], v.yr.at[c], device)


def chunk_land(v, p, c):
    at = v.chunks.at[(1 - p.y) * v.ra.shape[0] + c]
    return remote(v.ra.at[c], at, v.ys.at[c], v.yr.at[c], (p.dp ^ 1, p.ex))


def only_mid(c):
    return lax.rem(c, 6) == 2


def only_end(c):
    return lax.rem(c, 6) == 5


def chunk_own(v, p, src, c):
    to = p.y * v.ra.shape[0] + c
    return pltpu.make_async_copy(src.at[c], v.chunks.at[to], v.ls.at[c])


def tick(v, p, t):
    chunks = v.ra.shape[0]

    @pl.when(p.is_mid & (t < chunks))
    def _():
        c = jnp.minimum(t, chunks - 1)
        chunk_first(v, p, c).wait_recv()
        v.rb[c] = (v.ra[c].astype(F32) + v.rb[c].astype(F32)).astype(LOW)
        chunk_middle(v, p, c).start()

    @pl.when(p.is_mid & (t >= 2) & (t < chunks + 2))
    def _():
        c = jnp.maximum(t - 2, 0)
        chunk_middle(v, p, c).wait_recv()
        v.ra[c] = (v.rb[c].astype(F32) + v.rc[c].astype(F32)).astype(LOW)
        chunk_back(v, p, c).start()

        @pl.when(jnp.logical_not(only_end(c)))
        def _():
            chunk_pair(v, p, v.ra, c).start()

        chunk_own(v, p, v.ra, c).start()

    @pl.when(p.is_end & (t >= 4) & (t < chunks + 4))
    def _():
        c = jnp.maximum(t - 4, 0)
        chunk_middle(v, p, c).wait_recv()

        @pl.when(jnp.logical_not(only_mid(c)))
        def _():
            chunk_pair(v, p, v.rc, c).start()

        chunk_own(v, p, v.rc, c).start()

    @pl.when((t >= HAND) & (t < chunks + HAND))
    def _():
        c = jnp.maximum(t - HAND, 0)

        @pl.when(p.is_mid & only_mid(c))
        def _():
            chunk_land(v, p, c).wait_recv()
            chunk_cross(v, p, c, p.outer).start()

        @pl.when(p.is_end & only_end(c))
        def _():
            chunk_land(v, p, c).wait_recv()
            chunk_cross(v, p, c, p.toward).start()


def ticks(v, p, first, after):
    def one(t, carry):
        tick(v, p, t)
        return carry

    lax.fori_loop(first, after, one, 0)


def chunks_done(v, p):
    chunks = v.ra.shape[0]

    def one(c, carry):
        @pl.when(p.is_end)
        def _():
            chunk_first(v, p, c).wait_send()

            @pl.when(jnp.logical_not(only_mid(c)))
            def _():
                chunk_pair(v, p, v.rc, c).wait_send()

            chunk_own(v, p, v.rc, c).wait()

            @pl.when(only_end(c))
            def _():
                chunk_cross(v, p, c, p.toward).wait_send()

            @pl.when(jnp.logical_not(only_end(c)))
            def _():
                chunk_land(v, p, c).wait_recv()

        @pl.when(p.is_mid)
        def _():
            chunk_middle(v, p, c).wait_send()
            chunk_back(v, p, c).wait_send()

            @pl.when(jnp.logical_not(only_end(c)))
            def _():
                chunk_pair(v, p, v.ra, c).wait_send()

            chunk_own(v, p, v.ra, c).wait()

            @pl.when(only_mid(c))
            def _():
                chunk_cross(v, p, c, p.outer).wait_send()

            @pl.when(jnp.logical_not(only_mid(c)))
            def _():
                chunk_land(v, p, c).wait_recv()

        return carry

    lax.fori_loop(0, chunks, one, 0)


def weight_loads(v, p, j):
    return (
        pltpu.make_async_copy(v.we_all.at[p.y * 2 + j], v.we, v.wsem.at[0]),
        pltpu.make_async_copy(v.wr_all.at[p.y * 2 + j], v.wr, v.wsem.at[1]),
    )


def source_rows(r):
    return pl.ds(pl.multiple_of(r * CAP, CAP), CAP)


def slot_hits(v, r, j):
    sub = lax.broadcasted_iota(jnp.int32, (CAP, 2 * CAP), 0).astype(F32)
    return sub == v.ma[r, j:j + 1, :]


def dispatch(v, r, j):
    d = v.xa.shape[3]
    hit = slot_hits(v, r, j)
    pick = jnp.where(hit, 1.0, 0.0).astype(LOW)
    gate = jnp.sum(jnp.where(hit, v.ma[r, j + 2:j + 3, :], 0.0), 1, keepdims=True)
    at = source_rows(r)
    rows = dot(pick, v.xa[r].reshape(2 * CAP, d))
    v.pr[j, at, :] = rows.astype(LOW)
    v.xrt[:, at] = rows.T.astype(LOW)
    rows = gate * dot(pick, v.ca[r].reshape(2 * CAP, d))
    v.gr[j, at, :] = rows.astype(LOW)
    v.gpt[:, at] = rows.T.astype(LOW)


def columns(v, j, f):
    cols = pl.ds(pl.multiple_of(f * 256, 256), 256)
    step = 512
    for b in range(v.act.shape[0] // step):
        rows = slice(b * step, (b + 1) * step)
        value, slope = gelu_parts(dot(v.pr[j, rows, :], v.we[:, cols]))
        v.act[rows, cols] = value.astype(LOW)
        v.gh[rows, cols] = (dot_nt(v.gr[j, rows, :], v.wr[cols, :]) * slope).astype(LOW)


def weight_grads(v, p, j, f):
    cols = pl.ds(pl.multiple_of(f * 256, 256), 256)
    first = j * (v.ra.shape[0] // 2) + 2 * f
    v.ra[first] = dot(v.gpt[...], v.act[:, cols]).astype(LOW)
    v.ra[first + 1] = dot(v.xrt[...], v.gh[:, cols]).astype(LOW)

    @pl.when(p.is_end)
    def _():
        chunk_first(v, p, first).start()
        chunk_first(v, p, first + 1).start()


def produce(v, n, j):
    size = v.act.shape[0] // 2
    at = pl.ds(pl.multiple_of(n * size, size), size)
    v.pr[j, at, :] = dot(v.act[at, :], v.wr[...]).astype(LOW)
    v.gr[j, at, :] = dot_nt(v.gh[at, :], v.we[...]).astype(LOW)

    def gates(m, carry):
        r = n * (size // CAP) + m
        made = v.pr[j, source_rows(r), :].astype(F32)
        hit = slot_hits(v, r, j)
        pick = jnp.where(hit, 1.0, 0.0).astype(LOW)
        seen = dot(pick, v.ca[r].reshape(2 * CAP, made.shape[1]))
        inner = jnp.sum(made * seen, 1, keepdims=True)
        part = jnp.sum(jnp.where(hit, inner, 0.0), 0, keepdims=True)
        v.dgs[r, j] = jnp.broadcast_to(part, (8, 2 * CAP))
        return carry

    lax.fori_loop(0, size // CAP, gates, 0)


def gate_copy(v, p, r):
    return remote(v.dgs.at[r], v.dg.at[p.group(0)], v.gs.at[r], v.gv.at[r], p.peer(r))


def part_core(v, p, r, which):
    ref = (v.gr, v.pr)[which]
    at = 4 * which + lax.div(r, 2)
    return remote(ref.at[:, source_rows(r), :], v.xa.at[at], v.k1s.at[at], v.k1r.at[at], p.peer(1))


def part_x(v, p, r, which, i):
    ref = (v.gr, v.pr)[which]
    at = 4 * which + r // 2 - 1
    return remote(
        ref.at[i, source_rows(r), :], v.ca.at[at, i], v.k2s.at[at, i], v.k2r.at[at, i], p.peer(2)
    )


def part_y(v, p, which, i):
    ref = (v.gr, v.pr)[which]
    at = 4 * which + 1
    return remote(
        ref.at[i, source_rows(4), :], v.ca.at[at, i], v.k2s.at[at, i], v.k2r.at[at, i], p.peer(4)
    )


def combine(v, r, which):
    lane = lax.broadcasted_iota(jnp.int32, (2 * CAP, CAP), 1).astype(F32)
    meta = v.ma[r].T
    at = source_rows(r)
    ref = (v.gr, v.pr)[which]
    total = jnp.zeros((2 * CAP, ref.shape[2]), F32)
    for j in range(2):
        hit = lane == meta[:, j:j + 1]
        weight = 1.0 if which == 0 else meta[:, 2 + j:3 + j]
        total = total + dot(jnp.where(hit, weight, 0.0).astype(LOW), ref[j, at, :])
    ref[0, at, :] = total[:CAP].astype(LOW)
    ref[1, at, :] = total[CAP:].astype(LOW)


def send_parts(v, p, which):
    def odd(n, carry):
        r = 7 - 2 * n
        combine(v, r, which)
        part_core(v, p, r, which).start()
        return carry

    lax.fori_loop(0, 4, odd, 0)

    def even(n, carry):
        r = jnp.where(n < 2, 6 - 4 * n, 12 - 4 * n)
        combine(v, r, which)
        part_core(v, p, r, which).wait_recv()
        ref = (v.gr, v.pr)[which]
        at = source_rows(r)
        ref[:, at, :] = (
            ref[:, at, :].astype(F32) + v.xa[4 * which + lax.div(r, 2)].astype(F32)
        ).astype(LOW)
        return carry

    lax.fori_loop(0, 2, even, 0)
    if which == 0:
        for i in range(2):
            for r in (6, 2):
                part_x(v, p, r, which, i).start()
    lax.fori_loop(2, 4, even, 0)


def relay_parts(v, p, which, i):
    ref = (v.gr, v.pr)[which]
    part_x(v, p, 6, which, i).wait_recv()
    at = source_rows(4)
    ref[i, at, :] = (ref[i, at, :].astype(F32) + v.ca[4 * which + 2, i].astype(F32)).astype(LOW)
    part_y(v, p, which, i).start()
    part_x(v, p, 2, which, i).wait_recv()


def own_sum(v, i, which):
    ref = (v.gr, v.pr)[which]
    total = ref[i, 0:CAP, :].astype(F32) + v.ca[4 * which, i].astype(F32)
    return total + v.ca[4 * which + 1, i].astype(F32)


def piece(v, g, c, q):
    at = FIRST[g] + c * PIECE[g]
    return v.act.at[
        pl.ds(pl.multiple_of(at, 16), PIECE[g]), pl.ds(pl.multiple_of(q * 384, 128), 384)
    ]


def spans(g, start, count):
    while count > 0:
        n, row = divmod(start, PIECE[g])
        size = min(count, PIECE[g] - row)
        yield n, row, size
        start, count = start + size, count - size


def place_rows(v, g, start, value):
    d = value.shape[1]
    done = 0
    for n, row, size in spans(g, start, value.shape[0]):
        at = FIRST[g] + (n // 4) * PIECE[g] + row
        q = n % 4
        v.act[at:at + size, q * d:(q + 1) * d] = value[done:done + size].astype(LOW)
        done += size


def place_tasks(v, g, start, per_image):
    experts, d = per_image[0].shape
    for j in range(v.router1.shape[0]):
        mine = [jnp.where(v.task[i] == j, per_image[i], 0.0) for i in range(2)]
        total = mine[0] + mine[1]
        if experts < 16:
            total = jnp.concatenate([total, jnp.zeros((16 - experts, d), F32)], 0)
        place_rows(v, g, start + 16 * j, total)


def back_first(v, i):
    count, d = v.tok.shape
    half = count // 2
    heads = v.heads.shape[1]
    experts = v.router2.shape[1]
    rows = slice(i * half, (i + 1) * half)
    grad_gates = jnp.concatenate([v.dg[g, j, 0:1, rows] for g in range(8) for j in range(2)], 0)
    gates = v.g2[:, rows]
    grad_logits = gates * (grad_gates - jnp.sum(gates * grad_gates, 0, keepdims=True))
    grad_logits = grad_logits[0:experts].astype(LOW)
    gain = v.gain[1:2]
    grad = own_sum(v, i, 0) + dot_tn(grad_logits, v.router2[v.task[i]])
    normal, scale = center(v.mid[rows, :])
    grad_gain = jnp.sum(grad * normal, 0, keepdims=True)
    grad_bias = jnp.sum(grad, 0, keepdims=True)
    if i == 0:
        v.small[0, 1:2, :] = grad_gain
        v.small[0, 3:4, :] = grad_bias
    else:
        v.small[0, 1:2, :] = v.small[0, 1:2, :] + grad_gain
        v.small[0, 3:4, :] = v.small[0, 3:4, :] + grad_bias
    total = v.cot[i].astype(F32) + center_back(grad, normal, scale, gain)
    v.gtok[rows, :] = total
    low = total.astype(LOW)
    v.act[rows, BRANCH:BRANCH + d] = low
    v.act[rows, 0:heads] = dot_nt(low, v.wo[...]).astype(LOW)
    return dot(grad_logits, v.n2[i])


def back_middle(v, per_image):
    count, d = v.tok.shape
    place_rows(v, 0, 0, dot_tn(v.heads[...], v.act[0:count, BRANCH:BRANCH + d]))
    place_tasks(v, 0, v.heads.shape[1], per_image)


def back_attention(v, i, pause):
    count, d = v.tok.shape
    half = count // 2
    heads = v.heads.shape[1]
    head = v.kv.shape[2] // 2
    picks = v.pick.shape[1]
    experts = v.router1.shape[1]
    to_query, to_value = head_maps(heads // head, head)
    owner = lax.div(lax.broadcasted_iota(jnp.int32, (half, heads), 1), head).astype(F32)
    lane = lax.broadcasted_iota(jnp.int32, (half, experts), 1).astype(F32)
    rows = slice(i * half, (i + 1) * half)
    lower = slice(count + i * half, count + (i + 1) * half)
    kv = v.kv[i]
    gates = v.g1[rows, :]
    grad_gates = jnp.zeros((half, experts), F32)
    grad_pair = jnp.zeros((2 * head, 4 * half), F32)
    for k in range(picks):
        at = picks * i + k
        mine = owner == v.pickc[i, :, k:k + 1]
        named = lane == v.pickc[i, :, k:k + 1]
        gate = jnp.sum(jnp.where(named, gates, 0.0), 1, keepdims=True)
        grad_heads = v.act[rows, 0:heads]
        grad = dot(jnp.where(mine, grad_heads, jnp.zeros_like(grad_heads)), to_value)
        attended = v.att[at]
        total = attended[:, 0:1]
        grad_gates = grad_gates + jnp.where(named, jnp.sum(grad * attended, 1, keepdims=True), 0.0)
        grad = ((gate * grad).astype(LOW).astype(F32) / total).astype(LOW)
        inner = jnp.sum(grad.astype(F32) * attended, 1, keepdims=True)
        expo = v.gh[at * half:(at + 1) * half, 0:4 * half]
        grad_scores = (expo.astype(F32) * (dot_nt(grad, kv) - inner)).astype(LOW)
        grad_query = (dot(grad_scores, kv) * head ** -0.5).astype(LOW)
        spread = dot_nt(grad_query, to_query).astype(LOW)
        if k == 0:
            v.act[lower, 0:heads] = jnp.where(mine, spread, jnp.zeros_like(spread))
        else:
            v.act[lower, 0:heads] = jnp.where(mine, spread, v.act[lower, 0:heads])
        grad_pair = grad_pair + dot(v.q8[at].astype(F32).T.astype(LOW), grad_scores)
        grad_pair = grad_pair + dot(grad.astype(F32).T.astype(LOW), expo)
        pause(i, k)
    grad_logits = gates * (grad_gates - jnp.sum(gates * grad_gates, 1, keepdims=True))
    v.gl1[rows, :] = grad_logits.astype(LOW)
    for r in range(4):
        v.dkv[r, i] = grad_pair[:, r * half:(r + 1) * half].astype(LOW)


def pair_copy(v, p, r, i):
    return remote(v.dkv.at[r, i], v.din.at[r, i], v.ps.at[r, i], v.pr_sem.at[r, i], p.peer(r))


def pair_sum(v, i):
    pair = v.dkv[0, i].astype(F32)
    for r in (1, 2, 3):
        pair = pair + v.din[r, i].astype(F32)
    return pair


def back_query(v):
    count, d = v.tok.shape
    half = count // 2
    heads = v.heads.shape[1]
    width = v.kv.shape[2]
    grad = dot_tn(v.act[count:2 * count, 0:heads], v.n1[...])
    place_rows(v, 1, 0, grad[0:SPLIT])
    place_rows(v, 2, 0, grad[SPLIT:heads])
    rows = (slice(0, half), slice(half, count))
    per_image = [dot_tn(v.gl1[at, :], v.n1[at, :]) for at in rows]
    place_tasks(v, 2, heads - SPLIT + width, per_image)


def back_pair(v):
    count, d = v.tok.shape
    half = count // 2
    grad = dot(pair_sum(v, 0).astype(LOW), v.n1[0:half, :])
    grad = grad + dot(pair_sum(v, 1).astype(LOW), v.n1[half:count, :])
    place_rows(v, 2, v.heads.shape[1] - SPLIT, grad)


def back_last(v):
    count, d = v.tok.shape
    half = count // 2
    heads = v.heads.shape[1]
    gain = v.gain[0:1]
    grad_gain = jnp.zeros((1, d), F32)
    grad_bias = jnp.zeros((1, d), F32)
    for i in range(2):
        rows = slice(i * half, (i + 1) * half)
        lower = slice(count + i * half, count + (i + 1) * half)
        grad = dot(v.act[lower, 0:heads], v.wq[...])
        grad = grad + dot(pair_sum(v, i).T.astype(LOW), v.wkv[...])
        grad = grad + dot(v.gl1[rows, :], v.router1[v.task[i]])
        normal, scale = center(v.tok[rows, :].astype(F32))
        grad_gain = grad_gain + jnp.sum(grad * normal, 0, keepdims=True)
        grad_bias = grad_bias + jnp.sum(grad, 0, keepdims=True)
        v.gtok[rows, :] = v.gtok[rows, :] + center_back(grad, normal, scale, gain)
    v.small[0, 0:1, :] = grad_gain
    v.small[0, 2:3, :] = grad_bias


def count_usage(v):
    count, d = v.tok.shape
    half = count // 2
    picks = v.pick.shape[1]
    number = lax.broadcasted_iota(jnp.int32, (16, half), 0)
    task = lax.broadcasted_iota(jnp.int32, (16, 128), 1)
    v.small[0] = jnp.zeros_like(v.small[0])
    for which in range(2):
        table = jnp.zeros((16, 128), F32)
        for i in range(2):
            named = jnp.zeros((16, half), F32)
            for k in range(picks):
                if which == 0:
                    row = v.pick[i, k:k + 1, :]
                else:
                    row = v.pickt[k:k + 1, i * half:(i + 1) * half]
                named = named + jnp.where(number == row, 1.0, 0.0)
            table = table + jnp.where(task == v.task[i], jnp.sum(named, 1, keepdims=True), 0.0)
        v.small[0, 8 + 16 * which:24 + 16 * which, 0:128] = table


class Shared:
    def __init__(self, v, p, g):
        self.v, self.p, self.g = v, p, g
        core, mine = p.core, p.spot
        half_in, piece_in, zbuf, shared = v.half_in[g], v.piece_in[g], v.zbuf[g], v.shared[g]
        self.half_in, self.piece_in = half_in, piece_in

        def half(c):
            return v.act.at[pl.ds(pl.multiple_of(FIRST[g] + c * PIECE[g], 16), PIECE[g]), :]

        partner = p.peer(1)
        s, r = v.hs.at[g], v.hr.at[g]
        self.own_half = half(core)
        self.first = remote(half(1 - core), half_in, s.at[0], r.at[0], partner)
        self.scatter = [
            remote(piece(v, g, core, mine ^ q), piece_in.at[q - 1], s.at[q], r.at[q], p.plane(q))
            for q in (1, 2, 3)
        ]
        self.own = piece(v, g, core, mine)
        zown, zb, zc, zall = (zbuf.at[n] for n in range(4))
        self.z = (zown, zb, zc, zall)
        self.in_end = remote(zown, zb, s.at[4], r.at[4], p.toward)
        self.mid = remote(zb, zc, s.at[4], r.at[5], p.toward)
        self.out_mid = remote(zall, zall, s.at[5], r.at[6], p.outer)
        place = core * 4 + mine
        self.own_copy = pltpu.make_async_copy(zall, shared.at[place], v.osem.at[2 + g])
        self.gather = [
            remote(zall, shared.at[place], s.at[5 + q], r.at[6 + q], p.plane(q))
            for q in (1, 2, 3)
        ]
        self.arrive = [
            remote(zall, shared.at[core * 4 + (mine ^ q)], s.at[5 + q], r.at[6 + q], p.plane(q))
            for q in (1, 2, 3)
        ]
        ours = shared.at[pl.ds(core * 4, 4)]
        theirs = shared.at[pl.ds((1 - core) * 4, 4)]
        self.last = remote(ours, ours, s.at[9], r.at[10], partner)
        self.last_in = remote(theirs, theirs, s.at[9], r.at[10], partner)

    def stage(self, n):
        v, p, g = self.v, self.p, self.g
        zown, zb, zc, zall = self.z
        if n == 0:
            self.first.start()
        if n == 1:
            self.first.wait_recv()
            own = self.own_half
            own[...] = (own[...].astype(F32) + self.half_in[...].astype(F32)).astype(LOW)
            for copy in self.scatter:
                copy.start()
        if n == 2:
            for copy in self.scatter:
                copy.wait_recv()
            total = self.own[...].astype(F32)
            for q in (1, 2, 3):
                total = total + self.piece_in[q - 1].astype(F32)
            zown[...] = total.astype(LOW)

            @pl.when(p.is_end)
            def _():
                self.in_end.start()

        if n == 3:
            @pl.when(p.is_mid)
            def _():
                self.in_end.wait_recv()
                zb[...] = (zown[...].astype(F32) + zb[...].astype(F32)).astype(LOW)
                self.mid.start()

        if n == 4:
            @pl.when(p.is_mid)
            def _():
                self.mid.wait_recv()
                zall[...] = (zb[...].astype(F32) + zc[...].astype(F32)).astype(LOW)
                self.out_mid.start()

        if n == 5:
            @pl.when(p.is_end)
            def _():
                self.out_mid.wait_recv()

            self.own_copy.start()
            for copy in self.gather:
                copy.start()
        if n == 6:
            self.own_copy.wait()
            for copy in self.arrive:
                copy.wait_recv()
            self.last.start()
        if n == 7:
            self.last_in.wait_recv()
            for copy in [self.first, self.last, *self.scatter, *self.gather]:
                copy.wait_send()

            @pl.when(p.is_end)
            def _():
                self.in_end.wait_send()

            @pl.when(p.is_mid)
            def _():
                self.mid.wait_send()
                self.out_mid.wait_send()


class Small:
    def __init__(self, v, p):
        self.v, self.p = v, p

        def exchange(n, device):
            return remote(v.small.at[n], v.small_in.at[n], v.ss.at[n], v.sr.at[n], device)

        self.around = [exchange(0, p.peer(1)), exchange(1, p.plane(1)), exchange(2, p.plane(2))]
        self.in_end = exchange(3, p.toward)
        self.mid = exchange(4, p.toward)
        self.out_mid = remote(v.stats, v.stats, v.ss.at[5], v.sr.at[5], p.outer)

    def stage(self, n):
        v, p = self.v, self.p
        if n == 0:
            self.around[0].start()
        if n in (1, 2, 3):
            self.around[n - 1].wait_recv()
            v.small[n] = v.small[n - 1] + v.small_in[n - 1]
            if n < 3:
                self.around[n].start()
            else:
                @pl.when(p.is_end)
                def _():
                    self.in_end.start()

        if n == 4:
            @pl.when(p.is_mid)
            def _():
                self.in_end.wait_recv()
                v.small[4] = v.small[3] + v.small_in[3]
                self.mid.start()

        if n == 5:
            @pl.when(p.is_mid)
            def _():
                self.mid.wait_recv()
                v.stats[...] = v.small[4] + v.small_in[4]
                self.out_mid.start()

        if n == 6:
            @pl.when(p.is_end)
            def _():
                self.out_mid.wait_recv()
                self.in_end.wait_send()

            @pl.when(p.is_mid)
            def _():
                self.mid.wait_send()
                self.out_mid.wait_send()

            for copy in self.around:
                copy.wait_send()


def layer_kernel(v):
    p = Place()
    v.half_in = (v.half_in0, v.half_in1, v.half_in2)
    v.piece_in = (v.piece_in0, v.piece_in1, v.piece_in2)
    v.zbuf = (v.zbuf0, v.zbuf1, v.zbuf2)
    v.shared = (v.shared0, v.shared1, v.shared2)
    v.barrier = pltpu.get_barrier_semaphore()
    for r in range(1, 8):
        pl.semaphore_signal(v.barrier, 1, device_id=p.peer(r), device_id_type=MESH)
    pl.semaphore_signal(v.barrier, 1, device_id=p.toward, device_id_type=MESH)

    @pl.when(p.is_mid)
    def _():
        pl.semaphore_signal(v.barrier, 1, device_id=p.outer, device_id_type=MESH)

    for load in weight_loads(v, p, 0):
        load.start()
    front(v, p)

    spill = pltpu.make_async_copy(v.act.at[:, pl.ds(0, v.expo.shape[1])], v.expo, v.osem.at[1])
    spill.start()
    rows_far(v, p, 0)
    row_copy(v, p, 1, 0).wait_recv()
    row_copy(v, p, 1, 1).wait_recv()
    cot_copy(v, p, 1).wait_recv()
    meta_copy(v, p, 1).wait_recv()
    dispatch(v, 0, 0)
    dispatch(v, 1, 0)
    rows_near(v, p, 1)
    for load in weight_loads(v, p, 0):
        load.wait()
    for r in (2, 4):
        meta_copy(v, p, r).wait_recv()
        dispatch(v, r, 0)
    for r in (3, 5):
        for i in range(2):
            row_forward(v, p, r - 1, i).wait_recv()
        cot_forward(v, p, r - 1).wait_recv()
        meta_copy(v, p, r).wait_recv()
        dispatch(v, r, 0)
    rows_far(v, p, 1)
    meta_copy(v, p, 6).wait_recv()
    dispatch(v, 6, 0)
    for i in range(2):
        row_forward(v, p, 6, i).wait_recv()
    cot_forward(v, p, 6).wait_recv()
    meta_copy(v, p, 7).wait_recv()
    dispatch(v, 7, 0)
    spill.wait()

    def first_columns(f, carry):
        columns(v, 0, f)
        weight_grads(v, p, 0, f)

        return carry

    lax.fori_loop(0, 6, first_columns, 0)
    tick(v, p, 0)

    def first_produce(n, carry):
        produce(v, n, 0)
        tick(v, p, 1 + n)
        return carry

    lax.fori_loop(0, 2, first_produce, 0)
    for load in weight_loads(v, p, 1):
        load.start()

    def second_dispatch(r, carry):
        dispatch(v, r, 1)
        return carry

    lax.fori_loop(0, 8, second_dispatch, 0)
    tick(v, p, 3)
    for i in range(2):
        for r in (1, 2, 4):
            row_copy(v, p, r, i).wait_send()
        for r in (2, 4):
            row_relay(v, p, r, i).wait_send()
        for r in (2, 4, 6):
            row_forward(v, p, r, i).wait_send()
    pl.semaphore_signal(v.free_core, 1, device_id=p.peer(1), device_id_type=MESH)
    for load in weight_loads(v, p, 1):
        load.wait()

    def second_columns(f, carry):
        columns(v, 1, f)

        @pl.when(lax.rem(f, 2) == 1)
        def _():
            tick(v, p, 4 + lax.div(f, 2))

        return carry

    lax.fori_loop(0, 6, second_columns, 0)

    def second_produce(n, carry):
        produce(v, n, 1)
        tick(v, p, 7 + n)
        return carry

    lax.fori_loop(0, 2, second_produce, 0)
    for r in range(1, 8):
        gate_copy(v, p, r).start()
    v.dg[p.group(0)] = v.dgs[0]
    for r in (1, 2, 4):
        cot_copy(v, p, r).wait_send()
    for r in (2, 4):
        cot_relay(v, p, r).wait_send()
    for r in (2, 4, 6):
        cot_forward(v, p, r).wait_send()
    for q in (1, 2):
        pl.semaphore_signal(v.free_plane, 1, device_id=p.plane(q), device_id_type=MESH)
    pl.semaphore_wait(v.free_core, 1)
    pl.semaphore_wait(v.free_plane, 2)
    send_parts(v, p, 0)
    tick(v, p, 9)

    def second_grads(f, carry):
        weight_grads(v, p, 1, f)
        return carry

    lax.fori_loop(0, 6, second_grads, 0)
    refill = pltpu.make_async_copy(v.expo, v.gh.at[:, pl.ds(0, v.expo.shape[1])], v.osem.at[1])
    refill.start()
    relay_parts(v, p, 0, 0)
    tick(v, p, 10)
    send_parts(v, p, 1)
    tick(v, p, 11)
    count_usage(v)
    v.act[FIRST[0]:FIRST[2] + 2 * PIECE[2], :] = jnp.zeros(
        (2 * sum(PIECE), v.act.shape[1]), LOW
    )
    for r in range(1, 8):
        gate_copy(v, p, r).wait_recv()
    part_y(v, p, 0, 0).wait_recv()
    per_image = [back_first(v, 0)]
    relay_parts(v, p, 0, 1)
    for i in range(2):
        for r in (6, 2):
            part_x(v, p, r, 1, i).start()
    tick(v, p, 12)
    refill.wait()
    early, late, rest = Shared(v, p, 0), Shared(v, p, 1), Shared(v, p, 2)
    small = Small(v, p)

    def pause(i, k):
        at = 4 * i + k
        if at == 1:
            tick(v, p, 13)
        if at == 3:
            tick(v, p, 14)
        if at == 5:
            early.stage(1)
            tick(v, p, 17)
        if at == 7:
            early.stage(2)
            tick(v, p, 18)

    back_attention(v, 0, pause)
    for r in (1, 2, 3):
        pair_copy(v, p, r, 0).start()
    part_y(v, p, 0, 1).wait_recv()
    per_image.append(back_first(v, 1))
    tick(v, p, 15)
    back_middle(v, per_image)
    early.stage(0)
    relay_parts(v, p, 1, 0)
    relay_parts(v, p, 1, 1)
    tick(v, p, 16)
    back_attention(v, 1, pause)
    for r in (1, 2, 3):
        pair_copy(v, p, r, 1).start()
    back_query(v)
    late.stage(0)
    early.stage(3)
    for i in range(2):
        part_y(v, p, 1, i).wait_recv()
        rows = slice(i * CAP, (i + 1) * CAP)
        v.out[rows, :] = (v.mid[rows, :] + own_sum(v, i, 1)).astype(LOW)
    late.stage(1)
    for i in range(2):
        for r in (1, 2, 3):
            pair_copy(v, p, r, i).wait_recv()
    back_pair(v)
    rest.stage(0)
    tick(v, p, 19)
    early.stage(4)
    back_last(v)
    small.stage(0)
    rest.stage(1)
    late.stage(2)
    tick(v, p, 20)
    small.stage(1)
    early.stage(5)
    late.stage(3)
    tick(v, p, 21)
    small.stage(2)
    rest.stage(2)
    late.stage(4)
    tick(v, p, 22)
    small.stage(3)
    rest.stage(3)
    early.stage(6)
    late.stage(5)
    tick(v, p, 23)
    rest.stage(4)
    small.stage(4)
    tick(v, p, 24)
    rest.stage(5)
    small.stage(5)
    late.stage(6)
    tick(v, p, 25)
    small.stage(6)
    rest.stage(6)
    ticks(v, p, 26, 28)
    early.stage(7)
    late.stage(7)
    ticks(v, p, 28, v.ra.shape[0] + HAND)
    rest.stage(7)

    for i in range(2):
        for r in (1, 2, 3):
            pair_copy(v, p, r, i).wait_send()
    for r in (1, 2):
        kv_copy(v, p, r).wait_send()
    kv_forward(v, p).wait_send()
    for r in range(1, 8):
        meta_copy(v, p, r).wait_send()
        gate_copy(v, p, r).wait_send()
    for which in range(2):
        for r in (1, 3, 5, 7):
            part_core(v, p, r, which).wait_send()
        for i in range(2):
            for r in (2, 6):
                part_x(v, p, r, which, i).wait_send()
            part_y(v, p, which, i).wait_send()
    chunks_done(v, p)


def layer_call(tok, cot, pick, pickt, task, gain, bias, wq, wk, wv, wo, router1, router2, we, wr):
    count, d = tok.shape
    half = count // 2
    heads = wq.shape[0]
    width = 2 * wk.shape[0]
    picks = pick.shape[1]
    experts = router1.shape[1]
    ff = we.shape[2]
    chunks = 4 * ff // 256
    vm = pltpu.VMEM
    anywhere = pl.ANY
    dma = pltpu.SemaphoreType.DMA
    return run_kernel(
        layer_kernel, "layer",
        dict(
            tok=(tok, vm), cot=(cot, vm), pick=(pick, vm), pickt=(pickt, vm),
            task=(task, pltpu.SMEM), gain=(gain, vm), bias=(bias, vm), wq=(wq, vm), wk=(wk, vm),
            wv=(wv, vm), wo=(wo, vm), router1=(router1, vm), router2=(router2, vm),
            we_all=(we, anywhere), wr_all=(wr, anywhere),
        ),
        dict(
            out=((count, d), LOW, vm), gtok=((count, d), F32, vm),
            chunks=((2 * chunks, d, 256), LOW, anywhere),
            **{f"shared{g}": ((8, PIECE[g], d), LOW, anywhere) for g in range(3)},
            stats=((40, d), F32, vm), expo=((8 * CAP, 4 * half), LOW, anywhere),
        ),
        dict(
            n1=vm((count, d), LOW), n2=vm((2, half, d), LOW), mid=vm((count, d), F32),
            pickc=vm((2, half, 8), F32), wkv=vm((width, d), LOW),
            heads=vm((count, heads), LOW), kv=vm((2, 4 * half, width), LOW),
            q8=vm((2 * picks, half, width), LOW), att=vm((2 * picks, half, width), F32),
            g1=vm((count, experts), F32), g2=vm((16, count), F32), meta=vm((8, 16, count), F32),
            xa=vm((8, 2, half, d), LOW), ca=vm((8, 2, half, d), LOW),
            ma=vm((8, 16, count), F32), we=vm((d, ff), LOW), wr=vm((ff, d), LOW),
            xrt=vm((d, 8 * CAP), LOW), gpt=vm((d, 8 * CAP), LOW),
            act=vm((8 * CAP, ff), LOW), gh=vm((8 * CAP, ff), LOW),
            pr=vm((2, 8 * CAP, d), LOW), gr=vm((2, 8 * CAP, d), LOW),
            ra=vm((chunks, d, 256), LOW), rb=vm((chunks, d, 256), LOW), rc=vm((chunks, d, 256), LOW),
            dgs=vm((8, 2, 8, count), F32), dg=vm((8, 2, 8, count), F32),
            small=vm((5, 40, d), F32), small_in=vm((5, 40, d), F32),
            gl1=vm((count, experts), LOW),
            dkv=vm((4, 2, width, half), LOW), din=vm((4, 2, width, half), LOW),
            **{f"half_in{g}": vm((PIECE[g], 4 * d), LOW) for g in range(3)},
            **{f"piece_in{g}": vm((3, PIECE[g], d), LOW) for g in range(3)},
            **{f"zbuf{g}": vm((4, PIECE[g], d), LOW) for g in range(3)},
            cs=dma((16,)), cv=dma((16,)), ks=dma((4,)), kr=dma((4,)), xs=dma((16, 2)), xv=dma((16, 2)),
            ms=dma((8,)), mv=dma((8,)), gs=dma((8,)), gv=dma((8,)), wsem=dma((2,)), osem=dma((5,)),
            s1s=dma((chunks,)), s1r=dma((chunks,)), s2s=dma((chunks,)), s2r=dma((chunks,)),
            s3s=dma((chunks,)), ys=dma((chunks,)), yr=dma((chunks,)), y2s=dma((chunks,)), ls=dma((chunks,)),
            k1s=dma((8,)), k1r=dma((8,)), k2s=dma((8, 2)), k2r=dma((8, 2)),
            ps=dma((4, 2)), pr_sem=dma((4, 2)), ss=dma((6,)), sr=dma((6,)), hs=dma((3, 10)),
            hr=dma((3, 11)),
            free_core=pltpu.SemaphoreType.REGULAR, free_plane=pltpu.SemaphoreType.REGULAR,
        ),
        0,
    )


def widen_kernel(
    c_ref, s0_ref, s1_ref, s2_ref, stats_ref,
    reduce_ref, expand_ref, query_ref, out_ref, key_ref, value_ref, one_ref, two_ref,
    gain_ref, first_ref, second_ref, usage_ref,
):
    for n in range(c_ref.shape[0] // 2):
        at = slice(n * 256, (n + 1) * 256)
        reduce_ref[0, at, :] = c_ref[2 * n].astype(F32).T
        expand_ref[0, :, at] = c_ref[2 * n + 1].astype(F32)

    @pl.when((pl.program_id(0) == 0) & (pl.program_id(1) == 0))
    def _():
        refs = (s0_ref, s1_ref, s2_ref)

        def unpack(ref, g, start):
            done = 0
            for n, row, size in spans(g, start, ref.shape[0]):
                ref[done:done + size, :] = refs[g][n, row:row + size, :].astype(F32)
                done += size

        wide, head = query_ref.shape[0], key_ref.shape[0]
        unpack(out_ref, 0, 0)
        unpack(query_ref.at[0:SPLIT, :], 1, 0)
        unpack(query_ref.at[SPLIT:wide, :], 2, 0)
        unpack(key_ref, 2, wide - SPLIT)
        unpack(value_ref, 2, wide - SPLIT + head)
        for ref, g, start in ((one_ref, 2, wide - SPLIT + 2 * head), (two_ref, 0, wide)):
            for j in range(ref.shape[0]):
                for n, row, size in spans(g, start + 16 * j, 16):
                    ref[j] = refs[g][n, row:row + size, :].astype(F32)[0:ref.shape[1]]
        gain_ref[...] = stats_ref[0:2, :]
        first_ref[...] = stats_ref[2, :]
        second_ref[...] = stats_ref[3, :]
        tasks, _, experts = usage_ref.shape
        for which in range(2):
            table = stats_ref[8 + 16 * which:24 + 16 * which, 0:128].T
            usage_ref[:, which, :] = table[0:tasks, 0:experts]


def widen_call(chunks, shared, stats, slots, d, ff, wide, head, tasks, experts):
    n = ff // 256
    per = PER
    whole = pl.BlockSpec(memory_space=pltpu.VMEM)
    shapes = (
        (wide, d), (wide, d), (head, d), (head, d), (tasks, experts, d), (tasks, experts, d),
        (2, d), (d,), (d,), (tasks, 2, experts),
    )
    return pl.pallas_call(
        widen_kernel,
        name="widen",
        grid=(slots, n // per),
        in_specs=[
            pl.BlockSpec((2 * per, d, 256), lambda s, f: (s * (n // per) + f, 0, 0)),
            whole, whole, whole, whole,
        ],
        out_specs=(
            pl.BlockSpec((1, per * 256, d), lambda s, f: (s, f, 0)),
            pl.BlockSpec((1, d, per * 256), lambda s, f: (s, 0, f)),
            *[whole] * len(shapes),
        ),
        out_shape=(
            jax.ShapeDtypeStruct((slots, ff, d), F32),
            jax.ShapeDtypeStruct((slots, d, ff), F32),
            *[jax.ShapeDtypeStruct(shape, F32) for shape in shapes],
        ),
        compiler_params=pltpu.CompilerParams(vmem_limit_bytes=56 * MIB),
    )(chunks, *shared, stats)


def body_fast(
    tokens,
    task_ids,
    attention_picks,
    feedforward_picks,
    norm_gain,
    norm_bias,
    query_weight,
    key_weight,
    value_weight,
    output_weight,
    attention_router,
    feedforward_router,
    expand_weight,
    reduce_weight,
    cotangent,
):
    images, patches, width = tokens.shape
    count = images * patches
    tasks, _, experts = attention_router.shape
    head = key_weight.shape[1]
    picks = attention_picks.shape[2]
    slots = expand_weight.shape[0]
    ff = expand_weight.shape[2]
    wide = query_weight.shape[1]
    tok = tokens.reshape(count, width)
    pickt = feedforward_picks.reshape(count, picks).T
    b = layer_call(
        tok, cotangent, jnp.swapaxes(attention_picks, 1, 2), pickt, task_ids, norm_gain, norm_bias,
        query_weight.T, key_weight.T, value_weight.T, output_weight,
        jnp.swapaxes(attention_router, 1, 2), jnp.swapaxes(feedforward_router, 1, 2),
        expand_weight, reduce_weight,
    )
    (
        grad_reduce, grad_expand, grad_query, grad_out, grad_key, grad_value, grad_one, grad_two,
        grad_gain, grad_first, grad_second, usage,
    ) = widen_call(
        b.chunks, (b.shared0, b.shared1, b.shared2), b.stats, slots, width, ff, wide, head, tasks,
        experts,
    )
    return (
        b.out.reshape(images, patches, width),
        b.gtok.reshape(images, patches, width),
        grad_gain,
        grad_first,
        grad_second,
        grad_query.T,
        grad_key.T,
        grad_value.T,
        grad_out,
        jnp.swapaxes(grad_one, 1, 2),
        jnp.swapaxes(grad_two, 1, 2),
        grad_expand,
        grad_reduce,
        jnp.swapaxes(usage, 0, 1),
    )


def normalize(value, gain, bias):
    mean = jnp.mean(value, -1, keepdims=True)
    centred = value - mean
    spread = jnp.mean(centred * centred, -1, keepdims=True)
    return centred * lax.rsqrt(spread + EPS) * gain + bias


def gate_weights(logits, picks_hot):
    chosen = jnp.sum(picks_hot * logits[..., None, :], -1)
    return jax.nn.softmax(chosen, -1)


def activate(value):
    return jax.nn.gelu(value, approximate=True)


def body(
    tokens,
    task_ids,
    attention_picks,
    feedforward_picks,
    norm_gain,
    norm_bias,
    query_weight,
    key_weight,
    value_weight,
    output_weight,
    attention_router,
    feedforward_router,
    expand_weight,
    reduce_weight,
    cotangent,
):
    images, patches, width = tokens.shape
    count = images * patches
    tasks = attention_router.shape[0]
    experts = attention_router.shape[2]
    head = key_weight.shape[1]
    picks = attention_picks.shape[2]
    slots = expand_weight.shape[0]
    groups = lax.axis_size("expert")
    lanes = groups * slots
    f32 = jnp.float32
    low_type = jnp.bfloat16
    inputs = tokens.astype(f32).reshape(count, width)
    expert_range = jnp.arange(experts, dtype=jnp.int32)
    task_hot = (task_ids[:, None] == jnp.arange(tasks, dtype=jnp.int32)[None, :]).astype(f32)
    task_low = task_hot.astype(low_type)
    attend_hot = (attention_picks[..., None] == expert_range).astype(f32)
    attend_low = attend_hot.astype(low_type)
    choices = feedforward_picks.reshape(count, picks)
    feed_hot = (choices[..., None] == expert_range).astype(f32)
    flat = choices.reshape(count * picks)
    marks = (flat[:, None] == expert_range[None, :]).astype(jnp.int32)
    before = jnp.cumsum(marks, axis=0) - marks
    position = flat * CAP + jnp.sum(before * marks, axis=1)
    first, first_back = jax.vjp(normalize, inputs, norm_gain[0], norm_bias[0])
    normed_one = first.astype(low_type)
    shaped_one = normed_one.reshape(images, patches, width)
    router_one = jnp.einsum(
        "it,tde->ide", task_low, attention_router, preferred_element_type=f32
    ).astype(low_type)
    logits_one = jnp.einsum("ipd,ide->ipe", shaped_one, router_one, preferred_element_type=f32)
    gates_one, gates_one_back = jax.vjp(lambda value: gate_weights(value, attend_hot), logits_one)
    queries_all = jnp.dot(normed_one, query_weight, preferred_element_type=f32).astype(low_type)
    queries_all = queries_all.reshape(images, patches, experts, head)
    queries = jnp.einsum(
        "ipke,ipeh->ipkh", attend_low, queries_all, preferred_element_type=f32
    ).astype(low_type)
    queries = queries.reshape(images, patches * picks, head)
    key_value = jnp.concatenate([key_weight, value_weight], 1)
    pair = jnp.dot(normed_one, key_value, preferred_element_type=f32).astype(low_type)
    pair = pair.reshape(images, patches, 2 * head)
    pair_all = lax.all_gather(pair, "expert", axis=1, tiled=True)
    keys_all = pair_all[:, :, :head]
    values_all = pair_all[:, :, head:]
    scores = jnp.einsum("irh,ish->irs", queries, keys_all, preferred_element_type=f32) * 0.125
    top = jnp.max(scores, -1, keepdims=True)
    expo = jnp.exp(scores - top)
    total = jnp.sum(expo, -1, keepdims=True)
    log_total = top + jnp.log(total)
    probs_low = (expo / total).astype(low_type)
    attended = jnp.einsum("irs,ish->irh", probs_low, values_all, preferred_element_type=f32)
    attended = attended.reshape(images, patches, picks, head)
    weighted = gates_one[..., None] * attended
    heads = jnp.einsum("ipke,ipkh->ipeh", attend_hot, weighted, precision=HIGH)
    heads = heads.reshape(count, experts * head).astype(low_type)
    middle = inputs + jnp.dot(heads, output_weight, preferred_element_type=f32)
    second, second_back = jax.vjp(normalize, middle, norm_gain[1], norm_bias[1])
    normed_two = second.astype(low_type)
    shaped_two = normed_two.reshape(images, patches, width)
    router_two = jnp.einsum(
        "it,tde->ide", task_low, feedforward_router, preferred_element_type=f32
    ).astype(low_type)
    logits_two = jnp.einsum(
        "ipd,ide->ipe", shaped_two, router_two, preferred_element_type=f32
    ).reshape(count, experts)
    gates_two, gates_two_back = jax.vjp(lambda value: gate_weights(value, feed_hot), logits_two)
    outgoing = (
        jnp.zeros((lanes * CAP, width), low_type)
        .at[position]
        .set(jnp.repeat(normed_two, picks, axis=0))
    )
    outgoing = outgoing.reshape(groups, slots * CAP, width)
    received = lax.all_to_all(outgoing, "expert", split_axis=0, concat_axis=0, tiled=True).reshape(
        groups, slots, CAP, width
    )
    hidden = jnp.einsum("nscd,sdf->nscf", received, expand_weight, preferred_element_type=f32)
    activated, activate_back = jax.vjp(activate, hidden)
    active_low = activated.astype(low_type)
    produced = jnp.einsum(
        "nscf,sfd->nscd", active_low, reduce_weight, preferred_element_type=f32
    ).astype(low_type)
    produced = produced.reshape(groups, slots * CAP, width)
    returned = lax.all_to_all(produced, "expert", split_axis=0, concat_axis=0, tiled=True).reshape(
        lanes * CAP, width
    )
    picked = returned[position].astype(f32).reshape(count, picks, width)
    final = middle + jnp.sum(gates_two[..., None] * picked, 1)
    output = final.astype(low_type).reshape(images, patches, width)
    grad_final = cotangent.astype(f32).reshape(count, width)
    grad_gates_two = jnp.sum(picked * grad_final[:, None, :], -1)
    grad_picked = (
        (gates_two[..., None] * grad_final[:, None, :])
        .astype(low_type)
        .reshape(count * picks, width)
    )
    grad_send = jnp.zeros((lanes * CAP, width), low_type).at[position].set(grad_picked)
    grad_send = grad_send.reshape(groups, slots * CAP, width)
    grad_produced = lax.all_to_all(
        grad_send, "expert", split_axis=0, concat_axis=0, tiled=True
    ).reshape(groups, slots, CAP, width)
    grad_reduce = jnp.einsum(
        "nscf,nscd->sfd", active_low, grad_produced, preferred_element_type=f32
    )
    grad_active = jnp.einsum(
        "nscd,sfd->nscf", grad_produced, reduce_weight, preferred_element_type=f32
    )
    grad_hidden = activate_back(grad_active)[0].astype(low_type)
    grad_expand = jnp.einsum("nscd,nscf->sdf", received, grad_hidden, preferred_element_type=f32)
    grad_rows = jnp.einsum(
        "nscf,sdf->nscd", grad_hidden, expand_weight, preferred_element_type=f32
    ).astype(low_type)
    grad_rows = grad_rows.reshape(groups, slots * CAP, width)
    grad_back = lax.all_to_all(
        grad_rows, "expert", split_axis=0, concat_axis=0, tiled=True
    ).reshape(lanes * CAP, width)
    grad_normed_two = jnp.sum(grad_back[position].astype(f32).reshape(count, picks, width), 1)
    grad_logits_two = (
        gates_two_back(grad_gates_two)[0].astype(low_type).reshape(images, patches, experts)
    )
    per_image_two = jnp.einsum(
        "ipd,ipe->ide", shaped_two, grad_logits_two, preferred_element_type=f32
    )
    grad_feed_router = jnp.einsum("it,ide->tde", task_hot, per_image_two, precision=HIGH)
    grad_normed_two = grad_normed_two + jnp.einsum(
        "ipe,ide->ipd", grad_logits_two, router_two, preferred_element_type=f32
    ).reshape(count, width)
    grad_middle_norm, grad_gain_two, grad_bias_two = second_back(grad_normed_two)
    grad_middle = grad_final + grad_middle_norm
    grad_branch = grad_middle.astype(low_type)
    grad_output = jnp.einsum("tc,td->cd", heads, grad_branch, preferred_element_type=f32)
    grad_heads = jnp.einsum(
        "td,cd->tc", grad_branch, output_weight, preferred_element_type=f32
    ).astype(low_type)
    grad_heads = grad_heads.reshape(images, patches, experts, head)
    grad_selected = jnp.einsum(
        "ipke,ipeh->ipkh", attend_low, grad_heads, preferred_element_type=f32
    )
    grad_gates_one = jnp.sum(attended * grad_selected, -1)
    grad_attended = (
        (gates_one[..., None] * grad_selected)
        .astype(low_type)
        .reshape(images, patches * picks, head)
    )
    scores_back = jnp.einsum("irh,ish->irs", queries, keys_all, preferred_element_type=f32) * 0.125
    probs_back = jnp.exp(scores_back - log_total)
    grad_values = jnp.einsum(
        "irs,irh->ish", probs_back.astype(low_type), grad_attended, preferred_element_type=f32
    )
    grad_probs = jnp.einsum("irh,ish->irs", grad_attended, values_all, preferred_element_type=f32)
    inner_sum = jnp.sum(probs_back * grad_probs, -1, keepdims=True)
    grad_scores = (probs_back * (grad_probs - inner_sum)).astype(low_type)
    grad_query_sel = (
        jnp.einsum("irs,ish->irh", grad_scores, keys_all, preferred_element_type=f32) * 0.125
    )
    grad_keys = jnp.einsum("irs,irh->ish", grad_scores, queries, preferred_element_type=f32) * 0.125
    grad_pair = jnp.concatenate([grad_keys, grad_values], -1)
    pair_sum = lax.psum_scatter(
        grad_pair.astype(jnp.bfloat16), "expert", scatter_dimension=1, tiled=True
    ).astype(jnp.float32)
    pair_sum = pair_sum.astype(low_type).reshape(count, 2 * head)
    grad_query_sel = grad_query_sel.reshape(images, patches, picks, head)
    grad_queries_all = jnp.einsum("ipke,ipkh->ipeh", attend_hot, grad_query_sel, precision=HIGH)
    grad_queries_all = grad_queries_all.astype(low_type).reshape(count, experts * head)
    grad_logits_one = gates_one_back(grad_gates_one)[0].astype(low_type)
    per_image_one = jnp.einsum(
        "ipd,ipe->ide", shaped_one, grad_logits_one, preferred_element_type=f32
    )
    grad_attend_router = jnp.einsum("it,ide->tde", task_hot, per_image_one, precision=HIGH)
    grad_query = jnp.einsum("td,tc->dc", normed_one, grad_queries_all, preferred_element_type=f32)
    grad_key_value = jnp.einsum("td,tc->dc", normed_one, pair_sum, preferred_element_type=f32)
    grad_normed_one = jnp.einsum(
        "tc,dc->td", grad_queries_all, query_weight, preferred_element_type=f32
    )
    grad_normed_one = grad_normed_one + jnp.einsum(
        "tc,dc->td", pair_sum, key_value, preferred_element_type=f32
    )
    grad_normed_one = grad_normed_one + jnp.einsum(
        "ipe,ide->ipd", grad_logits_one, router_one, preferred_element_type=f32
    ).reshape(count, width)
    grad_inputs_norm, grad_gain_one, grad_bias_one = first_back(grad_normed_one)
    grad_tokens = (grad_middle + grad_inputs_norm).reshape(images, patches, width)
    grad_gain = jnp.stack([grad_gain_one, grad_gain_two])
    grad_bias = jnp.stack([grad_bias_one, grad_bias_two])
    feed_shaped = feed_hot.reshape(images, patches, picks, experts)
    usage = jnp.stack(
        [
            jnp.einsum("it,ipke->te", task_hot, attend_hot, precision=HIGH),
            jnp.einsum("it,ipke->te", task_hot, feed_shaped, precision=HIGH),
        ]
    )
    shared = lax.psum(
        (
            grad_query,
            grad_key_value,
            grad_output,
            grad_attend_router,
            grad_feed_router,
            grad_gain,
            grad_bias,
            usage,
        ),
        ("dp", "expert"),
    )
    grad_expand_sum, grad_reduce_sum = (
        lax.psum(grad_expand.astype(jnp.bfloat16), "dp").astype(jnp.float32),
        lax.psum(grad_reduce.astype(jnp.bfloat16), "dp").astype(jnp.float32),
    )
    grad_key_sum = shared[1][:, :head]
    grad_value_sum = shared[1][:, head:]
    return (
        output,
        grad_tokens,
        shared[5],
        shared[6][0],
        shared[6][1],
        shared[0],
        grad_key_sum,
        grad_value_sum,
        shared[2],
        shared[3],
        shared[4],
        grad_expand_sum,
        grad_reduce_sum,
        shared[7],
    )


def solution(mesh):
    placed = (
        P("dp", "expert", None),
        P("dp"),
        P("dp", "expert", None),
        P("dp", "expert", None, None),
        P(),
        P(),
        P(),
        P(),
        P(),
        P(),
        P(),
        P(),
        P("expert", None, None),
        P("expert", None, None),
        P("dp", "expert", None),
    )
    fast = mesh.shape["dp"] == 8 and mesh.shape["expert"] == 4
    return jax.shard_map(
        body_fast if fast else body,
        mesh=mesh,
        in_specs=placed,
        out_specs=(
            P("dp", "expert", None),
            P("dp", "expert", None),
            P(),
            P(),
            P(),
            P(),
            P(),
            P(),
            P(),
            P(),
            P(),
            P("expert", None, None),
            P("expert", None, None),
            P(),
        ),
        check_vma=False,
    )
```

```python
import types

import jax
import jax.numpy as jnp
from jax import lax
from jax.experimental import pallas as pl
from jax.experimental.pallas import tpu as pltpu
from jax.sharding import PartitionSpec as P

CAP = 256


EPS = 1e-06
HIGH = lax.Precision.HIGHEST
F32 = jnp.float32
LOW = jnp.bfloat16
MESH = pl.DeviceIdType.MESH
MIB = 2**20


def dot(a, b):
    return jnp.dot(a, b, preferred_element_type=F32)


def dot_nt(a, b):
    return lax.dot_general(a, b, (((1,), (1,)), ((), ())), preferred_element_type=F32)


def dot_tn(a, b):
    return lax.dot_general(a, b, (((0,), (0,)), ((), ())), preferred_element_type=F32)


def remote(src, dst, send, recv, device):
    return pltpu.make_async_remote_copy(
        src_ref=src, dst_ref=dst, send_sem=send, recv_sem=recv,
        device_id=device, device_id_type=MESH,
    )


def run_kernel(kernel, name, ins, outs, scratch, collective):
    names = [*ins, *outs, *scratch]

    def body(*refs):
        kernel(types.SimpleNamespace(**dict(zip(names, refs, strict=True))))

    made = pl.pallas_call(
        body,
        name=name,
        out_shape=[jax.ShapeDtypeStruct(shape, dtype) for shape, dtype, _ in outs.values()],
        in_specs=[pl.BlockSpec(memory_space=space) for _, space in ins.values()],
        out_specs=[pl.BlockSpec(memory_space=space) for _, _, space in outs.values()],
        scratch_shapes=list(scratch.values()),
        compiler_params=pltpu.CompilerParams(
            collective_id=collective, has_side_effects=True, vmem_limit_bytes=62 * MIB
        ),
    )(*[array for array, _ in ins.values()])
    return types.SimpleNamespace(**dict(zip(outs, made, strict=True)))


def center(value):
    mean = jnp.mean(value, -1, keepdims=True)
    centred = value - mean
    scale = lax.rsqrt(jnp.mean(centred * centred, -1, keepdims=True) + EPS)
    return centred * scale, scale


def center_back(grad, normal, scale, gain):
    inner = grad * gain
    mean = jnp.mean(inner, -1, keepdims=True)
    along = jnp.mean(inner * normal, -1, keepdims=True)
    return scale * (inner - mean - normal * along)


def head_maps(heads, head):
    row = lax.broadcasted_iota(jnp.int32, (heads * head, 2 * head), 0)
    row = lax.rem(row, head)
    col = lax.broadcasted_iota(jnp.int32, (heads * head, 2 * head), 1)
    low = jnp.where(row == col, 1.0, 0.0).astype(LOW)
    high = jnp.where(row + head == col, 1.0, 0.0).astype(LOW)
    return low, high


def masked_softmax(logits, chosen, axis):
    top = jnp.max(jnp.where(chosen, logits, -1e30), axis, keepdims=True)
    expo = jnp.where(chosen, jnp.exp(jnp.minimum(logits - top, 0.0)), 0.0)
    return expo / jnp.sum(expo, axis, keepdims=True)


PIECE = (160, 80, 96)
FIRST = (1024, 1344, 1504)
SPLIT = 640
BRANCH = 1024
HAND = 6
PER = 6


def gelu_parts(value):
    square = value * value
    inner = value * (0.7978845608028654 + 0.035677408136300125 * square)
    half = 0.5 + 0.5 * jnp.tanh(inner)
    act = value * half
    slope = half + act * (1.0 - half) * (1.5957691216057308 + 0.2140644488178007 * square)
    return act, slope


class Place:
    def __init__(self):
        self.dp = dp = lax.axis_index("dp")
        self.ex = lax.axis_index("expert")
        self.y = lax.rem(dp, 2)
        z = lax.div(dp, 2)
        self.is_end = (z == 0) | (z == 3)
        self.is_mid = (z == 1) | (z == 2)
        self.toward = (jnp.where(z < 2, dp + 2, dp - 2), self.ex)
        self.outer = (jnp.where(z == 1, dp - 2, jnp.where(z == 2, dp + 2, dp)), self.ex)
        self.core = lax.rem(self.ex, 2)
        self.spot = self.y * 2 + lax.div(self.ex, 2)

    def peer(self, r):
        return (self.dp ^ lax.div(r, 4), self.ex ^ lax.rem(r, 4))

    def plane(self, q):
        return (self.dp ^ lax.div(q, 2), self.ex ^ (2 * lax.rem(q, 2)))

    def group(self, r):
        return 2 * (self.ex ^ lax.rem(r, 4)) + (self.y ^ lax.div(r, 4))


def cot_copy(v, p, r):
    return remote(v.cot, v.ca.at[r], v.cs.at[r], v.cv.at[r], p.peer(r))


def cot_relay(v, p, to):
    at = pl.ds(0 if to == 2 else CAP // 2, CAP // 2)
    return remote(
        v.ca.at[6 - to, :, at, :], v.ca.at[6, :, at, :], v.cs.at[to + 1], v.cv.at[to + 8], p.peer(to)
    )


def cot_forward(v, p, r):
    return remote(v.ca.at[r], v.ca.at[r + 1], v.cs.at[r + 6], v.cv.at[r + 1], p.peer(1))


def row_copy(v, p, r, i):
    return remote(v.n2.at[i], v.xa.at[r, i], v.xs.at[r, i], v.xv.at[r, i], p.peer(r))


def row_relay(v, p, to, i):
    at = pl.ds(0 if to == 2 else CAP // 2, CAP // 2)
    return remote(
        v.xa.at[6 - to, i, at, :], v.xa.at[6, i, at, :],
        v.xs.at[to + 1, i], v.xv.at[to + 8, i], p.peer(to),
    )


def row_forward(v, p, r, i):
    return remote(
        v.xa.at[r, i], v.xa.at[r + 1, i], v.xs.at[r + 6, i], v.xv.at[r + 1, i], p.peer(1)
    )


def cot_near(v, p):
    for r in (4, 2):
        cot_copy(v, p, r).wait_recv()
        cot_relay(v, p, 6 - r).start()
        cot_forward(v, p, r).start()


def cot_far(v, p):
    cot_relay(v, p, 2).wait_recv()
    cot_relay(v, p, 4).wait_recv()
    cot_forward(v, p, 6).start()


def rows_near(v, p, i):
    for r in (4, 2):
        row_copy(v, p, r, i).wait_recv()
        row_relay(v, p, 6 - r, i).start()
        row_forward(v, p, r, i).start()


def rows_far(v, p, i):
    row_relay(v, p, 2, i).wait_recv()
    row_relay(v, p, 4, i).wait_recv()
    row_forward(v, p, 6, i).start()


def meta_copy(v, p, r):
    return remote(v.meta.at[p.group(r)], v.ma.at[r], v.ms.at[r], v.mv.at[r], p.peer(r))


def kv_copy(v, p, r):
    half = v.kv.shape[1] // 4
    return remote(
        v.kv.at[:, pl.ds(0, half), :], v.kv.at[:, pl.ds(r * half, half), :],
        v.ks.at[r], v.kr.at[r], p.peer(r),
    )


def kv_forward(v, p):
    half = v.kv.shape[1] // 4
    return remote(
        v.kv.at[:, pl.ds(2 * half, half), :], v.kv.at[:, pl.ds(3 * half, half), :],
        v.ks.at[3], v.kr.at[3], p.peer(1),
    )


def front(v, p):
    count, d = v.tok.shape
    half = count // 2
    heads = v.heads.shape[1]
    head = v.kv.shape[2] // 2
    picks = v.pick.shape[1]
    for i in range(2):
        named = jnp.concatenate([v.pick[i].astype(F32), jnp.zeros((8 - picks, half), F32)], 0)
        v.pickc[i] = named.T
    gain = v.gain[...]
    bias = v.bias[...]
    v.wkv[0:head, :] = v.wk[...]
    v.wkv[head:2 * head, :] = v.wv[...]
    for i in range(2):
        rows = slice(i * half, (i + 1) * half)
        normal, _ = center(v.tok[rows, :].astype(F32))
        normed = (normal * gain[0:1] + bias[0:1]).astype(LOW)
        v.n1[rows, :] = normed
        v.kv[i, 0:half, :] = dot_nt(normed, v.wkv[...]).astype(LOW)
    pl.semaphore_wait(v.barrier, jnp.where(p.is_mid, 9, 8))
    for r in (2, 1):
        kv_copy(v, p, r).start()
    for r in (4, 2, 1):
        cot_copy(v, p, r).start()
    v.ca[0] = v.cot[...]
    v.gh[0:count, 0:heads] = dot_nt(v.n1[...], v.wq[...]).astype(LOW)

    experts = v.router1.shape[1]
    number = lax.broadcasted_iota(jnp.int32, (16, count), 0)
    chosen = number == v.pickt[0:1, :]
    for k in range(1, picks):
        chosen = chosen | (number == v.pickt[k:k + 1, :])
    earlier = lax.broadcasted_iota(jnp.int32, (count, count), 0) < lax.broadcasted_iota(
        jnp.int32, (count, count), 1
    )
    before = dot(jnp.where(chosen, 1.0, 0.0).astype(LOW), jnp.where(earlier, 1.0, 0.0).astype(LOW))
    rank = jnp.where(chosen, before, -1.0)

    to_query, to_value = head_maps(heads // head, head)
    owner = lax.div(lax.broadcasted_iota(jnp.int32, (half, heads), 1), head).astype(F32)
    lane = lax.broadcasted_iota(jnp.int32, (half, experts), 1).astype(F32)
    wide = lax.broadcasted_iota(jnp.int32, (half, 2 * head), 1)
    kv_copy(v, p, 2).wait_recv()
    kv_forward(v, p).start()
    kv_copy(v, p, 1).wait_recv()
    kv_forward(v, p).wait_recv()

    for i in range(2):
        rows = slice(i * half, (i + 1) * half)
        logits = dot_nt(v.n1[rows, :], v.router1[v.task[i]])
        named = [lane == v.pickc[i, :, k:k + 1] for k in range(picks)]
        allowed = named[0]
        for k in range(1, picks):
            allowed = allowed | named[k]
        gates = masked_softmax(logits, allowed, 1)
        v.g1[rows, :] = gates
        kv = v.kv[i]
        for k in range(picks):
            at = picks * i + k
            if i == 1 and k == 2:
                cot_far(v, p)
                rows_near(v, p, 0)
            mine = owner == v.pickc[i, :, k:k + 1]
            gate = jnp.sum(jnp.where(named[k], gates, 0.0), 1, keepdims=True)
            all_queries = v.gh[rows, 0:heads]
            query = dot(jnp.where(mine, all_queries, jnp.zeros_like(all_queries)), to_query)
            query = (query * head ** -0.5).astype(LOW)
            v.q8[at] = query
            scores = dot_nt(query, kv)
            expo = jnp.exp(scores - jnp.max(scores, 1, keepdims=True))
            total = jnp.sum(expo, 1, keepdims=True)
            low = expo.astype(LOW)
            v.act[at * half:(at + 1) * half, 0:4 * half] = low
            attended = dot(low, kv) / total
            v.att[at] = jnp.where(wide == 0, total, attended)
            spread = dot_nt((gate * attended).astype(LOW), to_value).astype(LOW)
            if k == 0:
                v.heads[rows, :] = jnp.where(mine, spread, jnp.zeros_like(spread))
            else:
                v.heads[rows, :] = jnp.where(mine, spread, v.heads[rows, :])
        middle = v.tok[rows, :].astype(F32) + dot(v.heads[rows, :], v.wo[...])
        v.mid[rows, :] = middle
        normal, _ = center(middle)
        normed = (normal * gain[1:2] + bias[1:2]).astype(LOW)
        v.n2[i] = normed
        for r in (4, 2, 1):
            row_copy(v, p, r, i).start()
        v.xa[0, i] = normed
        logits = dot_nt(v.router2[v.task[i]], normed)
        logits = jnp.concatenate([logits, jnp.zeros((16 - experts, half), F32)], 0)
        gates = masked_softmax(logits, rank[:, rows] >= 0.0, 0)
        v.g2[:, rows] = gates
        for g in range(8):
            v.meta[g, 0:2, rows] = rank[2 * g:2 * g + 2, rows]
            v.meta[g, 2:4, rows] = gates[2 * g:2 * g + 2, :]
            v.meta[g, 4:16, rows] = jnp.zeros((12, half), F32)
        if i == 0:
            cot_near(v, p)
    v.ma[0] = v.meta[p.group(0)]
    for r in range(1, 8):
        meta_copy(v, p, r).start()


def chunk_first(v, p, c):
    return remote(v.ra.at[c], v.rb.at[c], v.s1s.at[c], v.s1r.at[c], p.toward)


def chunk_middle(v, p, c):
    return remote(v.rb.at[c], v.rc.at[c], v.s2s.at[c], v.s2r.at[c], p.toward)


def chunk_back(v, p, c):
    return remote(v.ra.at[c], v.rc.at[c], v.s3s.at[c], v.s2r.at[c], p.outer)


def chunk_pair(v, p, src, c):
    to = p.y * v.ra.shape[0] + c
    return remote(src.at[c], v.chunks.at[to], v.ys.at[c], v.yr.at[c], (p.dp ^ 1, p.ex))


def chunk_cross(v, p, c, device):
    at = v.chunks.at[(1 - p.y) * v.ra.shape[0] + c]
    return remote(at, at, v.y2s.at[c], v.yr.at[c], device)


def chunk_land(v, p, c):
    at = v.chunks.at[(1 - p.y) * v.ra.shape[0] + c]
    return remote(v.ra.at[c], at, v.ys.at[c], v.yr.at[c], (p.dp ^ 1, p.ex))


def only_mid(c):
    return lax.rem(c, 8) == 2


def only_end(c):
    return lax.rem(c, 8) == 5


def chunk_own(v, p, src, c):
    to = p.y * v.ra.shape[0] + c
    return pltpu.make_async_copy(src.at[c], v.chunks.at[to], v.ls.at[c])


def tick(v, p, t):
    chunks = v.ra.shape[0]

    @pl.when(p.is_mid & (t < chunks))
    def _():
        c = jnp.minimum(t, chunks - 1)
        chunk_first(v, p, c).wait_recv()
        v.rb[c] = (v.ra[c].astype(F32) + v.rb[c].astype(F32)).astype(LOW)
        chunk_middle(v, p, c).start()

    @pl.when(p.is_mid & (t >= 2) & (t < chunks + 2))
    def _():
        c = jnp.maximum(t - 2, 0)
        chunk_middle(v, p, c).wait_recv()
        v.ra[c] = (v.rb[c].astype(F32) + v.rc[c].astype(F32)).astype(LOW)
        chunk_back(v, p, c).start()

        @pl.when(jnp.logical_not(only_end(c)))
        def _():
            chunk_pair(v, p, v.ra, c).start()

        chunk_own(v, p, v.ra, c).start()

    @pl.when(p.is_end & (t >= 4) & (t < chunks + 4))
    def _():
        c = jnp.maximum(t - 4, 0)
        chunk_middle(v, p, c).wait_recv()

        @pl.when(jnp.logical_not(only_mid(c)))
        def _():
            chunk_pair(v, p, v.rc, c).start()

        chunk_own(v, p, v.rc, c).start()

    @pl.when((t >= HAND) & (t < chunks + HAND))
    def _():
        c = jnp.maximum(t - HAND, 0)

        @pl.when(p.is_mid & only_mid(c))
        def _():
            chunk_land(v, p, c).wait_recv()
            chunk_cross(v, p, c, p.outer).start()

        @pl.when(p.is_end & only_end(c))
        def _():
            chunk_land(v, p, c).wait_recv()
            chunk_cross(v, p, c, p.toward).start()


def ticks(v, p, first, after):
    def one(t, carry):
        tick(v, p, t)
        return carry

    lax.fori_loop(first, after, one, 0)


def chunks_done(v, p):
    chunks = v.ra.shape[0]

    def one(c, carry):
        @pl.when(p.is_end)
        def _():
            chunk_first(v, p, c).wait_send()

            @pl.when(jnp.logical_not(only_mid(c)))
            def _():
                chunk_pair(v, p, v.rc, c).wait_send()

            chunk_own(v, p, v.rc, c).wait()

            @pl.when(only_end(c))
            def _():
                chunk_cross(v, p, c, p.toward).wait_send()

            @pl.when(jnp.logical_not(only_end(c)))
            def _():
                chunk_land(v, p, c).wait_recv()

        @pl.when(p.is_mid)
        def _():
            chunk_middle(v, p, c).wait_send()
            chunk_back(v, p, c).wait_send()

            @pl.when(jnp.logical_not(only_end(c)))
            def _():
                chunk_pair(v, p, v.ra, c).wait_send()

            chunk_own(v, p, v.ra, c).wait()

            @pl.when(only_mid(c))
            def _():
                chunk_cross(v, p, c, p.outer).wait_send()

            @pl.when(jnp.logical_not(only_mid(c)))
            def _():
                chunk_land(v, p, c).wait_recv()

        return carry

    lax.fori_loop(0, chunks, one, 0)


def weight_loads(v, p, j):
    return (
        pltpu.make_async_copy(v.we_all.at[p.y * 2 + j], v.we, v.wsem.at[0]),
        pltpu.make_async_copy(v.wr_all.at[p.y * 2 + j], v.wr, v.wsem.at[1]),
    )


def source_rows(r):
    return pl.ds(pl.multiple_of(r * CAP, CAP), CAP)


def slot_hits(v, r, j):
    sub = lax.broadcasted_iota(jnp.int32, (CAP, 2 * CAP), 0).astype(F32)
    return sub == v.ma[r, j:j + 1, :]


def dispatch(v, r, j):
    d = v.xa.shape[3]
    hit = slot_hits(v, r, j)
    pick = jnp.where(hit, 1.0, 0.0).astype(LOW)
    gate = jnp.sum(jnp.where(hit, v.ma[r, j + 2:j + 3, :], 0.0), 1, keepdims=True)
    at = source_rows(r)
    rows = dot(pick, v.xa[r].reshape(2 * CAP, d))
    v.pr[j, at, :] = rows.astype(LOW)
    v.xrt[:, at] = rows.T.astype(LOW)
    rows = gate * dot(pick, v.ca[r].reshape(2 * CAP, d))
    v.gr[j, at, :] = rows.astype(LOW)
    v.gpt[:, at] = rows.T.astype(LOW)


def columns(v, j, f):
    cols = pl.ds(pl.multiple_of(f * 256, 256), 256)
    step = 512
    for b in range(v.act.shape[0] // step):
        rows = slice(b * step, (b + 1) * step)
        value, slope = gelu_parts(dot(v.pr[j, rows, :], v.we[:, cols]))
        v.act[rows, cols] = value.astype(LOW)
        v.gh[rows, cols] = (dot_nt(v.gr[j, rows, :], v.wr[cols, :]) * slope).astype(LOW)


def weight_grads(v, p, j, f):
    cols = pl.ds(pl.multiple_of(f * 256, 256), 256)
    first = j * (v.ra.shape[0] // 2) + 2 * f
    v.ra[first] = dot(v.gpt[...], v.act[:, cols]).astype(LOW)
    v.ra[first + 1] = dot(v.xrt[...], v.gh[:, cols]).astype(LOW)

    @pl.when(p.is_end)
    def _():
        chunk_first(v, p, first).start()
        chunk_first(v, p, first + 1).start()


def produce(v, n, j):
    size = v.act.shape[0] // 2
    at = pl.ds(pl.multiple_of(n * size, size), size)
    v.pr[j, at, :] = dot(v.act[at, :], v.wr[...]).astype(LOW)
    v.gr[j, at, :] = dot_nt(v.gh[at, :], v.we[...]).astype(LOW)

    def gates(m):
        r = n * (size // CAP) + m
        made = v.pr[j, source_rows(r), :].astype(F32)
        hit = slot_hits(v, r, j)
        pick = jnp.where(hit, 1.0, 0.0).astype(LOW)
        seen = dot(pick, v.ca[r].reshape(2 * CAP, made.shape[1]))
        inner = jnp.sum(made * seen, 1, keepdims=True)
        part = jnp.sum(jnp.where(hit, inner, 0.0), 0, keepdims=True)
        v.dgs[r, j] = jnp.broadcast_to(part, (8, 2 * CAP))

    for m in range(size // CAP):
        gates(m)


def gate_copy(v, p, r):
    return remote(v.dgs.at[r], v.dg.at[p.group(0)], v.gs.at[r], v.gv.at[r], p.peer(r))


def part_core(v, p, r, which):
    ref = (v.gr, v.pr)[which]
    at = 4 * which + lax.div(r, 2)
    return remote(ref.at[:, source_rows(r), :], v.xa.at[at], v.k1s.at[at], v.k1r.at[at], p.peer(1))


def part_x(v, p, r, which, i):
    ref = (v.gr, v.pr)[which]
    at = 4 * which + r // 2 - 1
    return remote(
        ref.at[i, source_rows(r), :], v.ca.at[at, i], v.k2s.at[at, i], v.k2r.at[at, i], p.peer(2)
    )


def part_y(v, p, which, i):
    ref = (v.gr, v.pr)[which]
    at = 4 * which + 1
    return remote(
        ref.at[i, source_rows(4), :], v.ca.at[at, i], v.k2s.at[at, i], v.k2r.at[at, i], p.peer(4)
    )


def combine(v, r, which):
    lane = lax.broadcasted_iota(jnp.int32, (2 * CAP, CAP), 1).astype(F32)
    meta = v.ma[r].T
    at = source_rows(r)
    ref = (v.gr, v.pr)[which]
    total = jnp.zeros((2 * CAP, ref.shape[2]), F32)
    for j in range(2):
        hit = lane == meta[:, j:j + 1]
        weight = 1.0 if which == 0 else meta[:, 2 + j:3 + j]
        total = total + dot(jnp.where(hit, weight, 0.0).astype(LOW), ref[j, at, :])
    ref[0, at, :] = total[:CAP].astype(LOW)
    ref[1, at, :] = total[CAP:].astype(LOW)


def send_parts(v, p, which):
    def odd(n, carry):
        r = 7 - 2 * n
        combine(v, r, which)
        part_core(v, p, r, which).start()
        return carry

    lax.fori_loop(0, 4, odd, 0)

    def even(n, carry):
        r = jnp.where(n < 2, 6 - 4 * n, 12 - 4 * n)
        combine(v, r, which)
        part_core(v, p, r, which).wait_recv()
        ref = (v.gr, v.pr)[which]
        at = source_rows(r)
        ref[:, at, :] = (
            ref[:, at, :].astype(F32) + v.xa[4 * which + lax.div(r, 2)].astype(F32)
        ).astype(LOW)
        return carry

    lax.fori_loop(0, 2, even, 0)
    if which == 0:
        for i in range(2):
            for r in (6, 2):
                part_x(v, p, r, which, i).start()
    lax.fori_loop(2, 4, even, 0)


def relay_parts(v, p, which, i):
    ref = (v.gr, v.pr)[which]
    part_x(v, p, 6, which, i).wait_recv()
    at = source_rows(4)
    ref[i, at, :] = (ref[i, at, :].astype(F32) + v.ca[4 * which + 2, i].astype(F32)).astype(LOW)
    part_y(v, p, which, i).start()
    part_x(v, p, 2, which, i).wait_recv()


def own_sum(v, i, which):
    ref = (v.gr, v.pr)[which]
    total = ref[i, 0:CAP, :].astype(F32) + v.ca[4 * which, i].astype(F32)
    return total + v.ca[4 * which + 1, i].astype(F32)


def piece(v, g, c, q):
    at = FIRST[g] + c * PIECE[g]
    return v.act.at[
        pl.ds(pl.multiple_of(at, 16), PIECE[g]), pl.ds(pl.multiple_of(q * 384, 128), 384)
    ]


def spans(g, start, count):
    while count > 0:
        n, row = divmod(start, PIECE[g])
        size = min(count, PIECE[g] - row)
        yield n, row, size
        start, count = start + size, count - size


def place_rows(v, g, start, value):
    d = value.shape[1]
    done = 0
    for n, row, size in spans(g, start, value.shape[0]):
        at = FIRST[g] + (n // 4) * PIECE[g] + row
        q = n % 4
        v.act[at:at + size, q * d:(q + 1) * d] = value[done:done + size].astype(LOW)
        done += size


def place_tasks(v, g, start, per_image):
    experts, d = per_image[0].shape
    for j in range(v.router1.shape[0]):
        mine = [jnp.where(v.task[i] == j, per_image[i], 0.0) for i in range(2)]
        total = mine[0] + mine[1]
        if experts < 16:
            total = jnp.concatenate([total, jnp.zeros((16 - experts, d), F32)], 0)
        place_rows(v, g, start + 16 * j, total)


def back_first(v, i):
    count, d = v.tok.shape
    half = count // 2
    heads = v.heads.shape[1]
    experts = v.router2.shape[1]
    rows = slice(i * half, (i + 1) * half)
    grad_gates = jnp.concatenate([v.dg[g, j, 0:1, rows] for g in range(8) for j in range(2)], 0)
    gates = v.g2[:, rows]
    grad_logits = gates * (grad_gates - jnp.sum(gates * grad_gates, 0, keepdims=True))
    grad_logits = grad_logits[0:experts].astype(LOW)
    gain = v.gain[1:2]
    grad = own_sum(v, i, 0) + dot_tn(grad_logits, v.router2[v.task[i]])
    normal, scale = center(v.mid[rows, :])
    grad_gain = jnp.sum(grad * normal, 0, keepdims=True)
    grad_bias = jnp.sum(grad, 0, keepdims=True)
    if i == 0:
        v.small[0, 1:2, :] = grad_gain
        v.small[0, 3:4, :] = grad_bias
    else:
        v.small[0, 1:2, :] = v.small[0, 1:2, :] + grad_gain
        v.small[0, 3:4, :] = v.small[0, 3:4, :] + grad_bias
    total = v.cot[i].astype(F32) + center_back(grad, normal, scale, gain)
    v.gtok[rows, :] = total
    low = total.astype(LOW)
    v.act[rows, BRANCH:BRANCH + d] = low
    v.act[rows, 0:heads] = dot_nt(low, v.wo[...]).astype(LOW)
    return dot(grad_logits, v.n2[i])


def back_middle(v, per_image):
    count, d = v.tok.shape
    place_rows(v, 0, 0, dot_tn(v.heads[...], v.act[0:count, BRANCH:BRANCH + d]))
    place_tasks(v, 0, v.heads.shape[1], per_image)


def back_attention(v, i, pause):
    count, d = v.tok.shape
    half = count // 2
    heads = v.heads.shape[1]
    head = v.kv.shape[2] // 2
    picks = v.pick.shape[1]
    experts = v.router1.shape[1]
    to_query, to_value = head_maps(heads // head, head)
    owner = lax.div(lax.broadcasted_iota(jnp.int32, (half, heads), 1), head).astype(F32)
    lane = lax.broadcasted_iota(jnp.int32, (half, experts), 1).astype(F32)
    rows = slice(i * half, (i + 1) * half)
    lower = slice(count + i * half, count + (i + 1) * half)
    kv = v.kv[i]
    gates = v.g1[rows, :]
    grad_gates = jnp.zeros((half, experts), F32)
    grad_pair = jnp.zeros((2 * head, 4 * half), F32)
    for k in range(picks):
        at = picks * i + k
        mine = owner == v.pickc[i, :, k:k + 1]
        named = lane == v.pickc[i, :, k:k + 1]
        gate = jnp.sum(jnp.where(named, gates, 0.0), 1, keepdims=True)
        grad_heads = v.act[rows, 0:heads]
        grad = dot(jnp.where(mine, grad_heads, jnp.zeros_like(grad_heads)), to_value)
        attended = v.att[at]
        total = attended[:, 0:1]
        grad_gates = grad_gates + jnp.where(named, jnp.sum(grad * attended, 1, keepdims=True), 0.0)
        grad = ((gate * grad).astype(LOW).astype(F32) / total).astype(LOW)
        inner = jnp.sum(grad.astype(F32) * attended, 1, keepdims=True)
        expo = v.gh[at * half:(at + 1) * half, 0:4 * half]
        grad_scores = (expo.astype(F32) * (dot_nt(grad, kv) - inner)).astype(LOW)
        grad_query = (dot(grad_scores, kv) * head ** -0.5).astype(LOW)
        spread = dot_nt(grad_query, to_query).astype(LOW)
        if k == 0:
            v.act[lower, 0:heads] = jnp.where(mine, spread, jnp.zeros_like(spread))
        else:
            v.act[lower, 0:heads] = jnp.where(mine, spread, v.act[lower, 0:heads])
        grad_pair = grad_pair + dot(v.q8[at].astype(F32).T.astype(LOW), grad_scores)
        grad_pair = grad_pair + dot(grad.astype(F32).T.astype(LOW), expo)
        pause(i, k)
    grad_logits = gates * (grad_gates - jnp.sum(gates * grad_gates, 1, keepdims=True))
    v.gl1[rows, :] = grad_logits.astype(LOW)
    for r in range(4):
        v.dkv[r, i] = grad_pair[:, r * half:(r + 1) * half].astype(LOW)


def pair_copy(v, p, r, i):
    return remote(v.dkv.at[r, i], v.din.at[r, i], v.ps.at[r, i], v.pr_sem.at[r, i], p.peer(r))


def pair_sum(v, i):
    pair = v.dkv[0, i].astype(F32)
    for r in (1, 2, 3):
        pair = pair + v.din[r, i].astype(F32)
    return pair


def back_query(v):
    count, d = v.tok.shape
    half = count // 2
    heads = v.heads.shape[1]
    width = v.kv.shape[2]
    grad = dot_tn(v.act[count:2 * count, 0:heads], v.n1[...])
    place_rows(v, 1, 0, grad[0:SPLIT])
    place_rows(v, 2, 0, grad[SPLIT:heads])
    rows = (slice(0, half), slice(half, count))
    per_image = [dot_tn(v.gl1[at, :], v.n1[at, :]) for at in rows]
    place_tasks(v, 2, heads - SPLIT + width, per_image)


def back_pair(v):
    count, d = v.tok.shape
    half = count // 2
    grad = dot(pair_sum(v, 0).astype(LOW), v.n1[0:half, :])
    grad = grad + dot(pair_sum(v, 1).astype(LOW), v.n1[half:count, :])
    place_rows(v, 2, v.heads.shape[1] - SPLIT, grad)


def back_last(v):
    count, d = v.tok.shape
    half = count // 2
    heads = v.heads.shape[1]
    gain = v.gain[0:1]
    grad_gain = jnp.zeros((1, d), F32)
    grad_bias = jnp.zeros((1, d), F32)
    for i in range(2):
        rows = slice(i * half, (i + 1) * half)
        lower = slice(count + i * half, count + (i + 1) * half)
        grad = dot(v.act[lower, 0:heads], v.wq[...])
        grad = grad + dot(pair_sum(v, i).T.astype(LOW), v.wkv[...])
        grad = grad + dot(v.gl1[rows, :], v.router1[v.task[i]])
        normal, scale = center(v.tok[rows, :].astype(F32))
        grad_gain = grad_gain + jnp.sum(grad * normal, 0, keepdims=True)
        grad_bias = grad_bias + jnp.sum(grad, 0, keepdims=True)
        v.gtok[rows, :] = v.gtok[rows, :] + center_back(grad, normal, scale, gain)
    v.small[0, 0:1, :] = grad_gain
    v.small[0, 2:3, :] = grad_bias


def count_usage(v):
    count, d = v.tok.shape
    half = count // 2
    picks = v.pick.shape[1]
    number = lax.broadcasted_iota(jnp.int32, (16, half), 0)
    task = lax.broadcasted_iota(jnp.int32, (16, 128), 1)
    v.small[0] = jnp.zeros_like(v.small[0])
    for which in range(2):
        table = jnp.zeros((16, 128), F32)
        for i in range(2):
            named = jnp.zeros((16, half), F32)
            for k in range(picks):
                if which == 0:
                    row = v.pick[i, k:k + 1, :]
                else:
                    row = v.pickt[k:k + 1, i * half:(i + 1) * half]
                named = named + jnp.where(number == row, 1.0, 0.0)
            table = table + jnp.where(task == v.task[i], jnp.sum(named, 1, keepdims=True), 0.0)
        v.small[0, 8 + 16 * which:24 + 16 * which, 0:128] = table


class Shared:
    def __init__(self, v, p, g):
        self.v, self.p, self.g = v, p, g
        core, mine = p.core, p.spot
        half_in, piece_in, zbuf, shared = v.half_in[g], v.piece_in[g], v.zbuf[g], v.shared[g]
        self.half_in, self.piece_in = half_in, piece_in

        def half(c):
            return v.act.at[pl.ds(pl.multiple_of(FIRST[g] + c * PIECE[g], 16), PIECE[g]), :]

        partner = p.peer(1)
        s, r = v.hs.at[g], v.hr.at[g]
        self.own_half = half(core)
        self.first = remote(half(1 - core), half_in, s.at[0], r.at[0], partner)
        beside, across = p.plane(1), p.plane(2)
        self.to_x = [
            remote(piece(v, g, core, mine ^ q), piece_in.at[n], s.at[n + 1], r.at[n + 1], beside)
            for n, q in enumerate((3, 1))
        ]
        self.own = piece(v, g, core, mine)
        self.other = piece(v, g, core, mine ^ 2)
        self.to_y = remote(self.other, piece_in.at[2], s.at[3], r.at[3], across)
        zown, zb, zc, zall = (zbuf.at[n] for n in range(4))
        self.z = (zown, zb, zc, zall)
        self.in_end = remote(zown, zb, s.at[4], r.at[4], p.toward)
        self.mid = remote(zb, zc, s.at[4], r.at[5], p.toward)
        self.out_mid = remote(zall, zall, s.at[5], r.at[6], p.outer)
        place = core * 4 + mine
        self.own_copy = pltpu.make_async_copy(zall, shared.at[place], v.osem.at[2 + g])
        self.back_y = remote(zall, shared.at[place], s.at[6], r.at[7], across)
        there = shared.at[core * 4 + (mine ^ 2)]
        self.from_y = remote(zall, there, s.at[6], r.at[7], across)
        self.back_x = [
            remote(ref, ref, s.at[7 + n], r.at[8 + n], beside)
            for n, ref in enumerate((shared.at[place], there))
        ]
        self.from_x = [
            remote(ref, ref, s.at[7 + n], r.at[8 + n], beside)
            for n, ref in enumerate(
                (shared.at[core * 4 + (mine ^ 1)], shared.at[core * 4 + (mine ^ 3)])
            )
        ]
        ours = shared.at[pl.ds(core * 4, 4)]
        theirs = shared.at[pl.ds((1 - core) * 4, 4)]
        self.last = remote(ours, ours, s.at[9], r.at[10], partner)
        self.last_in = remote(theirs, theirs, s.at[9], r.at[10], partner)

    def stage(self, n):
        v, p, g = self.v, self.p, self.g
        zown, zb, zc, zall = self.z
        if n == 0:
            self.first.start()
        if n == 1:
            self.first.wait_recv()
            own = self.own_half
            own[...] = (own[...].astype(F32) + self.half_in[...].astype(F32)).astype(LOW)
            for copy in self.to_x:
                copy.start()
        if n == 2:
            self.to_x[0].wait_recv()
            ref = self.other
            ref[...] = (ref[...].astype(F32) + self.piece_in[0].astype(F32)).astype(LOW)
            self.to_y.start()
        if n == 3:
            self.to_x[1].wait_recv()
            total = self.own[...].astype(F32) + self.piece_in[1].astype(F32)
            self.to_y.wait_recv()
            zown[...] = (total + self.piece_in[2].astype(F32)).astype(LOW)

            @pl.when(p.is_end)
            def _():
                self.in_end.start()

        if n == 4:
            @pl.when(p.is_mid)
            def _():
                self.in_end.wait_recv()
                zb[...] = (zown[...].astype(F32) + zb[...].astype(F32)).astype(LOW)
                self.mid.start()

        if n == 5:
            @pl.when(p.is_mid)
            def _():
                self.mid.wait_recv()
                zall[...] = (zb[...].astype(F32) + zc[...].astype(F32)).astype(LOW)
                self.out_mid.start()

        if n == 6:
            @pl.when(p.is_end)
            def _():
                self.out_mid.wait_recv()

            self.own_copy.start()
            self.back_y.start()
        if n == 7:
            self.own_copy.wait()
            self.from_y.wait_recv()
            for copy in self.back_x:
                copy.start()
        if n == 8:
            for copy in self.from_x:
                copy.wait_recv()
            self.last.start()
        if n == 9:
            self.last_in.wait_recv()
            for copy in [self.first, *self.to_x, self.to_y, self.back_y, *self.back_x, self.last]:
                copy.wait_send()

            @pl.when(p.is_end)
            def _():
                self.in_end.wait_send()

            @pl.when(p.is_mid)
            def _():
                self.mid.wait_send()
                self.out_mid.wait_send()


class Small:
    def __init__(self, v, p):
        self.v, self.p = v, p

        def exchange(n, device):
            return remote(v.small.at[n], v.small_in.at[n], v.ss.at[n], v.sr.at[n], device)

        self.around = [exchange(0, p.peer(1)), exchange(1, p.plane(1)), exchange(2, p.plane(2))]
        self.in_end = exchange(3, p.toward)
        self.mid = exchange(4, p.toward)
        self.out_mid = remote(v.stats, v.stats, v.ss.at[5], v.sr.at[5], p.outer)

    def stage(self, n):
        v, p = self.v, self.p
        if n == 0:
            self.around[0].start()
        if n in (1, 2, 3):
            self.around[n - 1].wait_recv()
            v.small[n] = v.small[n - 1] + v.small_in[n - 1]
            if n < 3:
                self.around[n].start()
            else:
                @pl.when(p.is_end)
                def _():
                    self.in_end.start()

        if n == 4:
            @pl.when(p.is_mid)
            def _():
                self.in_end.wait_recv()
                v.small[4] = v.small[3] + v.small_in[3]
                self.mid.start()

        if n == 5:
            @pl.when(p.is_mid)
            def _():
                self.mid.wait_recv()
                v.stats[...] = v.small[4] + v.small_in[4]
                self.out_mid.start()

        if n == 6:
            @pl.when(p.is_end)
            def _():
                self.out_mid.wait_recv()
                self.in_end.wait_send()

            @pl.when(p.is_mid)
            def _():
                self.mid.wait_send()
                self.out_mid.wait_send()

            for copy in self.around:
                copy.wait_send()


def layer_kernel(v):
    p = Place()
    v.half_in = (v.half_in0, v.half_in1, v.half_in2)
    v.piece_in = (v.piece_in0, v.piece_in1, v.piece_in2)
    v.zbuf = (v.zbuf0, v.zbuf1, v.zbuf2)
    v.shared = (v.shared0, v.shared1, v.shared2)
    v.barrier = pltpu.get_barrier_semaphore()
    for r in range(1, 8):
        pl.semaphore_signal(v.barrier, 1, device_id=p.peer(r), device_id_type=MESH)
    pl.semaphore_signal(v.barrier, 1, device_id=p.toward, device_id_type=MESH)

    @pl.when(p.is_mid)
    def _():
        pl.semaphore_signal(v.barrier, 1, device_id=p.outer, device_id_type=MESH)

    for load in weight_loads(v, p, 0):
        load.start()
    front(v, p)

    spill = pltpu.make_async_copy(v.act.at[:, pl.ds(0, v.expo.shape[1])], v.expo, v.osem.at[1])
    spill.start()
    rows_far(v, p, 0)
    row_copy(v, p, 1, 0).wait_recv()
    row_copy(v, p, 1, 1).wait_recv()
    cot_copy(v, p, 1).wait_recv()
    meta_copy(v, p, 1).wait_recv()
    dispatch(v, 0, 0)
    dispatch(v, 1, 0)
    rows_near(v, p, 1)
    for load in weight_loads(v, p, 0):
        load.wait()
    for r in (2, 4):
        meta_copy(v, p, r).wait_recv()
        dispatch(v, r, 0)
    for r in (3, 5):
        for i in range(2):
            row_forward(v, p, r - 1, i).wait_recv()
        cot_forward(v, p, r - 1).wait_recv()
        meta_copy(v, p, r).wait_recv()
        dispatch(v, r, 0)
    rows_far(v, p, 1)
    meta_copy(v, p, 6).wait_recv()
    dispatch(v, 6, 0)
    for i in range(2):
        row_forward(v, p, 6, i).wait_recv()
    cot_forward(v, p, 6).wait_recv()
    meta_copy(v, p, 7).wait_recv()
    dispatch(v, 7, 0)
    spill.wait()

    def first_columns(f, carry):
        columns(v, 0, f)
        weight_grads(v, p, 0, f)

        return carry

    lax.fori_loop(0, 6, first_columns, 0)
    tick(v, p, 0)

    def first_produce(n, carry):
        produce(v, n, 0)
        tick(v, p, 1 + n)
        return carry

    lax.fori_loop(0, 2, first_produce, 0)
    for load in weight_loads(v, p, 1):
        load.start()

    def second_dispatch(r, carry):
        dispatch(v, r, 1)
        return carry

    lax.fori_loop(0, 8, second_dispatch, 0)
    tick(v, p, 3)
    for i in range(2):
        for r in (1, 2, 4):
            row_copy(v, p, r, i).wait_send()
        for r in (2, 4):
            row_relay(v, p, r, i).wait_send()
        for r in (2, 4, 6):
            row_forward(v, p, r, i).wait_send()
    pl.semaphore_signal(v.free_core, 1, device_id=p.peer(1), device_id_type=MESH)
    for load in weight_loads(v, p, 1):
        load.wait()

    def second_columns(f, carry):
        columns(v, 1, f)

        @pl.when(lax.rem(f, 2) == 1)
        def _():
            tick(v, p, 4 + lax.div(f, 2))

        return carry

    lax.fori_loop(0, 6, second_columns, 0)

    def second_produce(n, carry):
        produce(v, n, 1)
        tick(v, p, 7 + n)
        return carry

    lax.fori_loop(0, 2, second_produce, 0)
    for r in range(1, 8):
        gate_copy(v, p, r).start()
    v.dg[p.group(0)] = v.dgs[0]
    for r in (1, 2, 4):
        cot_copy(v, p, r).wait_send()
    for r in (2, 4):
        cot_relay(v, p, r).wait_send()
    for r in (2, 4, 6):
        cot_forward(v, p, r).wait_send()
    for q in (1, 2):
        pl.semaphore_signal(v.free_plane, 1, device_id=p.plane(q), device_id_type=MESH)
    pl.semaphore_wait(v.free_core, 1)
    pl.semaphore_wait(v.free_plane, 2)
    send_parts(v, p, 0)
    tick(v, p, 9)

    def second_grads(f, carry):
        weight_grads(v, p, 1, f)
        return carry

    lax.fori_loop(0, 6, second_grads, 0)
    refill = pltpu.make_async_copy(v.expo, v.gh.at[:, pl.ds(0, v.expo.shape[1])], v.osem.at[1])
    refill.start()
    relay_parts(v, p, 0, 0)
    tick(v, p, 10)
    send_parts(v, p, 1)
    tick(v, p, 11)
    count_usage(v)
    v.act[FIRST[0]:FIRST[2] + 2 * PIECE[2], :] = jnp.zeros(
        (2 * sum(PIECE), v.act.shape[1]), LOW
    )
    for r in range(1, 8):
        gate_copy(v, p, r).wait_recv()
    part_y(v, p, 0, 0).wait_recv()
    per_image = [back_first(v, 0)]
    relay_parts(v, p, 0, 1)
    for i in range(2):
        for r in (6, 2):
            part_x(v, p, r, 1, i).start()
    tick(v, p, 12)
    refill.wait()
    early, late, rest = Shared(v, p, 0), Shared(v, p, 1), Shared(v, p, 2)
    small = Small(v, p)

    def pause(i, k):
        at = 4 * i + k
        if at == 1:
            tick(v, p, 13)
        if at == 3:
            tick(v, p, 14)
        if at == 5:
            early.stage(1)
            tick(v, p, 17)
        if at == 7:
            tick(v, p, 18)

    back_attention(v, 0, pause)
    for r in (1, 2, 3):
        pair_copy(v, p, r, 0).start()
    part_y(v, p, 0, 1).wait_recv()
    per_image.append(back_first(v, 1))
    tick(v, p, 15)
    back_middle(v, per_image)
    early.stage(0)
    tick(v, p, 16)
    back_attention(v, 1, pause)
    for r in (1, 2, 3):
        pair_copy(v, p, r, 1).start()
    back_query(v)
    late.stage(0)
    early.stage(2)
    tick(v, p, 19)
    late.stage(1)
    for i in range(2):
        for r in (1, 2, 3):
            pair_copy(v, p, r, i).wait_recv()
    back_pair(v)
    rest.stage(0)
    early.stage(3)
    back_last(v)
    small.stage(0)
    rest.stage(1)
    late.stage(2)
    tick(v, p, 20)
    small.stage(1)
    early.stage(4)
    rest.stage(2)
    late.stage(3)
    relay_parts(v, p, 1, 0)
    tick(v, p, 21)
    small.stage(2)
    early.stage(5)
    rest.stage(3)
    late.stage(4)
    relay_parts(v, p, 1, 1)
    tick(v, p, 22)
    small.stage(3)
    early.stage(6)
    rest.stage(4)
    late.stage(5)
    tick(v, p, 23)
    small.stage(4)
    rest.stage(5)
    late.stage(6)
    tick(v, p, 24)
    small.stage(5)
    early.stage(7)
    rest.stage(6)
    late.stage(7)
    for i in range(2):
        part_y(v, p, 1, i).wait_recv()
        rows = slice(i * CAP, (i + 1) * CAP)
        v.out[rows, :] = (v.mid[rows, :] + own_sum(v, i, 1)).astype(LOW)
    tick(v, p, 25)
    small.stage(6)
    early.stage(8)
    rest.stage(7)
    late.stage(8)
    ticks(v, p, 26, 28)
    rest.stage(8)
    early.stage(9)
    late.stage(9)
    ticks(v, p, 28, v.ra.shape[0] + HAND)
    rest.stage(9)

    for i in range(2):
        for r in (1, 2, 3):
            pair_copy(v, p, r, i).wait_send()
    for r in (1, 2):
        kv_copy(v, p, r).wait_send()
    kv_forward(v, p).wait_send()
    for r in range(1, 8):
        meta_copy(v, p, r).wait_send()
        gate_copy(v, p, r).wait_send()
    for which in range(2):
        for r in (1, 3, 5, 7):
            part_core(v, p, r, which).wait_send()
        for i in range(2):
            for r in (2, 6):
                part_x(v, p, r, which, i).wait_send()
            part_y(v, p, which, i).wait_send()
    chunks_done(v, p)


def layer_call(tok, cot, pick, pickt, task, gain, bias, wq, wk, wv, wo, router1, router2, we, wr):
    count, d = tok.shape
    half = count // 2
    heads = wq.shape[0]
    width = 2 * wk.shape[0]
    picks = pick.shape[1]
    experts = router1.shape[1]
    ff = we.shape[2]
    chunks = 4 * ff // 256
    vm = pltpu.VMEM
    anywhere = pl.ANY
    dma = pltpu.SemaphoreType.DMA
    return run_kernel(
        layer_kernel, "layer",
        dict(
            tok=(tok, vm), cot=(cot, vm), pick=(pick, vm), pickt=(pickt, vm),
            task=(task, pltpu.SMEM), gain=(gain, vm), bias=(bias, vm), wq=(wq, vm), wk=(wk, vm),
            wv=(wv, vm), wo=(wo, vm), router1=(router1, vm), router2=(router2, vm),
            we_all=(we, anywhere), wr_all=(wr, anywhere),
        ),
        dict(
            out=((count, d), LOW, vm), gtok=((count, d), F32, vm),
            chunks=((2 * chunks, d, 256), LOW, anywhere),
            **{f"shared{g}": ((8, PIECE[g], d), LOW, anywhere) for g in range(3)},
            stats=((40, d), F32, vm), expo=((8 * CAP, 4 * half), LOW, anywhere),
        ),
        dict(
            n1=vm((count, d), LOW), n2=vm((2, half, d), LOW), mid=vm((count, d), F32),
            pickc=vm((2, half, 8), F32), wkv=vm((width, d), LOW),
            heads=vm((count, heads), LOW), kv=vm((2, 4 * half, width), LOW),
            q8=vm((2 * picks, half, width), LOW), att=vm((2 * picks, half, width), F32),
            g1=vm((count, experts), F32), g2=vm((16, count), F32), meta=vm((8, 16, count), F32),
            xa=vm((8, 2, half, d), LOW), ca=vm((8, 2, half, d), LOW),
            ma=vm((8, 16, count), F32), we=vm((d, ff), LOW), wr=vm((ff, d), LOW),
            xrt=vm((d, 8 * CAP), LOW), gpt=vm((d, 8 * CAP), LOW),
            act=vm((8 * CAP, ff), LOW), gh=vm((8 * CAP, ff), LOW),
            pr=vm((2, 8 * CAP, d), LOW), gr=vm((2, 8 * CAP, d), LOW),
            ra=vm((chunks, d, 256), LOW), rb=vm((chunks, d, 256), LOW), rc=vm((chunks, d, 256), LOW),
            dgs=vm((8, 2, 8, count), F32), dg=vm((8, 2, 8, count), F32),
            small=vm((5, 40, d), F32), small_in=vm((5, 40, d), F32),
            gl1=vm((count, experts), LOW),
            dkv=vm((4, 2, width, half), LOW), din=vm((4, 2, width, half), LOW),
            **{f"half_in{g}": vm((PIECE[g], 4 * d), LOW) for g in range(3)},
            **{f"piece_in{g}": vm((3, PIECE[g], d), LOW) for g in range(3)},
            **{f"zbuf{g}": vm((4, PIECE[g], d), LOW) for g in range(3)},
            cs=dma((16,)), cv=dma((16,)), ks=dma((4,)), kr=dma((4,)), xs=dma((16, 2)), xv=dma((16, 2)),
            ms=dma((8,)), mv=dma((8,)), gs=dma((8,)), gv=dma((8,)), wsem=dma((2,)), osem=dma((5,)),
            s1s=dma((chunks,)), s1r=dma((chunks,)), s2s=dma((chunks,)), s2r=dma((chunks,)),
            s3s=dma((chunks,)), ys=dma((chunks,)), yr=dma((chunks,)), y2s=dma((chunks,)), ls=dma((chunks,)),
            k1s=dma((8,)), k1r=dma((8,)), k2s=dma((8, 2)), k2r=dma((8, 2)),
            ps=dma((4, 2)), pr_sem=dma((4, 2)), ss=dma((6,)), sr=dma((6,)), hs=dma((3, 10)),
            hr=dma((3, 11)),
            free_core=pltpu.SemaphoreType.REGULAR, free_plane=pltpu.SemaphoreType.REGULAR,
        ),
        0,
    )


def widen_kernel(
    c_ref, s0_ref, s1_ref, s2_ref, stats_ref,
    reduce_ref, expand_ref, query_ref, out_ref, key_ref, value_ref, one_ref, two_ref,
    gain_ref, first_ref, second_ref, usage_ref,
):
    for n in range(c_ref.shape[0] // 2):
        at = slice(n * 256, (n + 1) * 256)
        reduce_ref[0, at, :] = c_ref[2 * n].astype(F32).T
        expand_ref[0, :, at] = c_ref[2 * n + 1].astype(F32)

    @pl.when((pl.program_id(0) == 0) & (pl.program_id(1) == 0))
    def _():
        refs = (s0_ref, s1_ref, s2_ref)

        def unpack(ref, g, start):
            done = 0
            for n, row, size in spans(g, start, ref.shape[0]):
                ref[done:done + size, :] = refs[g][n, row:row + size, :].astype(F32)
                done += size

        wide, head = query_ref.shape[0], key_ref.shape[0]
        unpack(out_ref, 0, 0)
        unpack(query_ref.at[0:SPLIT, :], 1, 0)
        unpack(query_ref.at[SPLIT:wide, :], 2, 0)
        unpack(key_ref, 2, wide - SPLIT)
        unpack(value_ref, 2, wide - SPLIT + head)
        for ref, g, start in ((one_ref, 2, wide - SPLIT + 2 * head), (two_ref, 0, wide)):
            for j in range(ref.shape[0]):
                for n, row, size in spans(g, start + 16 * j, 16):
                    ref[j] = refs[g][n, row:row + size, :].astype(F32)[0:ref.shape[1]]
        gain_ref[...] = stats_ref[0:2, :]
        first_ref[...] = stats_ref[2, :]
        second_ref[...] = stats_ref[3, :]
        tasks, _, experts = usage_ref.shape
        for which in range(2):
            table = stats_ref[8 + 16 * which:24 + 16 * which, 0:128].T
            usage_ref[:, which, :] = table[0:tasks, 0:experts]


def widen_call(chunks, shared, stats, slots, d, ff, wide, head, tasks, experts):
    n = ff // 256
    per = PER
    whole = pl.BlockSpec(memory_space=pltpu.VMEM)
    shapes = (
        (wide, d), (wide, d), (head, d), (head, d), (tasks, experts, d), (tasks, experts, d),
        (2, d), (d,), (d,), (tasks, 2, experts),
    )
    return pl.pallas_call(
        widen_kernel,
        name="widen",
        grid=(slots, n // per),
        in_specs=[
            pl.BlockSpec((2 * per, d, 256), lambda s, f: (s * (n // per) + f, 0, 0)),
            whole, whole, whole, whole,
        ],
        out_specs=(
            pl.BlockSpec((1, per * 256, d), lambda s, f: (s, f, 0)),
            pl.BlockSpec((1, d, per * 256), lambda s, f: (s, 0, f)),
            *[whole] * len(shapes),
        ),
        out_shape=(
            jax.ShapeDtypeStruct((slots, ff, d), F32),
            jax.ShapeDtypeStruct((slots, d, ff), F32),
            *[jax.ShapeDtypeStruct(shape, F32) for shape in shapes],
        ),
        compiler_params=pltpu.CompilerParams(vmem_limit_bytes=56 * MIB),
    )(chunks, *shared, stats)


def body_fast(
    tokens,
    task_ids,
    attention_picks,
    feedforward_picks,
    norm_gain,
    norm_bias,
    query_weight,
    key_weight,
    value_weight,
    output_weight,
    attention_router,
    feedforward_router,
    expand_weight,
    reduce_weight,
    cotangent,
):
    images, patches, width = tokens.shape
    count = images * patches
    tasks, _, experts = attention_router.shape
    head = key_weight.shape[1]
    picks = attention_picks.shape[2]
    slots = expand_weight.shape[0]
    ff = expand_weight.shape[2]
    wide = query_weight.shape[1]
    tok = tokens.reshape(count, width)
    pickt = feedforward_picks.reshape(count, picks).T
    b = layer_call(
        tok, cotangent, jnp.swapaxes(attention_picks, 1, 2), pickt, task_ids, norm_gain, norm_bias,
        query_weight.T, key_weight.T, value_weight.T, output_weight,
        jnp.swapaxes(attention_router, 1, 2), jnp.swapaxes(feedforward_router, 1, 2),
        expand_weight, reduce_weight,
    )
    (
        grad_reduce, grad_expand, grad_query, grad_out, grad_key, grad_value, grad_one, grad_two,
        grad_gain, grad_first, grad_second, usage,
    ) = widen_call(
        b.chunks, (b.shared0, b.shared1, b.shared2), b.stats, slots, width, ff, wide, head, tasks,
        experts,
    )
    return (
        b.out.reshape(images, patches, width),
        b.gtok.reshape(images, patches, width),
        grad_gain,
        grad_first,
        grad_second,
        grad_query.T,
        grad_key.T,
        grad_value.T,
        grad_out,
        jnp.swapaxes(grad_one, 1, 2),
        jnp.swapaxes(grad_two, 1, 2),
        grad_expand,
        grad_reduce,
        jnp.swapaxes(usage, 0, 1),
    )


def normalize(value, gain, bias):
    mean = jnp.mean(value, -1, keepdims=True)
    centred = value - mean
    spread = jnp.mean(centred * centred, -1, keepdims=True)
    return centred * lax.rsqrt(spread + EPS) * gain + bias


def gate_weights(logits, picks_hot):
    chosen = jnp.sum(picks_hot * logits[..., None, :], -1)
    return jax.nn.softmax(chosen, -1)


def activate(value):
    return jax.nn.gelu(value, approximate=True)


def body(
    tokens,
    task_ids,
    attention_picks,
    feedforward_picks,
    norm_gain,
    norm_bias,
    query_weight,
    key_weight,
    value_weight,
    output_weight,
    attention_router,
    feedforward_router,
    expand_weight,
    reduce_weight,
    cotangent,
):
    images, patches, width = tokens.shape
    count = images * patches
    tasks = attention_router.shape[0]
    experts = attention_router.shape[2]
    head = key_weight.shape[1]
    picks = attention_picks.shape[2]
    slots = expand_weight.shape[0]
    groups = lax.axis_size("expert")
    lanes = groups * slots
    f32 = jnp.float32
    low_type = jnp.bfloat16
    inputs = tokens.astype(f32).reshape(count, width)
    expert_range = jnp.arange(experts, dtype=jnp.int32)
    task_hot = (task_ids[:, None] == jnp.arange(tasks, dtype=jnp.int32)[None, :]).astype(f32)
    task_low = task_hot.astype(low_type)
    attend_hot = (attention_picks[..., None] == expert_range).astype(f32)
    attend_low = attend_hot.astype(low_type)
    choices = feedforward_picks.reshape(count, picks)
    feed_hot = (choices[..., None] == expert_range).astype(f32)
    flat = choices.reshape(count * picks)
    marks = (flat[:, None] == expert_range[None, :]).astype(jnp.int32)
    before = jnp.cumsum(marks, axis=0) - marks
    position = flat * CAP + jnp.sum(before * marks, axis=1)
    first, first_back = jax.vjp(normalize, inputs, norm_gain[0], norm_bias[0])
    normed_one = first.astype(low_type)
    shaped_one = normed_one.reshape(images, patches, width)
    router_one = jnp.einsum(
        "it,tde->ide", task_low, attention_router, preferred_element_type=f32
    ).astype(low_type)
    logits_one = jnp.einsum("ipd,ide->ipe", shaped_one, router_one, preferred_element_type=f32)
    gates_one, gates_one_back = jax.vjp(lambda value: gate_weights(value, attend_hot), logits_one)
    queries_all = jnp.dot(normed_one, query_weight, preferred_element_type=f32).astype(low_type)
    queries_all = queries_all.reshape(images, patches, experts, head)
    queries = jnp.einsum(
        "ipke,ipeh->ipkh", attend_low, queries_all, preferred_element_type=f32
    ).astype(low_type)
    queries = queries.reshape(images, patches * picks, head)
    key_value = jnp.concatenate([key_weight, value_weight], 1)
    pair = jnp.dot(normed_one, key_value, preferred_element_type=f32).astype(low_type)
    pair = pair.reshape(images, patches, 2 * head)
    pair_all = lax.all_gather(pair, "expert", axis=1, tiled=True)
    keys_all = pair_all[:, :, :head]
    values_all = pair_all[:, :, head:]
    scores = jnp.einsum("irh,ish->irs", queries, keys_all, preferred_element_type=f32) * 0.125
    top = jnp.max(scores, -1, keepdims=True)
    expo = jnp.exp(scores - top)
    total = jnp.sum(expo, -1, keepdims=True)
    log_total = top + jnp.log(total)
    probs_low = (expo / total).astype(low_type)
    attended = jnp.einsum("irs,ish->irh", probs_low, values_all, preferred_element_type=f32)
    attended = attended.reshape(images, patches, picks, head)
    weighted = gates_one[..., None] * attended
    heads = jnp.einsum("ipke,ipkh->ipeh", attend_hot, weighted, precision=HIGH)
    heads = heads.reshape(count, experts * head).astype(low_type)
    middle = inputs + jnp.dot(heads, output_weight, preferred_element_type=f32)
    second, second_back = jax.vjp(normalize, middle, norm_gain[1], norm_bias[1])
    normed_two = second.astype(low_type)
    shaped_two = normed_two.reshape(images, patches, width)
    router_two = jnp.einsum(
        "it,tde->ide", task_low, feedforward_router, preferred_element_type=f32
    ).astype(low_type)
    logits_two = jnp.einsum(
        "ipd,ide->ipe", shaped_two, router_two, preferred_element_type=f32
    ).reshape(count, experts)
    gates_two, gates_two_back = jax.vjp(lambda value: gate_weights(value, feed_hot), logits_two)
    outgoing = (
        jnp.zeros((lanes * CAP, width), low_type)
        .at[position]
        .set(jnp.repeat(normed_two, picks, axis=0))
    )
    outgoing = outgoing.reshape(groups, slots * CAP, width)
    received = lax.all_to_all(outgoing, "expert", split_axis=0, concat_axis=0, tiled=True).reshape(
        groups, slots, CAP, width
    )
    hidden = jnp.einsum("nscd,sdf->nscf", received, expand_weight, preferred_element_type=f32)
    activated, activate_back = jax.vjp(activate, hidden)
    active_low = activated.astype(low_type)
    produced = jnp.einsum(
        "nscf,sfd->nscd", active_low, reduce_weight, preferred_element_type=f32
    ).astype(low_type)
    produced = produced.reshape(groups, slots * CAP, width)
    returned = lax.all_to_all(produced, "expert", split_axis=0, concat_axis=0, tiled=True).reshape(
        lanes * CAP, width
    )
    picked = returned[position].astype(f32).reshape(count, picks, width)
    final = middle + jnp.sum(gates_two[..., None] * picked, 1)
    output = final.astype(low_type).reshape(images, patches, width)
    grad_final = cotangent.astype(f32).reshape(count, width)
    grad_gates_two = jnp.sum(picked * grad_final[:, None, :], -1)
    grad_picked = (
        (gates_two[..., None] * grad_final[:, None, :])
        .astype(low_type)
        .reshape(count * picks, width)
    )
    grad_send = jnp.zeros((lanes * CAP, width), low_type).at[position].set(grad_picked)
    grad_send = grad_send.reshape(groups, slots * CAP, width)
    grad_produced = lax.all_to_all(
        grad_send, "expert", split_axis=0, concat_axis=0, tiled=True
    ).reshape(groups, slots, CAP, width)
    grad_reduce = jnp.einsum(
        "nscf,nscd->sfd", active_low, grad_produced, preferred_element_type=f32
    )
    grad_active = jnp.einsum(
        "nscd,sfd->nscf", grad_produced, reduce_weight, preferred_element_type=f32
    )
    grad_hidden = activate_back(grad_active)[0].astype(low_type)
    grad_expand = jnp.einsum("nscd,nscf->sdf", received, grad_hidden, preferred_element_type=f32)
    grad_rows = jnp.einsum(
        "nscf,sdf->nscd", grad_hidden, expand_weight, preferred_element_type=f32
    ).astype(low_type)
    grad_rows = grad_rows.reshape(groups, slots * CAP, width)
    grad_back = lax.all_to_all(
        grad_rows, "expert", split_axis=0, concat_axis=0, tiled=True
    ).reshape(lanes * CAP, width)
    grad_normed_two = jnp.sum(grad_back[position].astype(f32).reshape(count, picks, width), 1)
    grad_logits_two = (
        gates_two_back(grad_gates_two)[0].astype(low_type).reshape(images, patches, experts)
    )
    per_image_two = jnp.einsum(
        "ipd,ipe->ide", shaped_two, grad_logits_two, preferred_element_type=f32
    )
    grad_feed_router = jnp.einsum("it,ide->tde", task_hot, per_image_two, precision=HIGH)
    grad_normed_two = grad_normed_two + jnp.einsum(
        "ipe,ide->ipd", grad_logits_two, router_two, preferred_element_type=f32
    ).reshape(count, width)
    grad_middle_norm, grad_gain_two, grad_bias_two = second_back(grad_normed_two)
    grad_middle = grad_final + grad_middle_norm
    grad_branch = grad_middle.astype(low_type)
    grad_output = jnp.einsum("tc,td->cd", heads, grad_branch, preferred_element_type=f32)
    grad_heads = jnp.einsum(
        "td,cd->tc", grad_branch, output_weight, preferred_element_type=f32
    ).astype(low_type)
    grad_heads = grad_heads.reshape(images, patches, experts, head)
    grad_selected = jnp.einsum(
        "ipke,ipeh->ipkh", attend_low, grad_heads, preferred_element_type=f32
    )
    grad_gates_one = jnp.sum(attended * grad_selected, -1)
    grad_attended = (
        (gates_one[..., None] * grad_selected)
        .astype(low_type)
        .reshape(images, patches * picks, head)
    )
    scores_back = jnp.einsum("irh,ish->irs", queries, keys_all, preferred_element_type=f32) * 0.125
    probs_back = jnp.exp(scores_back - log_total)
    grad_values = jnp.einsum(
        "irs,irh->ish", probs_back.astype(low_type), grad_attended, preferred_element_type=f32
    )
    grad_probs = jnp.einsum("irh,ish->irs", grad_attended, values_all, preferred_element_type=f32)
    inner_sum = jnp.sum(probs_back * grad_probs, -1, keepdims=True)
    grad_scores = (probs_back * (grad_probs - inner_sum)).astype(low_type)
    grad_query_sel = (
        jnp.einsum("irs,ish->irh", grad_scores, keys_all, preferred_element_type=f32) * 0.125
    )
    grad_keys = jnp.einsum("irs,irh->ish", grad_scores, queries, preferred_element_type=f32) * 0.125
    grad_pair = jnp.concatenate([grad_keys, grad_values], -1)
    pair_sum = lax.psum_scatter(
        grad_pair.astype(jnp.bfloat16), "expert", scatter_dimension=1, tiled=True
    ).astype(jnp.float32)
    pair_sum = pair_sum.astype(low_type).reshape(count, 2 * head)
    grad_query_sel = grad_query_sel.reshape(images, patches, picks, head)
    grad_queries_all = jnp.einsum("ipke,ipkh->ipeh", attend_hot, grad_query_sel, precision=HIGH)
    grad_queries_all = grad_queries_all.astype(low_type).reshape(count, experts * head)
    grad_logits_one = gates_one_back(grad_gates_one)[0].astype(low_type)
    per_image_one = jnp.einsum(
        "ipd,ipe->ide", shaped_one, grad_logits_one, preferred_element_type=f32
    )
    grad_attend_router = jnp.einsum("it,ide->tde", task_hot, per_image_one, precision=HIGH)
    grad_query = jnp.einsum("td,tc->dc", normed_one, grad_queries_all, preferred_element_type=f32)
    grad_key_value = jnp.einsum("td,tc->dc", normed_one, pair_sum, preferred_element_type=f32)
    grad_normed_one = jnp.einsum(
        "tc,dc->td", grad_queries_all, query_weight, preferred_element_type=f32
    )
    grad_normed_one = grad_normed_one + jnp.einsum(
        "tc,dc->td", pair_sum, key_value, preferred_element_type=f32
    )
    grad_normed_one = grad_normed_one + jnp.einsum(
        "ipe,ide->ipd", grad_logits_one, router_one, preferred_element_type=f32
    ).reshape(count, width)
    grad_inputs_norm, grad_gain_one, grad_bias_one = first_back(grad_normed_one)
    grad_tokens = (grad_middle + grad_inputs_norm).reshape(images, patches, width)
    grad_gain = jnp.stack([grad_gain_one, grad_gain_two])
    grad_bias = jnp.stack([grad_bias_one, grad_bias_two])
    feed_shaped = feed_hot.reshape(images, patches, picks, experts)
    usage = jnp.stack(
        [
            jnp.einsum("it,ipke->te", task_hot, attend_hot, precision=HIGH),
            jnp.einsum("it,ipke->te", task_hot, feed_shaped, precision=HIGH),
        ]
    )
    shared = lax.psum(
        (
            grad_query,
            grad_key_value,
            grad_output,
            grad_attend_router,
            grad_feed_router,
            grad_gain,
            grad_bias,
            usage,
        ),
        ("dp", "expert"),
    )
    grad_expand_sum, grad_reduce_sum = (
        lax.psum(grad_expand.astype(jnp.bfloat16), "dp").astype(jnp.float32),
        lax.psum(grad_reduce.astype(jnp.bfloat16), "dp").astype(jnp.float32),
    )
    grad_key_sum = shared[1][:, :head]
    grad_value_sum = shared[1][:, head:]
    return (
        output,
        grad_tokens,
        shared[5],
        shared[6][0],
        shared[6][1],
        shared[0],
        grad_key_sum,
        grad_value_sum,
        shared[2],
        shared[3],
        shared[4],
        grad_expand_sum,
        grad_reduce_sum,
        shared[7],
    )


def solution(mesh):
    placed = (
        P("dp", "expert", None),
        P("dp"),
        P("dp", "expert", None),
        P("dp", "expert", None, None),
        P(),
        P(),
        P(),
        P(),
        P(),
        P(),
        P(),
        P(),
        P("expert", None, None),
        P("expert", None, None),
        P("dp", "expert", None),
    )
    fast = mesh.shape["dp"] == 8 and mesh.shape["expert"] == 4
    return jax.shard_map(
        body_fast if fast else body,
        mesh=mesh,
        in_specs=placed,
        out_specs=(
            P("dp", "expert", None),
            P("dp", "expert", None),
            P(),
            P(),
            P(),
            P(),
            P(),
            P(),
            P(),
            P(),
            P(),
            P("expert", None, None),
            P("expert", None, None),
            P(),
        ),
        check_vma=False,
    )
```

```python
import types

import jax
import jax.numpy as jnp
from jax import lax
from jax.experimental import pallas as pl
from jax.experimental.pallas import tpu as pltpu
from jax.sharding import PartitionSpec as P

CAP = 256


EPS = 1e-06
HIGH = lax.Precision.HIGHEST
F32 = jnp.float32
LOW = jnp.bfloat16
MESH = pl.DeviceIdType.MESH
MIB = 2**20


def dot(a, b):
    return jnp.dot(a, b, preferred_element_type=F32)


def dot_nt(a, b):
    return lax.dot_general(a, b, (((1,), (1,)), ((), ())), preferred_element_type=F32)


def dot_tn(a, b):
    return lax.dot_general(a, b, (((0,), (0,)), ((), ())), preferred_element_type=F32)


def remote(src, dst, send, recv, device):
    return pltpu.make_async_remote_copy(
        src_ref=src, dst_ref=dst, send_sem=send, recv_sem=recv,
        device_id=device, device_id_type=MESH,
    )


def run_kernel(kernel, name, ins, outs, scratch, collective):
    names = [*ins, *outs, *scratch]

    def body(*refs):
        kernel(types.SimpleNamespace(**dict(zip(names, refs, strict=True))))

    made = pl.pallas_call(
        body,
        name=name,
        out_shape=[jax.ShapeDtypeStruct(shape, dtype) for shape, dtype, _ in outs.values()],
        in_specs=[pl.BlockSpec(memory_space=space) for _, space in ins.values()],
        out_specs=[pl.BlockSpec(memory_space=space) for _, _, space in outs.values()],
        scratch_shapes=list(scratch.values()),
        compiler_params=pltpu.CompilerParams(
            collective_id=collective, has_side_effects=True, vmem_limit_bytes=62 * MIB
        ),
    )(*[array for array, _ in ins.values()])
    return types.SimpleNamespace(**dict(zip(outs, made, strict=True)))


def center(value):
    mean = jnp.mean(value, -1, keepdims=True)
    centred = value - mean
    scale = lax.rsqrt(jnp.mean(centred * centred, -1, keepdims=True) + EPS)
    return centred * scale, scale


def center_back(grad, normal, scale, gain):
    inner = grad * gain
    mean = jnp.mean(inner, -1, keepdims=True)
    along = jnp.mean(inner * normal, -1, keepdims=True)
    return scale * (inner - mean - normal * along)


def head_maps(heads, head):
    row = lax.broadcasted_iota(jnp.int32, (heads * head, 2 * head), 0)
    row = lax.rem(row, head)
    col = lax.broadcasted_iota(jnp.int32, (heads * head, 2 * head), 1)
    low = jnp.where(row == col, 1.0, 0.0).astype(LOW)
    high = jnp.where(row + head == col, 1.0, 0.0).astype(LOW)
    return low, high


def masked_softmax(logits, chosen, axis):
    top = jnp.max(jnp.where(chosen, logits, -1e30), axis, keepdims=True)
    expo = jnp.where(chosen, jnp.exp(jnp.minimum(logits - top, 0.0)), 0.0)
    return expo / jnp.sum(expo, axis, keepdims=True)


PIECE = (160, 80, 96)
FIRST = (1024, 1344, 1504)
SPLIT = 640
BRANCH = 1024
HAND = 6
PER = 6


def gelu_parts(value):
    square = value * value
    inner = value * (0.7978845608028654 + 0.035677408136300125 * square)
    half = 0.5 + 0.5 * jnp.tanh(inner)
    act = value * half
    slope = half + act * (1.0 - half) * (1.5957691216057308 + 0.2140644488178007 * square)
    return act, slope


class Place:
    def __init__(self):
        self.dp = dp = lax.axis_index("dp")
        self.ex = lax.axis_index("expert")
        self.y = lax.rem(dp, 2)
        z = lax.div(dp, 2)
        self.is_end = (z == 0) | (z == 3)
        self.is_mid = (z == 1) | (z == 2)
        self.toward = (jnp.where(z < 2, dp + 2, dp - 2), self.ex)
        self.outer = (jnp.where(z == 1, dp - 2, jnp.where(z == 2, dp + 2, dp)), self.ex)
        self.core = lax.rem(self.ex, 2)
        self.spot = self.y * 2 + lax.div(self.ex, 2)

    def peer(self, r):
        return (self.dp ^ lax.div(r, 4), self.ex ^ lax.rem(r, 4))

    def plane(self, q):
        return (self.dp ^ lax.div(q, 2), self.ex ^ (2 * lax.rem(q, 2)))

    def group(self, r):
        return 2 * (self.ex ^ lax.rem(r, 4)) + (self.y ^ lax.div(r, 4))


def cot_copy(v, p, r):
    return remote(v.cot, v.ca.at[r], v.cs.at[r], v.cv.at[r], p.peer(r))


def cot_relay(v, p, to):
    at = pl.ds(0 if to == 2 else CAP // 2, CAP // 2)
    return remote(
        v.ca.at[6 - to, :, at, :], v.ca.at[6, :, at, :], v.cs.at[to + 1], v.cv.at[to + 8], p.peer(to)
    )


def cot_forward(v, p, r):
    return remote(v.ca.at[r], v.ca.at[r + 1], v.cs.at[r + 6], v.cv.at[r + 1], p.peer(1))


def row_copy(v, p, r, i):
    return remote(v.n2.at[i], v.xa.at[r, i], v.xs.at[r, i], v.xv.at[r, i], p.peer(r))


def row_relay(v, p, to, i):
    at = pl.ds(0 if to == 2 else CAP // 2, CAP // 2)
    return remote(
        v.xa.at[6 - to, i, at, :], v.xa.at[6, i, at, :],
        v.xs.at[to + 1, i], v.xv.at[to + 8, i], p.peer(to),
    )


def row_forward(v, p, r, i):
    return remote(
        v.xa.at[r, i], v.xa.at[r + 1, i], v.xs.at[r + 6, i], v.xv.at[r + 1, i], p.peer(1)
    )


def cot_near(v, p):
    for r in (4, 2):
        cot_copy(v, p, r).wait_recv()
        cot_relay(v, p, 6 - r).start()
        cot_forward(v, p, r).start()


def cot_far(v, p):
    cot_relay(v, p, 2).wait_recv()
    cot_relay(v, p, 4).wait_recv()
    cot_forward(v, p, 6).start()


def rows_near(v, p, i):
    for r in (4, 2):
        row_copy(v, p, r, i).wait_recv()
        row_relay(v, p, 6 - r, i).start()
        row_forward(v, p, r, i).start()


def rows_far(v, p, i):
    row_relay(v, p, 2, i).wait_recv()
    row_relay(v, p, 4, i).wait_recv()
    row_forward(v, p, 6, i).start()


def meta_copy(v, p, r):
    return remote(v.meta.at[p.group(r)], v.ma.at[r], v.ms.at[r], v.mv.at[r], p.peer(r))


def kv_copy(v, p, r):
    half = v.kv.shape[1] // 4
    return remote(
        v.kv.at[:, pl.ds(0, half), :], v.kv.at[:, pl.ds(r * half, half), :],
        v.ks.at[r], v.kr.at[r], p.peer(r),
    )


def kv_forward(v, p):
    half = v.kv.shape[1] // 4
    return remote(
        v.kv.at[:, pl.ds(2 * half, half), :], v.kv.at[:, pl.ds(3 * half, half), :],
        v.ks.at[3], v.kr.at[3], p.peer(1),
    )


def front(v, p):
    count, d = v.tok.shape
    half = count // 2
    heads = v.heads.shape[1]
    head = v.kv.shape[2] // 2
    picks = v.pick.shape[1]
    for i in range(2):
        named = jnp.concatenate([v.pick[i].astype(F32), jnp.zeros((8 - picks, half), F32)], 0)
        v.pickc[i] = named.T
    gain = v.gain[...]
    bias = v.bias[...]
    v.wkv[0:head, :] = v.wk[...]
    v.wkv[head:2 * head, :] = v.wv[...]
    for i in range(2):
        rows = slice(i * half, (i + 1) * half)
        normal, _ = center(v.tok[rows, :].astype(F32))
        normed = (normal * gain[0:1] + bias[0:1]).astype(LOW)
        v.n1[rows, :] = normed
        v.kv[i, 0:half, :] = dot_nt(normed, v.wkv[...]).astype(LOW)
    pl.semaphore_wait(v.barrier, jnp.where(p.is_mid, 9, 8))
    for r in (2, 1):
        kv_copy(v, p, r).start()
    for r in (4, 2, 1):
        cot_copy(v, p, r).start()
    v.ca[0] = v.cot[...]
    v.gh[0:count, 0:heads] = dot_nt(v.n1[...], v.wq[...]).astype(LOW)

    experts = v.router1.shape[1]
    number = lax.broadcasted_iota(jnp.int32, (16, count), 0)
    chosen = number == v.pickt[0:1, :]
    for k in range(1, picks):
        chosen = chosen | (number == v.pickt[k:k + 1, :])
    earlier = lax.broadcasted_iota(jnp.int32, (count, count), 0) < lax.broadcasted_iota(
        jnp.int32, (count, count), 1
    )
    before = dot(jnp.where(chosen, 1.0, 0.0).astype(LOW), jnp.where(earlier, 1.0, 0.0).astype(LOW))
    rank = jnp.where(chosen, before, -1.0)

    to_query, to_value = head_maps(heads // head, head)
    owner = lax.div(lax.broadcasted_iota(jnp.int32, (half, heads), 1), head).astype(F32)
    lane = lax.broadcasted_iota(jnp.int32, (half, experts), 1).astype(F32)
    wide = lax.broadcasted_iota(jnp.int32, (half, 2 * head), 1)
    kv_copy(v, p, 2).wait_recv()
    kv_forward(v, p).start()
    kv_copy(v, p, 1).wait_recv()
    kv_forward(v, p).wait_recv()

    for i in range(2):
        rows = slice(i * half, (i + 1) * half)
        logits = dot_nt(v.n1[rows, :], v.router1[v.task[i]])
        named = [lane == v.pickc[i, :, k:k + 1] for k in range(picks)]
        allowed = named[0]
        for k in range(1, picks):
            allowed = allowed | named[k]
        gates = masked_softmax(logits, allowed, 1)
        v.g1[rows, :] = gates
        kv = v.kv[i]
        for k in range(picks):
            at = picks * i + k
            mine = owner == v.pickc[i, :, k:k + 1]
            gate = jnp.sum(jnp.where(named[k], gates, 0.0), 1, keepdims=True)
            all_queries = v.gh[rows, 0:heads]
            query = dot(jnp.where(mine, all_queries, jnp.zeros_like(all_queries)), to_query)
            query = (query * head ** -0.5).astype(LOW)
            v.q8[at] = query
            scores = dot_nt(query, kv)
            expo = jnp.exp(scores - jnp.max(scores, 1, keepdims=True))
            total = jnp.sum(expo, 1, keepdims=True)
            low = expo.astype(LOW)
            v.act[at * half:(at + 1) * half, 0:4 * half] = low
            attended = dot(low, kv) / total
            v.att[at] = jnp.where(wide == 0, total, attended)
            spread = dot_nt((gate * attended).astype(LOW), to_value).astype(LOW)
            if k == 0:
                v.heads[rows, :] = jnp.where(mine, spread, jnp.zeros_like(spread))
            else:
                v.heads[rows, :] = jnp.where(mine, spread, v.heads[rows, :])
        middle = v.tok[rows, :].astype(F32) + dot(v.heads[rows, :], v.wo[...])
        v.mid[rows, :] = middle
        normal, _ = center(middle)
        normed = (normal * gain[1:2] + bias[1:2]).astype(LOW)
        v.n2[i] = normed
        for r in (4, 2, 1):
            row_copy(v, p, r, i).start()
        v.xa[0, i] = normed
        logits = dot_nt(v.router2[v.task[i]], normed)
        logits = jnp.concatenate([logits, jnp.zeros((16 - experts, half), F32)], 0)
        gates = masked_softmax(logits, rank[:, rows] >= 0.0, 0)
        v.g2[:, rows] = gates
        for g in range(8):
            v.meta[g, 0:2, rows] = rank[2 * g:2 * g + 2, rows]
            v.meta[g, 2:4, rows] = gates[2 * g:2 * g + 2, :]
            v.meta[g, 4:16, rows] = jnp.zeros((12, half), F32)
        if i == 0:
            cot_near(v, p)
        else:
            cot_far(v, p)
            rows_near(v, p, 0)
    v.ma[0] = v.meta[p.group(0)]
    for r in range(1, 8):
        meta_copy(v, p, r).start()


def chunk_first(v, p, c):
    return remote(v.ra.at[c], v.rb.at[c], v.s1s.at[c], v.s1r.at[c], p.toward)


def chunk_middle(v, p, c):
    return remote(v.rb.at[c], v.rc.at[c], v.s2s.at[c], v.s2r.at[c], p.toward)


def chunk_back(v, p, c):
    return remote(v.ra.at[c], v.rc.at[c], v.s3s.at[c], v.s2r.at[c], p.outer)


def chunk_pair(v, p, src, c):
    to = p.y * v.ra.shape[0] + c
    return remote(src.at[c], v.chunks.at[to], v.ys.at[c], v.yr.at[c], (p.dp ^ 1, p.ex))


def chunk_cross(v, p, c, device):
    at = v.chunks.at[(1 - p.y) * v.ra.shape[0] + c]
    return remote(at, at, v.y2s.at[c], v.yr.at[c], device)


def chunk_land(v, p, c):
    at = v.chunks.at[(1 - p.y) * v.ra.shape[0] + c]
    return remote(v.ra.at[c], at, v.ys.at[c], v.yr.at[c], (p.dp ^ 1, p.ex))


def only_mid(c):
    return lax.rem(c, 8) == 2


def only_end(c):
    return lax.rem(c, 8) == 5


def chunk_own(v, p, src, c):
    to = p.y * v.ra.shape[0] + c
    return pltpu.make_async_copy(src.at[c], v.chunks.at[to], v.ls.at[c])


def tick(v, p, t):
    chunks = v.ra.shape[0]

    @pl.when(p.is_mid & (t < chunks))
    def _():
        c = jnp.minimum(t, chunks - 1)
        chunk_first(v, p, c).wait_recv()
        v.rb[c] = (v.ra[c].astype(F32) + v.rb[c].astype(F32)).astype(LOW)
        chunk_middle(v, p, c).start()

    @pl.when(p.is_mid & (t >= 2) & (t < chunks + 2))
    def _():
        c = jnp.maximum(t - 2, 0)
        chunk_middle(v, p, c).wait_recv()
        v.ra[c] = (v.rb[c].astype(F32) + v.rc[c].astype(F32)).astype(LOW)
        chunk_back(v, p, c).start()

        @pl.when(jnp.logical_not(only_end(c)))
        def _():
            chunk_pair(v, p, v.ra, c).start()

        chunk_own(v, p, v.ra, c).start()

    @pl.when(p.is_end & (t >= 4) & (t < chunks + 4))
    def _():
        c = jnp.maximum(t - 4, 0)
        chunk_middle(v, p, c).wait_recv()

        @pl.when(jnp.logical_not(only_mid(c)))
        def _():
            chunk_pair(v, p, v.rc, c).start()

        chunk_own(v, p, v.rc, c).start()

    @pl.when((t >= HAND) & (t < chunks + HAND))
    def _():
        c = jnp.maximum(t - HAND, 0)

        @pl.when(p.is_mid & only_mid(c))
        def _():
            chunk_land(v, p, c).wait_recv()
            chunk_cross(v, p, c, p.outer).start()

        @pl.when(p.is_end & only_end(c))
        def _():
            chunk_land(v, p, c).wait_recv()
            chunk_cross(v, p, c, p.toward).start()


def ticks(v, p, first, after):
    def one(t, carry):
        tick(v, p, t)
        return carry

    lax.fori_loop(first, after, one, 0)


def chunks_done(v, p):
    chunks = v.ra.shape[0]

    def one(c, carry):
        @pl.when(p.is_end)
        def _():
            chunk_first(v, p, c).wait_send()

            @pl.when(jnp.logical_not(only_mid(c)))
            def _():
                chunk_pair(v, p, v.rc, c).wait_send()

            chunk_own(v, p, v.rc, c).wait()

            @pl.when(only_end(c))
            def _():
                chunk_cross(v, p, c, p.toward).wait_send()

            @pl.when(jnp.logical_not(only_end(c)))
            def _():
                chunk_land(v, p, c).wait_recv()

        @pl.when(p.is_mid)
        def _():
            chunk_middle(v, p, c).wait_send()
            chunk_back(v, p, c).wait_send()

            @pl.when(jnp.logical_not(only_end(c)))
            def _():
                chunk_pair(v, p, v.ra, c).wait_send()

            chunk_own(v, p, v.ra, c).wait()

            @pl.when(only_mid(c))
            def _():
                chunk_cross(v, p, c, p.outer).wait_send()

            @pl.when(jnp.logical_not(only_mid(c)))
            def _():
                chunk_land(v, p, c).wait_recv()

        return carry

    lax.fori_loop(0, chunks, one, 0)


def weight_loads(v, p, j):
    return (
        pltpu.make_async_copy(v.we_all.at[p.y * 2 + j], v.we, v.wsem.at[0]),
        pltpu.make_async_copy(v.wr_all.at[p.y * 2 + j], v.wr, v.wsem.at[1]),
    )


def source_rows(r):
    return pl.ds(pl.multiple_of(r * CAP, CAP), CAP)


def slot_hits(v, r, j):
    sub = lax.broadcasted_iota(jnp.int32, (CAP, 2 * CAP), 0).astype(F32)
    return sub == v.ma[r, j:j + 1, :]


def dispatch(v, r, j):
    d = v.xa.shape[3]
    hit = slot_hits(v, r, j)
    pick = jnp.where(hit, 1.0, 0.0).astype(LOW)
    gate = jnp.sum(jnp.where(hit, v.ma[r, j + 2:j + 3, :], 0.0), 1, keepdims=True)
    at = source_rows(r)
    rows = dot(pick, v.xa[r].reshape(2 * CAP, d))
    v.pr[j, at, :] = rows.astype(LOW)
    v.xrt[:, at] = rows.T.astype(LOW)
    rows = gate * dot(pick, v.ca[r].reshape(2 * CAP, d))
    v.gr[j, at, :] = rows.astype(LOW)
    v.gpt[:, at] = rows.T.astype(LOW)


def columns(v, j, f):
    cols = pl.ds(pl.multiple_of(f * 256, 256), 256)
    step = 512
    for b in range(v.act.shape[0] // step):
        rows = slice(b * step, (b + 1) * step)
        value, slope = gelu_parts(dot(v.pr[j, rows, :], v.we[:, cols]))
        v.act[rows, cols] = value.astype(LOW)
        v.gh[rows, cols] = (dot_nt(v.gr[j, rows, :], v.wr[cols, :]) * slope).astype(LOW)


def weight_grads(v, p, j, f):
    cols = pl.ds(pl.multiple_of(f * 256, 256), 256)
    first = j * (v.ra.shape[0] // 2) + 2 * f
    v.ra[first] = dot(v.gpt[...], v.act[:, cols]).astype(LOW)
    v.ra[first + 1] = dot(v.xrt[...], v.gh[:, cols]).astype(LOW)

    @pl.when(p.is_end)
    def _():
        chunk_first(v, p, first).start()
        chunk_first(v, p, first + 1).start()


def produce(v, n, j):
    size = v.act.shape[0] // 2
    at = pl.ds(pl.multiple_of(n * size, size), size)
    v.pr[j, at, :] = dot(v.act[at, :], v.wr[...]).astype(LOW)
    v.gr[j, at, :] = dot_nt(v.gh[at, :], v.we[...]).astype(LOW)

    def gates(m):
        r = n * (size // CAP) + m
        made = v.pr[j, source_rows(r), :].astype(F32)
        hit = slot_hits(v, r, j)
        pick = jnp.where(hit, 1.0, 0.0).astype(LOW)
        seen = dot(pick, v.ca[r].reshape(2 * CAP, made.shape[1]))
        inner = jnp.sum(made * seen, 1, keepdims=True)
        part = jnp.sum(jnp.where(hit, inner, 0.0), 0, keepdims=True)
        v.dgs[r, j] = jnp.broadcast_to(part, (8, 2 * CAP))

    for m in range(size // CAP):
        gates(m)


def gate_copy(v, p, r):
    return remote(v.dgs.at[r], v.dg.at[p.group(0)], v.gs.at[r], v.gv.at[r], p.peer(r))


def part_core(v, p, r, which):
    ref = (v.gr, v.pr)[which]
    at = 4 * which + lax.div(r, 2)
    return remote(ref.at[:, source_rows(r), :], v.xa.at[at], v.k1s.at[at], v.k1r.at[at], p.peer(1))


def part_x(v, p, r, which, i):
    ref = (v.gr, v.pr)[which]
    at = 4 * which + r // 2 - 1
    return remote(
        ref.at[i, source_rows(r), :], v.ca.at[at, i], v.k2s.at[at, i], v.k2r.at[at, i], p.peer(2)
    )


def part_y(v, p, which, i):
    ref = (v.gr, v.pr)[which]
    at = 4 * which + 1
    return remote(
        ref.at[i, source_rows(4), :], v.ca.at[at, i], v.k2s.at[at, i], v.k2r.at[at, i], p.peer(4)
    )


def combine(v, r, which):
    lane = lax.broadcasted_iota(jnp.int32, (2 * CAP, CAP), 1).astype(F32)
    meta = v.ma[r].T
    at = source_rows(r)
    ref = (v.gr, v.pr)[which]
    total = jnp.zeros((2 * CAP, ref.shape[2]), F32)
    for j in range(2):
        hit = lane == meta[:, j:j + 1]
        weight = 1.0 if which == 0 else meta[:, 2 + j:3 + j]
        total = total + dot(jnp.where(hit, weight, 0.0).astype(LOW), ref[j, at, :])
    ref[0, at, :] = total[:CAP].astype(LOW)
    ref[1, at, :] = total[CAP:].astype(LOW)


def send_parts(v, p, which):
    def odd(n, carry):
        r = 7 - 2 * n
        combine(v, r, which)
        part_core(v, p, r, which).start()
        return carry

    lax.fori_loop(0, 4, odd, 0)

    def even(n, carry):
        r = jnp.where(n < 2, 6 - 4 * n, 12 - 4 * n)
        combine(v, r, which)
        part_core(v, p, r, which).wait_recv()
        ref = (v.gr, v.pr)[which]
        at = source_rows(r)
        ref[:, at, :] = (
            ref[:, at, :].astype(F32) + v.xa[4 * which + lax.div(r, 2)].astype(F32)
        ).astype(LOW)
        return carry

    lax.fori_loop(0, 2, even, 0)
    if which == 0:
        for i in range(2):
            for r in (6, 2):
                part_x(v, p, r, which, i).start()
    lax.fori_loop(2, 4, even, 0)


def relay_parts(v, p, which, i):
    ref = (v.gr, v.pr)[which]
    part_x(v, p, 6, which, i).wait_recv()
    at = source_rows(4)
    ref[i, at, :] = (ref[i, at, :].astype(F32) + v.ca[4 * which + 2, i].astype(F32)).astype(LOW)
    part_y(v, p, which, i).start()
    part_x(v, p, 2, which, i).wait_recv()


def own_sum(v, i, which):
    ref = (v.gr, v.pr)[which]
    total = ref[i, 0:CAP, :].astype(F32) + v.ca[4 * which, i].astype(F32)
    return total + v.ca[4 * which + 1, i].astype(F32)


def piece(v, g, c, q):
    at = FIRST[g] + c * PIECE[g]
    return v.act.at[
        pl.ds(pl.multiple_of(at, 16), PIECE[g]), pl.ds(pl.multiple_of(q * 384, 128), 384)
    ]


def spans(g, start, count):
    while count > 0:
        n, row = divmod(start, PIECE[g])
        size = min(count, PIECE[g] - row)
        yield n, row, size
        start, count = start + size, count - size


def place_rows(v, g, start, value):
    d = value.shape[1]
    done = 0
    for n, row, size in spans(g, start, value.shape[0]):
        at = FIRST[g] + (n // 4) * PIECE[g] + row
        q = n % 4
        v.act[at:at + size, q * d:(q + 1) * d] = value[done:done + size].astype(LOW)
        done += size


def place_tasks(v, g, start, per_image):
    experts, d = per_image[0].shape
    for j in range(v.router1.shape[0]):
        mine = [jnp.where(v.task[i] == j, per_image[i], 0.0) for i in range(2)]
        total = mine[0] + mine[1]
        if experts < 16:
            total = jnp.concatenate([total, jnp.zeros((16 - experts, d), F32)], 0)
        place_rows(v, g, start + 16 * j, total)


def back_first(v, i):
    count, d = v.tok.shape
    half = count // 2
    heads = v.heads.shape[1]
    experts = v.router2.shape[1]
    rows = slice(i * half, (i + 1) * half)
    grad_gates = jnp.concatenate([v.dg[g, j, 0:1, rows] for g in range(8) for j in range(2)], 0)
    gates = v.g2[:, rows]
    grad_logits = gates * (grad_gates - jnp.sum(gates * grad_gates, 0, keepdims=True))
    grad_logits = grad_logits[0:experts].astype(LOW)
    gain = v.gain[1:2]
    grad = own_sum(v, i, 0) + dot_tn(grad_logits, v.router2[v.task[i]])
    normal, scale = center(v.mid[rows, :])
    grad_gain = jnp.sum(grad * normal, 0, keepdims=True)
    grad_bias = jnp.sum(grad, 0, keepdims=True)
    if i == 0:
        v.small[0, 1:2, :] = grad_gain
        v.small[0, 3:4, :] = grad_bias
    else:
        v.small[0, 1:2, :] = v.small[0, 1:2, :] + grad_gain
        v.small[0, 3:4, :] = v.small[0, 3:4, :] + grad_bias
    total = v.cot[i].astype(F32) + center_back(grad, normal, scale, gain)
    v.gtok[rows, :] = total
    low = total.astype(LOW)
    v.act[rows, BRANCH:BRANCH + d] = low
    v.act[rows, 0:heads] = dot_nt(low, v.wo[...]).astype(LOW)
    return dot(grad_logits, v.n2[i])


def back_middle(v, per_image):
    count, d = v.tok.shape
    place_rows(v, 0, 0, dot_tn(v.heads[...], v.act[0:count, BRANCH:BRANCH + d]))
    place_tasks(v, 0, v.heads.shape[1], per_image)


def back_attention(v, i, pause):
    count, d = v.tok.shape
    half = count // 2
    heads = v.heads.shape[1]
    head = v.kv.shape[2] // 2
    picks = v.pick.shape[1]
    experts = v.router1.shape[1]
    to_query, to_value = head_maps(heads // head, head)
    owner = lax.div(lax.broadcasted_iota(jnp.int32, (half, heads), 1), head).astype(F32)
    lane = lax.broadcasted_iota(jnp.int32, (half, experts), 1).astype(F32)
    rows = slice(i * half, (i + 1) * half)
    lower = slice(count + i * half, count + (i + 1) * half)
    kv = v.kv[i]
    gates = v.g1[rows, :]
    grad_gates = jnp.zeros((half, experts), F32)
    grad_pair = jnp.zeros((2 * head, 4 * half), F32)
    for k in range(picks):
        at = picks * i + k
        mine = owner == v.pickc[i, :, k:k + 1]
        named = lane == v.pickc[i, :, k:k + 1]
        gate = jnp.sum(jnp.where(named, gates, 0.0), 1, keepdims=True)
        grad_heads = v.act[rows, 0:heads]
        grad = dot(jnp.where(mine, grad_heads, jnp.zeros_like(grad_heads)), to_value)
        attended = v.att[at]
        total = attended[:, 0:1]
        grad_gates = grad_gates + jnp.where(named, jnp.sum(grad * attended, 1, keepdims=True), 0.0)
        grad = ((gate * grad).astype(LOW).astype(F32) / total).astype(LOW)
        inner = jnp.sum(grad.astype(F32) * attended, 1, keepdims=True)
        expo = v.gh[at * half:(at + 1) * half, 0:4 * half]
        grad_scores = (expo.astype(F32) * (dot_nt(grad, kv) - inner)).astype(LOW)
        grad_query = (dot(grad_scores, kv) * head ** -0.5).astype(LOW)
        spread = dot_nt(grad_query, to_query).astype(LOW)
        if k == 0:
            v.act[lower, 0:heads] = jnp.where(mine, spread, jnp.zeros_like(spread))
        else:
            v.act[lower, 0:heads] = jnp.where(mine, spread, v.act[lower, 0:heads])
        grad_pair = grad_pair + dot(v.q8[at].astype(F32).T.astype(LOW), grad_scores)
        grad_pair = grad_pair + dot(grad.astype(F32).T.astype(LOW), expo)
        pause(i, k)
    grad_logits = gates * (grad_gates - jnp.sum(gates * grad_gates, 1, keepdims=True))
    v.gl1[rows, :] = grad_logits.astype(LOW)
    for r in range(4):
        v.dkv[r, i] = grad_pair[:, r * half:(r + 1) * half].astype(LOW)


def pair_copy(v, p, r, i):
    return remote(v.dkv.at[r, i], v.din.at[r, i], v.ps.at[r, i], v.pr_sem.at[r, i], p.peer(r))


def pair_sum(v, i):
    pair = v.dkv[0, i].astype(F32)
    for r in (1, 2, 3):
        pair = pair + v.din[r, i].astype(F32)
    return pair


def back_query(v):
    count, d = v.tok.shape
    half = count // 2
    heads = v.heads.shape[1]
    width = v.kv.shape[2]
    grad = dot_tn(v.act[count:2 * count, 0:heads], v.n1[...])
    place_rows(v, 1, 0, grad[0:SPLIT])
    place_rows(v, 2, 0, grad[SPLIT:heads])
    rows = (slice(0, half), slice(half, count))
    per_image = [dot_tn(v.gl1[at, :], v.n1[at, :]) for at in rows]
    place_tasks(v, 2, heads - SPLIT + width, per_image)


def back_pair(v):
    count, d = v.tok.shape
    half = count // 2
    grad = dot(pair_sum(v, 0).astype(LOW), v.n1[0:half, :])
    grad = grad + dot(pair_sum(v, 1).astype(LOW), v.n1[half:count, :])
    place_rows(v, 2, v.heads.shape[1] - SPLIT, grad)


def back_last(v):
    count, d = v.tok.shape
    half = count // 2
    heads = v.heads.shape[1]
    gain = v.gain[0:1]
    grad_gain = jnp.zeros((1, d), F32)
    grad_bias = jnp.zeros((1, d), F32)
    for i in range(2):
        rows = slice(i * half, (i + 1) * half)
        lower = slice(count + i * half, count + (i + 1) * half)
        grad = dot(v.act[lower, 0:heads], v.wq[...])
        grad = grad + dot(pair_sum(v, i).T.astype(LOW), v.wkv[...])
        grad = grad + dot(v.gl1[rows, :], v.router1[v.task[i]])
        normal, scale = center(v.tok[rows, :].astype(F32))
        grad_gain = grad_gain + jnp.sum(grad * normal, 0, keepdims=True)
        grad_bias = grad_bias + jnp.sum(grad, 0, keepdims=True)
        v.gtok[rows, :] = v.gtok[rows, :] + center_back(grad, normal, scale, gain)
    v.small[0, 0:1, :] = grad_gain
    v.small[0, 2:3, :] = grad_bias


def count_usage(v):
    count, d = v.tok.shape
    half = count // 2
    picks = v.pick.shape[1]
    number = lax.broadcasted_iota(jnp.int32, (16, half), 0)
    task = lax.broadcasted_iota(jnp.int32, (16, 128), 1)
    v.small[0] = jnp.zeros_like(v.small[0])
    for which in range(2):
        table = jnp.zeros((16, 128), F32)
        for i in range(2):
            named = jnp.zeros((16, half), F32)
            for k in range(picks):
                if which == 0:
                    row = v.pick[i, k:k + 1, :]
                else:
                    row = v.pickt[k:k + 1, i * half:(i + 1) * half]
                named = named + jnp.where(number == row, 1.0, 0.0)
            table = table + jnp.where(task == v.task[i], jnp.sum(named, 1, keepdims=True), 0.0)
        v.small[0, 8 + 16 * which:24 + 16 * which, 0:128] = table


class Shared:
    def __init__(self, v, p, g):
        self.v, self.p, self.g = v, p, g
        core, mine = p.core, p.spot
        half_in, piece_in, zbuf, shared = v.half_in[g], v.piece_in[g], v.zbuf[g], v.shared[g]
        self.half_in, self.piece_in = half_in, piece_in

        def half(c):
            return v.act.at[pl.ds(pl.multiple_of(FIRST[g] + c * PIECE[g], 16), PIECE[g]), :]

        partner = p.peer(1)
        s, r = v.hs.at[g], v.hr.at[g]
        self.own_half = half(core)
        self.first = remote(half(1 - core), half_in, s.at[0], r.at[0], partner)
        beside, across = p.plane(1), p.plane(2)
        self.to_x = [
            remote(piece(v, g, core, mine ^ q), piece_in.at[n], s.at[n + 1], r.at[n + 1], beside)
            for n, q in enumerate((3, 1))
        ]
        self.own = piece(v, g, core, mine)
        self.other = piece(v, g, core, mine ^ 2)
        self.to_y = remote(self.other, piece_in.at[2], s.at[3], r.at[3], across)
        zown, zb, zc, zall = (zbuf.at[n] for n in range(4))
        self.z = (zown, zb, zc, zall)
        self.in_end = remote(zown, zb, s.at[4], r.at[4], p.toward)
        self.mid = remote(zb, zc, s.at[4], r.at[5], p.toward)
        self.out_mid = remote(zall, zall, s.at[5], r.at[6], p.outer)
        place = core * 4 + mine
        self.own_copy = pltpu.make_async_copy(zall, shared.at[place], v.osem.at[2 + g])
        self.back_y = remote(zall, shared.at[place], s.at[6], r.at[7], across)
        there = shared.at[core * 4 + (mine ^ 2)]
        self.from_y = remote(zall, there, s.at[6], r.at[7], across)
        self.back_x = [
            remote(ref, ref, s.at[7 + n], r.at[8 + n], beside)
            for n, ref in enumerate((shared.at[place], there))
        ]
        self.from_x = [
            remote(ref, ref, s.at[7 + n], r.at[8 + n], beside)
            for n, ref in enumerate(
                (shared.at[core * 4 + (mine ^ 1)], shared.at[core * 4 + (mine ^ 3)])
            )
        ]
        ours = shared.at[pl.ds(core * 4, 4)]
        theirs = shared.at[pl.ds((1 - core) * 4, 4)]
        self.last = remote(ours, ours, s.at[9], r.at[10], partner)
        self.last_in = remote(theirs, theirs, s.at[9], r.at[10], partner)

    def stage(self, n):
        v, p, g = self.v, self.p, self.g
        zown, zb, zc, zall = self.z
        if n == 0:
            self.first.start()
        if n == 1:
            self.first.wait_recv()
            own = self.own_half
            own[...] = (own[...].astype(F32) + self.half_in[...].astype(F32)).astype(LOW)
            for copy in self.to_x:
                copy.start()
        if n == 2:
            self.to_x[0].wait_recv()
            ref = self.other
            ref[...] = (ref[...].astype(F32) + self.piece_in[0].astype(F32)).astype(LOW)
            self.to_y.start()
        if n == 3:
            self.to_x[1].wait_recv()
            total = self.own[...].astype(F32) + self.piece_in[1].astype(F32)
            self.to_y.wait_recv()
            zown[...] = (total + self.piece_in[2].astype(F32)).astype(LOW)

            @pl.when(p.is_end)
            def _():
                self.in_end.start()

        if n == 4:
            @pl.when(p.is_mid)
            def _():
                self.in_end.wait_recv()
                zb[...] = (zown[...].astype(F32) + zb[...].astype(F32)).astype(LOW)
                self.mid.start()

        if n == 5:
            @pl.when(p.is_mid)
            def _():
                self.mid.wait_recv()
                zall[...] = (zb[...].astype(F32) + zc[...].astype(F32)).astype(LOW)
                self.out_mid.start()

        if n == 6:
            @pl.when(p.is_end)
            def _():
                self.out_mid.wait_recv()

            self.own_copy.start()
            self.back_y.start()
        if n == 7:
            self.own_copy.wait()
            self.from_y.wait_recv()
            for copy in self.back_x:
                copy.start()
        if n == 8:
            for copy in self.from_x:
                copy.wait_recv()
            self.last.start()
        if n == 9:
            self.last_in.wait_recv()
            for copy in [self.first, *self.to_x, self.to_y, self.back_y, *self.back_x, self.last]:
                copy.wait_send()

            @pl.when(p.is_end)
            def _():
                self.in_end.wait_send()

            @pl.when(p.is_mid)
            def _():
                self.mid.wait_send()
                self.out_mid.wait_send()


class Small:
    def __init__(self, v, p):
        self.v, self.p = v, p

        def exchange(n, device):
            return remote(v.small.at[n], v.small_in.at[n], v.ss.at[n], v.sr.at[n], device)

        self.around = [exchange(0, p.peer(1)), exchange(1, p.plane(1)), exchange(2, p.plane(2))]
        self.in_end = exchange(3, p.toward)
        self.mid = exchange(4, p.toward)
        self.out_mid = remote(v.stats, v.stats, v.ss.at[5], v.sr.at[5], p.outer)

    def stage(self, n):
        v, p = self.v, self.p
        if n == 0:
            self.around[0].start()
        if n in (1, 2, 3):
            self.around[n - 1].wait_recv()
            v.small[n] = v.small[n - 1] + v.small_in[n - 1]
            if n < 3:
                self.around[n].start()
            else:
                @pl.when(p.is_end)
                def _():
                    self.in_end.start()

        if n == 4:
            @pl.when(p.is_mid)
            def _():
                self.in_end.wait_recv()
                v.small[4] = v.small[3] + v.small_in[3]
                self.mid.start()

        if n == 5:
            @pl.when(p.is_mid)
            def _():
                self.mid.wait_recv()
                v.stats[...] = v.small[4] + v.small_in[4]
                self.out_mid.start()

        if n == 6:
            @pl.when(p.is_end)
            def _():
                self.out_mid.wait_recv()
                self.in_end.wait_send()

            @pl.when(p.is_mid)
            def _():
                self.mid.wait_send()
                self.out_mid.wait_send()

            for copy in self.around:
                copy.wait_send()


def layer_kernel(v):
    p = Place()
    v.half_in = (v.half_in0, v.half_in1, v.half_in2)
    v.piece_in = (v.piece_in0, v.piece_in1, v.piece_in2)
    v.zbuf = (v.zbuf0, v.zbuf1, v.zbuf2)
    v.shared = (v.shared0, v.shared1, v.shared2)
    v.barrier = pltpu.get_barrier_semaphore()
    for r in range(1, 8):
        pl.semaphore_signal(v.barrier, 1, device_id=p.peer(r), device_id_type=MESH)
    pl.semaphore_signal(v.barrier, 1, device_id=p.toward, device_id_type=MESH)

    @pl.when(p.is_mid)
    def _():
        pl.semaphore_signal(v.barrier, 1, device_id=p.outer, device_id_type=MESH)

    for load in weight_loads(v, p, 0):
        load.start()
    front(v, p)

    spill = pltpu.make_async_copy(v.act.at[:, pl.ds(0, v.expo.shape[1])], v.expo, v.osem.at[1])
    spill.start()
    rows_far(v, p, 0)
    row_copy(v, p, 1, 0).wait_recv()
    row_copy(v, p, 1, 1).wait_recv()
    cot_copy(v, p, 1).wait_recv()
    meta_copy(v, p, 1).wait_recv()
    dispatch(v, 0, 0)
    dispatch(v, 1, 0)
    rows_near(v, p, 1)
    for load in weight_loads(v, p, 0):
        load.wait()
    for r in (2, 4):
        meta_copy(v, p, r).wait_recv()
        dispatch(v, r, 0)
    for r in (3, 5):
        for i in range(2):
            row_forward(v, p, r - 1, i).wait_recv()
        cot_forward(v, p, r - 1).wait_recv()
        meta_copy(v, p, r).wait_recv()
        dispatch(v, r, 0)
    rows_far(v, p, 1)
    meta_copy(v, p, 6).wait_recv()
    dispatch(v, 6, 0)
    for i in range(2):
        row_forward(v, p, 6, i).wait_recv()
    cot_forward(v, p, 6).wait_recv()
    meta_copy(v, p, 7).wait_recv()
    dispatch(v, 7, 0)
    spill.wait()

    def first_columns(f, carry):
        columns(v, 0, f)
        weight_grads(v, p, 0, f)

        return carry

    lax.fori_loop(0, 6, first_columns, 0, unroll=2)
    tick(v, p, 0)

    def first_produce(n, carry):
        produce(v, n, 0)
        tick(v, p, 1 + n)
        return carry

    lax.fori_loop(0, 2, first_produce, 0)
    for load in weight_loads(v, p, 1):
        load.start()

    def second_dispatch(r, carry):
        dispatch(v, r, 1)
        return carry

    lax.fori_loop(0, 8, second_dispatch, 0)
    tick(v, p, 3)
    for i in range(2):
        for r in (1, 2, 4):
            row_copy(v, p, r, i).wait_send()
        for r in (2, 4):
            row_relay(v, p, r, i).wait_send()
        for r in (2, 4, 6):
            row_forward(v, p, r, i).wait_send()
    pl.semaphore_signal(v.free_core, 1, device_id=p.peer(1), device_id_type=MESH)
    for load in weight_loads(v, p, 1):
        load.wait()

    def second_columns(f, carry):
        columns(v, 1, f)

        @pl.when(lax.rem(f, 2) == 1)
        def _():
            tick(v, p, 4 + lax.div(f, 2))

        return carry

    lax.fori_loop(0, 6, second_columns, 0, unroll=2)

    def second_produce(n, carry):
        produce(v, n, 1)
        tick(v, p, 7 + n)
        return carry

    lax.fori_loop(0, 2, second_produce, 0)
    for r in range(1, 8):
        gate_copy(v, p, r).start()
    v.dg[p.group(0)] = v.dgs[0]
    for r in (1, 2, 4):
        cot_copy(v, p, r).wait_send()
    for r in (2, 4):
        cot_relay(v, p, r).wait_send()
    for r in (2, 4, 6):
        cot_forward(v, p, r).wait_send()
    for q in (1, 2):
        pl.semaphore_signal(v.free_plane, 1, device_id=p.plane(q), device_id_type=MESH)
    pl.semaphore_wait(v.free_core, 1)
    pl.semaphore_wait(v.free_plane, 2)
    send_parts(v, p, 0)
    tick(v, p, 9)

    def second_grads(f, carry):
        weight_grads(v, p, 1, f)
        return carry

    lax.fori_loop(0, 6, second_grads, 0)
    refill = pltpu.make_async_copy(v.expo, v.gh.at[:, pl.ds(0, v.expo.shape[1])], v.osem.at[1])
    refill.start()
    relay_parts(v, p, 0, 0)
    tick(v, p, 10)
    send_parts(v, p, 1)
    for i in range(2):
        for r in (6, 2):
            part_x(v, p, r, 1, i).start()
    tick(v, p, 11)
    count_usage(v)
    v.act[FIRST[0]:FIRST[2] + 2 * PIECE[2], :] = jnp.zeros(
        (2 * sum(PIECE), v.act.shape[1]), LOW
    )
    for r in range(1, 8):
        gate_copy(v, p, r).wait_recv()
    part_y(v, p, 0, 0).wait_recv()
    per_image = [back_first(v, 0)]
    relay_parts(v, p, 0, 1)
    tick(v, p, 12)
    refill.wait()
    early, late, rest = Shared(v, p, 0), Shared(v, p, 1), Shared(v, p, 2)
    small = Small(v, p)

    def pause(i, k):
        at = 4 * i + k
        if at == 1:
            tick(v, p, 13)
        if at == 3:
            tick(v, p, 14)
        if at == 5:
            early.stage(1)
            tick(v, p, 17)
        if at == 7:
            tick(v, p, 18)

    back_attention(v, 0, pause)
    for r in (1, 2, 3):
        pair_copy(v, p, r, 0).start()
    part_y(v, p, 0, 1).wait_recv()
    per_image.append(back_first(v, 1))
    tick(v, p, 15)
    back_middle(v, per_image)
    early.stage(0)
    tick(v, p, 16)
    back_attention(v, 1, pause)
    for r in (1, 2, 3):
        pair_copy(v, p, r, 1).start()
    back_query(v)
    late.stage(0)
    early.stage(2)
    tick(v, p, 19)
    late.stage(1)
    for i in range(2):
        for r in (1, 2, 3):
            pair_copy(v, p, r, i).wait_recv()
    back_pair(v)
    rest.stage(0)
    early.stage(3)
    back_last(v)
    small.stage(0)
    rest.stage(1)
    late.stage(2)
    tick(v, p, 20)
    small.stage(1)
    early.stage(4)
    rest.stage(2)
    late.stage(3)
    relay_parts(v, p, 1, 0)
    tick(v, p, 21)
    small.stage(2)
    early.stage(5)
    rest.stage(3)
    late.stage(4)
    relay_parts(v, p, 1, 1)
    tick(v, p, 22)
    small.stage(3)
    early.stage(6)
    rest.stage(4)
    late.stage(5)
    tick(v, p, 23)
    small.stage(4)
    rest.stage(5)
    late.stage(6)
    tick(v, p, 24)
    small.stage(5)
    early.stage(7)
    rest.stage(6)
    late.stage(7)
    for i in range(2):
        part_y(v, p, 1, i).wait_recv()
        rows = slice(i * CAP, (i + 1) * CAP)
        v.out[rows, :] = (v.mid[rows, :] + own_sum(v, i, 1)).astype(LOW)
    tick(v, p, 25)
    small.stage(6)
    early.stage(8)
    rest.stage(7)
    late.stage(8)
    ticks(v, p, 26, 28)
    rest.stage(8)
    early.stage(9)
    late.stage(9)
    ticks(v, p, 28, v.ra.shape[0] + HAND)
    rest.stage(9)

    for i in range(2):
        for r in (1, 2, 3):
            pair_copy(v, p, r, i).wait_send()
    for r in (1, 2):
        kv_copy(v, p, r).wait_send()
    kv_forward(v, p).wait_send()
    for r in range(1, 8):
        meta_copy(v, p, r).wait_send()
        gate_copy(v, p, r).wait_send()
    for which in range(2):
        for r in (1, 3, 5, 7):
            part_core(v, p, r, which).wait_send()
        for i in range(2):
            for r in (2, 6):
                part_x(v, p, r, which, i).wait_send()
            part_y(v, p, which, i).wait_send()
    chunks_done(v, p)


def layer_call(tok, cot, pick, pickt, task, gain, bias, wq, wk, wv, wo, router1, router2, we, wr):
    count, d = tok.shape
    half = count // 2
    heads = wq.shape[0]
    width = 2 * wk.shape[0]
    picks = pick.shape[1]
    experts = router1.shape[1]
    ff = we.shape[2]
    chunks = 4 * ff // 256
    vm = pltpu.VMEM
    anywhere = pl.ANY
    dma = pltpu.SemaphoreType.DMA
    return run_kernel(
        layer_kernel, "layer",
        dict(
            tok=(tok, vm), cot=(cot, vm), pick=(pick, vm), pickt=(pickt, vm),
            task=(task, pltpu.SMEM), gain=(gain, vm), bias=(bias, vm), wq=(wq, vm), wk=(wk, vm),
            wv=(wv, vm), wo=(wo, vm), router1=(router1, vm), router2=(router2, vm),
            we_all=(we, anywhere), wr_all=(wr, anywhere),
        ),
        dict(
            out=((count, d), LOW, vm), gtok=((count, d), F32, vm),
            chunks=((2 * chunks, d, 256), LOW, anywhere),
            **{f"shared{g}": ((8, PIECE[g], d), LOW, anywhere) for g in range(3)},
            stats=((40, d), F32, vm), expo=((8 * CAP, 4 * half), LOW, anywhere),
        ),
        dict(
            n1=vm((count, d), LOW), n2=vm((2, half, d), LOW), mid=vm((count, d), F32),
            pickc=vm((2, half, 8), F32), wkv=vm((width, d), LOW),
            heads=vm((count, heads), LOW), kv=vm((2, 4 * half, width), LOW),
            q8=vm((2 * picks, half, width), LOW), att=vm((2 * picks, half, width), F32),
            g1=vm((count, experts), F32), g2=vm((16, count), F32), meta=vm((8, 16, count), F32),
            xa=vm((8, 2, half, d), LOW), ca=vm((8, 2, half, d), LOW),
            ma=vm((8, 16, count), F32), we=vm((d, ff), LOW), wr=vm((ff, d), LOW),
            xrt=vm((d, 8 * CAP), LOW), gpt=vm((d, 8 * CAP), LOW),
            act=vm((8 * CAP, ff), LOW), gh=vm((8 * CAP, ff), LOW),
            pr=vm((2, 8 * CAP, d), LOW), gr=vm((2, 8 * CAP, d), LOW),
            ra=vm((chunks, d, 256), LOW), rb=vm((chunks, d, 256), LOW), rc=vm((chunks, d, 256), LOW),
            dgs=vm((8, 2, 8, count), F32), dg=vm((8, 2, 8, count), F32),
            small=vm((5, 40, d), F32), small_in=vm((5, 40, d), F32),
            gl1=vm((count, experts), LOW),
            dkv=vm((4, 2, width, half), LOW), din=vm((4, 2, width, half), LOW),
            **{f"half_in{g}": vm((PIECE[g], 4 * d), LOW) for g in range(3)},
            **{f"piece_in{g}": vm((3, PIECE[g], d), LOW) for g in range(3)},
            **{f"zbuf{g}": vm((4, PIECE[g], d), LOW) for g in range(3)},
            cs=dma((16,)), cv=dma((16,)), ks=dma((4,)), kr=dma((4,)), xs=dma((16, 2)), xv=dma((16, 2)),
            ms=dma((8,)), mv=dma((8,)), gs=dma((8,)), gv=dma((8,)), wsem=dma((2,)), osem=dma((5,)),
            s1s=dma((chunks,)), s1r=dma((chunks,)), s2s=dma((chunks,)), s2r=dma((chunks,)),
            s3s=dma((chunks,)), ys=dma((chunks,)), yr=dma((chunks,)), y2s=dma((chunks,)), ls=dma((chunks,)),
            k1s=dma((8,)), k1r=dma((8,)), k2s=dma((8, 2)), k2r=dma((8, 2)),
            ps=dma((4, 2)), pr_sem=dma((4, 2)), ss=dma((6,)), sr=dma((6,)), hs=dma((3, 10)),
            hr=dma((3, 11)),
            free_core=pltpu.SemaphoreType.REGULAR, free_plane=pltpu.SemaphoreType.REGULAR,
        ),
        0,
    )


def widen_kernel(
    c_ref, s0_ref, s1_ref, s2_ref, stats_ref,
    reduce_ref, expand_ref, query_ref, out_ref, key_ref, value_ref, one_ref, two_ref,
    gain_ref, first_ref, second_ref, usage_ref,
):
    for n in range(c_ref.shape[0] // 2):
        at = slice(n * 256, (n + 1) * 256)
        reduce_ref[0, at, :] = c_ref[2 * n].astype(F32).T
        expand_ref[0, :, at] = c_ref[2 * n + 1].astype(F32)

    @pl.when((pl.program_id(0) == 0) & (pl.program_id(1) == 0))
    def _():
        refs = (s0_ref, s1_ref, s2_ref)

        def unpack(ref, g, start):
            done = 0
            for n, row, size in spans(g, start, ref.shape[0]):
                ref[done:done + size, :] = refs[g][n, row:row + size, :].astype(F32)
                done += size

        wide, head = query_ref.shape[0], key_ref.shape[0]
        unpack(out_ref, 0, 0)
        unpack(query_ref.at[0:SPLIT, :], 1, 0)
        unpack(query_ref.at[SPLIT:wide, :], 2, 0)
        unpack(key_ref, 2, wide - SPLIT)
        unpack(value_ref, 2, wide - SPLIT + head)
        for ref, g, start in ((one_ref, 2, wide - SPLIT + 2 * head), (two_ref, 0, wide)):
            for j in range(ref.shape[0]):
                for n, row, size in spans(g, start + 16 * j, 16):
                    ref[j] = refs[g][n, row:row + size, :].astype(F32)[0:ref.shape[1]]
        gain_ref[...] = stats_ref[0:2, :]
        first_ref[...] = stats_ref[2, :]
        second_ref[...] = stats_ref[3, :]
        tasks, _, experts = usage_ref.shape
        for which in range(2):
            table = stats_ref[8 + 16 * which:24 + 16 * which, 0:128].T
            usage_ref[:, which, :] = table[0:tasks, 0:experts]


def widen_call(chunks, shared, stats, slots, d, ff, wide, head, tasks, experts):
    n = ff // 256
    per = PER
    whole = pl.BlockSpec(memory_space=pltpu.VMEM)
    shapes = (
        (wide, d), (wide, d), (head, d), (head, d), (tasks, experts, d), (tasks, experts, d),
        (2, d), (d,), (d,), (tasks, 2, experts),
    )
    return pl.pallas_call(
        widen_kernel,
        name="widen",
        grid=(slots, n // per),
        in_specs=[
            pl.BlockSpec((2 * per, d, 256), lambda s, f: (s * (n // per) + f, 0, 0)),
            whole, whole, whole, whole,
        ],
        out_specs=(
            pl.BlockSpec((1, per * 256, d), lambda s, f: (s, f, 0)),
            pl.BlockSpec((1, d, per * 256), lambda s, f: (s, 0, f)),
            *[whole] * len(shapes),
        ),
        out_shape=(
            jax.ShapeDtypeStruct((slots, ff, d), F32),
            jax.ShapeDtypeStruct((slots, d, ff), F32),
            *[jax.ShapeDtypeStruct(shape, F32) for shape in shapes],
        ),
        compiler_params=pltpu.CompilerParams(vmem_limit_bytes=56 * MIB),
    )(chunks, *shared, stats)


def body_fast(
    tokens,
    task_ids,
    attention_picks,
    feedforward_picks,
    norm_gain,
    norm_bias,
    query_weight,
    key_weight,
    value_weight,
    output_weight,
    attention_router,
    feedforward_router,
    expand_weight,
    reduce_weight,
    cotangent,
):
    images, patches, width = tokens.shape
    count = images * patches
    tasks, _, experts = attention_router.shape
    head = key_weight.shape[1]
    picks = attention_picks.shape[2]
    slots = expand_weight.shape[0]
    ff = expand_weight.shape[2]
    wide = query_weight.shape[1]
    tok = tokens.reshape(count, width)
    pickt = feedforward_picks.reshape(count, picks).T
    b = layer_call(
        tok, cotangent, jnp.swapaxes(attention_picks, 1, 2), pickt, task_ids, norm_gain, norm_bias,
        query_weight.T, key_weight.T, value_weight.T, output_weight,
        jnp.swapaxes(attention_router, 1, 2), jnp.swapaxes(feedforward_router, 1, 2),
        expand_weight, reduce_weight,
    )
    (
        grad_reduce, grad_expand, grad_query, grad_out, grad_key, grad_value, grad_one, grad_two,
        grad_gain, grad_first, grad_second, usage,
    ) = widen_call(
        b.chunks, (b.shared0, b.shared1, b.shared2), b.stats, slots, width, ff, wide, head, tasks,
        experts,
    )
    return (
        b.out.reshape(images, patches, width),
        b.gtok.reshape(images, patches, width),
        grad_gain,
        grad_first,
        grad_second,
        grad_query.T,
        grad_key.T,
        grad_value.T,
        grad_out,
        jnp.swapaxes(grad_one, 1, 2),
        jnp.swapaxes(grad_two, 1, 2),
        grad_expand,
        grad_reduce,
        jnp.swapaxes(usage, 0, 1),
    )


def normalize(value, gain, bias):
    mean = jnp.mean(value, -1, keepdims=True)
    centred = value - mean
    spread = jnp.mean(centred * centred, -1, keepdims=True)
    return centred * lax.rsqrt(spread + EPS) * gain + bias


def gate_weights(logits, picks_hot):
    chosen = jnp.sum(picks_hot * logits[..., None, :], -1)
    return jax.nn.softmax(chosen, -1)


def activate(value):
    return jax.nn.gelu(value, approximate=True)


def body(
    tokens,
    task_ids,
    attention_picks,
    feedforward_picks,
    norm_gain,
    norm_bias,
    query_weight,
    key_weight,
    value_weight,
    output_weight,
    attention_router,
    feedforward_router,
    expand_weight,
    reduce_weight,
    cotangent,
):
    images, patches, width = tokens.shape
    count = images * patches
    tasks = attention_router.shape[0]
    experts = attention_router.shape[2]
    head = key_weight.shape[1]
    picks = attention_picks.shape[2]
    slots = expand_weight.shape[0]
    groups = lax.axis_size("expert")
    lanes = groups * slots
    f32 = jnp.float32
    low_type = jnp.bfloat16
    inputs = tokens.astype(f32).reshape(count, width)
    expert_range = jnp.arange(experts, dtype=jnp.int32)
    task_hot = (task_ids[:, None] == jnp.arange(tasks, dtype=jnp.int32)[None, :]).astype(f32)
    task_low = task_hot.astype(low_type)
    attend_hot = (attention_picks[..., None] == expert_range).astype(f32)
    attend_low = attend_hot.astype(low_type)
    choices = feedforward_picks.reshape(count, picks)
    feed_hot = (choices[..., None] == expert_range).astype(f32)
    flat = choices.reshape(count * picks)
    marks = (flat[:, None] == expert_range[None, :]).astype(jnp.int32)
    before = jnp.cumsum(marks, axis=0) - marks
    position = flat * CAP + jnp.sum(before * marks, axis=1)
    first, first_back = jax.vjp(normalize, inputs, norm_gain[0], norm_bias[0])
    normed_one = first.astype(low_type)
    shaped_one = normed_one.reshape(images, patches, width)
    router_one = jnp.einsum(
        "it,tde->ide", task_low, attention_router, preferred_element_type=f32
    ).astype(low_type)
    logits_one = jnp.einsum("ipd,ide->ipe", shaped_one, router_one, preferred_element_type=f32)
    gates_one, gates_one_back = jax.vjp(lambda value: gate_weights(value, attend_hot), logits_one)
    queries_all = jnp.dot(normed_one, query_weight, preferred_element_type=f32).astype(low_type)
    queries_all = queries_all.reshape(images, patches, experts, head)
    queries = jnp.einsum(
        "ipke,ipeh->ipkh", attend_low, queries_all, preferred_element_type=f32
    ).astype(low_type)
    queries = queries.reshape(images, patches * picks, head)
    key_value = jnp.concatenate([key_weight, value_weight], 1)
    pair = jnp.dot(normed_one, key_value, preferred_element_type=f32).astype(low_type)
    pair = pair.reshape(images, patches, 2 * head)
    pair_all = lax.all_gather(pair, "expert", axis=1, tiled=True)
    keys_all = pair_all[:, :, :head]
    values_all = pair_all[:, :, head:]
    scores = jnp.einsum("irh,ish->irs", queries, keys_all, preferred_element_type=f32) * 0.125
    top = jnp.max(scores, -1, keepdims=True)
    expo = jnp.exp(scores - top)
    total = jnp.sum(expo, -1, keepdims=True)
    log_total = top + jnp.log(total)
    probs_low = (expo / total).astype(low_type)
    attended = jnp.einsum("irs,ish->irh", probs_low, values_all, preferred_element_type=f32)
    attended = attended.reshape(images, patches, picks, head)
    weighted = gates_one[..., None] * attended
    heads = jnp.einsum("ipke,ipkh->ipeh", attend_hot, weighted, precision=HIGH)
    heads = heads.reshape(count, experts * head).astype(low_type)
    middle = inputs + jnp.dot(heads, output_weight, preferred_element_type=f32)
    second, second_back = jax.vjp(normalize, middle, norm_gain[1], norm_bias[1])
    normed_two = second.astype(low_type)
    shaped_two = normed_two.reshape(images, patches, width)
    router_two = jnp.einsum(
        "it,tde->ide", task_low, feedforward_router, preferred_element_type=f32
    ).astype(low_type)
    logits_two = jnp.einsum(
        "ipd,ide->ipe", shaped_two, router_two, preferred_element_type=f32
    ).reshape(count, experts)
    gates_two, gates_two_back = jax.vjp(lambda value: gate_weights(value, feed_hot), logits_two)
    outgoing = (
        jnp.zeros((lanes * CAP, width), low_type)
        .at[position]
        .set(jnp.repeat(normed_two, picks, axis=0))
    )
    outgoing = outgoing.reshape(groups, slots * CAP, width)
    received = lax.all_to_all(outgoing, "expert", split_axis=0, concat_axis=0, tiled=True).reshape(
        groups, slots, CAP, width
    )
    hidden = jnp.einsum("nscd,sdf->nscf", received, expand_weight, preferred_element_type=f32)
    activated, activate_back = jax.vjp(activate, hidden)
    active_low = activated.astype(low_type)
    produced = jnp.einsum(
        "nscf,sfd->nscd", active_low, reduce_weight, preferred_element_type=f32
    ).astype(low_type)
    produced = produced.reshape(groups, slots * CAP, width)
    returned = lax.all_to_all(produced, "expert", split_axis=0, concat_axis=0, tiled=True).reshape(
        lanes * CAP, width
    )
    picked = returned[position].astype(f32).reshape(count, picks, width)
    final = middle + jnp.sum(gates_two[..., None] * picked, 1)
    output = final.astype(low_type).reshape(images, patches, width)
    grad_final = cotangent.astype(f32).reshape(count, width)
    grad_gates_two = jnp.sum(picked * grad_final[:, None, :], -1)
    grad_picked = (
        (gates_two[..., None] * grad_final[:, None, :])
        .astype(low_type)
        .reshape(count * picks, width)
    )
    grad_send = jnp.zeros((lanes * CAP, width), low_type).at[position].set(grad_picked)
    grad_send = grad_send.reshape(groups, slots * CAP, width)
    grad_produced = lax.all_to_all(
        grad_send, "expert", split_axis=0, concat_axis=0, tiled=True
    ).reshape(groups, slots, CAP, width)
    grad_reduce = jnp.einsum(
        "nscf,nscd->sfd", active_low, grad_produced, preferred_element_type=f32
    )
    grad_active = jnp.einsum(
        "nscd,sfd->nscf", grad_produced, reduce_weight, preferred_element_type=f32
    )
    grad_hidden = activate_back(grad_active)[0].astype(low_type)
    grad_expand = jnp.einsum("nscd,nscf->sdf", received, grad_hidden, preferred_element_type=f32)
    grad_rows = jnp.einsum(
        "nscf,sdf->nscd", grad_hidden, expand_weight, preferred_element_type=f32
    ).astype(low_type)
    grad_rows = grad_rows.reshape(groups, slots * CAP, width)
    grad_back = lax.all_to_all(
        grad_rows, "expert", split_axis=0, concat_axis=0, tiled=True
    ).reshape(lanes * CAP, width)
    grad_normed_two = jnp.sum(grad_back[position].astype(f32).reshape(count, picks, width), 1)
    grad_logits_two = (
        gates_two_back(grad_gates_two)[0].astype(low_type).reshape(images, patches, experts)
    )
    per_image_two = jnp.einsum(
        "ipd,ipe->ide", shaped_two, grad_logits_two, preferred_element_type=f32
    )
    grad_feed_router = jnp.einsum("it,ide->tde", task_hot, per_image_two, precision=HIGH)
    grad_normed_two = grad_normed_two + jnp.einsum(
        "ipe,ide->ipd", grad_logits_two, router_two, preferred_element_type=f32
    ).reshape(count, width)
    grad_middle_norm, grad_gain_two, grad_bias_two = second_back(grad_normed_two)
    grad_middle = grad_final + grad_middle_norm
    grad_branch = grad_middle.astype(low_type)
    grad_output = jnp.einsum("tc,td->cd", heads, grad_branch, preferred_element_type=f32)
    grad_heads = jnp.einsum(
        "td,cd->tc", grad_branch, output_weight, preferred_element_type=f32
    ).astype(low_type)
    grad_heads = grad_heads.reshape(images, patches, experts, head)
    grad_selected = jnp.einsum(
        "ipke,ipeh->ipkh", attend_low, grad_heads, preferred_element_type=f32
    )
    grad_gates_one = jnp.sum(attended * grad_selected, -1)
    grad_attended = (
        (gates_one[..., None] * grad_selected)
        .astype(low_type)
        .reshape(images, patches * picks, head)
    )
    scores_back = jnp.einsum("irh,ish->irs", queries, keys_all, preferred_element_type=f32) * 0.125
    probs_back = jnp.exp(scores_back - log_total)
    grad_values = jnp.einsum(
        "irs,irh->ish", probs_back.astype(low_type), grad_attended, preferred_element_type=f32
    )
    grad_probs = jnp.einsum("irh,ish->irs", grad_attended, values_all, preferred_element_type=f32)
    inner_sum = jnp.sum(probs_back * grad_probs, -1, keepdims=True)
    grad_scores = (probs_back * (grad_probs - inner_sum)).astype(low_type)
    grad_query_sel = (
        jnp.einsum("irs,ish->irh", grad_scores, keys_all, preferred_element_type=f32) * 0.125
    )
    grad_keys = jnp.einsum("irs,irh->ish", grad_scores, queries, preferred_element_type=f32) * 0.125
    grad_pair = jnp.concatenate([grad_keys, grad_values], -1)
    pair_sum = lax.psum_scatter(
        grad_pair.astype(jnp.bfloat16), "expert", scatter_dimension=1, tiled=True
    ).astype(jnp.float32)
    pair_sum = pair_sum.astype(low_type).reshape(count, 2 * head)
    grad_query_sel = grad_query_sel.reshape(images, patches, picks, head)
    grad_queries_all = jnp.einsum("ipke,ipkh->ipeh", attend_hot, grad_query_sel, precision=HIGH)
    grad_queries_all = grad_queries_all.astype(low_type).reshape(count, experts * head)
    grad_logits_one = gates_one_back(grad_gates_one)[0].astype(low_type)
    per_image_one = jnp.einsum(
        "ipd,ipe->ide", shaped_one, grad_logits_one, preferred_element_type=f32
    )
    grad_attend_router = jnp.einsum("it,ide->tde", task_hot, per_image_one, precision=HIGH)
    grad_query = jnp.einsum("td,tc->dc", normed_one, grad_queries_all, preferred_element_type=f32)
    grad_key_value = jnp.einsum("td,tc->dc", normed_one, pair_sum, preferred_element_type=f32)
    grad_normed_one = jnp.einsum(
        "tc,dc->td", grad_queries_all, query_weight, preferred_element_type=f32
    )
    grad_normed_one = grad_normed_one + jnp.einsum(
        "tc,dc->td", pair_sum, key_value, preferred_element_type=f32
    )
    grad_normed_one = grad_normed_one + jnp.einsum(
        "ipe,ide->ipd", grad_logits_one, router_one, preferred_element_type=f32
    ).reshape(count, width)
    grad_inputs_norm, grad_gain_one, grad_bias_one = first_back(grad_normed_one)
    grad_tokens = (grad_middle + grad_inputs_norm).reshape(images, patches, width)
    grad_gain = jnp.stack([grad_gain_one, grad_gain_two])
    grad_bias = jnp.stack([grad_bias_one, grad_bias_two])
    feed_shaped = feed_hot.reshape(images, patches, picks, experts)
    usage = jnp.stack(
        [
            jnp.einsum("it,ipke->te", task_hot, attend_hot, precision=HIGH),
            jnp.einsum("it,ipke->te", task_hot, feed_shaped, precision=HIGH),
        ]
    )
    shared = lax.psum(
        (
            grad_query,
            grad_key_value,
            grad_output,
            grad_attend_router,
            grad_feed_router,
            grad_gain,
            grad_bias,
            usage,
        ),
        ("dp", "expert"),
    )
    grad_expand_sum, grad_reduce_sum = (
        lax.psum(grad_expand.astype(jnp.bfloat16), "dp").astype(jnp.float32),
        lax.psum(grad_reduce.astype(jnp.bfloat16), "dp").astype(jnp.float32),
    )
    grad_key_sum = shared[1][:, :head]
    grad_value_sum = shared[1][:, head:]
    return (
        output,
        grad_tokens,
        shared[5],
        shared[6][0],
        shared[6][1],
        shared[0],
        grad_key_sum,
        grad_value_sum,
        shared[2],
        shared[3],
        shared[4],
        grad_expand_sum,
        grad_reduce_sum,
        shared[7],
    )


def solution(mesh):
    placed = (
        P("dp", "expert", None),
        P("dp"),
        P("dp", "expert", None),
        P("dp", "expert", None, None),
        P(),
        P(),
        P(),
        P(),
        P(),
        P(),
        P(),
        P(),
        P("expert", None, None),
        P("expert", None, None),
        P("dp", "expert", None),
    )
    fast = mesh.shape["dp"] == 8 and mesh.shape["expert"] == 4
    return jax.shard_map(
        body_fast if fast else body,
        mesh=mesh,
        in_specs=placed,
        out_specs=(
            P("dp", "expert", None),
            P("dp", "expert", None),
            P(),
            P(),
            P(),
            P(),
            P(),
            P(),
            P(),
            P(),
            P(),
            P("expert", None, None),
            P("expert", None, None),
            P(),
        ),
        check_vma=False,
    )
```
